32 devices in a mesh: batch: 4 (over x, core), seq: 8 (over z, y).
Axes of the slice: x: 2, y: 2, z: 4, core: 2. Of those that a mesh axis runs over, the one named last changes fastest.
Arguments:
- tokens: bfloat16 [8, 1, 1152, 512], P('batch', None, 'seq'), may hold values from -5 to 5
- cotangent: bfloat16 [8, 1, 1152, 512], P('batch', None, 'seq'), may hold values from -5 to 5
- doc_lengths: int32 [8, 1, 4], P('batch'), may hold values from 1 to 336, 384 in all within a row
- owners: int32 [6], replicated, may hold values from 0 to 3, as said below
- master: float32 [4, 8, 512, 512], P('batch', None, 'seq'), as said below
- first_moment: float32 [4, 8, 512, 512], P('batch', None, 'seq'), may hold values from -32 to 32
- second_moment: float32 [4, 8, 512, 512], P('batch', None, 'seq'), may hold values from 92.16 to 1228.8
- ln_gain: float32 [2, 512], replicated, may hold values from 0.5 to 1.5
- ln_bias: float32 [2, 512], replicated, may hold values from -1.2 to 1.2
- norm_m: float32 [4, 512], replicated, may hold values from -32 to 32
- norm_v: float32 [4, 512], replicated, may hold values from 92.16 to 1228.8
- slopes: float32 [8], replicated, may hold values from 0.0013020834 to 0.1
- slope_m: float32 [8], replicated, may hold values from -32768 to 32768
- slope_v: float32 [8], replicated, may hold values from 3072000 to 307200000
Outputs:
- mixed: float32 [8, 1, 1152, 512], P('batch', None, 'seq')
- input_grad: float32 [8, 1, 1152, 512], P('batch', None, 'seq')
- new_master: float32 [4, 8, 512, 512], P('batch', None, 'seq')
- new_first: float32 [4, 8, 512, 512], P('batch', None, 'seq')
- new_second: float32 [4, 8, 512, 512], P('batch', None, 'seq')
- new_low: bfloat16 [4, 8, 512, 512], P('batch', None, 'seq')
- new_norm: float32 [4, 512], replicated
- new_norm_m: float32 [4, 512], replicated
- new_norm_v: float32 [4, 512], replicated
- new_slopes: float32 [8], replicated
- new_slope_m: float32 [8], replicated
- new_slope_v: float32 [8], replicated
The draws below stay inside these ranges and needn't reach their ends.
Inputs may be any that keep to these rules, and one draw needn't show every extreme that they name: The owner of the two feed-forward matrices owns no other matrix and holds exactly 8 blocks; the pooling and query-key-value matrices have different owners; no owner holds more than 8 blocks. `master`: slots beyond an owner's blocks hold values that are only copied.
All inputs are finite; a program needn't handle non-finite values.
Results may differ from the reference program's by a relative error of at most 0.014.
Values may be sent and summed in bfloat16 or wider, within the bound.
A program may use at most 192 MiB of HBM per device.

```python
import math
import jax
import jax.numpy as jnp
import numpy as np
from jax import lax

D = 512
H = 8
FF = 2048
DOCS = 4
SLOTS = 8
STEP = 10
LANES = 1
LANE_UNITS = 384
QB = 384
LANE_TOK = 1152
MB_ALL = 8
UNITS_ALL = 3072
MOST = 336
N_BATCH = 4


def owner_table(key):
    base = jax.random.fold_in(key, 17)
    keys_list = jax.random.split(base, 5)
    largest = jax.random.randint(keys_list[0], (), 0, N_BATCH)
    first_other = jax.random.randint(keys_list[1], (), 0, N_BATCH - 1)
    pool_owner = (largest + 1 + first_other) % N_BATCH
    second_other = jax.random.randint(keys_list[2], (), 0, N_BATCH - 2)
    second_other = second_other + (second_other >= first_other).astype(jnp.int32)
    qkv_owner = (largest + 1 + second_other) % N_BATCH
    out_owner = (largest + 1 + jax.random.randint(keys_list[3], (), 0, N_BATCH - 1)) % N_BATCH
    up_owner = (largest + 1 + jax.random.randint(keys_list[4], (), 0, N_BATCH - 1)) % N_BATCH
    return jnp.stack([pool_owner, qkv_owner, out_owner, largest, largest, up_owner]).astype(jnp.int32)


def draw_owners(key, part):
    return owner_table(key)


def draw_master(key, part):
    owners = owner_table(key)
    sizes = [3, 3, 1, FF // D, FF // D, 3]
    factors = [(3.0 * D) ** (-0.5), D ** (-0.5), 6.0 * D ** (-0.5), D ** (-0.5), FF ** (-0.5), D ** (-0.5)]
    device = jnp.arange(N_BATCH, dtype=jnp.int32)[:, None]
    slot_ids = jnp.arange(SLOTS, dtype=jnp.int32)[None, :]
    factor = jnp.full((N_BATCH, SLOTS), D ** (-0.5), jnp.float32)
    for matrix_id in range(6):
        shared = jnp.zeros((), jnp.int32)
        for earlier_id in range(matrix_id):
            shared = shared + jnp.where(owners[earlier_id] == owners[matrix_id], sizes[earlier_id], 0).astype(jnp.int32)
        inside = (device == owners[matrix_id]) & (slot_ids >= shared) & (slot_ids < shared + sizes[matrix_id])
        factor = jnp.where(inside, jnp.float32(factors[matrix_id]), factor)
    noise = jax.random.normal(jax.random.fold_in(key, 29), (N_BATCH, SLOTS, D, D), jnp.float32)
    return noise * factor[:, :, None, None]


def block_scale(rng, extent, cuts, least, high):
    level = 1.0
    for position, shards_of in cuts:
        draws = jax.random.uniform(jax.random.fold_in(jax.random.fold_in(rng, 6), position), (shards_of,), jnp.float32, least / len(cuts), high / len(cuts))
        level = level * jnp.repeat(jnp.exp(draws), extent[position] // shards_of).reshape((-1,) + (1,) * (len(extent) - 1 - position))
    return level


def profile(amount, total, bound, slope):
    weights = [(1 << 20) // math.isqrt(rank ** slope) + 1 for rank in range(2, amount + 1)]
    rest, given = total - bound - (amount - 1), [1] * (amount - 1)
    while rest > 0:
        free = [i for i in range(amount - 1) if given[i] < bound]
        mass, budget = sum([weights[i] for i in free]), rest
        for i in free:
            more = min(bound - given[i], max(1, budget * weights[i] // mass), rest)
            given[i] = given[i] + more
            rest = rest - more
    return np.array([bound] + given)


def uneven_parts(rng, amount, total, reach, slope):
    if amount == 2:
        one = jax.random.randint(rng, (), max(1, total - reach), min(reach, total - 1) + 1)
        return jnp.stack([one, total - one])
    tallies = jnp.asarray(profile(amount, total, reach, slope), jnp.int32)
    pairs = (amount - 1) // 2
    source_of, taker = tallies[1:1 + 2 * pairs:2], tallies[2:2 + 2 * pairs:2]
    room = jnp.minimum(source_of - 1, reach - taker)
    shifted = jax.random.randint(jax.random.fold_in(rng, 1), (pairs,), 0, 1 << 20) % (room + 1)
    tallies = tallies.at[1:1 + 2 * pairs:2].set(source_of - shifted).at[2:2 + 2 * pairs:2].set(taker + shifted)
    return tallies[jax.random.permutation(jax.random.fold_in(rng, 2), amount)]


def bell_draw(key, dims, deviation, most, cuts=(), kind=jnp.bfloat16):
    values = deviation * jax.random.normal(key, dims, jnp.float32)
    if cuts:
        values = values * block_scale(key, dims, cuts, -0.22, 0.18)
    return jnp.clip(values, -most, most).astype(kind)


def setup_inputs(seed: int = 0) -> dict:
    streams_of = jax.random.split(jax.random.key(seed), 15)
    return {
        "tokens": bell_draw(streams_of[0], (MB_ALL, LANES, LANE_TOK, D), 1.0, 5.0, ((0, 4), (2, 8))),
        "cotangent": bell_draw(streams_of[1], (MB_ALL, LANES, LANE_TOK, D), 1.0, 5.0, ((0, 4), (2, 8))),
        "doc_lengths": jax.vmap(lambda own: uneven_parts(own, DOCS, LANE_UNITS, MOST, 2))(jax.random.split(streams_of[2], MB_ALL * LANES)).reshape((MB_ALL, LANES, DOCS)).astype(jnp.int32),
        "owners": draw_owners(jax.random.fold_in(streams_of[14], 71), 0),
        "master": draw_master(jax.random.fold_in(streams_of[14], 71), 0),
        "first_moment": bell_draw(streams_of[5], (N_BATCH, SLOTS, D, D), (0.11 * UNITS_ALL ** 0.5), 32.0, ((0, 4), (2, 8)), jnp.float32),
        "second_moment": jnp.clip(jnp.exp(math.log(1228.8) - 2.5902672 * jax.random.uniform(streams_of[6], (N_BATCH, SLOTS, D, D), jnp.float32) ** block_scale(streams_of[6], (N_BATCH, SLOTS, D, D), ((0, 4), (2, 8)), -0.2, 0.2)), 92.16, 1228.8),
        "ln_gain": jnp.clip(1.0 + 0.1 * jax.random.normal(streams_of[7], (2, D), jnp.float32), 0.5, 1.5),
        "ln_bias": bell_draw(streams_of[8], (2, D), 0.3, 1.2, (), jnp.float32),
        "norm_m": bell_draw(streams_of[9], (4, D), (0.11 * UNITS_ALL ** 0.5), 32.0, (), jnp.float32),
        "norm_v": jnp.clip(jnp.exp(jax.random.uniform(streams_of[10], (4, D), jnp.float32, math.log(92.16), math.log(1228.8))), 92.16, 1228.8),
        "slopes": jnp.clip(jnp.exp(jax.random.uniform(streams_of[11], (H,), jnp.float32, math.log(0.0013020834), math.log(0.1))), 0.0013020834, 0.1),
        "slope_m": bell_draw(streams_of[12], (H,), (100 * UNITS_ALL ** 0.5), 32768.0, (), jnp.float32),
        "slope_v": jnp.clip(jnp.exp(jax.random.uniform(streams_of[13], (H,), jnp.float32, math.log(3072000), math.log(307200000))), 3072000, 307200000),
    }


@jax.custom_vjp
def low(v):
    return lax.optimization_barrier(v.astype(jnp.bfloat16)).astype(jnp.float32)

@jax.custom_vjp
def low_back(v):
    return v

def low_keep(v):
    return (low(v), None)

def low_pass(kept, grad):
    return (grad,)

def back_keep(v):
    return (v, None)

def back_low(kept, grad):
    return (low(grad),)
low.defvjp(low_keep, low_pass)
low_back.defvjp(back_keep, back_low)
beta_one = 0.9
beta_two = 0.95
adam_eps = 1e-08
decay_rate = 0.1
rate_matrix = 0.02
rate_norm = 0.2
rate_slope = 0.01
ln_eps = 1e-05
masked_score = -1000000000.0
row_kinds = (True, False, True, False, True, False)

def matmul(left, right):
    return jnp.dot(left, right, precision=lax.Precision.HIGHEST)

def layer_norm(values, gain, shift):
    center = lax.optimization_barrier(jnp.mean(values, -1, keepdims=True))
    centred = values - center
    spread = lax.optimization_barrier(jnp.mean(centred * centred, -1, keepdims=True))
    return centred * lax.rsqrt(spread + ln_eps) * gain + shift

def block_counts(features, hidden):
    return [3, 3, 1, hidden // features, hidden // features, 3]

def block_starts(owners, sizes):
    starts_list = []
    for matrix_id in range(len(sizes)):
        shared = jnp.zeros((), jnp.int32)
        for earlier_id in range(matrix_id):
            shared = shared + jnp.where(owners[earlier_id] == owners[matrix_id], sizes[earlier_id], 0).astype(jnp.int32)
        starts_list.append(shared)
    return starts_list

def slot_table(owners, device, sizes, slot_count):
    starts_list = block_starts(owners, sizes)
    slot_ids = jnp.arange(slot_count, dtype=jnp.int32)
    numbers = jnp.arange(sum(sizes), dtype=jnp.int32)
    slot_map = jnp.zeros(device.shape + (slot_count, sum(sizes)), jnp.float32)
    block_base = 0
    for matrix_id in range(len(sizes)):
        inside = (owners[matrix_id] == device[..., None]) & (slot_ids >= starts_list[matrix_id]) & (slot_ids < starts_list[matrix_id] + sizes[matrix_id])
        target = block_base + slot_ids - starts_list[matrix_id]
        slot_map = slot_map + (inside[..., None] & (target[:, None] == numbers[None, :])).astype(jnp.float32)
        block_base += sizes[matrix_id]
    return slot_map

def to_matrix(blocks, by_rows):
    if by_rows:
        return blocks.reshape(-1, blocks.shape[2])
    return blocks.transpose(1, 0, 2).reshape(blocks.shape[1], -1)

def to_blocks(matrix, by_rows, features):
    if by_rows:
        return matrix.reshape(-1, features, features)
    return matrix.reshape(features, -1, features).transpose(1, 0, 2)

def adam_update(weight, gradient, first_moment, second, fix_first, fix_second, rate, decay):
    first_new = beta_one * first_moment + (1.0 - beta_one) * gradient
    second_new = beta_two * second + (1.0 - beta_two) * gradient * gradient
    direction = first_new / fix_first / (jnp.sqrt(second_new / fix_second) + adam_eps)
    return (weight - rate * (direction + decay * weight), first_new, second_new)

def attention(queries, key_rows, values, segment, slopes):
    unit_count, head_count, head_width = queries.shape
    col_ids = jnp.arange(unit_count, dtype=jnp.int32)

    def per_block(lane_item):
        query_block, start_row = lane_item
        row_ids = start_row + jnp.arange(QB, dtype=jnp.int32)
        distance = (row_ids[:, None] - col_ids[None, :]).astype(jnp.float32)
        seg_rows = lax.dynamic_slice_in_dim(segment, start_row, QB)
        allowed = (seg_rows[:, None] == segment[None, :]) & (col_ids[None, :] <= row_ids[:, None])
        raw_score = jnp.einsum('qhd,khd->hqk', query_block, key_rows, precision=lax.Precision.HIGHEST) * 0.125 - slopes[:, None, None] * distance[None]
        scores = jnp.where(allowed[None], low_back(raw_score), masked_score)
        probability = jax.nn.softmax(scores, -1)
        return jnp.einsum('hqk,khd->qhd', low(probability), values, precision=lax.Precision.HIGHEST)
    row_starts = jnp.arange(unit_count // QB, dtype=jnp.int32) * QB
    attended_all = lax.map(jax.checkpoint(per_block), (queries.reshape(-1, QB, head_count, head_width), row_starts))
    return attended_all.reshape(unit_count, head_count * head_width)

def lane_forward(lane_tokens, lengths, params):
    matrices, ln_gain, ln_bias, slopes = params
    pool_weight, qkv_weight, out_weight, in_weight, back_weight, up_weight = matrices
    features = lane_tokens.shape[1]
    unit_count = lane_tokens.shape[0] // 3
    head_count = slopes.shape[0]
    doc_ends = jnp.cumsum(lengths).astype(jnp.int32)
    positions = jnp.arange(unit_count, dtype=jnp.int32)
    segment = lax.optimization_barrier(jnp.sum((positions[:, None] >= doc_ends[None, :-1]).astype(jnp.int32), 1))
    doc_starts = jnp.concatenate([jnp.zeros((1,), jnp.int32), doc_ends[:-1]])
    keep_mask = 1.0 - jnp.any(positions[:, None] == doc_starts[None, :], 1).astype(jnp.float32)
    triple = lane_tokens.reshape(unit_count, 3, features)
    earlier = jnp.concatenate([jnp.zeros((1, 2, features), jnp.float32), triple[:-1, 1:3]], 0) * keep_mask[:, None, None]
    pieces = jnp.concatenate([earlier, triple[:, 0:1]], 1).reshape(unit_count, 3 * features)
    pooled = low_back(matmul(pieces, pool_weight))
    normed = low(layer_norm(pooled, ln_gain[0], ln_bias[0]))
    projected = low(low_back(matmul(normed, qkv_weight))).reshape(unit_count, 3, head_count, features // head_count)
    attended = attention(projected[:, 0], projected[:, 1], projected[:, 2], segment, slopes)
    attended = low(low_back(attended))
    residual = pooled + low_back(matmul(attended, out_weight))
    normed_two = low(layer_norm(residual, ln_gain[1], ln_bias[1]))
    hidden = low_back(matmul(normed_two, in_weight))
    activated = low(jax.nn.gelu(hidden, approximate=True))
    shortened = residual + low_back(matmul(activated, back_weight))
    upward = matmul(low(shortened), up_weight)
    return lane_tokens + upward.reshape(unit_count * 3, features)

def reference(tokens, cotangent, doc_lengths, owners, master, first_moment, second_moment, ln_gain, ln_bias, norm_m, norm_v, slopes, slope_m, slope_v):
    sizes = block_counts(D, FF)
    starts_list = block_starts(owners, sizes)
    low_master = master.astype(jnp.bfloat16).astype(jnp.float32)
    zero_index = jnp.zeros((), jnp.int32)
    matrices = []
    for matrix_id in range(6):
        blocks = lax.dynamic_slice(low_master, (owners[matrix_id], starts_list[matrix_id], zero_index, zero_index), (1, sizes[matrix_id], D, D))[0]
        matrices.append(to_matrix(blocks, row_kinds[matrix_id]))
    lane_stack = tokens.astype(jnp.float32).reshape(-1, LANE_TOK, D)
    length_stack = doc_lengths.reshape(-1, DOCS)

    def forward_all(stacked, params):

        def per_lane(unused, lane_item):
            return (unused, jax.checkpoint(lane_forward)(lane_item[0], lane_item[1], params))
        return lax.scan(per_lane, jnp.zeros((), jnp.float32), (stacked, length_stack))[1]
    params = (tuple(matrices), ln_gain, ln_bias, slopes)
    mixed, pullback = jax.vjp(forward_all, lane_stack, params)
    grad_tokens, grad_params = pullback(cotangent.astype(jnp.float32).reshape(lane_stack.shape))
    grad_matrices, grad_gain, grad_bias, grad_slopes = grad_params
    grad_blocks = jnp.concatenate([to_blocks(grad_matrices[matrix_id], row_kinds[matrix_id], D) for matrix_id in range(6)], 0)
    slot_map = slot_table(owners, jnp.arange(N_BATCH, dtype=jnp.int32), sizes, SLOTS)
    is_owned = lax.optimization_barrier(jnp.sum(slot_map, -1))[..., None, None] > 0.5
    slot_grads = jnp.einsum('ojb,brc->ojrc', slot_map, grad_blocks, precision=lax.Precision.HIGHEST)
    step_float = jnp.float32(STEP)
    fix_first = 1.0 - jnp.power(jnp.float32(beta_one), step_float)
    fix_second = 1.0 - jnp.power(jnp.float32(beta_two), step_float)
    new_weight, new_first, new_second = adam_update(master, slot_grads, first_moment, second_moment, fix_first, fix_second, rate_matrix, decay_rate)
    new_weight = jnp.where(is_owned, new_weight, master)
    new_first = jnp.where(is_owned, new_first, first_moment)
    new_second = jnp.where(is_owned, new_second, second_moment)
    norm_now = jnp.concatenate([ln_gain, ln_bias], 0)
    norm_grad = jnp.concatenate([grad_gain, grad_bias], 0)
    new_norm, new_norm_m, new_norm_v = adam_update(norm_now, norm_grad, norm_m, norm_v, fix_first, fix_second, rate_norm, 0.0)
    new_slopes, new_slope_m, new_slope_v = adam_update(slopes, grad_slopes, slope_m, slope_v, fix_first, fix_second, rate_slope, 0.0)
    return (mixed.reshape(tokens.shape), grad_tokens.reshape(tokens.shape), new_weight, new_first, new_second, new_weight.astype(jnp.bfloat16), new_norm, new_norm_m, new_norm_v, new_slopes, new_slope_m, new_slope_v)
```

```python
import jax
import jax.numpy as jnp
from jax import lax
from jax.sharding import PartitionSpec as P

FF = 2048
STEP = 10


beta_one = 0.9
beta_two = 0.95
adam_eps = 1e-08
decay_rate = 0.1
rate_matrix = 0.02
rate_norm = 0.2
rate_slope = 0.01
ln_eps = 1e-05
masked_score = -1000000000.0
row_kinds = (True, False, True, False, True, False)


def broadcast(value, axis, source):
    kept = jnp.where(lax.axis_index(axis) == source, value, 0).astype(value.dtype)
    return lax.psum(kept, axis)


def running_total(lengths):
    count = lengths.shape[-1]
    ends = [lengths[..., 0]]
    for index in range(1, count):
        ends.append(ends[-1] + lengths[..., index])
    return jnp.stack(ends, -1)


def for_sending(value):

    def short(part):
        return part.astype(jnp.bfloat16) if part.dtype == jnp.float32 else part

    return jax.tree.map(short, value)


def passed_along(value, axis, by):
    peers = lax.axis_size(axis)
    pairs = [(i, i + by) for i in range(peers) if 0 <= i + by < peers]
    return lax.ppermute(value, axis, pairs)


def layer_norm(values, gain, shift):
    center = jnp.mean(values, -1, keepdims=True)
    centred = values - center
    spread = jnp.mean(centred * centred, -1, keepdims=True)
    return centred * lax.rsqrt(spread + ln_eps) * gain + shift


def gelu_tanh(values):
    return jax.nn.gelu(values, approximate=True)


def block_counts(features, hidden):
    return [3, 3, 1, hidden // features, hidden // features, 3]


def block_starts(owners, sizes):
    starts_list = []
    for matrix_id in range(len(sizes)):
        shared = jnp.zeros((), jnp.int32)
        for earlier_id in range(matrix_id):
            shared = shared + jnp.where(
                owners[earlier_id] == owners[matrix_id], sizes[earlier_id], 0
            ).astype(jnp.int32)
        starts_list.append(shared)
    return starts_list


def slot_table(owners, device, sizes, slot_count):
    starts_list = block_starts(owners, sizes)
    slot_ids = jnp.arange(slot_count, dtype=jnp.int32)
    numbers = jnp.arange(sum(sizes), dtype=jnp.int32)
    slot_map = jnp.zeros((slot_count, sum(sizes)), jnp.float32)
    block_base = 0
    for matrix_id in range(len(sizes)):
        inside = (
            (owners[matrix_id] == device)
            & (slot_ids >= starts_list[matrix_id])
            & (slot_ids < starts_list[matrix_id] + sizes[matrix_id])
        )
        target = block_base + slot_ids - starts_list[matrix_id]
        slot_map = slot_map + (inside[:, None] & (target[:, None] == numbers[None, :])).astype(
            jnp.float32
        )
        block_base += sizes[matrix_id]
    return slot_map


def to_matrix(blocks, by_rows):
    if by_rows:
        return blocks.reshape(-1, blocks.shape[2])
    return blocks.transpose(1, 0, 2).reshape(blocks.shape[1], -1)


def to_blocks(matrix, by_rows, features):
    if by_rows:
        return matrix.reshape(-1, features, features)
    return matrix.reshape(features, -1, features).transpose(1, 0, 2)


def all_blocks(matrices, features):
    return jnp.concatenate(
        [to_blocks(matrices[matrix_id], row_kinds[matrix_id], features) for matrix_id in range(6)],
        0,
    )


def adam_update(weight, gradient, first_moment, second, fix_first, fix_second, rate, decay):
    first_new = beta_one * first_moment + (1.0 - beta_one) * gradient
    second_new = beta_two * second + (1.0 - beta_two) * gradient * gradient
    direction = first_new / fix_first / (jnp.sqrt(second_new / fix_second) + adam_eps)
    return (weight - rate * (direction + decay * weight), first_new, second_new)


def scores_for(query_block, key_rows, start_row, segment, head_slope):
    block_rows = query_block.shape[0]
    row_total = key_rows.shape[0]
    row_ids = start_row + jnp.arange(block_rows, dtype=jnp.int32)
    col_ids = jnp.arange(row_total, dtype=jnp.int32)
    distance = (row_ids[:, None] - col_ids[None, :]).astype(jnp.float32)
    seg_rows = lax.dynamic_slice_in_dim(segment, start_row, block_rows)
    allowed = (seg_rows[:, None] == segment[None, :]) & (col_ids[None, :] <= row_ids[:, None])
    raw_score = (
        jnp.dot(query_block, key_rows.T, preferred_element_type=jnp.float32) * 0.125
        - head_slope * distance
    )
    return (jnp.where(allowed, raw_score, masked_score), distance)


def attend(queries, key_rows, values, segment, head_slope, block_rows):
    row_total, head_width = queries.shape

    def per_block(start_row):
        query_block = lax.dynamic_slice_in_dim(queries, start_row, block_rows)
        scores, distance = scores_for(query_block, key_rows, start_row, segment, head_slope)
        largest = jnp.max(scores, -1, keepdims=True)
        log_total = largest + jnp.log(jnp.sum(jnp.exp(scores - largest), -1, keepdims=True))
        probability = jnp.exp(scores - log_total).astype(jnp.bfloat16)
        return (jnp.dot(probability, values, preferred_element_type=jnp.float32), log_total[:, 0])

    row_starts = jnp.arange(row_total // block_rows, dtype=jnp.int32) * block_rows
    attended, log_totals = lax.map(per_block, row_starts)
    return (attended.reshape(row_total, head_width), log_totals.reshape(row_total))


def attend_back(queries, key_rows, values, segment, head_slope, log_totals, grad_out, block_rows):
    row_total, head_width = queries.shape

    def per_block(carried, start_row):
        grad_keys, grad_values, grad_slope = carried
        query_block = lax.dynamic_slice_in_dim(queries, start_row, block_rows)
        grad_block = lax.dynamic_slice_in_dim(grad_out, start_row, block_rows)
        total_block = lax.dynamic_slice_in_dim(log_totals, start_row, block_rows)
        scores, distance = scores_for(query_block, key_rows, start_row, segment, head_slope)
        probability = jnp.exp(scores - total_block[:, None])
        grad_prob = jnp.dot(grad_block, values.T, preferred_element_type=jnp.float32)
        grad_score = (
            probability * (grad_prob - jnp.sum(probability * grad_prob, -1, keepdims=True))
        ).astype(jnp.bfloat16)
        grad_query = jnp.dot(grad_score, key_rows, preferred_element_type=jnp.float32) * 0.125
        grad_keys = (
            grad_keys
            + jnp.dot(grad_score.T, query_block, preferred_element_type=jnp.float32) * 0.125
        )
        grad_values = grad_values + jnp.dot(
            probability.astype(jnp.bfloat16).T, grad_block, preferred_element_type=jnp.float32
        )
        grad_slope = grad_slope - jnp.sum(grad_score.astype(jnp.float32) * distance)
        return ((grad_keys, grad_values, grad_slope), grad_query)

    row_starts = jnp.arange(row_total // block_rows, dtype=jnp.int32) * block_rows
    initial = (
        jnp.zeros((row_total, head_width), jnp.float32),
        jnp.zeros((row_total, head_width), jnp.float32),
        jnp.zeros((), jnp.float32),
    )
    (grad_keys, grad_values, grad_slope), grad_queries = lax.scan(per_block, initial, row_starts)
    return (grad_queries.reshape(row_total, head_width), grad_keys, grad_values, grad_slope)


def body(
    tokens,
    cotangent,
    doc_lengths,
    owners,
    master,
    first_moment,
    second_moment,
    ln_gain,
    ln_bias,
    norm_m,
    norm_v,
    slopes,
    slope_m,
    slope_v,
):
    micro_count, lane_count, tok_rows, features = tokens.shape
    unit_rows = tok_rows // 3
    seq_devices = lax.axis_size("seq")
    head_count = slopes.shape[0]
    head_width = features // head_count
    lane_units = unit_rows * seq_devices
    block_rows = min(512, lane_units)
    unit_total = lane_count * unit_rows
    slot_count = master.shape[1]
    sizes = block_counts(features, FF)
    starts_list = block_starts(owners, sizes)
    batch_rank = lax.axis_index("batch")
    seq_rank = lax.axis_index("seq")
    lane_rank = seq_rank // head_count
    head_rank = seq_rank % head_count
    low_slots = master[0].astype(jnp.bfloat16)
    fetched = []
    for matrix_id in range(6):
        owned_rows = lax.dynamic_slice_in_dim(
            low_slots, starts_list[matrix_id], sizes[matrix_id], 0
        )
        fetched.append(broadcast(owned_rows, "batch", owners[matrix_id]))
    gathered = lax.all_gather(for_sending(tuple(fetched)), "seq", axis=1, tiled=True)
    pool_weight, qkv_weight, out_weight, in_weight, back_weight, up_weight = [
        to_matrix(gathered[matrix_id], row_kinds[matrix_id]) for matrix_id in range(6)
    ]
    doc_ends = running_total(doc_lengths)
    doc_starts = jnp.concatenate(
        [jnp.zeros((micro_count, lane_count, 1), jnp.int32), doc_ends[..., :-1]], -1
    )
    unit_ids = seq_rank * unit_rows + jnp.arange(unit_rows, dtype=jnp.int32)
    keep_mask = 1.0 - jnp.any(
        unit_ids[None, None, :, None] == doc_starts[:, :, None, :], -1
    ).astype(jnp.float32)
    triples = tokens.reshape(micro_count, lane_count, unit_rows, 3, features)
    tail_tokens = triples[:, :, -1, 1:3]
    arrived = passed_along(tail_tokens, "seq", 1)
    lane_pick = jnp.arange(lane_count, dtype=jnp.int32) == lane_rank
    head_pick = jnp.arange(head_count, dtype=jnp.int32) == head_rank
    head_slope = jnp.sum(jnp.where(head_pick, slopes, 0.0))
    positions = jnp.arange(lane_units, dtype=jnp.int32)
    gain_grad = jnp.zeros((2, features), jnp.float32)
    bias_grad = jnp.zeros((2, features), jnp.float32)
    slope_grad = jnp.zeros((), jnp.float32)
    summed = None
    mixed_parts = []
    grad_parts = []
    outgoing = []
    for micro in range(micro_count):
        triple_now = triples[micro]
        keep_now = keep_mask[micro]
        earlier = jnp.concatenate([arrived[micro][:, None], triple_now[:, :-1, 1:3]], 1) * keep_now[
            :, :, None, None
        ].astype(jnp.bfloat16)
        pool_input = jnp.concatenate([earlier, triple_now[:, :, 0:1]], 2).reshape(
            unit_total, 3 * features
        )
        pooled = jnp.dot(pool_input, pool_weight, preferred_element_type=jnp.float32)
        normed = layer_norm(pooled, ln_gain[0], ln_bias[0]).astype(jnp.bfloat16)
        projected = jnp.dot(normed, qkv_weight, preferred_element_type=jnp.float32).astype(
            jnp.bfloat16
        )
        outbound = (
            projected.reshape(lane_count, unit_rows, 3, head_count, head_width)
            .transpose(0, 3, 1, 2, 4)
            .reshape(lane_count * head_count, unit_rows * 3 * head_width)
        )
        received = lax.all_to_all(outbound, "seq", split_axis=0, concat_axis=1, tiled=True).reshape(
            lane_units, 3, head_width
        )
        queries = received[:, 0]
        key_rows = received[:, 1]
        values = received[:, 2]
        lengths = jnp.sum(jnp.where(lane_pick[:, None], doc_lengths[micro], 0), 0)
        lane_ends = running_total(lengths)
        segment = jnp.sum((positions[:, None] >= lane_ends[None, :-1]).astype(jnp.int32), 1)
        attended, log_totals = attend(queries, key_rows, values, segment, head_slope, block_rows)
        returned = lax.all_to_all(
            attended.astype(jnp.bfloat16).reshape(1, lane_units * head_width),
            "seq",
            split_axis=1,
            concat_axis=0,
            tiled=True,
        )
        merged = (
            returned.reshape(lane_count, head_count, unit_rows, head_width)
            .transpose(0, 2, 1, 3)
            .reshape(unit_total, features)
        )
        residual = pooled + jnp.dot(merged, out_weight, preferred_element_type=jnp.float32)
        normed_two = layer_norm(residual, ln_gain[1], ln_bias[1]).astype(jnp.bfloat16)
        hidden = jnp.dot(normed_two, in_weight, preferred_element_type=jnp.float32)
        activated = gelu_tanh(hidden).astype(jnp.bfloat16)
        shortened = residual + jnp.dot(activated, back_weight, preferred_element_type=jnp.float32)
        short_low = shortened.astype(jnp.bfloat16)
        upward = jnp.dot(short_low, up_weight, preferred_element_type=jnp.float32).reshape(
            lane_count, unit_rows * 3, features
        )
        mixed_parts.append(tokens[micro].astype(jnp.float32) + upward)
        grad_upward = cotangent[micro].reshape(unit_total, 3 * features)
        sum_up = jnp.dot(short_low.T, grad_upward, preferred_element_type=jnp.float32)
        grad_short = jnp.dot(grad_upward, up_weight.T, preferred_element_type=jnp.float32)
        grad_short_low = grad_short.astype(jnp.bfloat16)
        sum_back = jnp.dot(activated.T, grad_short_low, preferred_element_type=jnp.float32)
        grad_activated = jnp.dot(grad_short_low, back_weight.T, preferred_element_type=jnp.float32)
        grad_hidden = jax.vjp(gelu_tanh, hidden)[1](grad_activated)[0].astype(jnp.bfloat16)
        sum_in = jnp.dot(normed_two.T, grad_hidden, preferred_element_type=jnp.float32)
        grad_normed_two = jnp.dot(grad_hidden, in_weight.T, preferred_element_type=jnp.float32)
        norm_two_back = jax.vjp(layer_norm, residual, ln_gain[1], ln_bias[1])[1]
        grad_resid_norm, grad_gain_two, grad_bias_two = norm_two_back(grad_normed_two)
        grad_residual = grad_short + grad_resid_norm
        grad_resid_low = grad_residual.astype(jnp.bfloat16)
        sum_out = jnp.dot(merged.T, grad_resid_low, preferred_element_type=jnp.float32)
        grad_merged = jnp.dot(
            grad_resid_low, out_weight.T, preferred_element_type=jnp.float32
        ).astype(jnp.bfloat16)
        back_outbound = (
            grad_merged.reshape(lane_count, unit_rows, head_count, head_width)
            .transpose(0, 2, 1, 3)
            .reshape(lane_count * head_count, unit_rows * head_width)
        )
        grad_attended = lax.all_to_all(
            back_outbound, "seq", split_axis=0, concat_axis=1, tiled=True
        ).reshape(lane_units, head_width)
        grad_queries, grad_keys, grad_values, grad_slope = attend_back(
            queries, key_rows, values, segment, head_slope, log_totals, grad_attended, block_rows
        )
        grad_heads = (
            jnp.stack([grad_queries, grad_keys, grad_values], 1)
            .astype(jnp.bfloat16)
            .reshape(1, lane_units * 3 * head_width)
        )
        grad_arrived = lax.all_to_all(grad_heads, "seq", split_axis=1, concat_axis=0, tiled=True)
        grad_projected = (
            grad_arrived.reshape(lane_count, head_count, unit_rows, 3, head_width)
            .transpose(0, 2, 3, 1, 4)
            .reshape(unit_total, 3 * features)
        )
        sum_qkv = jnp.dot(normed.T, grad_projected, preferred_element_type=jnp.float32)
        grad_normed = jnp.dot(grad_projected, qkv_weight.T, preferred_element_type=jnp.float32)
        norm_one_back = jax.vjp(layer_norm, pooled, ln_gain[0], ln_bias[0])[1]
        grad_pool_norm, grad_gain_one, grad_bias_one = norm_one_back(grad_normed)
        grad_pooled_low = (grad_residual + grad_pool_norm).astype(jnp.bfloat16)
        sum_pool = jnp.dot(pool_input.T, grad_pooled_low, preferred_element_type=jnp.float32)
        grad_pieces = jnp.dot(
            grad_pooled_low, pool_weight.T, preferred_element_type=jnp.float32
        ).reshape(lane_count, unit_rows, 3, features)
        grad_earlier = grad_pieces[:, :, 0:2] * keep_now[:, :, None, None]
        outgoing.append(grad_earlier[:, 0])
        following = jnp.concatenate(
            [grad_earlier[:, 1:], jnp.zeros((lane_count, 1, 2, features), jnp.float32)], 1
        )
        token_grad = jnp.concatenate([grad_pieces[:, :, 2:3], following], 2).reshape(
            lane_count, unit_rows * 3, features
        )
        grad_parts.append(cotangent[micro].astype(jnp.float32) + token_grad)
        gain_grad = gain_grad + jnp.stack([grad_gain_one, grad_gain_two])
        bias_grad = bias_grad + jnp.stack([grad_bias_one, grad_bias_two])
        slope_grad = slope_grad + grad_slope
        micro_grads = [sum_pool, sum_qkv, sum_out, sum_in, sum_back, sum_up]
        summed = (
            micro_grads
            if summed is None
            else [left + right for left, right in zip(summed, micro_grads)]
        )
    reduced = lax.psum_scatter(all_blocks(summed, features), "seq", scatter_dimension=1, tiled=True)
    incoming = passed_along(jnp.stack(outgoing).astype(jnp.bfloat16), "seq", -1).astype(jnp.float32)
    grad_tokens = jnp.stack(grad_parts).reshape(micro_count, lane_count, unit_rows, 3, features)
    grad_tokens = grad_tokens.at[:, :, -1, 1:3].add(incoming).reshape(tokens.shape)
    reduced_all = lax.psum(reduced, "batch")
    norm_grad, slopes_grad = lax.psum(
        (jnp.concatenate([gain_grad, bias_grad], 0), jnp.where(head_pick, slope_grad, 0.0)),
        ("batch", "seq"),
    )
    slot_map = slot_table(owners, batch_rank, sizes, slot_count)
    is_owned = jnp.sum(slot_map, -1)[:, None, None] > 0.5
    slot_grads = jnp.einsum("jb,brc->jrc", slot_map, reduced_all, precision=lax.Precision.HIGHEST)
    step_float = jnp.float32(STEP)
    fix_first = 1.0 - jnp.power(jnp.float32(beta_one), step_float)
    fix_second = 1.0 - jnp.power(jnp.float32(beta_two), step_float)
    new_weight, new_first, new_second = adam_update(
        master[0],
        slot_grads,
        first_moment[0],
        second_moment[0],
        fix_first,
        fix_second,
        rate_matrix,
        decay_rate,
    )
    new_weight = jnp.where(is_owned, new_weight, master[0])
    new_first = jnp.where(is_owned, new_first, first_moment[0])
    new_second = jnp.where(is_owned, new_second, second_moment[0])
    norm_now = jnp.concatenate([ln_gain, ln_bias], 0)
    new_norm, new_norm_m, new_norm_v = adam_update(
        norm_now, norm_grad, norm_m, norm_v, fix_first, fix_second, rate_norm, 0.0
    )
    new_slopes, new_slope_m, new_slope_v = adam_update(
        slopes, slopes_grad, slope_m, slope_v, fix_first, fix_second, rate_slope, 0.0
    )
    return (
        jnp.stack(mixed_parts),
        grad_tokens,
        new_weight[None],
        new_first[None],
        new_second[None],
        new_weight[None].astype(jnp.bfloat16),
        new_norm,
        new_norm_m,
        new_norm_v,
        new_slopes,
        new_slope_m,
        new_slope_v,
    )


def solution(mesh):
    in_specs = (
        P("batch", None, "seq", None),
        P("batch", None, "seq", None),
        P("batch", None, None),
        P(),
        P("batch", None, "seq", None),
        P("batch", None, "seq", None),
        P("batch", None, "seq", None),
        P(),
        P(),
        P(),
        P(),
        P(),
        P(),
        P(),
    )
    out_specs = (
        P("batch", None, "seq", None),
        P("batch", None, "seq", None),
        P("batch", None, "seq", None),
        P("batch", None, "seq", None),
        P("batch", None, "seq", None),
        P("batch", None, "seq", None),
        P(),
        P(),
        P(),
        P(),
        P(),
        P(),
    )
    return jax.shard_map(body, mesh=mesh, in_specs=in_specs, out_specs=out_specs, check_vma=False)
```

```python
import math

import jax
import jax.numpy as jnp
from jax import lax
from jax.experimental import pallas as pl
from jax.experimental.pallas import tpu as pltpu
from jax.sharding import PartitionSpec as P

FF = 2048
STEP = 10


beta_one = 0.9
beta_two = 0.95
adam_eps = 1e-08
decay_rate = 0.1
rate_matrix = 0.02
rate_norm = 0.2
rate_slope = 0.01
ln_eps = 1e-05
masked_score = -1000000000.0
row_kinds = (True, False, True, False, True, False)


def broadcast(value, axis, source):
    kept = jnp.where(lax.axis_index(axis) == source, value, 0).astype(value.dtype)
    return lax.psum(kept, axis)


def running_total(lengths):
    count = lengths.shape[-1]
    ends = [lengths[..., 0]]
    for index in range(1, count):
        ends.append(ends[-1] + lengths[..., index])
    return jnp.stack(ends, -1)


def for_sending(value):

    def short(part):
        return part.astype(jnp.bfloat16) if part.dtype == jnp.float32 else part

    return jax.tree.map(short, value)


def passed_along(value, axis, by):
    peers = lax.axis_size(axis)
    pairs = [(i, i + by) for i in range(peers) if 0 <= i + by < peers]
    return lax.ppermute(value, axis, pairs)


def layer_norm(values, gain, shift):
    center = jnp.mean(values, -1, keepdims=True)
    centred = values - center
    spread = jnp.mean(centred * centred, -1, keepdims=True)
    return centred * lax.rsqrt(spread + ln_eps) * gain + shift


def gelu_tanh(values):
    return jax.nn.gelu(values, approximate=True)


def block_counts(features, hidden):
    return [3, 3, 1, hidden // features, hidden // features, 3]


def block_starts(owners, sizes):
    starts_list = []
    for matrix_id in range(len(sizes)):
        shared = jnp.zeros((), jnp.int32)
        for earlier_id in range(matrix_id):
            shared = shared + jnp.where(
                owners[earlier_id] == owners[matrix_id], sizes[earlier_id], 0
            ).astype(jnp.int32)
        starts_list.append(shared)
    return starts_list


def slot_table(owners, device, sizes, slot_count):
    starts_list = block_starts(owners, sizes)
    slot_ids = jnp.arange(slot_count, dtype=jnp.int32)
    numbers = jnp.arange(sum(sizes), dtype=jnp.int32)
    slot_map = jnp.zeros((slot_count, sum(sizes)), jnp.float32)
    block_base = 0
    for matrix_id in range(len(sizes)):
        inside = (
            (owners[matrix_id] == device)
            & (slot_ids >= starts_list[matrix_id])
            & (slot_ids < starts_list[matrix_id] + sizes[matrix_id])
        )
        target = block_base + slot_ids - starts_list[matrix_id]
        slot_map = slot_map + (inside[:, None] & (target[:, None] == numbers[None, :])).astype(
            jnp.float32
        )
        block_base += sizes[matrix_id]
    return slot_map


def to_matrix(blocks, by_rows):
    if by_rows:
        return blocks.reshape(-1, blocks.shape[2])
    return blocks.transpose(1, 0, 2).reshape(blocks.shape[1], -1)


def to_blocks(matrix, by_rows, features):
    if by_rows:
        return matrix.reshape(-1, features, features)
    return matrix.reshape(features, -1, features).transpose(1, 0, 2)


def all_blocks(matrices, features):
    return jnp.concatenate(
        [to_blocks(matrices[matrix_id], row_kinds[matrix_id], features) for matrix_id in range(6)],
        0,
    )


def adam_update(weight, gradient, first_moment, second, fix_first, fix_second, rate, decay):
    first_new = beta_one * first_moment + (1.0 - beta_one) * gradient
    second_new = beta_two * second + (1.0 - beta_two) * gradient * gradient
    direction = first_new / fix_first / (jnp.sqrt(second_new / fix_second) + adam_eps)
    return (weight - rate * (direction + decay * weight), first_new, second_new)


def scores_for(query_block, key_rows, start_row, segment, head_slope):
    block_rows = query_block.shape[0]
    row_total = key_rows.shape[0]
    row_ids = start_row + jnp.arange(block_rows, dtype=jnp.int32)
    col_ids = jnp.arange(row_total, dtype=jnp.int32)
    distance = (row_ids[:, None] - col_ids[None, :]).astype(jnp.float32)
    seg_rows = lax.dynamic_slice_in_dim(segment, start_row, block_rows)
    allowed = (seg_rows[:, None] == segment[None, :]) & (col_ids[None, :] <= row_ids[:, None])
    raw_score = (
        jnp.dot(query_block, key_rows.T, preferred_element_type=jnp.float32) * 0.125
        - head_slope * distance
    )
    return (jnp.where(allowed, raw_score, masked_score), distance)


def attend(queries, key_rows, values, segment, head_slope, block_rows):
    row_total, head_width = queries.shape

    def per_block(start_row):
        query_block = lax.dynamic_slice_in_dim(queries, start_row, block_rows)
        scores, distance = scores_for(query_block, key_rows, start_row, segment, head_slope)
        largest = jnp.max(scores, -1, keepdims=True)
        log_total = largest + jnp.log(jnp.sum(jnp.exp(scores - largest), -1, keepdims=True))
        probability = jnp.exp(scores - log_total).astype(jnp.bfloat16)
        return (jnp.dot(probability, values, preferred_element_type=jnp.float32), log_total[:, 0])

    row_starts = jnp.arange(row_total // block_rows, dtype=jnp.int32) * block_rows
    attended, log_totals = lax.map(per_block, row_starts)
    return (attended.reshape(row_total, head_width), log_totals.reshape(row_total))


def attend_back(queries, key_rows, values, segment, head_slope, log_totals, grad_out, block_rows):
    row_total, head_width = queries.shape

    def per_block(carried, start_row):
        grad_keys, grad_values, grad_slope = carried
        query_block = lax.dynamic_slice_in_dim(queries, start_row, block_rows)
        grad_block = lax.dynamic_slice_in_dim(grad_out, start_row, block_rows)
        total_block = lax.dynamic_slice_in_dim(log_totals, start_row, block_rows)
        scores, distance = scores_for(query_block, key_rows, start_row, segment, head_slope)
        probability = jnp.exp(scores - total_block[:, None])
        grad_prob = jnp.dot(grad_block, values.T, preferred_element_type=jnp.float32)
        grad_score = (
            probability * (grad_prob - jnp.sum(probability * grad_prob, -1, keepdims=True))
        ).astype(jnp.bfloat16)
        grad_query = jnp.dot(grad_score, key_rows, preferred_element_type=jnp.float32) * 0.125
        grad_keys = (
            grad_keys
            + jnp.dot(grad_score.T, query_block, preferred_element_type=jnp.float32) * 0.125
        )
        grad_values = grad_values + jnp.dot(
            probability.astype(jnp.bfloat16).T, grad_block, preferred_element_type=jnp.float32
        )
        grad_slope = grad_slope - jnp.sum(grad_score.astype(jnp.float32) * distance)
        return ((grad_keys, grad_values, grad_slope), grad_query)

    row_starts = jnp.arange(row_total // block_rows, dtype=jnp.int32) * block_rows
    initial = (
        jnp.zeros((row_total, head_width), jnp.float32),
        jnp.zeros((row_total, head_width), jnp.float32),
        jnp.zeros((), jnp.float32),
    )
    (grad_keys, grad_values, grad_slope), grad_queries = lax.scan(per_block, initial, row_starts)
    return (grad_queries.reshape(row_total, head_width), grad_keys, grad_values, grad_slope)


def body(
    tokens,
    cotangent,
    doc_lengths,
    owners,
    master,
    first_moment,
    second_moment,
    ln_gain,
    ln_bias,
    norm_m,
    norm_v,
    slopes,
    slope_m,
    slope_v,
):
    micro_count, lane_count, tok_rows, features = tokens.shape
    unit_rows = tok_rows // 3
    seq_devices = lax.axis_size("seq")
    head_count = slopes.shape[0]
    head_width = features // head_count
    lane_units = unit_rows * seq_devices
    block_rows = min(512, lane_units)
    unit_total = lane_count * unit_rows
    slot_count = master.shape[1]
    sizes = block_counts(features, FF)
    starts_list = block_starts(owners, sizes)
    batch_rank = lax.axis_index("batch")
    seq_rank = lax.axis_index("seq")
    lane_rank = seq_rank // head_count
    head_rank = seq_rank % head_count
    low_slots = master[0].astype(jnp.bfloat16)
    fetched = []
    for matrix_id in range(6):
        owned_rows = lax.dynamic_slice_in_dim(
            low_slots, starts_list[matrix_id], sizes[matrix_id], 0
        )
        fetched.append(broadcast(owned_rows, "batch", owners[matrix_id]))
    gathered = lax.all_gather(for_sending(tuple(fetched)), "seq", axis=1, tiled=True)
    pool_weight, qkv_weight, out_weight, in_weight, back_weight, up_weight = [
        to_matrix(gathered[matrix_id], row_kinds[matrix_id]) for matrix_id in range(6)
    ]
    doc_ends = running_total(doc_lengths)
    doc_starts = jnp.concatenate(
        [jnp.zeros((micro_count, lane_count, 1), jnp.int32), doc_ends[..., :-1]], -1
    )
    unit_ids = seq_rank * unit_rows + jnp.arange(unit_rows, dtype=jnp.int32)
    keep_mask = 1.0 - jnp.any(
        unit_ids[None, None, :, None] == doc_starts[:, :, None, :], -1
    ).astype(jnp.float32)
    triples = tokens.reshape(micro_count, lane_count, unit_rows, 3, features)
    tail_tokens = triples[:, :, -1, 1:3]
    arrived = passed_along(tail_tokens, "seq", 1)
    lane_pick = jnp.arange(lane_count, dtype=jnp.int32) == lane_rank
    head_pick = jnp.arange(head_count, dtype=jnp.int32) == head_rank
    head_slope = jnp.sum(jnp.where(head_pick, slopes, 0.0))
    positions = jnp.arange(lane_units, dtype=jnp.int32)
    gain_grad = jnp.zeros((2, features), jnp.float32)
    bias_grad = jnp.zeros((2, features), jnp.float32)
    slope_grad = jnp.zeros((), jnp.float32)
    summed = None
    mixed_parts = []
    grad_parts = []
    outgoing = []
    for micro in range(micro_count):
        triple_now = triples[micro]
        keep_now = keep_mask[micro]
        earlier = jnp.concatenate([arrived[micro][:, None], triple_now[:, :-1, 1:3]], 1) * keep_now[
            :, :, None, None
        ].astype(jnp.bfloat16)
        pool_input = jnp.concatenate([earlier, triple_now[:, :, 0:1]], 2).reshape(
            unit_total, 3 * features
        )
        pooled = jnp.dot(pool_input, pool_weight, preferred_element_type=jnp.float32)
        normed = layer_norm(pooled, ln_gain[0], ln_bias[0]).astype(jnp.bfloat16)
        projected = jnp.dot(normed, qkv_weight, preferred_element_type=jnp.float32).astype(
            jnp.bfloat16
        )
        outbound = (
            projected.reshape(lane_count, unit_rows, 3, head_count, head_width)
            .transpose(0, 3, 1, 2, 4)
            .reshape(lane_count * head_count, unit_rows * 3 * head_width)
        )
        received = lax.all_to_all(outbound, "seq", split_axis=0, concat_axis=1, tiled=True).reshape(
            lane_units, 3, head_width
        )
        queries = received[:, 0]
        key_rows = received[:, 1]
        values = received[:, 2]
        lengths = jnp.sum(jnp.where(lane_pick[:, None], doc_lengths[micro], 0), 0)
        lane_ends = running_total(lengths)
        segment = jnp.sum((positions[:, None] >= lane_ends[None, :-1]).astype(jnp.int32), 1)
        attended, log_totals = attend(queries, key_rows, values, segment, head_slope, block_rows)
        returned = lax.all_to_all(
            attended.astype(jnp.bfloat16).reshape(1, lane_units * head_width),
            "seq",
            split_axis=1,
            concat_axis=0,
            tiled=True,
        )
        merged = (
            returned.reshape(lane_count, head_count, unit_rows, head_width)
            .transpose(0, 2, 1, 3)
            .reshape(unit_total, features)
        )
        residual = pooled + jnp.dot(merged, out_weight, preferred_element_type=jnp.float32)
        normed_two = layer_norm(residual, ln_gain[1], ln_bias[1]).astype(jnp.bfloat16)
        hidden = jnp.dot(normed_two, in_weight, preferred_element_type=jnp.float32)
        activated = gelu_tanh(hidden).astype(jnp.bfloat16)
        shortened = residual + jnp.dot(activated, back_weight, preferred_element_type=jnp.float32)
        short_low = shortened.astype(jnp.bfloat16)
        upward = jnp.dot(short_low, up_weight, preferred_element_type=jnp.float32).reshape(
            lane_count, unit_rows * 3, features
        )
        mixed_parts.append(tokens[micro].astype(jnp.float32) + upward)
        grad_upward = cotangent[micro].reshape(unit_total, 3 * features)
        sum_up = jnp.dot(short_low.T, grad_upward, preferred_element_type=jnp.float32)
        grad_short = jnp.dot(grad_upward, up_weight.T, preferred_element_type=jnp.float32)
        grad_short_low = grad_short.astype(jnp.bfloat16)
        sum_back = jnp.dot(activated.T, grad_short_low, preferred_element_type=jnp.float32)
        grad_activated = jnp.dot(grad_short_low, back_weight.T, preferred_element_type=jnp.float32)
        grad_hidden = jax.vjp(gelu_tanh, hidden)[1](grad_activated)[0].astype(jnp.bfloat16)
        sum_in = jnp.dot(normed_two.T, grad_hidden, preferred_element_type=jnp.float32)
        grad_normed_two = jnp.dot(grad_hidden, in_weight.T, preferred_element_type=jnp.float32)
        norm_two_back = jax.vjp(layer_norm, residual, ln_gain[1], ln_bias[1])[1]
        grad_resid_norm, grad_gain_two, grad_bias_two = norm_two_back(grad_normed_two)
        grad_residual = grad_short + grad_resid_norm
        grad_resid_low = grad_residual.astype(jnp.bfloat16)
        sum_out = jnp.dot(merged.T, grad_resid_low, preferred_element_type=jnp.float32)
        grad_merged = jnp.dot(
            grad_resid_low, out_weight.T, preferred_element_type=jnp.float32
        ).astype(jnp.bfloat16)
        back_outbound = (
            grad_merged.reshape(lane_count, unit_rows, head_count, head_width)
            .transpose(0, 2, 1, 3)
            .reshape(lane_count * head_count, unit_rows * head_width)
        )
        grad_attended = lax.all_to_all(
            back_outbound, "seq", split_axis=0, concat_axis=1, tiled=True
        ).reshape(lane_units, head_width)
        grad_queries, grad_keys, grad_values, grad_slope = attend_back(
            queries, key_rows, values, segment, head_slope, log_totals, grad_attended, block_rows
        )
        grad_heads = (
            jnp.stack([grad_queries, grad_keys, grad_values], 1)
            .astype(jnp.bfloat16)
            .reshape(1, lane_units * 3 * head_width)
        )
        grad_arrived = lax.all_to_all(grad_heads, "seq", split_axis=1, concat_axis=0, tiled=True)
        grad_projected = (
            grad_arrived.reshape(lane_count, head_count, unit_rows, 3, head_width)
            .transpose(0, 2, 3, 1, 4)
            .reshape(unit_total, 3 * features)
        )
        sum_qkv = jnp.dot(normed.T, grad_projected, preferred_element_type=jnp.float32)
        grad_normed = jnp.dot(grad_projected, qkv_weight.T, preferred_element_type=jnp.float32)
        norm_one_back = jax.vjp(layer_norm, pooled, ln_gain[0], ln_bias[0])[1]
        grad_pool_norm, grad_gain_one, grad_bias_one = norm_one_back(grad_normed)
        grad_pooled_low = (grad_residual + grad_pool_norm).astype(jnp.bfloat16)
        sum_pool = jnp.dot(pool_input.T, grad_pooled_low, preferred_element_type=jnp.float32)
        grad_pieces = jnp.dot(
            grad_pooled_low, pool_weight.T, preferred_element_type=jnp.float32
        ).reshape(lane_count, unit_rows, 3, features)
        grad_earlier = grad_pieces[:, :, 0:2] * keep_now[:, :, None, None]
        outgoing.append(grad_earlier[:, 0])
        following = jnp.concatenate(
            [grad_earlier[:, 1:], jnp.zeros((lane_count, 1, 2, features), jnp.float32)], 1
        )
        token_grad = jnp.concatenate([grad_pieces[:, :, 2:3], following], 2).reshape(
            lane_count, unit_rows * 3, features
        )
        grad_parts.append(cotangent[micro].astype(jnp.float32) + token_grad)
        gain_grad = gain_grad + jnp.stack([grad_gain_one, grad_gain_two])
        bias_grad = bias_grad + jnp.stack([grad_bias_one, grad_bias_two])
        slope_grad = slope_grad + grad_slope
        micro_grads = [sum_pool, sum_qkv, sum_out, sum_in, sum_back, sum_up]
        summed = (
            micro_grads
            if summed is None
            else [left + right for left, right in zip(summed, micro_grads)]
        )
    reduced = lax.psum_scatter(all_blocks(summed, features), "seq", scatter_dimension=1, tiled=True)
    incoming = passed_along(jnp.stack(outgoing).astype(jnp.bfloat16), "seq", -1).astype(jnp.float32)
    grad_tokens = jnp.stack(grad_parts).reshape(micro_count, lane_count, unit_rows, 3, features)
    grad_tokens = grad_tokens.at[:, :, -1, 1:3].add(incoming).reshape(tokens.shape)
    reduced_all = lax.psum(reduced, "batch")
    norm_grad, slopes_grad = lax.psum(
        (jnp.concatenate([gain_grad, bias_grad], 0), jnp.where(head_pick, slope_grad, 0.0)),
        ("batch", "seq"),
    )
    slot_map = slot_table(owners, batch_rank, sizes, slot_count)
    is_owned = jnp.sum(slot_map, -1)[:, None, None] > 0.5
    slot_grads = jnp.einsum("jb,brc->jrc", slot_map, reduced_all, precision=lax.Precision.HIGHEST)
    step_float = jnp.float32(STEP)
    fix_first = 1.0 - jnp.power(jnp.float32(beta_one), step_float)
    fix_second = 1.0 - jnp.power(jnp.float32(beta_two), step_float)
    new_weight, new_first, new_second = adam_update(
        master[0],
        slot_grads,
        first_moment[0],
        second_moment[0],
        fix_first,
        fix_second,
        rate_matrix,
        decay_rate,
    )
    new_weight = jnp.where(is_owned, new_weight, master[0])
    new_first = jnp.where(is_owned, new_first, first_moment[0])
    new_second = jnp.where(is_owned, new_second, second_moment[0])
    norm_now = jnp.concatenate([ln_gain, ln_bias], 0)
    new_norm, new_norm_m, new_norm_v = adam_update(
        norm_now, norm_grad, norm_m, norm_v, fix_first, fix_second, rate_norm, 0.0
    )
    new_slopes, new_slope_m, new_slope_v = adam_update(
        slopes, slopes_grad, slope_m, slope_v, fix_first, fix_second, rate_slope, 0.0
    )
    return (
        jnp.stack(mixed_parts),
        grad_tokens,
        new_weight[None],
        new_first[None],
        new_second[None],
        new_weight[None].astype(jnp.bfloat16),
        new_norm,
        new_norm_m,
        new_norm_v,
        new_slopes,
        new_slope_m,
        new_slope_v,
    )


MESH = pl.DeviceIdType.MESH
LOW = jnp.bfloat16
WIDE = jnp.float32
TILE = 128


class Plan:
    def __init__(self):
        self.tasks = {}

    def add(self, name, run, deps=(), waits=(), sends=(), cost=0.1, rank=0):
        assert name not in self.tasks
        self.tasks[name] = (run, tuple(deps), tuple(waits), tuple(sends), cost, rank)

    def order(self):
        now, done, arrival, free, listed = 0.0, set(), {}, {}, []
        left = list(self.tasks)
        while left:
            best = None
            for place, name in enumerate(left):
                run, deps, waits, sends, cost, rank = self.tasks[name]
                if any(d not in done for d in deps) or any(w not in arrival for w in waits):
                    continue
                begin = max([now] + [arrival[w] for w in waits])
                key = (begin, rank, place)
                if best is None or key < best[0]:
                    best = (key, name)
            name = best[1]
            run, deps, waits, sends, cost, rank = self.tasks[name]
            now = best[0][0] + cost
            for message, link, size in sends:
                rate, delay = LINKS[link]
                begin = max(now, free.get(link, 0.0))
                free[link] = begin + size / rate
                arrival[message] = free[link] + delay
            done.add(name)
            left.remove(name)
            listed.append((name, now))
        return listed


LINKS = {
    "c": (400e3, 1.0),
    "x": (52e3, 2.3),
    "r": (52e3, 2.3),
    "l": (52e3, 2.3),
    "f": (60e3, 4.0),
}


def start_of(owners, matrix_id, sizes):
    shared = jnp.int32(0)
    for earlier_id in range(matrix_id):
        shared = shared + jnp.where(owners[earlier_id] == owners[matrix_id], sizes[earlier_id], 0)
    return shared


def over_last(fn, value):
    return fn(value, axis=-1, keepdims=True)


def contract(left, right, left_dim, right_dim):
    return lax.dot_general(
        left, right, (((left_dim,), (right_dim,)), ((), ())), preferred_element_type=WIDE
    )


def gelu_parts(value):
    scale = math.sqrt(2.0 / math.pi)
    inner = jnp.tanh(scale * (value + 0.044715 * (value * value * value)))
    return inner, scale * (1.0 + 3 * 0.044715 * value * value)


def main_kernel(dims, refs):
    units, features, hidden_width, heads, micros, sizes = dims
    owners, docs, slopes, gain, bias, tok_hbm, cot_hbm, master_hbm = refs[:8]
    mixed_hbm, grad_hbm, red, small = refs[8:12]
    (
        w, masters, mine, other, core_in, both, x_in, tok, cot, tail_in, wide_tok, wide_cot, x_pool, x_norm, x_att,
        x_two, x_act, x_short, d_up, d_low, d_inner, d_res, d_qkv, d_pool, pooled, hat_one, hat_two, root_one, root_two,
        resid, hidden, short_grad, res_grad, q_out, q_in, a_out, a_in, da_out, da_in, dq_out, dq_in, probs, mixed, grad,
        wide_up, wide_grad, edge_in, g, right_in, left_in, fin_out, fin_in, co_out, co_in, sums, sums_in, sends, recvs, local,
    ) = refs[12:]
    half = features // 2
    width = features // heads
    rows_of = masters.shape[1]
    count = heads
    tokens = 3 * units
    own = micros * units
    pair_width = 2 * width
    b, s = lax.axis_index("batch"), lax.axis_index("seq")
    x, c = b // 2, b % 2
    z, y = s // 2, s % 2
    spot = y * (7 - 2 * z) + z

    def seq_of(position):
        far = position // 4
        return 2 * (position + far * (7 - 2 * position)) + far

    def at(offset):
        return lax.rem(spot + offset + 2 * count, count)

    def rows_at(offset, part=0, length=rows_of):
        return pl.ds(pl.multiple_of(seq_of(at(offset)) * rows_of + part, 16), length)

    my_half = pl.ds(pl.multiple_of(c * half, half), half)
    other_half = pl.ds(pl.multiple_of((1 - c) * half, half), half)
    core_peer = (x * 2 + 1 - c, s)
    x_peer = ((1 - x) * 2 + c, s)
    right_peer = (b, seq_of(at(1)))
    left_peer = (b, seq_of(at(-1)))
    plan = Plan()
    flying = {}

    def send(name, source, target, device):
        index = len(flying)
        flying[name] = pltpu.make_async_remote_copy(
            src_ref=source,
            dst_ref=target,
            send_sem=sends.at[index],
            recv_sem=recvs.at[index],
            device_id=device,
            device_id_type=MESH,
        )
        flying[name].start()

    def nothing():
        pass

    loads = [
        pltpu.make_async_copy(master_hbm, masters, local.at[0]),
        pltpu.make_async_copy(tok_hbm, tok, local.at[1]),
        pltpu.make_async_copy(cot_hbm, cot, local.at[2]),
    ]
    for copy in loads:
        copy.start()
    barrier = pltpu.get_barrier_semaphore()
    for step in range(1, count):
        pl.semaphore_signal(
            barrier, inc=1, device_id=(b, lax.rem(s + step, count)), device_id_type=MESH
        )
    for device in (core_peer, x_peer):
        pl.semaphore_signal(barrier, inc=1, device_id=device, device_id_type=MESH)
    pl.semaphore_wait(barrier, count + 1)

    chunks, first = [], 0
    for size in sizes:
        chunks.append((first, first + size))
        first += size
    gather_order = (0, 1, 2, 3, 5, 4)
    plan.add("ms", loads[0].wait, cost=0.5)

    def contribute(k):
        def run():
            lo, hi = chunks[k]
            mask = (owners[k] == b).astype(WIDE)
            begin = start_of(owners, k, sizes)
            for block in range(lo, hi):
                slot = jnp.minimum(begin + (block - lo), masters.shape[0] - 1)
                mine[block] = (masters[slot, :, my_half] * mask).astype(LOW)
                other[block] = (masters[slot, :, other_half] * mask).astype(LOW)
            send(("g0", k), other.at[lo:hi], core_in.at[lo:hi], core_peer)

        return run

    def join_cores(k):
        def run():
            lo, hi = chunks[k]
            flying[("g0", k)].wait_recv()
            both[lo:hi] = mine[lo:hi] + core_in[lo:hi]
            send(("g1", k), both.at[lo:hi], x_in.at[lo:hi], x_peer)

        return run

    def piece(k, offset, part=0, length=rows_of):
        lo, hi = chunks[k]
        return w.at[lo:hi, c, rows_at(offset, part, length)]

    def join_x(k):
        def run():
            lo, hi = chunks[k]
            flying[("g1", k)].wait_recv()
            w[lo:hi, c, rows_at(0)] = both[lo:hi] + x_in[lo:hi]
            send(("R", 1, k), piece(k, 0), piece(k, 0), right_peer)
            send(("L", 1, k), piece(k, 0), piece(k, 0), left_peer)

        return run

    def forward_piece(k, side, step):
        def run():
            flying[(side, step - 1, k)].wait_recv()
            if step == 5:
                return
            offset = (1 - step) if side == "R" else (step - 1)
            part = piece(k, offset)
            if step == 4:
                part = piece(k, offset, 0 if side == "R" else rows_of // 2, rows_of // 2)
            send((side, step, k), part, part, right_peer if side == "R" else left_peer)

        return run

    def distribute(k):
        def run():
            lo, hi = chunks[k]
            send(("D", k), w.at[lo:hi, c], w.at[lo:hi, c], core_peer)

        return run

    def arrive(*names):
        def run():
            for name in names:
                flying[name].wait_recv()

        return run

    piece_bytes = rows_of * half * 2
    for k in gather_order:
        lo, hi = chunks[k]
        load = (hi - lo) * piece_bytes
        plan.add(
            ("co", k), contribute(k), ["ms"], sends=[(("g0", k), "c", load)], cost=0.15 * (hi - lo)
        )
        plan.add(
            ("cs", k), join_cores(k), [("co", k)], [("g0", k)], [(("g1", k), "x", load)], 0.05 * (hi - lo)
        )
        plan.add(
            ("x", k), join_x(k), [("cs", k)], [("g1", k)],
            [(("R", 1, k), "r", load), (("L", 1, k), "l", load)], 0.05 * (hi - lo),
        )
        for step in (2, 3, 4, 5):
            for side, link in (("R", "r"), ("L", "l")):
                out = [((side, step, k), link, load if step < 4 else load // 2)] if step < 5 else []
                before = ("x", k) if step == 2 else (side, step - 1, "f", k)
                plan.add(
                    (side, step, "f", k), forward_piece(k, side, step), [before], [(side, step - 1, k)], out, 0.05
                )
        plan.add(
            ("di", k), distribute(k), [("R", 5, "f", k), ("L", 5, "f", k)], sends=[(("D", k), "c", 8 * load)], cost=0.05
        )
        plan.add(("h", k), arrive(("D", k)), [("di", k)], [("D", k)], cost=0.02)

    def exchange(name, buffer):
        send(name, buffer.at[0:own], buffer.at[own : 2 * own], core_peer)

    def shared(name, columns):
        return (name, "c", own * columns * 2)

    lead = 16
    tiles = range(features // TILE)

    def columns_at(tile, base=0):
        return slice(base + tile * TILE, base + (tile + 1) * TILE)

    def ends_of(micro):
        ends = []
        total = jnp.int32(0)
        for index in range(docs.shape[1] - 1):
            total = total + docs[micro, index]
            ends.append(total)
        return ends

    def kept(micro):
        ids = s * units + lax.broadcasted_iota(jnp.int32, (units, 1), 0)
        starts = (ids == 0).astype(jnp.int32)
        for end in ends_of(micro):
            starts = starts | (ids == end).astype(jnp.int32)
        return starts == 0

    def load_tokens():
        loads[1].wait()
        send("tl", tok.at[:, tokens - lead :], tail_in, (b, lax.rem(s + 1, count)))
        for micro in range(micros):
            for tile in tiles:
                wide_tok[micro, tile, lead:] = tok[micro, :, columns_at(tile)].astype(WIDE)

    def load_cotangent():
        loads[2].wait()
        for micro in range(micros):
            for tile in tiles:
                wide_cot[micro, tile] = cot[micro, :, columns_at(tile)].astype(WIDE)
                for r in range(3):
                    d_up[micro * units : (micro + 1) * units, columns_at(tile, r * features)] = wide_cot[
                        micro, tile, pl.ds(r, units, stride=3), :
                    ].astype(LOW)
        exchange("eu", d_up)

    def make_pieces():
        flying["tl"].wait_recv()
        for micro in range(micros):
            keep = kept(micro)
            for tile in tiles:
                wide_tok[micro, tile, :lead] = tail_in[micro, :, columns_at(tile)].astype(WIDE)
                for r in range(3):
                    part = wide_tok[micro, tile, pl.ds(lead - 2 + r, units, stride=3), :]
                    if r < 2:
                        part = jnp.where(keep, part, 0.0)
                    x_pool[micro * units : (micro + 1) * units, columns_at(tile, r * features)] = part.astype(LOW)
        exchange("ep", x_pool)

    plan.add("tok", load_tokens, sends=[("tl", "f", 2 * lead * features * 2)], cost=0.3, rank=1)
    plan.add(
        "pc", make_pieces, ["tok"], ["tl"], [shared("ep", 3 * features)], 0.5, rank=1
    )
    plan.add("cot", load_cotangent, (), (), [shared("eu", 3 * features)], 0.5, rank=2)

    def normal(value, which, hat, root):
        centred = value - over_last(jnp.mean, value)
        scale = lax.rsqrt(over_last(jnp.mean, centred * centred) + ln_eps)
        unit = centred * scale
        hat[...] = unit
        root[...] = scale
        return (unit * gain[which : which + 1, :] + bias[which : which + 1, :]).astype(LOW)

    def both_halves(make):
        return jnp.concatenate([make(0), make(1)], axis=1)

    def pool():
        def side(h):
            total = None
            for r in range(3):
                term = contract(x_pool[0:own, r * features : (r + 1) * features], w[r, h], 1, 0)
                total = term if total is None else total + term
            return total

        value = both_halves(side)
        pooled[...] = value
        x_norm[0:own] = normal(value, 0, hat_one, root_one)
        exchange("en", x_norm)

    lane = lambda: lax.broadcasted_iota(jnp.int32, (1, pair_width), 1)

    def swap(value):
        return pltpu.roll(value, width, axis=1)

    def to_heads(tile, target, pair, row):
        low_lanes = lane() < width
        first, second = tile[:units], tile[units:]
        target[2 * pair, row : row + units] = jnp.where(low_lanes, first, swap(second)).astype(LOW)
        target[2 * pair + 1, row : row + units] = jnp.where(low_lanes, swap(first), second).astype(LOW)

    def from_heads(source, pair, row):
        low_lanes = lane() < width
        even = source[2 * pair, row : row + units].astype(WIDE)
        odd = source[2 * pair + 1, row : row + units].astype(WIDE)
        return jnp.where(low_lanes, even, swap(odd)).astype(LOW), jnp.where(low_lanes, swap(even), odd).astype(LOW)

    def spread(name, source, target):
        for step in range(1, count):
            there = lax.rem(s + step, count)
            send((name, step), source.at[there], target.at[s], (b, there))
        target[s] = source[s]

    def spread_names(name):
        return [(name, step) for step in range(1, count)]

    def spread_sends(name, rows):
        return [((name, step), "f", rows * pair_width * 2) for step in range(1, count)]

    def project():
        for part in range(3):
            for h in range(2):
                value = contract(x_norm[0:own], w[3 + part, h], 1, 0)
                for tile in range(half // pair_width):
                    to_heads(
                        value[:, tile * pair_width : (tile + 1) * pair_width],
                        q_out,
                        h * (half // pair_width) + tile,
                        part * units,
                    )
        spread("q", q_out, q_in)

    lane_units = units * count

    def heads_of(source, part):
        return source[:, part * units : (part + 1) * units, :].reshape(lane_units, pair_width)

    def lanes_of(micro):
        return (lane() // width == micro).astype(WIDE).astype(LOW)

    def distances():
        row_ids = lax.broadcasted_iota(jnp.int32, (lane_units, lane_units), 0)
        col_ids = lax.broadcasted_iota(jnp.int32, (lane_units, lane_units), 1)
        return row_ids - col_ids

    def attend_now():
        arrive(*spread_names("q"))()
        queries, keys, values = (heads_of(q_in, part) for part in range(3))
        slope = slopes[s]
        total = None
        for micro in range(micros):
            gap = distances()
            row_seg = jnp.zeros((lane_units, 1), jnp.int32)
            col_seg = jnp.zeros((1, lane_units), jnp.int32)
            for end in ends_of(micro):
                row_seg += (lax.broadcasted_iota(jnp.int32, (lane_units, 1), 0) >= end).astype(jnp.int32)
                col_seg += (lax.broadcasted_iota(jnp.int32, (1, lane_units), 1) >= end).astype(jnp.int32)
            allowed = (row_seg == col_seg) & (gap >= 0)
            mask = lanes_of(micro)
            raw = contract(queries * mask, keys, 1, 1) * 0.125 - slope * gap.astype(WIDE)
            scores = jnp.where(allowed, raw, masked_score)
            raised = jnp.exp(scores - over_last(jnp.max, scores))
            probability = raised / over_last(jnp.sum, raised)
            probs[micro] = probability
            term = contract(probability.astype(LOW), values * mask, 1, 0)
            total = term if total is None else total + term
        a_out[...] = total.astype(LOW).reshape(count, units, pair_width)
        spread("a", a_out, a_in)

    def merge():
        arrive(*spread_names("a"))()
        for pair in range(heads // 2):
            columns = slice(pair * pair_width, (pair + 1) * pair_width)
            first, second = from_heads(a_in, pair, 0)
            x_att[0:units, columns] = first
            x_att[units:own, columns] = second
        exchange("ea", x_att)

    def project_out():
        value = pooled[...] + both_halves(lambda h: contract(x_att[0:own], w[6, h], 1, 0))
        resid[...] = value
        x_two[0:own] = normal(value, 1, hat_two, root_two)
        exchange("et", x_two)

    hidden_blocks = hidden_width // features
    in_base = 7
    back_base = in_base + hidden_blocks
    up_base = back_base + hidden_blocks

    def widen(j):
        def run():
            for h in range(2):
                columns = slice(j * features + h * half, j * features + (h + 1) * half)
                value = contract(x_two[0:own], w[in_base + j, h], 1, 0)
                hidden[:, columns] = value
                inner, _ = gelu_parts(value)
                x_act[0:own, columns] = (0.5 * value * (1.0 + inner)).astype(LOW)
            if j == hidden_blocks - 1:
                exchange("ec", x_act)

        return run

    def narrow():
        def side(h):
            total = resid[:, h * half : (h + 1) * half]
            for j in range(hidden_blocks):
                total = total + contract(
                    x_act[0:own, j * features : (j + 1) * features], w[back_base + j, h], 1, 0
                )
            return total

        x_short[0:own] = both_halves(side).astype(LOW)
        exchange("es", x_short)

    outs = [
        pltpu.make_async_copy(mixed, mixed_hbm, local.at[3]),
        pltpu.make_async_copy(grad, grad_hbm, local.at[4]),
    ]

    def lift(r):
        def run():
            for h in range(2):
                value = contract(x_short[0:own], w[up_base + r, h], 1, 0)
                for micro in range(micros):
                    for tile in range(half // TILE):
                        wide_up[micro, h * (half // TILE) + tile, pl.ds(r, units, stride=3), :] = value[
                            micro * units : (micro + 1) * units, columns_at(tile)
                        ]
            if r == 2:
                for micro in range(micros):
                    for tile in tiles:
                        columns = columns_at(tile)
                        mixed[micro, :, columns] = tok[micro, :, columns].astype(WIDE) + wide_up[micro, tile]
                outs[0].start()

        return run

    plan.add("po", pool, ["pc", ("h", 0)], (), [shared("en", features)], 1.0, rank=3)
    plan.add("pr", project, ["po", ("h", 1)], (), spread_sends("q", 3 * units), 1.5, rank=3)
    plan.add("at", attend_now, ["pr"], spread_names("q"), spread_sends("a", units), 3.0, rank=3)
    plan.add("me", merge, ["at"], spread_names("a"), [shared("ea", features)], 0.3, rank=3)
    plan.add("ou", project_out, ["me", ("h", 2)], (), [shared("et", features)], 0.6, rank=3)
    for j in range(hidden_blocks):
        last = j == hidden_blocks - 1
        plan.add(
            ("wi", j), widen(j), ["ou", ("h", 3)] + ([("wi", i) for i in range(j)] if last else []), (),
            [shared("ec", hidden_width)] if last else (), 0.5, rank=3,
        )
    plan.add(
        "na", narrow, [("wi", j) for j in range(hidden_blocks)] + [("h", 4)], (), [shared("es", features)], 1.0,
        rank=3,
    )
    for r in range(3):
        plan.add(
            ("li", r), lift(r), ["na", ("h", 5), "tok"] + ([("li", i) for i in range(r)]), (), (), 0.4, rank=8
        )

    def back_short():
        total = None
        for r in range(3):
            for h in range(2):
                begin = r * features + h * half
                term = contract(d_up[0:own, begin : begin + half], w[up_base + r, h], 1, 1)
                total = term if total is None else total + term
        short_grad[...] = total
        d_low[0:own] = total.astype(LOW)
        exchange("el", d_low)

    def back_widen(j):
        def run():
            total = contract(d_low[0:own, 0:half], w[back_base + j, 0], 1, 1)
            total = total + contract(d_low[0:own, half:features], w[back_base + j, 1], 1, 1)
            columns = slice(j * features, (j + 1) * features)
            value = hidden[:, columns]
            inner, slope = gelu_parts(value)
            factor = 0.5 * (1.0 + inner) + 0.5 * value * (1.0 - inner * inner) * slope
            d_inner[0:own, columns] = (total * factor).astype(LOW)
            if j == hidden_blocks - 1:
                exchange("ei", d_inner)

        return run

    def back_normal(value, which, hat, root):
        unit = hat[...]
        sums[which : which + 1, :] = jnp.sum(value * unit, axis=0, keepdims=True)
        sums[2 + which : 3 + which, :] = jnp.sum(value, axis=0, keepdims=True)
        scaled = value * gain[which : which + 1, :]
        return root[...] * (
            scaled - over_last(jnp.mean, scaled) - unit * over_last(jnp.mean, scaled * unit)
        )

    def back_two():
        total = None
        for j in range(hidden_blocks):
            for h in range(2):
                begin = j * features + h * half
                term = contract(d_inner[0:own, begin : begin + half], w[in_base + j, h], 1, 1)
                total = term if total is None else total + term
        value = short_grad[...] + back_normal(total, 1, hat_two, root_two)
        res_grad[...] = value
        d_res[0:own] = value.astype(LOW)
        exchange("er", d_res)

    def back_out():
        value = contract(d_res[0:own, 0:half], w[6, 0], 1, 1)
        value = value + contract(d_res[0:own, half:features], w[6, 1], 1, 1)
        for pair in range(heads // 2):
            to_heads(value[:, pair * pair_width : (pair + 1) * pair_width], da_out, pair, 0)
        spread("da", da_out, da_in)

    def back_attend():
        arrive(*spread_names("da"))()
        queries, keys, values = (heads_of(q_in, part) for part in range(3))
        grads = da_in[...].reshape(lane_units, pair_width)
        totals = [None, None, None]
        slope_total = jnp.zeros((1, 1), WIDE)
        for micro in range(micros):
            mask = lanes_of(micro)
            own_grads = grads * mask
            probability = probs[micro]
            grad_prob = contract(own_grads, values, 1, 1)
            scaled = probability * grad_prob
            score = scaled - probability * over_last(jnp.sum, scaled)
            low_score = score.astype(LOW)
            gap = distances().astype(WIDE)
            slope_total = slope_total - jnp.sum(
                jnp.sum(low_score.astype(WIDE) * gap, axis=0, keepdims=True), axis=1, keepdims=True
            )
            terms = (
                contract(low_score, keys * mask, 1, 0) * 0.125,
                contract(low_score, queries * mask, 0, 0) * 0.125,
                contract(probability.astype(LOW), own_grads, 0, 0),
            )
            totals = [term if total is None else total + term for total, term in zip(totals, terms)]
        for part in range(3):
            dq_out[:, part * units : (part + 1) * units, :] = (
                totals[part].astype(LOW).reshape(count, units, pair_width)
            )
        spread("dq", dq_out, dq_in)
        places = lax.broadcasted_iota(jnp.int32, (1, features), 1)
        sums[4:5, :] = jnp.where(places == s, slope_total, 0.0)
        sums[5:8, :] = jnp.zeros((3, features), WIDE)

    def back_project():
        arrive(*spread_names("dq"))()
        for part in range(3):
            for pair in range(heads // 2):
                begin = part * features + pair * pair_width
                first, second = from_heads(dq_in, pair, part * units)
                d_qkv[0:units, begin : begin + pair_width] = first
                d_qkv[units:own, begin : begin + pair_width] = second
        exchange("eq", d_qkv)

    def back_one():
        total = None
        for part in range(3):
            for h in range(2):
                begin = part * features + h * half
                term = contract(d_qkv[0:own, begin : begin + half], w[3 + part, h], 1, 1)
                total = term if total is None else total + term
        value = res_grad[...] + back_normal(total, 0, hat_one, root_one)
        d_pool[0:own] = value.astype(LOW)
        exchange("ed1", d_pool)

    def back_pieces():
        for r in range(3):
            value = contract(d_pool[0:own, 0:half], w[r, 0], 1, 1)
            value = value + contract(d_pool[0:own, half:features], w[r, 1], 1, 1)
            for micro in range(micros):
                part = value[micro * units : (micro + 1) * units]
                if r < 2:
                    part = jnp.where(kept(micro), part, 0.0)
                for tile in tiles:
                    wide_grad[micro, tile, pl.ds(6 + r, units, stride=3), :] = part[:, columns_at(tile)]
        send("ed", wide_grad.at[:, :, 0:8], edge_in, (b, lax.rem(s + count - 1, count)))

    def finish_grad():
        flying["ed"].wait_recv()
        inside = (s < count - 1).astype(WIDE)
        for micro in range(micros):
            for tile in tiles:
                columns = columns_at(tile)
                wide_grad[micro, tile, 6 + tokens : 8 + tokens, :] = edge_in[micro, tile, 6:8, :] * inside
                grad[micro, :, columns] = cot[micro, :, columns].astype(WIDE) + wide_grad[micro, tile, 8 : 8 + tokens]
        outs[1].start()

    plan.add("bs", back_short, ["cot", ("h", 5)], (), [shared("el", features)], 1.0, rank=4)
    for j in range(hidden_blocks):
        last = j == hidden_blocks - 1
        plan.add(
            ("bw", j), back_widen(j),
            ["bs", ("h", 4), ("wi", j)] + ([("bw", i) for i in range(j)] if last else []), (),
            [shared("ei", hidden_width)] if last else (), 0.5, rank=4,
        )
    plan.add(
        "b2", back_two, [("bw", j) for j in range(hidden_blocks)] + [("h", 3)], (),
        [shared("er", features)], 1.2, rank=4,
    )
    plan.add("bo", back_out, ["b2", ("h", 2)], (), spread_sends("da", units), 0.6, rank=4)
    plan.add("ba", back_attend, ["bo", "at"], spread_names("da"), spread_sends("dq", 3 * units), 4.0, rank=4)
    plan.add("bp", back_project, ["ba"], spread_names("dq"), [shared("eq", 3 * features)], 0.5, rank=4)
    plan.add("b1", back_one, ["bp"], (), [shared("ed1", features)], 1.2, rank=4)
    plan.add("bx", back_pieces, ["b1"], (), [("ed", "f", 2 * 8 * features * 4)], 1.0, rank=9)
    plan.add("fg", finish_grad, ["bx", "cot"], ["ed"], (), 0.3, rank=9)

    def add_pair(step, device):
        def run():
            if step > 0:
                flying[("s", step - 1)].wait_recv()
                sums[8 * step : 8 * step + 8] = sums[8 * step - 8 : 8 * step] + sums_in[8 * step - 8 : 8 * step]
            if device is not None:
                send(("s", step), sums.at[8 * step : 8 * step + 8], sums_in.at[8 * step : 8 * step + 8], device)
            else:
                small[...] = sums[8 * step : 8 * step + 8]

        return run

    partners = [
        core_peer,
        x_peer,
        (b, 2 * z + 1 - y),
        (b, 2 * (z + 1 - 2 * (z % 2)) + y),
        (b, 2 * lax.rem(z + 2, 4) + y),
        None,
    ]
    for step, device in enumerate(partners):
        plan.add(
            ("sum", step), add_pair(step, device), ["b1", "ba"] if step == 0 else [("sum", step - 1)],
            [("s", step - 1)] if step else (), [(("s", step), "f", 8 * features * 4)] if device is not None else (), 0.1,
            rank=0,
        )

    for name, columns in (
        ("ep", "pc"), ("en", "po"), ("ea", "me"), ("et", "ou"), ("ec", ("wi", hidden_blocks - 1)),
        ("es", "na"), ("eu", "cot"), ("el", "bs"), ("ei", ("bw", hidden_blocks - 1)),
        ("er", "b2"), ("eq", "bp"), ("ed1", "b1"),
    ):
        plan.add(("got", name), arrive(name), [columns], [name], cost=0.02)

    def columns_of(block):
        return pl.ds(pl.multiple_of(block * features + c * half, half), half)

    def outer(block, left, left_block, right, right_block):
        def run():
            rows = left[:, left_block * features : (left_block + 1) * features]
            g[block] = contract(rows, right[:, columns_of(right_block)], 0, 0).astype(LOW)

        return run

    weight_grads = []
    for r in range(3):
        weight_grads.append((r, x_pool, r, d_pool, 0, [("got", "ep"), ("got", "ed1")]))
        weight_grads.append((3 + r, x_norm, 0, d_qkv, r, [("got", "en"), ("got", "eq")]))
        weight_grads.append((up_base + r, x_short, 0, d_up, r, [("got", "es"), ("got", "eu")]))
    weight_grads.append((6, x_att, 0, d_res, 0, [("got", "ea"), ("got", "er")]))
    for j in range(hidden_blocks):
        weight_grads.append((in_base + j, x_two, 0, d_inner, j, [("got", "et"), ("got", "ei")]))
        weight_grads.append((back_base + j, x_act, j, d_low, 0, [("got", "ec"), ("got", "el")]))
    for block, left, left_block, right, right_block, deps in weight_grads:
        plan.add(("gr", block), outer(block, left, left_block, right, right_block), deps, cost=0.5, rank=5)

    def first_step(k, side):
        def run():
            lo, hi = chunks[k]
            part = 0 if side == "R" else rows_of // 2
            source = g.at[lo:hi, rows_at(4, part, rows_of // 2)]
            inbox = right_in if side == "R" else left_in
            send(
                (side, "s", 1, k), source, inbox.at[0, lo:hi, part : part + rows_of // 2],
                right_peer if side == "R" else left_peer,
            )

        return run

    def next_step(k, side, step):
        def run():
            lo, hi = chunks[k]
            inbox = right_in if side == "R" else left_in
            offset = (5 - step) if side == "R" else (step - 5)
            flying[(side, "s", step - 1, k)].wait_recv()
            part, length = 0, rows_of
            if step == 2:
                part, length = (0 if side == "R" else rows_of // 2), rows_of // 2
            rows = rows_at(offset, part, length)
            g[lo:hi, rows] = g[lo:hi, rows] + inbox[step - 2, lo:hi, part : part + length]
            send(
                (side, "s", step, k), g.at[lo:hi, rows_at(offset)], inbox.at[step - 1, lo:hi],
                right_peer if side == "R" else left_peer,
            )

        return run

    def finish(k):
        def run():
            lo, hi = chunks[k]
            flying[("R", "s", 4, k)].wait_recv()
            flying[("L", "s", 4, k)].wait_recv()
            total = g[lo:hi, rows_at(0)].astype(WIDE) + right_in[3, lo:hi].astype(WIDE) + left_in[3, lo:hi].astype(WIDE)
            fin_out[lo:hi] = total.astype(LOW)
            send(("rx", k), fin_out.at[lo:hi], fin_in.at[lo:hi], x_peer)

        return run

    def finish_x(k):
        def run():
            lo, hi = chunks[k]
            flying[("rx", k)].wait_recv()
            total = (fin_out[lo:hi].astype(WIDE) + fin_in[lo:hi].astype(WIDE)).astype(LOW)
            co_out[lo:hi] = total
            red[lo:hi, :, my_half] = total
            send(("rc", k), co_out.at[lo:hi], co_in.at[lo:hi], core_peer)

        return run

    def finish_core(k):
        def run():
            lo, hi = chunks[k]
            flying[("rc", k)].wait_recv()
            red[lo:hi, :, other_half] = co_in[lo:hi]

        return run

    for k in (5, 4, 3, 2, 1, 0):
        lo, hi = chunks[k]
        load = (hi - lo) * piece_bytes
        for side, link in (("R", "r"), ("L", "l")):
            plan.add(
                (side, "r", 1, k), first_step(k, side), [("gr", block) for block in range(lo, hi)], (),
                [((side, "s", 1, k), link, load // 2)], 0.05,
            )
        for step in (2, 3, 4):
            for side, link in (("R", "r"), ("L", "l")):
                plan.add(
                    (side, "r", step, k), next_step(k, side, step), [(side, "r", step - 1, k)], [(side, "s", step - 1, k)],
                    [((side, "s", step, k), link, load)], 0.05 * (hi - lo),
                )
        plan.add(
            ("fi", k), finish(k), [("R", "r", 4, k), ("L", "r", 4, k)], [("R", "s", 4, k), ("L", "s", 4, k)], [(("rx", k), "x", load)],
            0.05 * (hi - lo),
        )
        plan.add(
            ("fx", k), finish_x(k), [("fi", k)], [("rx", k)], [(("rc", k), "c", load)], 0.05 * (hi - lo)
        )
        plan.add(("fc", k), finish_core(k), [("fx", k)], [("rc", k)], (), 0.03 * (hi - lo))

    for name, _ in plan.order():
        plan.tasks[name][0]()
    for name, copy in flying.items():
        copy.wait_send()
    for copy in outs:
        copy.wait()


def adam_kernel(sizes, refs):
    owners, red, small, norm, norm_m, norm_v, slope, slope_m, slope_v, master, first, second, mixed, grad = refs[:14]
    (
        new_w, new_m, new_v, new_low, norm_out, norm_m_out, norm_v_out, slope_out, slope_m_out, slope_v_out, mixed_out,
        grad_out, sems,
    ) = refs[14:]
    step = pl.program_id(0)
    copies = [
        pltpu.make_async_copy(mixed, mixed_out, sems.at[0]),
        pltpu.make_async_copy(grad, grad_out, sems.at[1]),
    ]
    fix_first = 1.0 - beta_one**STEP
    fix_second = 1.0 - beta_two**STEP

    @pl.when(step == 0)
    def _():
        for copy in copies:
            copy.start()
        norm_out[...], norm_m_out[...], norm_v_out[...] = adam_update(
            norm[...], small[0:4], norm_m[...], norm_v[...], fix_first, fix_second, rate_norm, 0.0
        )
        heads = slope.shape[1]
        slope_out[...], slope_m_out[...], slope_v_out[...] = adam_update(
            slope[...], small[4:5, 0:heads], slope_m[...], slope_v[...], fix_first, fix_second, rate_slope, 0.0
        )

    me = lax.axis_index("batch")
    block, held, base = jnp.int32(0), jnp.int32(0), 0
    for matrix_id, size in enumerate(sizes):
        begin = start_of(owners, matrix_id, sizes)
        inside = (owners[matrix_id] == me) & (step >= begin) & (step < begin + size)
        block = jnp.where(inside, base + step - begin, block)
        held = jnp.where(inside, 1, held)
        base += size
    gradient = red[block].astype(WIDE)
    values = adam_update(
        master[0], gradient, first[0], second[0], fix_first, fix_second, rate_matrix, decay_rate
    )
    keep = jnp.full(gradient.shape, held, jnp.int32) > 0
    weight = jnp.where(keep, values[0], master[0])
    new_w[0] = weight
    new_m[0] = jnp.where(keep, values[1], first[0])
    new_v[0] = jnp.where(keep, values[2], second[0])
    new_low[0] = weight.astype(LOW)

    @pl.when(step == pl.num_programs(0) - 1)
    def _():
        for copy in copies:
            copy.wait()


def fused_body(tokens, cotangent, doc_lengths, owners, master, first_moment, second_moment, ln_gain, ln_bias, norm_m, norm_v, slopes, slope_m, slope_v):
    micros, _, tok_rows, features = tokens.shape
    units, heads, width = tok_rows // 3, slopes.shape[0], features // slopes.shape[0]
    sizes = tuple(block_counts(features, FF))
    blocks, own, half = sum(sizes), micros * units, features // 2
    slots, rows = master.shape[1], master.shape[2]
    lane_units = units * heads
    split = features // TILE
    hbm, vmem, smem = (pl.BlockSpec(memory_space=m) for m in (pl.ANY, pltpu.VMEM, pltpu.SMEM))
    low = lambda *shape: pltpu.VMEM(shape, LOW)
    wide = lambda *shape: pltpu.VMEM(shape, WIDE)
    pieces = lambda: low(blocks, rows, half)
    both = lambda columns: low(2 * own, columns)
    scratch = [
        low(blocks, 2, features, half), wide(slots, rows, features), pieces(), pieces(), pieces(), pieces(), pieces(),
        low(micros, tok_rows, features), low(micros, tok_rows, features), low(micros, 16, features),
        wide(micros, split, 16 + tok_rows, TILE), wide(micros, split, tok_rows, TILE),
        both(3 * features), both(features), both(features), both(features), both(FF), both(features),
        both(3 * features), both(features), both(FF), both(features), both(3 * features), both(features),
        wide(own, features), wide(own, features), wide(own, features), wide(own, 1), wide(own, 1),
        wide(own, features), wide(own, FF), wide(own, features), wide(own, features),
        low(heads, 3 * units, 2 * width), low(heads, 3 * units, 2 * width), low(heads, units, 2 * width),
        low(heads, units, 2 * width), low(heads, units, 2 * width), low(heads, units, 2 * width),
        low(heads, 3 * units, 2 * width), low(heads, 3 * units, 2 * width),
        wide(micros, lane_units, lane_units), wide(micros, tok_rows, features), wide(micros, tok_rows, features),
        wide(micros, split, tok_rows, TILE), wide(micros, split, 8 + tok_rows, TILE), wide(micros, split, 8, TILE), low(blocks, features, half), low(4, blocks, rows, half), low(4, blocks, rows, half),
        pieces(), pieces(), pieces(), pieces(), wide(48, features), wide(40, features),
        pltpu.SemaphoreType.DMA((200,)), pltpu.SemaphoreType.DMA((200,)), pltpu.SemaphoreType.DMA((5,)),
    ]
    token_shape = (micros, tok_rows, features)
    dims = (units, features, FF, heads, micros, sizes)
    mixed, grad, red, small = pl.pallas_call(
        lambda *refs: main_kernel(dims, refs),
        out_shape=(
            jax.ShapeDtypeStruct(token_shape, WIDE),
            jax.ShapeDtypeStruct(token_shape, WIDE),
            jax.ShapeDtypeStruct((blocks, rows, features), LOW),
            jax.ShapeDtypeStruct((8, features), WIDE),
        ),
        in_specs=[smem, smem, smem, vmem, vmem, hbm, hbm, hbm],
        out_specs=(hbm, hbm, vmem, vmem),
        scratch_shapes=scratch,
        compiler_params=pltpu.CompilerParams(
            collective_id=0, has_side_effects=True, vmem_limit_bytes=60 * 2**20
        ),
        name="block",
    )(
        owners, doc_lengths[:, 0], slopes, ln_gain, ln_bias, tokens[:, 0], cotangent[:, 0], master[0]
    )
    slot = pl.BlockSpec((1, rows, features), lambda j: (j, 0, 0))
    moment_shape = jax.ShapeDtypeStruct((slots, rows, features), WIDE)
    norm_shape = jax.ShapeDtypeStruct((4, features), WIDE)
    slope_shape = jax.ShapeDtypeStruct((1, heads), WIDE)
    out = pl.pallas_call(
        lambda *refs: adam_kernel(sizes, refs),
        grid=(slots,),
        out_shape=(
            moment_shape, moment_shape, moment_shape, jax.ShapeDtypeStruct((slots, rows, features), LOW),
            norm_shape, norm_shape, norm_shape, slope_shape, slope_shape, slope_shape,
            jax.ShapeDtypeStruct(token_shape, WIDE), jax.ShapeDtypeStruct(token_shape, WIDE),
        ),
        in_specs=[smem] + [vmem] * 8 + [slot] * 3 + [hbm] * 2,
        out_specs=(slot, slot, slot, slot, vmem, vmem, vmem, vmem, vmem, vmem, hbm, hbm),
        scratch_shapes=[pltpu.SemaphoreType.DMA((2,))],
        compiler_params=pltpu.CompilerParams(dimension_semantics=("arbitrary",)),
        name="adam",
    )(
        owners, red, small, jnp.concatenate([ln_gain, ln_bias], 0), norm_m, norm_v, slopes[None], slope_m[None],
        slope_v[None], master[0], first_moment[0], second_moment[0], mixed, grad,
    )
    new_w, new_m, new_v, new_low, norm, norm_m, norm_v, slope, slope_m, slope_v, mixed, grad = out
    return (
        mixed[:, None], grad[:, None], new_w[None], new_m[None], new_v[None], new_low[None], norm, norm_m, norm_v,
        slope[0], slope_m[0], slope_v[0],
    )


def fits(mesh, shapes):
    return mesh.shape["batch"] == 4 and mesh.shape["seq"] == 8 and shapes[0].shape[1] == 1


def solution(mesh):
    in_specs = (
        P("batch", None, "seq", None),
        P("batch", None, "seq", None),
        P("batch", None, None),
        P(),
        P("batch", None, "seq", None),
        P("batch", None, "seq", None),
        P("batch", None, "seq", None),
        P(),
        P(),
        P(),
        P(),
        P(),
        P(),
        P(),
    )
    out_specs = (
        P("batch", None, "seq", None),
        P("batch", None, "seq", None),
        P("batch", None, "seq", None),
        P("batch", None, "seq", None),
        P("batch", None, "seq", None),
        P("batch", None, "seq", None),
        P(),
        P(),
        P(),
        P(),
        P(),
        P(),
    )

    def whole(*args):
        part = fused_body if fits(mesh, args) else body
        return jax.shard_map(
            part, mesh=mesh, in_specs=in_specs, out_specs=out_specs, check_vma=False
        )(*args)

    return whole
```

```python
import math

import jax
import jax.numpy as jnp
from jax import lax
from jax.experimental import pallas as pl
from jax.experimental.pallas import tpu as pltpu
from jax.sharding import PartitionSpec as P

FF = 2048
STEP = 10


beta_one = 0.9
beta_two = 0.95
adam_eps = 1e-08
decay_rate = 0.1
rate_matrix = 0.02
rate_norm = 0.2
rate_slope = 0.01
ln_eps = 1e-05
masked_score = -1000000000.0
row_kinds = (True, False, True, False, True, False)


def broadcast(value, axis, source):
    kept = jnp.where(lax.axis_index(axis) == source, value, 0).astype(value.dtype)
    return lax.psum(kept, axis)


def running_total(lengths):
    count = lengths.shape[-1]
    ends = [lengths[..., 0]]
    for index in range(1, count):
        ends.append(ends[-1] + lengths[..., index])
    return jnp.stack(ends, -1)


def for_sending(value):

    def short(part):
        return part.astype(jnp.bfloat16) if part.dtype == jnp.float32 else part

    return jax.tree.map(short, value)


def passed_along(value, axis, by):
    peers = lax.axis_size(axis)
    pairs = [(i, i + by) for i in range(peers) if 0 <= i + by < peers]
    return lax.ppermute(value, axis, pairs)


def layer_norm(values, gain, shift):
    center = jnp.mean(values, -1, keepdims=True)
    centred = values - center
    spread = jnp.mean(centred * centred, -1, keepdims=True)
    return centred * lax.rsqrt(spread + ln_eps) * gain + shift


def gelu_tanh(values):
    return jax.nn.gelu(values, approximate=True)


def block_counts(features, hidden):
    return [3, 3, 1, hidden // features, hidden // features, 3]


def block_starts(owners, sizes):
    starts_list = []
    for matrix_id in range(len(sizes)):
        shared = jnp.zeros((), jnp.int32)
        for earlier_id in range(matrix_id):
            shared = shared + jnp.where(
                owners[earlier_id] == owners[matrix_id], sizes[earlier_id], 0
            ).astype(jnp.int32)
        starts_list.append(shared)
    return starts_list


def slot_table(owners, device, sizes, slot_count):
    starts_list = block_starts(owners, sizes)
    slot_ids = jnp.arange(slot_count, dtype=jnp.int32)
    numbers = jnp.arange(sum(sizes), dtype=jnp.int32)
    slot_map = jnp.zeros((slot_count, sum(sizes)), jnp.float32)
    block_base = 0
    for matrix_id in range(len(sizes)):
        inside = (
            (owners[matrix_id] == device)
            & (slot_ids >= starts_list[matrix_id])
            & (slot_ids < starts_list[matrix_id] + sizes[matrix_id])
        )
        target = block_base + slot_ids - starts_list[matrix_id]
        slot_map = slot_map + (inside[:, None] & (target[:, None] == numbers[None, :])).astype(
            jnp.float32
        )
        block_base += sizes[matrix_id]
    return slot_map


def to_matrix(blocks, by_rows):
    if by_rows:
        return blocks.reshape(-1, blocks.shape[2])
    return blocks.transpose(1, 0, 2).reshape(blocks.shape[1], -1)


def to_blocks(matrix, by_rows, features):
    if by_rows:
        return matrix.reshape(-1, features, features)
    return matrix.reshape(features, -1, features).transpose(1, 0, 2)


def all_blocks(matrices, features):
    return jnp.concatenate(
        [to_blocks(matrices[matrix_id], row_kinds[matrix_id], features) for matrix_id in range(6)],
        0,
    )


def adam_update(weight, gradient, first_moment, second, fix_first, fix_second, rate, decay):
    first_new = beta_one * first_moment + (1.0 - beta_one) * gradient
    second_new = beta_two * second + (1.0 - beta_two) * gradient * gradient
    direction = first_new / fix_first / (jnp.sqrt(second_new / fix_second) + adam_eps)
    return (weight - rate * (direction + decay * weight), first_new, second_new)


def scores_for(query_block, key_rows, start_row, segment, head_slope):
    block_rows = query_block.shape[0]
    row_total = key_rows.shape[0]
    row_ids = start_row + jnp.arange(block_rows, dtype=jnp.int32)
    col_ids = jnp.arange(row_total, dtype=jnp.int32)
    distance = (row_ids[:, None] - col_ids[None, :]).astype(jnp.float32)
    seg_rows = lax.dynamic_slice_in_dim(segment, start_row, block_rows)
    allowed = (seg_rows[:, None] == segment[None, :]) & (col_ids[None, :] <= row_ids[:, None])
    raw_score = (
        jnp.dot(query_block, key_rows.T, preferred_element_type=jnp.float32) * 0.125
        - head_slope * distance
    )
    return (jnp.where(allowed, raw_score, masked_score), distance)


def attend(queries, key_rows, values, segment, head_slope, block_rows):
    row_total, head_width = queries.shape

    def per_block(start_row):
        query_block = lax.dynamic_slice_in_dim(queries, start_row, block_rows)
        scores, distance = scores_for(query_block, key_rows, start_row, segment, head_slope)
        largest = jnp.max(scores, -1, keepdims=True)
        log_total = largest + jnp.log(jnp.sum(jnp.exp(scores - largest), -1, keepdims=True))
        probability = jnp.exp(scores - log_total).astype(jnp.bfloat16)
        return (jnp.dot(probability, values, preferred_element_type=jnp.float32), log_total[:, 0])

    row_starts = jnp.arange(row_total // block_rows, dtype=jnp.int32) * block_rows
    attended, log_totals = lax.map(per_block, row_starts)
    return (attended.reshape(row_total, head_width), log_totals.reshape(row_total))


def attend_back(queries, key_rows, values, segment, head_slope, log_totals, grad_out, block_rows):
    row_total, head_width = queries.shape

    def per_block(carried, start_row):
        grad_keys, grad_values, grad_slope = carried
        query_block = lax.dynamic_slice_in_dim(queries, start_row, block_rows)
        grad_block = lax.dynamic_slice_in_dim(grad_out, start_row, block_rows)
        total_block = lax.dynamic_slice_in_dim(log_totals, start_row, block_rows)
        scores, distance = scores_for(query_block, key_rows, start_row, segment, head_slope)
        probability = jnp.exp(scores - total_block[:, None])
        grad_prob = jnp.dot(grad_block, values.T, preferred_element_type=jnp.float32)
        grad_score = (
            probability * (grad_prob - jnp.sum(probability * grad_prob, -1, keepdims=True))
        ).astype(jnp.bfloat16)
        grad_query = jnp.dot(grad_score, key_rows, preferred_element_type=jnp.float32) * 0.125
        grad_keys = (
            grad_keys
            + jnp.dot(grad_score.T, query_block, preferred_element_type=jnp.float32) * 0.125
        )
        grad_values = grad_values + jnp.dot(
            probability.astype(jnp.bfloat16).T, grad_block, preferred_element_type=jnp.float32
        )
        grad_slope = grad_slope - jnp.sum(grad_score.astype(jnp.float32) * distance)
        return ((grad_keys, grad_values, grad_slope), grad_query)

    row_starts = jnp.arange(row_total // block_rows, dtype=jnp.int32) * block_rows
    initial = (
        jnp.zeros((row_total, head_width), jnp.float32),
        jnp.zeros((row_total, head_width), jnp.float32),
        jnp.zeros((), jnp.float32),
    )
    (grad_keys, grad_values, grad_slope), grad_queries = lax.scan(per_block, initial, row_starts)
    return (grad_queries.reshape(row_total, head_width), grad_keys, grad_values, grad_slope)


def body(
    tokens,
    cotangent,
    doc_lengths,
    owners,
    master,
    first_moment,
    second_moment,
    ln_gain,
    ln_bias,
    norm_m,
    norm_v,
    slopes,
    slope_m,
    slope_v,
):
    micro_count, lane_count, tok_rows, features = tokens.shape
    unit_rows = tok_rows // 3
    seq_devices = lax.axis_size("seq")
    head_count = slopes.shape[0]
    head_width = features // head_count
    lane_units = unit_rows * seq_devices
    block_rows = min(512, lane_units)
    unit_total = lane_count * unit_rows
    slot_count = master.shape[1]
    sizes = block_counts(features, FF)
    starts_list = block_starts(owners, sizes)
    batch_rank = lax.axis_index("batch")
    seq_rank = lax.axis_index("seq")
    lane_rank = seq_rank // head_count
    head_rank = seq_rank % head_count
    low_slots = master[0].astype(jnp.bfloat16)
    fetched = []
    for matrix_id in range(6):
        owned_rows = lax.dynamic_slice_in_dim(
            low_slots, starts_list[matrix_id], sizes[matrix_id], 0
        )
        fetched.append(broadcast(owned_rows, "batch", owners[matrix_id]))
    gathered = lax.all_gather(for_sending(tuple(fetched)), "seq", axis=1, tiled=True)
    pool_weight, qkv_weight, out_weight, in_weight, back_weight, up_weight = [
        to_matrix(gathered[matrix_id], row_kinds[matrix_id]) for matrix_id in range(6)
    ]
    doc_ends = running_total(doc_lengths)
    doc_starts = jnp.concatenate(
        [jnp.zeros((micro_count, lane_count, 1), jnp.int32), doc_ends[..., :-1]], -1
    )
    unit_ids = seq_rank * unit_rows + jnp.arange(unit_rows, dtype=jnp.int32)
    keep_mask = 1.0 - jnp.any(
        unit_ids[None, None, :, None] == doc_starts[:, :, None, :], -1
    ).astype(jnp.float32)
    triples = tokens.reshape(micro_count, lane_count, unit_rows, 3, features)
    tail_tokens = triples[:, :, -1, 1:3]
    arrived = passed_along(tail_tokens, "seq", 1)
    lane_pick = jnp.arange(lane_count, dtype=jnp.int32) == lane_rank
    head_pick = jnp.arange(head_count, dtype=jnp.int32) == head_rank
    head_slope = jnp.sum(jnp.where(head_pick, slopes, 0.0))
    positions = jnp.arange(lane_units, dtype=jnp.int32)
    gain_grad = jnp.zeros((2, features), jnp.float32)
    bias_grad = jnp.zeros((2, features), jnp.float32)
    slope_grad = jnp.zeros((), jnp.float32)
    summed = None
    mixed_parts = []
    grad_parts = []
    outgoing = []
    for micro in range(micro_count):
        triple_now = triples[micro]
        keep_now = keep_mask[micro]
        earlier = jnp.concatenate([arrived[micro][:, None], triple_now[:, :-1, 1:3]], 1) * keep_now[
            :, :, None, None
        ].astype(jnp.bfloat16)
        pool_input = jnp.concatenate([earlier, triple_now[:, :, 0:1]], 2).reshape(
            unit_total, 3 * features
        )
        pooled = jnp.dot(pool_input, pool_weight, preferred_element_type=jnp.float32)
        normed = layer_norm(pooled, ln_gain[0], ln_bias[0]).astype(jnp.bfloat16)
        projected = jnp.dot(normed, qkv_weight, preferred_element_type=jnp.float32).astype(
            jnp.bfloat16
        )
        outbound = (
            projected.reshape(lane_count, unit_rows, 3, head_count, head_width)
            .transpose(0, 3, 1, 2, 4)
            .reshape(lane_count * head_count, unit_rows * 3 * head_width)
        )
        received = lax.all_to_all(outbound, "seq", split_axis=0, concat_axis=1, tiled=True).reshape(
            lane_units, 3, head_width
        )
        queries = received[:, 0]
        key_rows = received[:, 1]
        values = received[:, 2]
        lengths = jnp.sum(jnp.where(lane_pick[:, None], doc_lengths[micro], 0), 0)
        lane_ends = running_total(lengths)
        segment = jnp.sum((positions[:, None] >= lane_ends[None, :-1]).astype(jnp.int32), 1)
        attended, log_totals = attend(queries, key_rows, values, segment, head_slope, block_rows)
        returned = lax.all_to_all(
            attended.astype(jnp.bfloat16).reshape(1, lane_units * head_width),
            "seq",
            split_axis=1,
            concat_axis=0,
            tiled=True,
        )
        merged = (
            returned.reshape(lane_count, head_count, unit_rows, head_width)
            .transpose(0, 2, 1, 3)
            .reshape(unit_total, features)
        )
        residual = pooled + jnp.dot(merged, out_weight, preferred_element_type=jnp.float32)
        normed_two = layer_norm(residual, ln_gain[1], ln_bias[1]).astype(jnp.bfloat16)
        hidden = jnp.dot(normed_two, in_weight, preferred_element_type=jnp.float32)
        activated = gelu_tanh(hidden).astype(jnp.bfloat16)
        shortened = residual + jnp.dot(activated, back_weight, preferred_element_type=jnp.float32)
        short_low = shortened.astype(jnp.bfloat16)
        upward = jnp.dot(short_low, up_weight, preferred_element_type=jnp.float32).reshape(
            lane_count, unit_rows * 3, features
        )
        mixed_parts.append(tokens[micro].astype(jnp.float32) + upward)
        grad_upward = cotangent[micro].reshape(unit_total, 3 * features)
        sum_up = jnp.dot(short_low.T, grad_upward, preferred_element_type=jnp.float32)
        grad_short = jnp.dot(grad_upward, up_weight.T, preferred_element_type=jnp.float32)
        grad_short_low = grad_short.astype(jnp.bfloat16)
        sum_back = jnp.dot(activated.T, grad_short_low, preferred_element_type=jnp.float32)
        grad_activated = jnp.dot(grad_short_low, back_weight.T, preferred_element_type=jnp.float32)
        grad_hidden = jax.vjp(gelu_tanh, hidden)[1](grad_activated)[0].astype(jnp.bfloat16)
        sum_in = jnp.dot(normed_two.T, grad_hidden, preferred_element_type=jnp.float32)
        grad_normed_two = jnp.dot(grad_hidden, in_weight.T, preferred_element_type=jnp.float32)
        norm_two_back = jax.vjp(layer_norm, residual, ln_gain[1], ln_bias[1])[1]
        grad_resid_norm, grad_gain_two, grad_bias_two = norm_two_back(grad_normed_two)
        grad_residual = grad_short + grad_resid_norm
        grad_resid_low = grad_residual.astype(jnp.bfloat16)
        sum_out = jnp.dot(merged.T, grad_resid_low, preferred_element_type=jnp.float32)
        grad_merged = jnp.dot(
            grad_resid_low, out_weight.T, preferred_element_type=jnp.float32
        ).astype(jnp.bfloat16)
        back_outbound = (
            grad_merged.reshape(lane_count, unit_rows, head_count, head_width)
            .transpose(0, 2, 1, 3)
            .reshape(lane_count * head_count, unit_rows * head_width)
        )
        grad_attended = lax.all_to_all(
            back_outbound, "seq", split_axis=0, concat_axis=1, tiled=True
        ).reshape(lane_units, head_width)
        grad_queries, grad_keys, grad_values, grad_slope = attend_back(
            queries, key_rows, values, segment, head_slope, log_totals, grad_attended, block_rows
        )
        grad_heads = (
            jnp.stack([grad_queries, grad_keys, grad_values], 1)
            .astype(jnp.bfloat16)
            .reshape(1, lane_units * 3 * head_width)
        )
        grad_arrived = lax.all_to_all(grad_heads, "seq", split_axis=1, concat_axis=0, tiled=True)
        grad_projected = (
            grad_arrived.reshape(lane_count, head_count, unit_rows, 3, head_width)
            .transpose(0, 2, 3, 1, 4)
            .reshape(unit_total, 3 * features)
        )
        sum_qkv = jnp.dot(normed.T, grad_projected, preferred_element_type=jnp.float32)
        grad_normed = jnp.dot(grad_projected, qkv_weight.T, preferred_element_type=jnp.float32)
        norm_one_back = jax.vjp(layer_norm, pooled, ln_gain[0], ln_bias[0])[1]
        grad_pool_norm, grad_gain_one, grad_bias_one = norm_one_back(grad_normed)
        grad_pooled_low = (grad_residual + grad_pool_norm).astype(jnp.bfloat16)
        sum_pool = jnp.dot(pool_input.T, grad_pooled_low, preferred_element_type=jnp.float32)
        grad_pieces = jnp.dot(
            grad_pooled_low, pool_weight.T, preferred_element_type=jnp.float32
        ).reshape(lane_count, unit_rows, 3, features)
        grad_earlier = grad_pieces[:, :, 0:2] * keep_now[:, :, None, None]
        outgoing.append(grad_earlier[:, 0])
        following = jnp.concatenate(
            [grad_earlier[:, 1:], jnp.zeros((lane_count, 1, 2, features), jnp.float32)], 1
        )
        token_grad = jnp.concatenate([grad_pieces[:, :, 2:3], following], 2).reshape(
            lane_count, unit_rows * 3, features
        )
        grad_parts.append(cotangent[micro].astype(jnp.float32) + token_grad)
        gain_grad = gain_grad + jnp.stack([grad_gain_one, grad_gain_two])
        bias_grad = bias_grad + jnp.stack([grad_bias_one, grad_bias_two])
        slope_grad = slope_grad + grad_slope
        micro_grads = [sum_pool, sum_qkv, sum_out, sum_in, sum_back, sum_up]
        summed = (
            micro_grads
            if summed is None
            else [left + right for left, right in zip(summed, micro_grads)]
        )
    reduced = lax.psum_scatter(all_blocks(summed, features), "seq", scatter_dimension=1, tiled=True)
    incoming = passed_along(jnp.stack(outgoing).astype(jnp.bfloat16), "seq", -1).astype(jnp.float32)
    grad_tokens = jnp.stack(grad_parts).reshape(micro_count, lane_count, unit_rows, 3, features)
    grad_tokens = grad_tokens.at[:, :, -1, 1:3].add(incoming).reshape(tokens.shape)
    reduced_all = lax.psum(reduced, "batch")
    norm_grad, slopes_grad = lax.psum(
        (jnp.concatenate([gain_grad, bias_grad], 0), jnp.where(head_pick, slope_grad, 0.0)),
        ("batch", "seq"),
    )
    slot_map = slot_table(owners, batch_rank, sizes, slot_count)
    is_owned = jnp.sum(slot_map, -1)[:, None, None] > 0.5
    slot_grads = jnp.einsum("jb,brc->jrc", slot_map, reduced_all, precision=lax.Precision.HIGHEST)
    step_float = jnp.float32(STEP)
    fix_first = 1.0 - jnp.power(jnp.float32(beta_one), step_float)
    fix_second = 1.0 - jnp.power(jnp.float32(beta_two), step_float)
    new_weight, new_first, new_second = adam_update(
        master[0],
        slot_grads,
        first_moment[0],
        second_moment[0],
        fix_first,
        fix_second,
        rate_matrix,
        decay_rate,
    )
    new_weight = jnp.where(is_owned, new_weight, master[0])
    new_first = jnp.where(is_owned, new_first, first_moment[0])
    new_second = jnp.where(is_owned, new_second, second_moment[0])
    norm_now = jnp.concatenate([ln_gain, ln_bias], 0)
    new_norm, new_norm_m, new_norm_v = adam_update(
        norm_now, norm_grad, norm_m, norm_v, fix_first, fix_second, rate_norm, 0.0
    )
    new_slopes, new_slope_m, new_slope_v = adam_update(
        slopes, slopes_grad, slope_m, slope_v, fix_first, fix_second, rate_slope, 0.0
    )
    return (
        jnp.stack(mixed_parts),
        grad_tokens,
        new_weight[None],
        new_first[None],
        new_second[None],
        new_weight[None].astype(jnp.bfloat16),
        new_norm,
        new_norm_m,
        new_norm_v,
        new_slopes,
        new_slope_m,
        new_slope_v,
    )


MESH = pl.DeviceIdType.MESH
LOW = jnp.bfloat16
WIDE = jnp.float32
TILE = 128


class Plan:
    def __init__(self):
        self.tasks = {}

    def add(self, name, run, deps=(), waits=(), sends=(), cost=0.1, rank=0):
        assert name not in self.tasks
        self.tasks[name] = (run, tuple(deps), tuple(waits), tuple(sends), cost, rank)

    def order(self):
        now, done, arrival, free, listed = 0.0, set(), {}, {}, []
        left = list(self.tasks)
        while left:
            best = None
            for place, name in enumerate(left):
                run, deps, waits, sends, cost, rank = self.tasks[name]
                if any(d not in done for d in deps) or any(w not in arrival for w in waits):
                    continue
                begin = max([now] + [arrival[w] for w in waits] + [free.get(m[1], 0.0) - SLACK for m in sends])
                key = (begin, rank, place)
                if best is None or key < best[0]:
                    best = (key, name)
            name = best[1]
            run, deps, waits, sends, cost, rank = self.tasks[name]
            now = best[0][0] + cost
            for message, link, size in sends:
                rate, delay = LINKS[link]
                begin = max(now, free.get(link, 0.0))
                free[link] = begin + size / rate
                arrival[message] = free[link] + delay
            done.add(name)
            left.remove(name)
            listed.append((name, now))
        return listed


SLACK = 1.5
LINKS = {
    "c": (400e3, 1.0),
    "x": (52e3, 2.3),
    "r": (52e3, 2.3),
    "l": (52e3, 2.3),
    "f": (60e3, 4.0),
}


def start_of(owners, matrix_id, sizes):
    shared = jnp.int32(0)
    for earlier_id in range(matrix_id):
        shared = shared + jnp.where(owners[earlier_id] == owners[matrix_id], sizes[earlier_id], 0)
    return shared


def over_last(fn, value):
    return fn(value, axis=-1, keepdims=True)


def contract(left, right, left_dim, right_dim):
    return lax.dot_general(
        left, right, (((left_dim,), (right_dim,)), ((), ())), preferred_element_type=WIDE
    )


def gelu_parts(value):
    scale = math.sqrt(2.0 / math.pi)
    inner = jnp.tanh(scale * (value + 0.044715 * (value * value * value)))
    return inner, scale * (1.0 + 3 * 0.044715 * value * value)


def main_kernel(dims, refs):
    units, features, hidden_width, heads, micros, sizes = dims
    owners, docs, slopes, gain, bias, tok_hbm, cot_hbm, master_hbm = refs[:8]
    mixed_hbm, grad_hbm, red, small = refs[8:12]
    (
        w, masters, mine, other, core_in, both, x_in, tok, cot, tail_in, wide_tok, wide_cot, x_pool, x_norm, x_att,
        x_two, x_act, x_short, d_up, d_low, d_inner, d_res, d_qkv, d_pool, pooled, hat_one, hat_two, root_one, root_two,
        resid, hidden, short_grad, res_grad, q_out, q_in, a_out, a_in, da_out, da_in, dq_out, dq_in, probs, mixed, grad,
        wide_up, wide_grad, edge_in, x_near, x_wide, g, right_in, left_in, fin_out, fin_in, co_out, co_in, sums, sums_in, sends, recvs, local,
    ) = refs[12:]
    half = features // 2
    width = features // heads
    rows_of = masters.shape[1]
    count = heads
    tokens = 3 * units
    own = micros * units
    pair_width = 2 * width
    b, s = lax.axis_index("batch"), lax.axis_index("seq")
    x, c = b // 2, b % 2
    z, y = s // 2, s % 2
    spot = y * (7 - 2 * z) + z

    def seq_of(position):
        far = position // 4
        return 2 * (position + far * (7 - 2 * position)) + far

    def at(offset):
        return lax.rem(spot + offset + 2 * count, count)

    def rows_at(offset, part=0, length=rows_of):
        return pl.ds(pl.multiple_of(seq_of(at(offset)) * rows_of + part, 16), length)

    my_half = pl.ds(pl.multiple_of(c * half, half), half)
    other_half = pl.ds(pl.multiple_of((1 - c) * half, half), half)
    core_peer = (x * 2 + 1 - c, s)
    x_peer = ((1 - x) * 2 + c, s)
    right_peer = (b, seq_of(at(1)))
    left_peer = (b, seq_of(at(-1)))
    plan = Plan()
    flying = {}

    def send(name, source, target, device):
        index = len(flying)
        flying[name] = pltpu.make_async_remote_copy(
            src_ref=source,
            dst_ref=target,
            send_sem=sends.at[index],
            recv_sem=recvs.at[index],
            device_id=device,
            device_id_type=MESH,
        )
        flying[name].start()

    def nothing():
        pass

    loads = [
        pltpu.make_async_copy(master_hbm, masters, local.at[0]),
        pltpu.make_async_copy(tok_hbm, tok, local.at[1]),
        pltpu.make_async_copy(cot_hbm, cot, local.at[2]),
    ]
    for copy in loads:
        copy.start()
    barrier = pltpu.get_barrier_semaphore()
    for step in range(1, count):
        pl.semaphore_signal(
            barrier, inc=1, device_id=(b, lax.rem(s + step, count)), device_id_type=MESH
        )
    for device in (core_peer, x_peer):
        pl.semaphore_signal(barrier, inc=1, device_id=device, device_id_type=MESH)
    pl.semaphore_wait(barrier, count + 1)

    spans, first = [], 0
    for size in sizes:
        spans.append((first, first + size))
        first += size
    in_base, back_base, up_base = spans[3][0], spans[4][0], spans[5][0]
    hidden_blocks = sizes[3]
    ours = in_base + x * hidden_blocks
    theirs = in_base + (1 - x) * hidden_blocks
    plan.add("ms", loads[0].wait, cost=0.5)

    def contribute(k):
        def run():
            lo, hi = spans[k]
            mask = (owners[k] == b).astype(WIDE)
            begin = start_of(owners, k, sizes)
            for block in range(lo, hi):
                slot = jnp.minimum(begin + (block - lo), masters.shape[0] - 1)
                mine[block] = (masters[slot, :, my_half] * mask).astype(LOW)
                other[block] = (masters[slot, :, other_half] * mask).astype(LOW)
            send(("g0", k), other.at[lo:hi], core_in.at[lo:hi], core_peer)

        return run

    def join_cores(k):
        def run():
            lo, hi = spans[k]
            flying[("g0", k)].wait_recv()
            both[lo:hi] = mine[lo:hi] + core_in[lo:hi]

        return run

    part = hidden_blocks // 2
    gathers = [
        ("p", (0,), spans[0][0], None, sizes[0]),
        ("q", (1,), spans[1][0], None, sizes[1]),
        ("F", (3, 4), ours, theirs, part),
        ("G", (3, 4), ours + part, theirs + part, part),
        ("o", (2,), spans[2][0], None, sizes[2]),
        ("u", (5,), up_base, None, sizes[5]),
    ]
    piece_bytes = rows_of * half * 2

    def gather_chunk(order, name, parents, here, there, size):
        split = there is not None
        load = size * piece_bytes
        blocks = pl.ds(here, size)
        away = pl.ds(there, size) if split else blocks

        def piece(offset, part=0, length=rows_of):
            return w.at[blocks, c, rows_at(offset, part, length)]

        def join_here():
            send(("g1", name), both.at[away], x_in.at[away], x_peer)

        def join_x():
            flying[("g1", name)].wait_recv()
            w[blocks, c, rows_at(0)] = both[blocks] + x_in[blocks]
            send(("R", 1, name), piece(0), piece(0), right_peer)
            send(("L", 1, name), piece(0), piece(0), left_peer)

        def onward(side, step):
            def run():
                flying[(side, step - 1, name)].wait_recv()
                if step == 5:
                    return
                offset = (1 - step) if side == "R" else (step - 1)
                part = piece(offset)
                if step == 4:
                    part = piece(offset, 0 if side == "R" else rows_of // 2, rows_of // 2)
                send((side, step, name), part, part, right_peer if side == "R" else left_peer)

            return run

        def across(side, step):
            def run():
                offset = -step if side == "R" else step
                part = piece(offset)
                if step == 4:
                    part = piece(offset, 0 if side == "R" else rows_of // 2, rows_of // 2)
                send(("X", side, step, name), part, part, x_peer)

            return run

        def distribute(which, span):
            def run():
                send((which, name), w.at[span, c], w.at[span, c], core_peer)

            return run

        rank = order * 0.1
        plan.add(("cx", name), join_here, [("cs", k) for k in parents], (), [(("g1", name), "x", load)], 0.05, rank)
        plan.add(
            ("x", name), join_x, [("cx", name)], [("g1", name)],
            [(("R", 1, name), "r", load), (("L", 1, name), "l", load)], 0.05, rank,
        )
        crossing = []

        def cross(side, step, after):
            message = ("X", side, step, name)
            plan.add(message, across(side, step), [after], (), [(message, "x", load if step < 4 else load // 2)], 0.05, rank + 0.05)
            crossing.append(message)

        if split:
            cross("R", 0, ("x", name))
        for step in (2, 3, 4, 5):
            for side, link in (("R", "r"), ("L", "l")):
                out = [((side, step, name), link, load if step < 4 else load // 2)] if step < 5 else []
                before = ("x", name) if step == 2 else (side, step - 1, "f", name)
                plan.add((side, step, "f", name), onward(side, step), [before], [(side, step - 1, name)], out, 0.05, rank)
                if split:
                    cross(side, step - 1, (side, step, "f", name))
        ends = [("R", 5, "f", name), ("L", 5, "f", name)]
        plan.add(("di", name), distribute("D", blocks), ends, (), [(("D", name), "c", 8 * load)], 0.05, rank)
        plan.add(("h", name), arrive(("D", name)), [("di", name)], [("D", name)], (), 0.02, rank)
        if split:
            plan.add(("xw", name), arrive(*crossing), crossing, crossing, (), 0.05, rank)
            plan.add(("dy", name), distribute("E", away), [("xw", name)], (), [(("E", name), "c", 8 * load)], 0.05, rank)
            plan.add(("hy", name), arrive(("E", name)), [("dy", name)], [("E", name)], (), 0.02, rank)

    def arrive(*names):
        def run():
            for name in names:
                flying[name].wait_recv()

        return run

    for k in (0, 1, 3, 4, 2, 5):
        lo, hi = spans[k]
        load = (hi - lo) * piece_bytes
        plan.add(("co", k), contribute(k), ["ms"], (), [(("g0", k), "c", load)], 0.04 * (hi - lo), 0.1)
        plan.add(("cs", k), join_cores(k), [("co", k)], [("g0", k)], (), 0.02 * (hi - lo), 0.1)
    for order, chunk in enumerate(gathers):
        gather_chunk(order, *chunk)

    def exchange(name, buffer):
        send(name, buffer.at[0:own], buffer.at[own : 2 * own], core_peer)

    def shared(name, columns):
        return (name, "c", own * columns * 2)

    lead = 16
    tiles = range(features // TILE)

    def columns_at(tile, base=0):
        return slice(base + tile * TILE, base + (tile + 1) * TILE)

    def ends_of(micro):
        ends = []
        total = jnp.int32(0)
        for index in range(docs.shape[1] - 1):
            total = total + docs[micro, index]
            ends.append(total)
        return ends

    def kept(micro):
        ids = s * units + lax.broadcasted_iota(jnp.int32, (units, 1), 0)
        starts = (ids == 0).astype(jnp.int32)
        for end in ends_of(micro):
            starts = starts | (ids == end).astype(jnp.int32)
        return starts == 0

    def load_tokens():
        loads[1].wait()
        send("tl", tok.at[:, tokens - lead :], tail_in, (b, lax.rem(s + 1, count)))
        for micro in range(micros):
            for tile in tiles:
                wide_tok[micro, tile, lead:] = tok[micro, :, columns_at(tile)].astype(WIDE)

    def load_cotangent():
        loads[2].wait()
        for micro in range(micros):
            for tile in tiles:
                wide_cot[micro, tile] = cot[micro, :, columns_at(tile)].astype(WIDE)
                for r in range(3):
                    d_up[micro * units : (micro + 1) * units, columns_at(tile, r * features)] = wide_cot[
                        micro, tile, pl.ds(r, units, stride=3), :
                    ].astype(LOW)
        exchange("eu", d_up)

    def make_pieces():
        flying["tl"].wait_recv()
        for micro in range(micros):
            keep = kept(micro)
            for tile in tiles:
                wide_tok[micro, tile, :lead] = tail_in[micro, :, columns_at(tile)].astype(WIDE)
                for r in range(3):
                    part = wide_tok[micro, tile, pl.ds(lead - 2 + r, units, stride=3), :]
                    if r < 2:
                        part = jnp.where(keep, part, 0.0)
                    x_pool[micro * units : (micro + 1) * units, columns_at(tile, r * features)] = part.astype(LOW)
        exchange("ep", x_pool)

    plan.add("tok", load_tokens, sends=[("tl", "f", 2 * lead * features * 2)], cost=0.3, rank=1)
    plan.add(
        "pc", make_pieces, ["tok"], ["tl"], [shared("ep", 3 * features)], 0.5, rank=1
    )
    plan.add("cot", load_cotangent, (), (), [shared("eu", 3 * features)], 0.5, rank=2)

    def normal(value, which, hat, root):
        centred = value - over_last(jnp.mean, value)
        scale = lax.rsqrt(over_last(jnp.mean, centred * centred) + ln_eps)
        unit = centred * scale
        hat[...] = unit
        root[...] = scale
        return (unit * gain[which : which + 1, :] + bias[which : which + 1, :]).astype(LOW)

    def both_halves(make):
        return jnp.concatenate([make(0), make(1)], axis=1)

    def pool():
        def side(h):
            total = None
            for r in range(3):
                term = contract(x_pool[0:own, r * features : (r + 1) * features], w[r, h], 1, 0)
                total = term if total is None else total + term
            return total

        value = both_halves(side)
        pooled[...] = value
        x_norm[0:own] = normal(value, 0, hat_one, root_one)
        exchange("en", x_norm)

    lane = lambda: lax.broadcasted_iota(jnp.int32, (1, pair_width), 1)

    def swap(value):
        return pltpu.roll(value, width, axis=1)

    def to_heads(tile, target, pair, row):
        low_lanes = lane() < width
        first, second = tile[:units], tile[units:]
        target[2 * pair, row : row + units] = jnp.where(low_lanes, first, swap(second)).astype(LOW)
        target[2 * pair + 1, row : row + units] = jnp.where(low_lanes, swap(first), second).astype(LOW)

    def from_heads(source, pair, row):
        low_lanes = lane() < width
        even = source[2 * pair, row : row + units].astype(WIDE)
        odd = source[2 * pair + 1, row : row + units].astype(WIDE)
        return jnp.where(low_lanes, even, swap(odd)).astype(LOW), jnp.where(low_lanes, swap(even), odd).astype(LOW)

    def spread(name, source, target):
        for step in range(1, count):
            there = lax.rem(s + step, count)
            send((name, step), source.at[there], target.at[s], (b, there))
        target[s] = source[s]

    def spread_names(name):
        return [(name, step) for step in range(1, count)]

    def spread_sends(name, rows):
        return [((name, step), "f", rows * pair_width * 2) for step in range(1, count)]

    def project():
        for part in range(3):
            for h in range(2):
                value = contract(x_norm[0:own], w[3 + part, h], 1, 0)
                for tile in range(half // pair_width):
                    to_heads(
                        value[:, tile * pair_width : (tile + 1) * pair_width],
                        q_out,
                        h * (half // pair_width) + tile,
                        part * units,
                    )
        spread("q", q_out, q_in)

    lane_units = units * count

    def heads_of(source, part):
        return source[:, part * units : (part + 1) * units, :].reshape(lane_units, pair_width)

    def lanes_of(micro):
        return (lane() // width == micro).astype(WIDE).astype(LOW)

    def distances():
        row_ids = lax.broadcasted_iota(jnp.int32, (lane_units, lane_units), 0)
        col_ids = lax.broadcasted_iota(jnp.int32, (lane_units, lane_units), 1)
        return row_ids - col_ids

    def attend_now():
        arrive(*spread_names("q"))()
        queries, keys, values = (heads_of(q_in, part) for part in range(3))
        slope = slopes[s]
        total = None
        for micro in range(micros):
            gap = distances()
            row_seg = jnp.zeros((lane_units, 1), jnp.int32)
            col_seg = jnp.zeros((1, lane_units), jnp.int32)
            for end in ends_of(micro):
                row_seg += (lax.broadcasted_iota(jnp.int32, (lane_units, 1), 0) >= end).astype(jnp.int32)
                col_seg += (lax.broadcasted_iota(jnp.int32, (1, lane_units), 1) >= end).astype(jnp.int32)
            allowed = (row_seg == col_seg) & (gap >= 0)
            mask = lanes_of(micro)
            raw = contract(queries * mask, keys, 1, 1) * 0.125 - slope * gap.astype(WIDE)
            scores = jnp.where(allowed, raw, masked_score)
            raised = jnp.exp(scores - over_last(jnp.max, scores))
            probability = raised / over_last(jnp.sum, raised)
            probs[micro] = probability
            term = contract(probability.astype(LOW), values * mask, 1, 0)
            total = term if total is None else total + term
        a_out[...] = total.astype(LOW).reshape(count, units, pair_width)
        spread("a", a_out, a_in)

    def merge():
        arrive(*spread_names("a"))()
        for pair in range(heads // 2):
            columns = slice(pair * pair_width, (pair + 1) * pair_width)
            first, second = from_heads(a_in, pair, 0)
            x_att[0:units, columns] = first
            x_att[units:own, columns] = second
        exchange("ea", x_att)

    def project_out():
        value = pooled[...] + both_halves(lambda h: contract(x_att[0:own], w[6, h], 1, 0))
        resid[...] = value
        x_two[0:own] = normal(value, 1, hat_two, root_two)
        exchange("et", x_two)


    def widen(j):
        def run():
            for h in range(2):
                columns = slice(j * features + h * half, j * features + (h + 1) * half)
                value = contract(x_two[0:own], w[in_base + j, h], 1, 0)
                hidden[:, columns] = value
                inner, _ = gelu_parts(value)
                x_act[0:own, columns] = (0.5 * value * (1.0 + inner)).astype(LOW)
            if j == hidden_blocks - 1:
                exchange("ec", x_act)

        return run

    def narrow():
        def side(h):
            total = resid[:, h * half : (h + 1) * half]
            for j in range(hidden_blocks):
                total = total + contract(
                    x_act[0:own, j * features : (j + 1) * features], w[back_base + j, h], 1, 0
                )
            return total

        x_short[0:own] = both_halves(side).astype(LOW)
        exchange("es", x_short)

    outs = [
        pltpu.make_async_copy(mixed, mixed_hbm, local.at[3]),
        pltpu.make_async_copy(grad, grad_hbm, local.at[4]),
    ]

    def lift(r):
        def run():
            for h in range(2):
                value = contract(x_short[0:own], w[up_base + r, h], 1, 0)
                for micro in range(micros):
                    for tile in range(half // TILE):
                        wide_up[micro, h * (half // TILE) + tile, pl.ds(r, units, stride=3), :] = value[
                            micro * units : (micro + 1) * units, columns_at(tile)
                        ]
            if r == 2:
                for micro in range(micros):
                    for tile in tiles:
                        columns = columns_at(tile)
                        mixed[micro, :, columns] = tok[micro, :, columns].astype(WIDE) + wide_up[micro, tile]
                outs[0].start()

        return run

    plan.add("po", pool, ["pc", ("h", "p")], (), [shared("en", features)], 0.6, rank=3)
    plan.add("pr", project, ["po", ("h", "q")], (), spread_sends("q", 3 * units), 0.6, rank=3)
    plan.add("at", attend_now, ["pr"], spread_names("q"), spread_sends("a", units), 1.1, rank=3)
    plan.add("me", merge, ["at"], spread_names("a"), [shared("ea", features)], 0.15, rank=3)
    plan.add("ou", project_out, ["me", ("h", "o")], (), [shared("et", features)], 0.45, rank=3)
    for j in range(hidden_blocks):
        last = j == hidden_blocks - 1
        plan.add(
            ("wi", j), widen(j), ["ou", ("h", "F"), ("hy", "F"), ("h", "G"), ("hy", "G")] + ([("wi", i) for i in range(j)] if last else []), (),
            [shared("ec", hidden_width)] if last else (), 0.3, rank=3,
        )
    plan.add(
        "na", narrow, [("wi", j) for j in range(hidden_blocks)] + [("h", "F"), ("hy", "F"), ("h", "G"), ("hy", "G")], (), [shared("es", features)], 0.5,
        rank=3,
    )
    for r in range(3):
        plan.add(
            ("li", r), lift(r), ["na", ("h", "u"), "tok"] + ([("li", i) for i in range(r)]), (), (), 0.3, rank=8
        )

    def back_short():
        total = None
        for r in range(3):
            for h in range(2):
                begin = r * features + h * half
                term = contract(d_up[0:own, begin : begin + half], w[up_base + r, h], 1, 1)
                total = term if total is None else total + term
        short_grad[...] = total
        d_low[0:own] = total.astype(LOW)
        exchange("el", d_low)

    def back_widen(j):
        def run():
            total = contract(d_low[0:own, 0:half], w[back_base + j, 0], 1, 1)
            total = total + contract(d_low[0:own, half:features], w[back_base + j, 1], 1, 1)
            columns = slice(j * features, (j + 1) * features)
            value = hidden[:, columns]
            inner, slope = gelu_parts(value)
            factor = 0.5 * (1.0 + inner) + 0.5 * value * (1.0 - inner * inner) * slope
            d_inner[0:own, columns] = (total * factor).astype(LOW)
            if j == hidden_blocks - 1:
                exchange("ei", d_inner)

        return run

    def back_normal(value, which, hat, root):
        unit = hat[...]
        sums[which : which + 1, :] = jnp.sum(value * unit, axis=0, keepdims=True)
        sums[2 + which : 3 + which, :] = jnp.sum(value, axis=0, keepdims=True)
        scaled = value * gain[which : which + 1, :]
        return root[...] * (
            scaled - over_last(jnp.mean, scaled) - unit * over_last(jnp.mean, scaled * unit)
        )

    def back_two():
        total = None
        for j in range(hidden_blocks):
            for h in range(2):
                begin = j * features + h * half
                term = contract(d_inner[0:own, begin : begin + half], w[in_base + j, h], 1, 1)
                total = term if total is None else total + term
        value = short_grad[...] + back_normal(total, 1, hat_two, root_two)
        res_grad[...] = value
        d_res[0:own] = value.astype(LOW)
        exchange("er", d_res)

    def back_out():
        value = contract(d_res[0:own, 0:half], w[6, 0], 1, 1)
        value = value + contract(d_res[0:own, half:features], w[6, 1], 1, 1)
        for pair in range(heads // 2):
            to_heads(value[:, pair * pair_width : (pair + 1) * pair_width], da_out, pair, 0)
        spread("da", da_out, da_in)

    def back_attend():
        arrive(*spread_names("da"))()
        queries, keys, values = (heads_of(q_in, part) for part in range(3))
        grads = da_in[...].reshape(lane_units, pair_width)
        totals = [None, None, None]
        slope_total = jnp.zeros((1, 1), WIDE)
        for micro in range(micros):
            mask = lanes_of(micro)
            own_grads = grads * mask
            probability = probs[micro]
            grad_prob = contract(own_grads, values, 1, 1)
            scaled = probability * grad_prob
            score = scaled - probability * over_last(jnp.sum, scaled)
            low_score = score.astype(LOW)
            gap = distances().astype(WIDE)
            slope_total = slope_total - jnp.sum(
                jnp.sum(low_score.astype(WIDE) * gap, axis=0, keepdims=True), axis=1, keepdims=True
            )
            terms = (
                contract(low_score, keys * mask, 1, 0) * 0.125,
                contract(low_score, queries * mask, 0, 0) * 0.125,
                contract(probability.astype(LOW), own_grads, 0, 0),
            )
            totals = [term if total is None else total + term for total, term in zip(totals, terms)]
        for part in range(3):
            dq_out[:, part * units : (part + 1) * units, :] = (
                totals[part].astype(LOW).reshape(count, units, pair_width)
            )
        spread("dq", dq_out, dq_in)
        places = lax.broadcasted_iota(jnp.int32, (1, features), 1)
        sums[4:5, :] = jnp.where(places == s, slope_total, 0.0)
        sums[5:8, :] = jnp.zeros((3, features), WIDE)

    def back_project():
        arrive(*spread_names("dq"))()
        for part in range(3):
            for pair in range(heads // 2):
                begin = part * features + pair * pair_width
                first, second = from_heads(dq_in, pair, part * units)
                d_qkv[0:units, begin : begin + pair_width] = first
                d_qkv[units:own, begin : begin + pair_width] = second
        exchange("eq", d_qkv)

    def back_one():
        total = None
        for part in range(3):
            for h in range(2):
                begin = part * features + h * half
                term = contract(d_qkv[0:own, begin : begin + half], w[3 + part, h], 1, 1)
                total = term if total is None else total + term
        value = res_grad[...] + back_normal(total, 0, hat_one, root_one)
        d_pool[0:own] = value.astype(LOW)
        exchange("ed1", d_pool)

    def back_pieces():
        for r in range(3):
            value = contract(d_pool[0:own, 0:half], w[r, 0], 1, 1)
            value = value + contract(d_pool[0:own, half:features], w[r, 1], 1, 1)
            for micro in range(micros):
                part = value[micro * units : (micro + 1) * units]
                if r < 2:
                    part = jnp.where(kept(micro), part, 0.0)
                for tile in tiles:
                    wide_grad[micro, tile, pl.ds(6 + r, units, stride=3), :] = part[:, columns_at(tile)]
        send("ed", wide_grad.at[:, :, 0:8], edge_in, (b, lax.rem(s + count - 1, count)))

    def finish_grad():
        flying["ed"].wait_recv()
        inside = (s < count - 1).astype(WIDE)
        for micro in range(micros):
            for tile in tiles:
                columns = columns_at(tile)
                wide_grad[micro, tile, 6 + tokens : 8 + tokens, :] = edge_in[micro, tile, 6:8, :] * inside
                grad[micro, :, columns] = cot[micro, :, columns].astype(WIDE) + wide_grad[micro, tile, 8 : 8 + tokens]
        outs[1].start()

    plan.add("bs", back_short, ["cot", ("h", "u")], (), [shared("el", features)], 0.65, rank=4)
    for j in range(hidden_blocks):
        last = j == hidden_blocks - 1
        plan.add(
            ("bw", j), back_widen(j),
            ["bs", ("h", "F"), ("hy", "F"), ("h", "G"), ("hy", "G"), ("wi", j)] + ([("bw", i) for i in range(j)] if last else []), (),
            [shared("ei", hidden_width)] if last else (), 0.35, rank=4,
        )
    plan.add(
        "b2", back_two, [("bw", j) for j in range(hidden_blocks)] + [("h", "F"), ("hy", "F"), ("h", "G"), ("hy", "G")], (),
        [shared("er", features)], 0.9, rank=4,
    )
    plan.add("bo", back_out, ["b2", ("h", "o")], (), spread_sends("da", units), 0.45, rank=4)
    plan.add("ba", back_attend, ["bo", "at"], spread_names("da"), spread_sends("dq", 3 * units), 1.4, rank=4)
    plan.add("bp", back_project, ["ba"], spread_names("dq"), [shared("eq", 3 * features)], 0.2, rank=4)
    plan.add("b1", back_one, ["bp"], (), [shared("ed1", features)], 0.75, rank=4)
    plan.add("bx", back_pieces, ["b1"], (), [("ed", "f", 2 * 8 * features * 4)], 0.65, rank=9)
    plan.add("fg", finish_grad, ["bx", "cot"], ["ed"], (), 0.3, rank=9)

    def add_pair(step, device):
        def run():
            if step > 0:
                flying[("s", step - 1)].wait_recv()
                sums[8 * step : 8 * step + 8] = sums[8 * step - 8 : 8 * step] + sums_in[8 * step - 8 : 8 * step]
            if device is not None:
                send(("s", step), sums.at[8 * step : 8 * step + 8], sums_in.at[8 * step : 8 * step + 8], device)
            else:
                small[...] = sums[8 * step : 8 * step + 8]

        return run

    partners = [
        core_peer,
        x_peer,
        (b, 2 * z + 1 - y),
        (b, 2 * (z + 1 - 2 * (z % 2)) + y),
        (b, 2 * lax.rem(z + 2, 4) + y),
        None,
    ]
    for step, device in enumerate(partners):
        plan.add(
            ("sum", step), add_pair(step, device), ["b1", "ba"] if step == 0 else [("sum", step - 1)],
            [("s", step - 1)] if step else (), [(("s", step), "f", 8 * features * 4)] if device is not None else (), 0.1,
            rank=0,
        )

    for name, columns in (
        ("ep", "pc"), ("en", "po"), ("ea", "me"), ("et", "ou"), ("ec", ("wi", hidden_blocks - 1)),
        ("es", "na"), ("eu", "cot"), ("el", "bs"), ("ei", ("bw", hidden_blocks - 1)),
        ("er", "b2"), ("eq", "bp"), ("ed1", "b1"),
    ):
        plan.add(("got", name), arrive(name), [columns], [name], cost=0.02)

    def columns_of(block):
        return pl.ds(pl.multiple_of(block * features + c * half, half), half)

    def outer(block, left, left_block, right, right_block):
        def run():
            rows = left[:, left_block * features : (left_block + 1) * features]
            g[block] = contract(rows, right[:, columns_of(right_block)], 0, 0).astype(LOW)

        return run

    def send_either(name, first_source, second_source, target):
        index = len(flying)
        copies = [
            pltpu.make_async_remote_copy(
                src_ref=source, dst_ref=target, send_sem=sends.at[index], recv_sem=recvs.at[index], device_id=x_peer,
                device_id_type=MESH,
            )
            for source in (first_source, second_source)
        ]
        flying[name] = copies[0]
        for plane in range(2):
            pl.when(x == plane)(copies[plane].start)

    def near_away():
        send_either("sn", d_low.at[0:own], x_two.at[0:own], x_near.at[0:own])

    def near_core():
        arrive("sn")()
        exchange("cn", x_near)

    def wide_away(j):
        columns = slice(j * features, (j + 1) * features)

        def run():
            source = (x_act.at[0:own, columns], d_inner.at[0:own, columns])
            send_either(("sw", j), *source, x_wide.at[0:own, columns])

        return run

    def wide_core(j):
        columns = slice(j * features, (j + 1) * features)

        def run():
            arrive(("sw", j))()
            send(("cw", j), x_wide.at[0:own, columns], x_wide.at[own : 2 * own, columns], core_peer)

        return run

    def outer_split(j):
        columns = slice(j * features, (j + 1) * features)

        def run():
            @pl.when(x == 0)
            def _():
                total = contract(x_two[...], d_inner[:, columns_of(j)], 0, 0)
                g[in_base + j] = (total + contract(x_near[...], x_wide[:, columns_of(j)], 0, 0)).astype(LOW)

            @pl.when(x == 1)
            def _():
                total = contract(x_act[:, columns], d_low[:, my_half], 0, 0)
                g[back_base + j] = (total + contract(x_wide[:, columns], x_near[:, my_half], 0, 0)).astype(LOW)

        return run

    lump = own * features * 2
    plan.add("sn", near_away, ["bs", "ou"], (), [("sn", "x", lump)], 0.05, 2)
    plan.add("nc", near_core, ["sn"], ["sn"], [("cn", "c", lump)], 0.05, 2)
    plan.add(("got", "cn"), arrive("cn"), ["nc"], ["cn"], (), 0.02, 2)
    for j in range(hidden_blocks):
        plan.add(("sw", j), wide_away(j), [("wi", j), ("bw", j)], (), [(("sw", j), "x", lump)], 0.05, 2)
        plan.add(("wc", j), wide_core(j), [("sw", j)], [("sw", j)], [(("cw", j), "c", lump)], 0.05, 2)
        plan.add(("got", "cw", j), arrive(("cw", j)), [("wc", j)], [("cw", j)], (), 0.02, 2)
        deps = [("got", e) for e in ("et", "ec", "el", "ei", "cn")] + [("got", "cw", j)]
        plan.add(("gr", j, "s"), outer_split(j), deps, cost=0.6, rank=4.5)
    weight_grads = []
    for r in range(3):
        weight_grads.append((r, x_pool, r, d_pool, 0, [("got", "ep"), ("got", "ed1")]))
        weight_grads.append((3 + r, x_norm, 0, d_qkv, r, [("got", "en"), ("got", "eq")]))
        weight_grads.append((up_base + r, x_short, 0, d_up, r, [("got", "es"), ("got", "eu")]))
    weight_grads.append((6, x_att, 0, d_res, 0, [("got", "ea"), ("got", "er")]))
    for block, left, left_block, right, right_block, deps in weight_grads:
        plan.add(("gr", block), outer(block, left, left_block, right, right_block), deps, cost=0.3, rank=5)

    def scatter_chunk(order, name, here, there, size, deps):
        split = there is not None
        blocks = pl.ds(here, size)
        load = size * piece_bytes
        rank = 1 + order * 0.1

        def first_step(side):
            def run():
                part = 0 if side == "R" else rows_of // 2
                inbox = right_in if side == "R" else left_in
                send(
                    (side, "s", 1, name), g.at[blocks, rows_at(4, part, rows_of // 2)],
                    inbox.at[0, blocks, part : part + rows_of // 2], right_peer if side == "R" else left_peer,
                )

            return run

        def next_step(side, step):
            def run():
                inbox = right_in if side == "R" else left_in
                offset = (5 - step) if side == "R" else (step - 5)
                flying[(side, "s", step - 1, name)].wait_recv()
                part, length = 0, rows_of
                if step == 2:
                    part, length = (0 if side == "R" else rows_of // 2), rows_of // 2
                rows = rows_at(offset, part, length)
                g[blocks, rows] = g[blocks, rows] + inbox[step - 2, blocks, part : part + length]
                send(
                    (side, "s", step, name), g.at[blocks, rows_at(offset)], inbox.at[step - 1, blocks],
                    right_peer if side == "R" else left_peer,
                )

            return run

        def finish():
            arrive(("R", "s", 4, name), ("L", "s", 4, name))()
            total = g[blocks, rows_at(0)].astype(WIDE) + right_in[3, blocks].astype(WIDE) + left_in[3, blocks].astype(WIDE)
            fin_out[blocks] = total.astype(LOW)
            send(("rx", name), fin_out.at[blocks], fin_in.at[blocks], x_peer)
            if split:
                red[blocks, :, my_half] = fin_out[blocks]
                send(("rc", name), fin_out.at[blocks], co_in.at[blocks], core_peer)

        def finish_x():
            arrive(("rx", name))()
            if split:
                away = pl.ds(there, size)
                red[away, :, my_half] = fin_in[away]
                send(("rd", name), fin_in.at[away], co_in.at[away], core_peer)
            else:
                total = (fin_out[blocks].astype(WIDE) + fin_in[blocks].astype(WIDE)).astype(LOW)
                co_out[blocks] = total
                red[blocks, :, my_half] = total
                send(("rc", name), co_out.at[blocks], co_in.at[blocks], core_peer)

        def finish_core():
            arrive(("rc", name))()
            red[blocks, :, other_half] = co_in[blocks]
            if split:
                arrive(("rd", name))()
                away = pl.ds(there, size)
                red[away, :, other_half] = co_in[away]

        sides = (("R", "r"), ("L", "l"))
        for side, link in sides:
            plan.add((side, "r", 1, name), first_step(side), deps, (), [((side, "s", 1, name), link, load // 2)], 0.05, rank)
        for step in (2, 3, 4):
            for side, link in sides:
                plan.add(
                    (side, "r", step, name), next_step(side, step), [(side, "r", step - 1, name)],
                    [(side, "s", step - 1, name)], [((side, "s", step, name), link, load)], 0.02 * size, rank,
                )
        own_out = [(("rc", name), "c", load)]
        plan.add(
            ("fi", name), finish, [("R", "r", 4, name), ("L", "r", 4, name)], [("R", "s", 4, name), ("L", "s", 4, name)],
            [(("rx", name), "x", load)] + (own_out if split else []), 0.02 * size, rank,
        )
        late_out = [(("rd", name), "c", load)] if split else own_out
        plan.add(("fx", name), finish_x, [("fi", name)], [("rx", name)], late_out, 0.02 * size, rank)
        plan.add(
            ("fc", name), finish_core, [("fx", name)], [("rc", name)] + ([("rd", name)] if split else []), (), 0.02 * size, rank
        )

    scatters = [("u", up_base, None, sizes[5], [("gr", up_base + r) for r in range(3)])]
    scatters.append(("F", ours, theirs, part, [("gr", j, "s") for j in range(part)]))
    scatters.append(("G", ours + part, theirs + part, part, [("gr", j, "s") for j in range(part, 2 * part)]))
    scatters.append(("o", spans[2][0], None, 1, [("gr", spans[2][0])]))
    for block in range(spans[1][0], spans[1][1]):
        scatters.append((block, block, None, 1, [("gr", block)]))
    for block in range(spans[0][0], spans[0][1]):
        scatters.append((block, block, None, 1, [("gr", block)]))
    for order, chunk in enumerate(scatters):
        scatter_chunk(order, *chunk)

    for name, _ in plan.order():
        plan.tasks[name][0]()
    for name, copy in flying.items():
        copy.wait_send()
    for copy in outs:
        copy.wait()


def adam_kernel(sizes, refs):
    owners, red, small, gain, bias, norm_m, norm_v, slope, slope_m, slope_v, master, first, second, mixed, grad = refs[:15]
    (
        new_w, new_m, new_v, new_low, norm_out, norm_m_out, norm_v_out, slope_out, slope_m_out, slope_v_out, mixed_out,
        grad_out,
    ) = refs[15:]
    step = pl.program_id(0)
    fix_first = 1.0 - beta_one**STEP
    fix_second = 1.0 - beta_two**STEP
    mixed_out[...] = mixed[...]
    grad_out[...] = grad[...]

    @pl.when(step == 0)
    def _():
        for begin, values in ((0, gain), (2, bias)):
            rows = slice(begin, begin + 2)
            norm_out[rows], norm_m_out[rows], norm_v_out[rows] = adam_update(
                values[...], small[rows], norm_m[rows], norm_v[rows], fix_first, fix_second, rate_norm, 0.0
            )
        heads = slope.shape[1]
        slope_out[...], slope_m_out[...], slope_v_out[...] = adam_update(
            slope[...], small[4:5, 0:heads], slope_m[...], slope_v[...], fix_first, fix_second, rate_slope, 0.0
        )

    me = lax.axis_index("batch")
    for place in range(master.shape[0]):
        slot = step * master.shape[0] + place
        block, held, base = jnp.int32(0), jnp.int32(0), 0
        for matrix_id, size in enumerate(sizes):
            begin = start_of(owners, matrix_id, sizes)
            inside = (owners[matrix_id] == me) & (slot >= begin) & (slot < begin + size)
            block = jnp.where(inside, base + slot - begin, block)
            held = jnp.where(inside, 1, held)
            base += size
        gradient = red[block].astype(WIDE)
        values = adam_update(
            master[place], gradient, first[place], second[place], fix_first, fix_second, rate_matrix, decay_rate
        )
        keep = jnp.full(gradient.shape, held, jnp.int32) > 0
        weight = jnp.where(keep, values[0], master[place])
        new_w[place] = weight
        new_m[place] = jnp.where(keep, values[1], first[place])
        new_v[place] = jnp.where(keep, values[2], second[place])
        new_low[place] = weight.astype(LOW)


def fused_body(tokens, cotangent, doc_lengths, owners, master, first_moment, second_moment, ln_gain, ln_bias, norm_m, norm_v, slopes, slope_m, slope_v):
    micros, _, tok_rows, features = tokens.shape
    units, heads, width = tok_rows // 3, slopes.shape[0], features // slopes.shape[0]
    sizes = tuple(block_counts(features, FF))
    blocks, own, half = sum(sizes), micros * units, features // 2
    slots, rows = master.shape[1], master.shape[2]
    lane_units = units * heads
    split = features // TILE
    hbm, vmem, smem = (pl.BlockSpec(memory_space=m) for m in (pl.ANY, pltpu.VMEM, pltpu.SMEM))
    low = lambda *shape: pltpu.VMEM(shape, LOW)
    wide = lambda *shape: pltpu.VMEM(shape, WIDE)
    pieces = lambda: low(blocks, rows, half)
    both = lambda columns: low(2 * own, columns)
    scratch = [
        low(blocks, 2, features, half), wide(slots, rows, features), pieces(), pieces(), pieces(), pieces(), pieces(),
        low(micros, tok_rows, features), low(micros, tok_rows, features), low(micros, 16, features),
        wide(micros, split, 16 + tok_rows, TILE), wide(micros, split, tok_rows, TILE),
        both(3 * features), both(features), both(features), both(features), both(FF), both(features),
        both(3 * features), both(features), both(FF), both(features), both(3 * features), both(features),
        wide(own, features), wide(own, features), wide(own, features), wide(own, 1), wide(own, 1),
        wide(own, features), wide(own, FF), wide(own, features), wide(own, features),
        low(heads, 3 * units, 2 * width), low(heads, 3 * units, 2 * width), low(heads, units, 2 * width),
        low(heads, units, 2 * width), low(heads, units, 2 * width), low(heads, units, 2 * width),
        low(heads, 3 * units, 2 * width), low(heads, 3 * units, 2 * width),
        wide(micros, lane_units, lane_units), wide(micros, tok_rows, features), wide(micros, tok_rows, features),
        wide(micros, split, tok_rows, TILE), wide(micros, split, 8 + tok_rows, TILE), wide(micros, split, 8, TILE),
        low(2 * own, features), low(2 * own, FF), low(blocks, features, half), low(4, blocks, rows, half), low(4, blocks, rows, half),
        pieces(), pieces(), pieces(), pieces(), wide(48, features), wide(40, features),
        pltpu.SemaphoreType.DMA((260,)), pltpu.SemaphoreType.DMA((260,)), pltpu.SemaphoreType.DMA((5,)),
    ]
    token_shape = (micros, tok_rows, features)
    dims = (units, features, FF, heads, micros, sizes)
    mixed, grad, red, small = pl.pallas_call(
        lambda *refs: main_kernel(dims, refs),
        out_shape=(
            jax.ShapeDtypeStruct(token_shape, WIDE),
            jax.ShapeDtypeStruct(token_shape, WIDE),
            jax.ShapeDtypeStruct((blocks, rows, features), LOW),
            jax.ShapeDtypeStruct((8, features), WIDE),
        ),
        in_specs=[smem, smem, smem, vmem, vmem, hbm, hbm, hbm],
        out_specs=(hbm, hbm, vmem, vmem),
        scratch_shapes=scratch,
        compiler_params=pltpu.CompilerParams(
            collective_id=0, has_side_effects=True, vmem_limit_bytes=60 * 2**20
        ),
        name="block",
    )(
        owners, doc_lengths[:, 0], slopes, ln_gain, ln_bias, tokens[:, 0], cotangent[:, 0], master[0]
    )
    steps = 4
    slot = pl.BlockSpec((slots // steps, rows, features), lambda j: (j, 0, 0))
    flat = (micros * tok_rows, features)
    some = pl.BlockSpec((flat[0] // steps, features), lambda j: (j, 0))
    moment_shape = jax.ShapeDtypeStruct((slots, rows, features), WIDE)
    norm_shape = jax.ShapeDtypeStruct((4, features), WIDE)
    slope_shape = jax.ShapeDtypeStruct((1, heads), WIDE)
    out = pl.pallas_call(
        lambda *refs: adam_kernel(sizes, refs),
        grid=(steps,),
        out_shape=(
            moment_shape, moment_shape, moment_shape, jax.ShapeDtypeStruct((slots, rows, features), LOW),
            norm_shape, norm_shape, norm_shape, slope_shape, slope_shape, slope_shape,
            jax.ShapeDtypeStruct(flat, WIDE), jax.ShapeDtypeStruct(flat, WIDE),
        ),
        in_specs=[smem] + [vmem] * 9 + [slot] * 3 + [some] * 2,
        out_specs=(slot, slot, slot, slot, vmem, vmem, vmem, vmem, vmem, vmem, some, some),
        compiler_params=pltpu.CompilerParams(dimension_semantics=("arbitrary",)),
        name="adam",
    )(
        owners, red, small, ln_gain, ln_bias, norm_m, norm_v, slopes[None], slope_m[None],
        slope_v[None], master[0], first_moment[0], second_moment[0],
        mixed.reshape(flat), grad.reshape(flat),
    )
    new_w, new_m, new_v, new_low, norm, norm_m, norm_v, slope, slope_m, slope_v, mixed, grad = out
    return (
        mixed.reshape(tokens.shape), grad.reshape(tokens.shape), new_w[None], new_m[None], new_v[None], new_low[None], norm, norm_m, norm_v,
        slope[0], slope_m[0], slope_v[0],
    )


def fits(mesh, shapes):
    return mesh.shape["batch"] == 4 and mesh.shape["seq"] == 8 and shapes[0].shape[1] == 1


def solution(mesh):
    in_specs = (
        P("batch", None, "seq", None),
        P("batch", None, "seq", None),
        P("batch", None, None),
        P(),
        P("batch", None, "seq", None),
        P("batch", None, "seq", None),
        P("batch", None, "seq", None),
        P(),
        P(),
        P(),
        P(),
        P(),
        P(),
        P(),
    )
    out_specs = (
        P("batch", None, "seq", None),
        P("batch", None, "seq", None),
        P("batch", None, "seq", None),
        P("batch", None, "seq", None),
        P("batch", None, "seq", None),
        P("batch", None, "seq", None),
        P(),
        P(),
        P(),
        P(),
        P(),
        P(),
    )

    def whole(*args):
        part = fused_body if fits(mesh, args) else body
        return jax.shard_map(
            part, mesh=mesh, in_specs=in_specs, out_specs=out_specs, check_vma=False
        )(*args)

    return whole
```

```python
import math

import jax
import jax.numpy as jnp
from jax import lax
from jax.experimental import pallas as pl
from jax.experimental.pallas import tpu as pltpu
from jax.sharding import PartitionSpec as P

FF = 2048
STEP = 10


beta_one = 0.9
beta_two = 0.95
adam_eps = 1e-08
decay_rate = 0.1
rate_matrix = 0.02
rate_norm = 0.2
rate_slope = 0.01
ln_eps = 1e-05
masked_score = -1000000000.0
row_kinds = (True, False, True, False, True, False)


def broadcast(value, axis, source):
    kept = jnp.where(lax.axis_index(axis) == source, value, 0).astype(value.dtype)
    return lax.psum(kept, axis)


def running_total(lengths):
    count = lengths.shape[-1]
    ends = [lengths[..., 0]]
    for index in range(1, count):
        ends.append(ends[-1] + lengths[..., index])
    return jnp.stack(ends, -1)


def for_sending(value):

    def short(part):
        return part.astype(jnp.bfloat16) if part.dtype == jnp.float32 else part

    return jax.tree.map(short, value)


def passed_along(value, axis, by):
    peers = lax.axis_size(axis)
    pairs = [(i, i + by) for i in range(peers) if 0 <= i + by < peers]
    return lax.ppermute(value, axis, pairs)


def layer_norm(values, gain, shift):
    center = jnp.mean(values, -1, keepdims=True)
    centred = values - center
    spread = jnp.mean(centred * centred, -1, keepdims=True)
    return centred * lax.rsqrt(spread + ln_eps) * gain + shift


def gelu_tanh(values):
    return jax.nn.gelu(values, approximate=True)


def block_counts(features, hidden):
    return [3, 3, 1, hidden // features, hidden // features, 3]


def block_starts(owners, sizes):
    starts_list = []
    for matrix_id in range(len(sizes)):
        shared = jnp.zeros((), jnp.int32)
        for earlier_id in range(matrix_id):
            shared = shared + jnp.where(
                owners[earlier_id] == owners[matrix_id], sizes[earlier_id], 0
            ).astype(jnp.int32)
        starts_list.append(shared)
    return starts_list


def slot_table(owners, device, sizes, slot_count):
    starts_list = block_starts(owners, sizes)
    slot_ids = jnp.arange(slot_count, dtype=jnp.int32)
    numbers = jnp.arange(sum(sizes), dtype=jnp.int32)
    slot_map = jnp.zeros((slot_count, sum(sizes)), jnp.float32)
    block_base = 0
    for matrix_id in range(len(sizes)):
        inside = (
            (owners[matrix_id] == device)
            & (slot_ids >= starts_list[matrix_id])
            & (slot_ids < starts_list[matrix_id] + sizes[matrix_id])
        )
        target = block_base + slot_ids - starts_list[matrix_id]
        slot_map = slot_map + (inside[:, None] & (target[:, None] == numbers[None, :])).astype(
            jnp.float32
        )
        block_base += sizes[matrix_id]
    return slot_map


def to_matrix(blocks, by_rows):
    if by_rows:
        return blocks.reshape(-1, blocks.shape[2])
    return blocks.transpose(1, 0, 2).reshape(blocks.shape[1], -1)


def to_blocks(matrix, by_rows, features):
    if by_rows:
        return matrix.reshape(-1, features, features)
    return matrix.reshape(features, -1, features).transpose(1, 0, 2)


def all_blocks(matrices, features):
    return jnp.concatenate(
        [to_blocks(matrices[matrix_id], row_kinds[matrix_id], features) for matrix_id in range(6)],
        0,
    )


def adam_update(weight, gradient, first_moment, second, fix_first, fix_second, rate, decay):
    first_new = beta_one * first_moment + (1.0 - beta_one) * gradient
    second_new = beta_two * second + (1.0 - beta_two) * gradient * gradient
    direction = first_new / fix_first / (jnp.sqrt(second_new / fix_second) + adam_eps)
    return (weight - rate * (direction + decay * weight), first_new, second_new)


def scores_for(query_block, key_rows, start_row, segment, head_slope):
    block_rows = query_block.shape[0]
    row_total = key_rows.shape[0]
    row_ids = start_row + jnp.arange(block_rows, dtype=jnp.int32)
    col_ids = jnp.arange(row_total, dtype=jnp.int32)
    distance = (row_ids[:, None] - col_ids[None, :]).astype(jnp.float32)
    seg_rows = lax.dynamic_slice_in_dim(segment, start_row, block_rows)
    allowed = (seg_rows[:, None] == segment[None, :]) & (col_ids[None, :] <= row_ids[:, None])
    raw_score = (
        jnp.dot(query_block, key_rows.T, preferred_element_type=jnp.float32) * 0.125
        - head_slope * distance
    )
    return (jnp.where(allowed, raw_score, masked_score), distance)


def attend(queries, key_rows, values, segment, head_slope, block_rows):
    row_total, head_width = queries.shape

    def per_block(start_row):
        query_block = lax.dynamic_slice_in_dim(queries, start_row, block_rows)
        scores, distance = scores_for(query_block, key_rows, start_row, segment, head_slope)
        largest = jnp.max(scores, -1, keepdims=True)
        log_total = largest + jnp.log(jnp.sum(jnp.exp(scores - largest), -1, keepdims=True))
        probability = jnp.exp(scores - log_total).astype(jnp.bfloat16)
        return (jnp.dot(probability, values, preferred_element_type=jnp.float32), log_total[:, 0])

    row_starts = jnp.arange(row_total // block_rows, dtype=jnp.int32) * block_rows
    attended, log_totals = lax.map(per_block, row_starts)
    return (attended.reshape(row_total, head_width), log_totals.reshape(row_total))


def attend_back(queries, key_rows, values, segment, head_slope, log_totals, grad_out, block_rows):
    row_total, head_width = queries.shape

    def per_block(carried, start_row):
        grad_keys, grad_values, grad_slope = carried
        query_block = lax.dynamic_slice_in_dim(queries, start_row, block_rows)
        grad_block = lax.dynamic_slice_in_dim(grad_out, start_row, block_rows)
        total_block = lax.dynamic_slice_in_dim(log_totals, start_row, block_rows)
        scores, distance = scores_for(query_block, key_rows, start_row, segment, head_slope)
        probability = jnp.exp(scores - total_block[:, None])
        grad_prob = jnp.dot(grad_block, values.T, preferred_element_type=jnp.float32)
        grad_score = (
            probability * (grad_prob - jnp.sum(probability * grad_prob, -1, keepdims=True))
        ).astype(jnp.bfloat16)
        grad_query = jnp.dot(grad_score, key_rows, preferred_element_type=jnp.float32) * 0.125
        grad_keys = (
            grad_keys
            + jnp.dot(grad_score.T, query_block, preferred_element_type=jnp.float32) * 0.125
        )
        grad_values = grad_values + jnp.dot(
            probability.astype(jnp.bfloat16).T, grad_block, preferred_element_type=jnp.float32
        )
        grad_slope = grad_slope - jnp.sum(grad_score.astype(jnp.float32) * distance)
        return ((grad_keys, grad_values, grad_slope), grad_query)

    row_starts = jnp.arange(row_total // block_rows, dtype=jnp.int32) * block_rows
    initial = (
        jnp.zeros((row_total, head_width), jnp.float32),
        jnp.zeros((row_total, head_width), jnp.float32),
        jnp.zeros((), jnp.float32),
    )
    (grad_keys, grad_values, grad_slope), grad_queries = lax.scan(per_block, initial, row_starts)
    return (grad_queries.reshape(row_total, head_width), grad_keys, grad_values, grad_slope)


def body(
    tokens,
    cotangent,
    doc_lengths,
    owners,
    master,
    first_moment,
    second_moment,
    ln_gain,
    ln_bias,
    norm_m,
    norm_v,
    slopes,
    slope_m,
    slope_v,
):
    micro_count, lane_count, tok_rows, features = tokens.shape
    unit_rows = tok_rows // 3
    seq_devices = lax.axis_size("seq")
    head_count = slopes.shape[0]
    head_width = features // head_count
    lane_units = unit_rows * seq_devices
    block_rows = min(512, lane_units)
    unit_total = lane_count * unit_rows
    slot_count = master.shape[1]
    sizes = block_counts(features, FF)
    starts_list = block_starts(owners, sizes)
    batch_rank = lax.axis_index("batch")
    seq_rank = lax.axis_index("seq")
    lane_rank = seq_rank // head_count
    head_rank = seq_rank % head_count
    low_slots = master[0].astype(jnp.bfloat16)
    fetched = []
    for matrix_id in range(6):
        owned_rows = lax.dynamic_slice_in_dim(
            low_slots, starts_list[matrix_id], sizes[matrix_id], 0
        )
        fetched.append(broadcast(owned_rows, "batch", owners[matrix_id]))
    gathered = lax.all_gather(for_sending(tuple(fetched)), "seq", axis=1, tiled=True)
    pool_weight, qkv_weight, out_weight, in_weight, back_weight, up_weight = [
        to_matrix(gathered[matrix_id], row_kinds[matrix_id]) for matrix_id in range(6)
    ]
    doc_ends = running_total(doc_lengths)
    doc_starts = jnp.concatenate(
        [jnp.zeros((micro_count, lane_count, 1), jnp.int32), doc_ends[..., :-1]], -1
    )
    unit_ids = seq_rank * unit_rows + jnp.arange(unit_rows, dtype=jnp.int32)
    keep_mask = 1.0 - jnp.any(
        unit_ids[None, None, :, None] == doc_starts[:, :, None, :], -1
    ).astype(jnp.float32)
    triples = tokens.reshape(micro_count, lane_count, unit_rows, 3, features)
    tail_tokens = triples[:, :, -1, 1:3]
    arrived = passed_along(tail_tokens, "seq", 1)
    lane_pick = jnp.arange(lane_count, dtype=jnp.int32) == lane_rank
    head_pick = jnp.arange(head_count, dtype=jnp.int32) == head_rank
    head_slope = jnp.sum(jnp.where(head_pick, slopes, 0.0))
    positions = jnp.arange(lane_units, dtype=jnp.int32)
    gain_grad = jnp.zeros((2, features), jnp.float32)
    bias_grad = jnp.zeros((2, features), jnp.float32)
    slope_grad = jnp.zeros((), jnp.float32)
    summed = None
    mixed_parts = []
    grad_parts = []
    outgoing = []
    for micro in range(micro_count):
        triple_now = triples[micro]
        keep_now = keep_mask[micro]
        earlier = jnp.concatenate([arrived[micro][:, None], triple_now[:, :-1, 1:3]], 1) * keep_now[
            :, :, None, None
        ].astype(jnp.bfloat16)
        pool_input = jnp.concatenate([earlier, triple_now[:, :, 0:1]], 2).reshape(
            unit_total, 3 * features
        )
        pooled = jnp.dot(pool_input, pool_weight, preferred_element_type=jnp.float32)
        normed = layer_norm(pooled, ln_gain[0], ln_bias[0]).astype(jnp.bfloat16)
        projected = jnp.dot(normed, qkv_weight, preferred_element_type=jnp.float32).astype(
            jnp.bfloat16
        )
        outbound = (
            projected.reshape(lane_count, unit_rows, 3, head_count, head_width)
            .transpose(0, 3, 1, 2, 4)
            .reshape(lane_count * head_count, unit_rows * 3 * head_width)
        )
        received = lax.all_to_all(outbound, "seq", split_axis=0, concat_axis=1, tiled=True).reshape(
            lane_units, 3, head_width
        )
        queries = received[:, 0]
        key_rows = received[:, 1]
        values = received[:, 2]
        lengths = jnp.sum(jnp.where(lane_pick[:, None], doc_lengths[micro], 0), 0)
        lane_ends = running_total(lengths)
        segment = jnp.sum((positions[:, None] >= lane_ends[None, :-1]).astype(jnp.int32), 1)
        attended, log_totals = attend(queries, key_rows, values, segment, head_slope, block_rows)
        returned = lax.all_to_all(
            attended.astype(jnp.bfloat16).reshape(1, lane_units * head_width),
            "seq",
            split_axis=1,
            concat_axis=0,
            tiled=True,
        )
        merged = (
            returned.reshape(lane_count, head_count, unit_rows, head_width)
            .transpose(0, 2, 1, 3)
            .reshape(unit_total, features)
        )
        residual = pooled + jnp.dot(merged, out_weight, preferred_element_type=jnp.float32)
        normed_two = layer_norm(residual, ln_gain[1], ln_bias[1]).astype(jnp.bfloat16)
        hidden = jnp.dot(normed_two, in_weight, preferred_element_type=jnp.float32)
        activated = gelu_tanh(hidden).astype(jnp.bfloat16)
        shortened = residual + jnp.dot(activated, back_weight, preferred_element_type=jnp.float32)
        short_low = shortened.astype(jnp.bfloat16)
        upward = jnp.dot(short_low, up_weight, preferred_element_type=jnp.float32).reshape(
            lane_count, unit_rows * 3, features
        )
        mixed_parts.append(tokens[micro].astype(jnp.float32) + upward)
        grad_upward = cotangent[micro].reshape(unit_total, 3 * features)
        sum_up = jnp.dot(short_low.T, grad_upward, preferred_element_type=jnp.float32)
        grad_short = jnp.dot(grad_upward, up_weight.T, preferred_element_type=jnp.float32)
        grad_short_low = grad_short.astype(jnp.bfloat16)
        sum_back = jnp.dot(activated.T, grad_short_low, preferred_element_type=jnp.float32)
        grad_activated = jnp.dot(grad_short_low, back_weight.T, preferred_element_type=jnp.float32)
        grad_hidden = jax.vjp(gelu_tanh, hidden)[1](grad_activated)[0].astype(jnp.bfloat16)
        sum_in = jnp.dot(normed_two.T, grad_hidden, preferred_element_type=jnp.float32)
        grad_normed_two = jnp.dot(grad_hidden, in_weight.T, preferred_element_type=jnp.float32)
        norm_two_back = jax.vjp(layer_norm, residual, ln_gain[1], ln_bias[1])[1]
        grad_resid_norm, grad_gain_two, grad_bias_two = norm_two_back(grad_normed_two)
        grad_residual = grad_short + grad_resid_norm
        grad_resid_low = grad_residual.astype(jnp.bfloat16)
        sum_out = jnp.dot(merged.T, grad_resid_low, preferred_element_type=jnp.float32)
        grad_merged = jnp.dot(
            grad_resid_low, out_weight.T, preferred_element_type=jnp.float32
        ).astype(jnp.bfloat16)
        back_outbound = (
            grad_merged.reshape(lane_count, unit_rows, head_count, head_width)
            .transpose(0, 2, 1, 3)
            .reshape(lane_count * head_count, unit_rows * head_width)
        )
        grad_attended = lax.all_to_all(
            back_outbound, "seq", split_axis=0, concat_axis=1, tiled=True
        ).reshape(lane_units, head_width)
        grad_queries, grad_keys, grad_values, grad_slope = attend_back(
            queries, key_rows, values, segment, head_slope, log_totals, grad_attended, block_rows
        )
        grad_heads = (
            jnp.stack([grad_queries, grad_keys, grad_values], 1)
            .astype(jnp.bfloat16)
            .reshape(1, lane_units * 3 * head_width)
        )
        grad_arrived = lax.all_to_all(grad_heads, "seq", split_axis=1, concat_axis=0, tiled=True)
        grad_projected = (
            grad_arrived.reshape(lane_count, head_count, unit_rows, 3, head_width)
            .transpose(0, 2, 3, 1, 4)
            .reshape(unit_total, 3 * features)
        )
        sum_qkv = jnp.dot(normed.T, grad_projected, preferred_element_type=jnp.float32)
        grad_normed = jnp.dot(grad_projected, qkv_weight.T, preferred_element_type=jnp.float32)
        norm_one_back = jax.vjp(layer_norm, pooled, ln_gain[0], ln_bias[0])[1]
        grad_pool_norm, grad_gain_one, grad_bias_one = norm_one_back(grad_normed)
        grad_pooled_low = (grad_residual + grad_pool_norm).astype(jnp.bfloat16)
        sum_pool = jnp.dot(pool_input.T, grad_pooled_low, preferred_element_type=jnp.float32)
        grad_pieces = jnp.dot(
            grad_pooled_low, pool_weight.T, preferred_element_type=jnp.float32
        ).reshape(lane_count, unit_rows, 3, features)
        grad_earlier = grad_pieces[:, :, 0:2] * keep_now[:, :, None, None]
        outgoing.append(grad_earlier[:, 0])
        following = jnp.concatenate(
            [grad_earlier[:, 1:], jnp.zeros((lane_count, 1, 2, features), jnp.float32)], 1
        )
        token_grad = jnp.concatenate([grad_pieces[:, :, 2:3], following], 2).reshape(
            lane_count, unit_rows * 3, features
        )
        grad_parts.append(cotangent[micro].astype(jnp.float32) + token_grad)
        gain_grad = gain_grad + jnp.stack([grad_gain_one, grad_gain_two])
        bias_grad = bias_grad + jnp.stack([grad_bias_one, grad_bias_two])
        slope_grad = slope_grad + grad_slope
        micro_grads = [sum_pool, sum_qkv, sum_out, sum_in, sum_back, sum_up]
        summed = (
            micro_grads
            if summed is None
            else [left + right for left, right in zip(summed, micro_grads)]
        )
    reduced = lax.psum_scatter(all_blocks(summed, features), "seq", scatter_dimension=1, tiled=True)
    incoming = passed_along(jnp.stack(outgoing).astype(jnp.bfloat16), "seq", -1).astype(jnp.float32)
    grad_tokens = jnp.stack(grad_parts).reshape(micro_count, lane_count, unit_rows, 3, features)
    grad_tokens = grad_tokens.at[:, :, -1, 1:3].add(incoming).reshape(tokens.shape)
    reduced_all = lax.psum(reduced, "batch")
    norm_grad, slopes_grad = lax.psum(
        (jnp.concatenate([gain_grad, bias_grad], 0), jnp.where(head_pick, slope_grad, 0.0)),
        ("batch", "seq"),
    )
    slot_map = slot_table(owners, batch_rank, sizes, slot_count)
    is_owned = jnp.sum(slot_map, -1)[:, None, None] > 0.5
    slot_grads = jnp.einsum("jb,brc->jrc", slot_map, reduced_all, precision=lax.Precision.HIGHEST)
    step_float = jnp.float32(STEP)
    fix_first = 1.0 - jnp.power(jnp.float32(beta_one), step_float)
    fix_second = 1.0 - jnp.power(jnp.float32(beta_two), step_float)
    new_weight, new_first, new_second = adam_update(
        master[0],
        slot_grads,
        first_moment[0],
        second_moment[0],
        fix_first,
        fix_second,
        rate_matrix,
        decay_rate,
    )
    new_weight = jnp.where(is_owned, new_weight, master[0])
    new_first = jnp.where(is_owned, new_first, first_moment[0])
    new_second = jnp.where(is_owned, new_second, second_moment[0])
    norm_now = jnp.concatenate([ln_gain, ln_bias], 0)
    new_norm, new_norm_m, new_norm_v = adam_update(
        norm_now, norm_grad, norm_m, norm_v, fix_first, fix_second, rate_norm, 0.0
    )
    new_slopes, new_slope_m, new_slope_v = adam_update(
        slopes, slopes_grad, slope_m, slope_v, fix_first, fix_second, rate_slope, 0.0
    )
    return (
        jnp.stack(mixed_parts),
        grad_tokens,
        new_weight[None],
        new_first[None],
        new_second[None],
        new_weight[None].astype(jnp.bfloat16),
        new_norm,
        new_norm_m,
        new_norm_v,
        new_slopes,
        new_slope_m,
        new_slope_v,
    )


MESH = pl.DeviceIdType.MESH
LOW = jnp.bfloat16
WIDE = jnp.float32
TILE = 128


class Plan:
    def __init__(self):
        self.tasks = {}

    def add(self, name, run, deps=(), waits=(), sends=(), cost=0.1, rank=0):
        assert name not in self.tasks
        self.tasks[name] = (run, tuple(deps), tuple(waits), tuple(sends), cost, rank)

    def order(self):
        now, done, arrival, free, listed = 0.0, set(), {}, {}, []
        left = list(self.tasks)
        while left:
            best = None
            for place, name in enumerate(left):
                run, deps, waits, sends, cost, rank = self.tasks[name]
                if any(d not in done for d in deps) or any(w not in arrival for w in waits):
                    continue
                begin = max([now] + [arrival[w] for w in waits] + [free.get(m[1], 0.0) - SLACK for m in sends])
                key = (begin, rank, place)
                if best is None or key < best[0]:
                    best = (key, name)
            name = best[1]
            run, deps, waits, sends, cost, rank = self.tasks[name]
            now = best[0][0] + cost
            for message, link, size in sends:
                rate, delay = LINKS[link]
                lanes = ("f", "r", "l") if link == "f" else (link,)
                end = max([now] + [free.get(lane, 0.0) for lane in lanes]) + size / rate
                free.update({lane: end for lane in lanes})
                arrival[message] = end + delay
            done.add(name)
            left.remove(name)
            listed.append((name, now))
        return listed


SLACK = 1.5
SENDS, RECEIVES = 48, 172
GATHERS = (
    (0, 0, 1, 0.0),
    (0, 1, 1, 0.01),
    (0, 2, 1, 0.02),
    (1, 0, 1, 0.1),
    (1, 1, 1, 0.11),
    (1, 2, 1, 0.12),
    (3, 0, 2, 0.2),
    (3, 2, 2, 0.22),
    (2, 0, 1, 0.3),
    (5, 0, 3, 0.4),
)
TURN = {5: 0, 1: 1}
SCATTERS = (
    (5, 0, 3, 1.0),
    (3, 0, 2, 1.1),
    (3, 2, 2, 1.2),
    (2, 0, 1, 1.3),
    (0, 0, 1, 0.7),
    (0, 1, 1, 0.71),
    (0, 2, 1, 0.72),
    (1, 0, 3, 0.8),
)
LINKS = {
    "c": (400e3, 1.0),
    "x": (52e3, 2.3),
    "r": (52e3, 2.3),
    "l": (52e3, 2.3),
    "f": (46e3, 3.3),
}


def start_of(owners, matrix_id, sizes):
    shared = jnp.int32(0)
    for earlier_id in range(matrix_id):
        shared = shared + jnp.where(owners[earlier_id] == owners[matrix_id], sizes[earlier_id], 0)
    return shared


def over_last(fn, value):
    return fn(value, axis=-1, keepdims=True)


def contract(left, right, left_dim, right_dim):
    return lax.dot_general(
        left, right, (((left_dim,), (right_dim,)), ((), ())), preferred_element_type=WIDE
    )


def gelu_parts(value):
    scale = math.sqrt(2.0 / math.pi)
    inner = jnp.tanh(scale * (value + 0.044715 * (value * value * value)))
    return inner, scale * (1.0 + 3 * 0.044715 * value * value)


def main_kernel(dims, refs):
    units, features, hidden_width, heads, micros, sizes = dims
    owners, docs, slopes, gain, bias, tok_hbm, cot_hbm, master_hbm = refs[:8]
    mixed_hbm, grad_hbm, red, small = refs[8:12]
    (
        w, masters, mine, other, core_in, both, x_in, tok, cot, tail_in, wide_tok, wide_cot, x_pool, x_norm, x_att,
        x_two, x_act, x_short, d_up, d_low, d_inner, d_res, d_qkv, d_pool, pooled, hat_one, hat_two, root_one, root_two,
        resid, hidden, short_grad, res_grad, q_out, q_in, a_out, a_in, da_out, da_in, dq_out, dq_in, probs, mixed, grad,
        wide_up, wide_grad, edge_in, x_near, x_wide, t_left, t_out, t_in, g, right_in, left_in, fin_out, fin_in, co_out, co_in, sums, sums_in, sends, recvs, local,
    ) = refs[12:]
    half = features // 2
    width = features // heads
    rows_of = masters.shape[1]
    count = heads
    tokens = 3 * units
    own = micros * units
    pair_width = 2 * width
    b, s = lax.axis_index("batch"), lax.axis_index("seq")
    x, c = b // 2, b % 2
    z, y = s // 2, s % 2
    spot = y * (7 - 2 * z) + z

    def seq_of(position):
        far = position // 4
        return 2 * (position + far * (7 - 2 * position)) + far

    def at(offset):
        return lax.rem(spot + offset + 2 * count, count)

    def rows_at(offset, part=0, length=rows_of):
        return pl.ds(pl.multiple_of(seq_of(at(offset)) * rows_of + part, 16), length)

    my_half = pl.ds(pl.multiple_of(c * half, half), half)
    other_half = pl.ds(pl.multiple_of((1 - c) * half, half), half)
    core_peer = (x * 2 + 1 - c, s)
    x_peer = ((1 - x) * 2 + c, s)
    right_peer = (b, seq_of(at(1)))
    left_peer = (b, seq_of(at(-1)))
    plan = Plan()
    flying, started, boxes = {}, [], {}

    def launch(name, copies, starts, group):
        if len(started) >= SENDS:
            started[len(started) - SENDS].wait_send()
        started.append(copies[0])
        flying[name] = copies[0]
        for start in starts:
            start()

    def describe(source, target, device, group):
        box = boxes.setdefault(group, len(boxes))
        return pltpu.make_async_remote_copy(
            src_ref=source,
            dst_ref=target,
            send_sem=sends.at[len(started) % SENDS],
            recv_sem=recvs.at[box],
            device_id=device,
            device_id_type=MESH,
        )

    def send(name, source, target, device, group=None):
        copy = describe(source, target, device, group or name)
        launch(name, [copy], [copy.start], group or name)

    def gather_up(group, whole):
        describe(whole, whole, core_peer, group).wait_recv()

    loads = [
        pltpu.make_async_copy(master_hbm, masters, local.at[0]),
        pltpu.make_async_copy(tok_hbm, tok, local.at[1]),
        pltpu.make_async_copy(cot_hbm, cot, local.at[2]),
    ]
    for copy in loads:
        copy.start()
    barrier = pltpu.get_barrier_semaphore()
    for step in range(1, count):
        pl.semaphore_signal(
            barrier, inc=1, device_id=(b, lax.rem(s + step, count)), device_id_type=MESH
        )
    for device in (core_peer, x_peer):
        pl.semaphore_signal(barrier, inc=1, device_id=device, device_id_type=MESH)
    pl.semaphore_wait(barrier, count + 1)

    spans, first = [], 0
    for size in sizes:
        spans.append((first, first + size))
        first += size
    in_base, back_base, up_base = spans[3][0], spans[4][0], spans[5][0]
    hidden_blocks = sizes[3]
    ours = in_base + x * hidden_blocks
    theirs = in_base + (1 - x) * hidden_blocks
    plan.add("ms", loads[0].wait, cost=0.5)

    def contribute(k):
        def run():
            lo, hi = spans[k]
            mask = (owners[k] == b).astype(WIDE)
            begin = start_of(owners, k, sizes)
            for block in range(lo, hi):
                slot = jnp.minimum(begin + (block - lo), masters.shape[0] - 1)
                mine[block] = (masters[slot, :, my_half] * mask).astype(LOW)
                other[block] = (masters[slot, :, other_half] * mask).astype(LOW)
            send(("g0", k), other.at[lo:hi], core_in.at[lo:hi], core_peer)

        return run

    def join_cores(k):
        def run():
            lo, hi = spans[k]
            flying[("g0", k)].wait_recv()
            both[lo:hi] = mine[lo:hi] + core_in[lo:hi]

        return run

    have = {k: [] for k in range(6)}
    gathers = []
    for k, offset, size, rank in GATHERS:
        name = ("w", k, offset)
        if k == 3:
            gathers.append((rank, name, (3, 4), ours + offset, theirs + offset, size))
            have[3] += [("h", name), ("hy", name)]
        else:
            gathers.append((rank, name, (k,), spans[k][0] + offset, None, size))
            have[k] += [("h", name)]
    piece_bytes = rows_of * half * 2

    def gather_chunk(rank, name, parents, here, there, size):
        split = there is not None
        load = size * piece_bytes
        blocks = pl.ds(here, size)
        away = pl.ds(there, size) if split else blocks

        def piece(offset, part=0, length=rows_of):
            return w.at[blocks, c, rows_at(offset, part, length)]

        def join_here():
            send(("g1", name), both.at[away], x_in.at[away], x_peer)

        def join_x():
            flying[("g1", name)].wait_recv()
            w[blocks, c, rows_at(0)] = both[blocks] + x_in[blocks]
            send(("R", 1, name), piece(0), piece(0), right_peer, (1, name))
            send(("L", 1, name), piece(0), piece(0), left_peer, (1, name))

        def onward(step):
            def run():
                gather_up((step - 1, name), w.at[blocks, c, 0 : rows_of * (2 if step < 5 else 1)])
                if step == 5:
                    return
                for side, offset, peer in (("R", 1 - step, right_peer), ("L", step - 1, left_peer)):
                    part = piece(offset)
                    if step == 4:
                        part = piece(offset, 0 if side == "R" else rows_of // 2, rows_of // 2)
                    send((side, step, name), part, part, peer, (step, name))

            return run

        def across(step):
            def run():
                for side, offset in (("R", -step), ("L", step)):
                    part = piece(offset)
                    if step == 4:
                        part = piece(offset, 0 if side == "R" else rows_of // 2, rows_of // 2)
                    if step > 0 or side == "R":
                        send(("X", side, step, name), part, part, x_peer, ("X", name))

            return run

        def distribute(which, span):
            def run():
                send((which, name), w.at[span, c], w.at[span, c], core_peer)

            return run

        plan.add(("cx", name), join_here, [("cs", k) for k in parents], (), [(("g1", name), "x", load)], 0.05, rank)
        plan.add(
            ("x", name), join_x, [("cx", name)], [("g1", name)],
            [(("R", 1, name), "r", load), (("L", 1, name), "l", load)], 0.05, rank,
        )
        crossing = []

        def cross(step, after):
            messages = [("X", side, step, name) for side in ("RL" if step else "R")]
            size_of = load if step < 4 else load // 2
            plan.add(("X", step, name), across(step), [after], (), [(m, "x", size_of) for m in messages], 0.05, rank + 0.05)
            crossing.extend(messages)

        if split:
            cross(0, ("x", name))
        for step in (2, 3, 4, 5):
            size_of = load if step < 4 else load // 2
            out = [((side, step, name), link, size_of) for side, link in (("R", "r"), ("L", "l"))] if step < 5 else []
            before = ("x", name) if step == 2 else (step - 1, "f", name)
            waits = [(side, step - 1, name) for side in "RL"]
            plan.add((step, "f", name), onward(step), [before], waits, out, 0.05, rank)
            if split:
                cross(step - 1, (step, "f", name))
        plan.add(("di", name), distribute("D", blocks), [(5, "f", name)], (), [(("D", name), "c", 8 * load)], 0.05, rank)
        plan.add(("h", name), arrive(("D", name)), [("di", name)], [("D", name)], (), 0.02, rank)
        if split:
            whole = w.at[pl.ds(there, size), c]
            last = [("X", step, name) for step in range(5)]
            plan.add(("xw", name), lambda: gather_up(("X", name), whole), last, crossing, (), 0.05, rank)
            plan.add(("dy", name), distribute("E", away), [("xw", name)], (), [(("E", name), "c", 8 * load)], 0.05, rank)
            plan.add(("hy", name), arrive(("E", name)), [("dy", name)], [("E", name)], (), 0.02, rank)

    def arrive(*names):
        def run():
            for name in names:
                flying[name].wait_recv()

        return run

    for k in (0, 1, 3, 4, 2, 5):
        lo, hi = spans[k]
        load = (hi - lo) * piece_bytes
        plan.add(("co", k), contribute(k), ["ms"], (), [(("g0", k), "c", load)], 0.04 * (hi - lo), 0.1)
        plan.add(("cs", k), join_cores(k), [("co", k)], [("g0", k)], (), 0.02 * (hi - lo), 0.1)
    for chunk in gathers:
        gather_chunk(*chunk)

    def exchange(name, buffer):
        send(name, buffer.at[0:own], buffer.at[own : 2 * own], core_peer)

    def shared(name, columns):
        return (name, "c", own * columns * 2)

    lead = 16
    tiles = range(features // TILE)

    def columns_at(tile, base=0):
        return slice(base + tile * TILE, base + (tile + 1) * TILE)

    def ends_of(micro):
        ends = []
        total = jnp.int32(0)
        for index in range(docs.shape[1] - 1):
            total = total + docs[micro, index]
            ends.append(total)
        return ends

    def kept(micro):
        ids = s * units + lax.broadcasted_iota(jnp.int32, (units, 1), 0)
        starts = (ids == 0).astype(jnp.int32)
        for end in ends_of(micro):
            starts = starts | (ids == end).astype(jnp.int32)
        return starts == 0

    def load_tokens():
        loads[1].wait()
        send("tl", tok.at[:, tokens - lead :], tail_in, (b, lax.rem(s + 1, count)))
        for micro in range(micros):
            for tile in tiles:
                wide_tok[micro, tile, lead:] = tok[micro, :, columns_at(tile)].astype(WIDE)

    def load_cotangent():
        loads[2].wait()
        for micro in range(micros):
            for tile in tiles:
                wide_cot[micro, tile] = cot[micro, :, columns_at(tile)].astype(WIDE)
                for r in range(3):
                    d_up[micro * units : (micro + 1) * units, columns_at(tile, r * features)] = wide_cot[
                        micro, tile, pl.ds(r, units, stride=3), :
                    ].astype(LOW)
        exchange("eu", d_up)

    def make_pieces():
        flying["tl"].wait_recv()
        for micro in range(micros):
            keep = kept(micro)
            for tile in tiles:
                wide_tok[micro, tile, :lead] = tail_in[micro, :, columns_at(tile)].astype(WIDE)
                for r in range(3):
                    part = wide_tok[micro, tile, pl.ds(lead - 2 + r, units, stride=3), :]
                    if r < 2:
                        part = jnp.where(keep, part, 0.0)
                    x_pool[micro * units : (micro + 1) * units, columns_at(tile, r * features)] = part.astype(LOW)
        exchange("ep", x_pool)

    plan.add("tok", load_tokens, sends=[("tl", "f", 2 * lead * features * 2)], cost=0.3, rank=1)
    plan.add(
        "pc", make_pieces, ["tok"], ["tl"], [shared("ep", 3 * features)], 0.5, rank=1
    )
    plan.add("cot", load_cotangent, (), (), [shared("eu", 3 * features)], 0.5, rank=2)

    def normal(value, which, hat, root):
        centred = value - over_last(jnp.mean, value)
        scale = lax.rsqrt(over_last(jnp.mean, centred * centred) + ln_eps)
        unit = centred * scale
        hat[...] = unit
        root[...] = scale
        return (unit * gain[which : which + 1, :] + bias[which : which + 1, :]).astype(LOW)

    def both_halves(make):
        return jnp.concatenate([make(0), make(1)], axis=1)

    def pool():
        def side(h):
            total = None
            for r in range(3):
                term = contract(x_pool[0:own, r * features : (r + 1) * features], w[r, h], 1, 0)
                total = term if total is None else total + term
            return total

        value = both_halves(side)
        pooled[...] = value
        x_norm[0:own] = normal(value, 0, hat_one, root_one)
        exchange("en", x_norm)

    lane = lambda: lax.broadcasted_iota(jnp.int32, (1, pair_width), 1)

    def swap(value):
        return pltpu.roll(value, width, axis=1)

    def to_heads(tile, target, pair, row):
        low_lanes = lane() < width
        first, second = tile[:units], tile[units:]
        target[2 * pair, row : row + units] = jnp.where(low_lanes, first, swap(second)).astype(LOW)
        target[2 * pair + 1, row : row + units] = jnp.where(low_lanes, swap(first), second).astype(LOW)

    def from_heads(source, pair, row):
        low_lanes = lane() < width
        even = source[2 * pair, row : row + units].astype(WIDE)
        odd = source[2 * pair + 1, row : row + units].astype(WIDE)
        return jnp.where(low_lanes, even, swap(odd)).astype(LOW), jnp.where(low_lanes, swap(even), odd).astype(LOW)

    def spread(name, source, target):
        for step in range(1, count):
            there = lax.rem(s + step, count)
            send((name, step), source.at[there], target.at[s], (b, there), name)
        target[s] = source[s]

    def spread_names(name):
        return [(name, step) for step in range(1, count)]

    def spread_sends(name, rows):
        return [((name, step), "f", rows * pair_width * 2) for step in range(1, count)]

    def project():
        for part in range(3):
            for h in range(2):
                value = contract(x_norm[0:own], w[3 + part, h], 1, 0)
                for tile in range(half // pair_width):
                    to_heads(
                        value[:, tile * pair_width : (tile + 1) * pair_width],
                        q_out,
                        h * (half // pair_width) + tile,
                        part * units,
                    )
        spread("q", q_out, q_in)

    lane_units = units * count

    def heads_of(source, part):
        return source[:, part * units : (part + 1) * units, :].reshape(lane_units, pair_width)

    def lanes_of(micro):
        return (lane() // width == micro).astype(WIDE).astype(LOW)

    def distances():
        row_ids = lax.broadcasted_iota(jnp.int32, (lane_units, lane_units), 0)
        col_ids = lax.broadcasted_iota(jnp.int32, (lane_units, lane_units), 1)
        return row_ids - col_ids

    def attend_now():
        gather_up("q", q_in.at[0 : count - 1])
        queries, keys, values = (heads_of(q_in, part) for part in range(3))
        slope = slopes[s]
        total = None
        for micro in range(micros):
            gap = distances()
            row_seg = jnp.zeros((lane_units, 1), jnp.int32)
            col_seg = jnp.zeros((1, lane_units), jnp.int32)
            for end in ends_of(micro):
                row_seg += (lax.broadcasted_iota(jnp.int32, (lane_units, 1), 0) >= end).astype(jnp.int32)
                col_seg += (lax.broadcasted_iota(jnp.int32, (1, lane_units), 1) >= end).astype(jnp.int32)
            allowed = (row_seg == col_seg) & (gap >= 0)
            mask = lanes_of(micro)
            raw = contract(queries * mask, keys, 1, 1) * 0.125 - slope * gap.astype(WIDE)
            scores = jnp.where(allowed, raw, masked_score)
            raised = jnp.exp(scores - over_last(jnp.max, scores))
            probability = raised / over_last(jnp.sum, raised)
            probs[micro] = probability
            term = contract(probability.astype(LOW), values * mask, 1, 0)
            total = term if total is None else total + term
        a_out[...] = total.astype(LOW).reshape(count, units, pair_width)
        spread("a", a_out, a_in)

    def merge():
        gather_up("a", a_in.at[0 : count - 1])
        for pair in range(heads // 2):
            columns = slice(pair * pair_width, (pair + 1) * pair_width)
            first, second = from_heads(a_in, pair, 0)
            x_att[0:units, columns] = first
            x_att[units:own, columns] = second
        exchange("ea", x_att)

    def project_out():
        value = pooled[...] + both_halves(lambda h: contract(x_att[0:own], w[6, h], 1, 0))
        resid[...] = value
        x_two[0:own] = normal(value, 1, hat_two, root_two)
        exchange("et", x_two)


    def widen(j):
        def run():
            for h in range(2):
                columns = slice(j * features + h * half, j * features + (h + 1) * half)
                value = contract(x_two[0:own], w[in_base + j, h], 1, 0)
                hidden[:, columns] = value
                inner, _ = gelu_parts(value)
                x_act[0:own, columns] = (0.5 * value * (1.0 + inner)).astype(LOW)
            if j == hidden_blocks - 1:
                exchange("ec", x_act)

        return run

    def narrow():
        def side(h):
            total = resid[:, h * half : (h + 1) * half]
            for j in range(hidden_blocks):
                total = total + contract(
                    x_act[0:own, j * features : (j + 1) * features], w[back_base + j, h], 1, 0
                )
            return total

        x_short[0:own] = both_halves(side).astype(LOW)
        exchange("es", x_short)

    outs = [
        pltpu.make_async_copy(mixed, mixed_hbm, local.at[3]),
        pltpu.make_async_copy(grad, grad_hbm, local.at[4]),
    ]

    def lift(r):
        def run():
            for h in range(2):
                value = contract(x_short[0:own], w[up_base + r, h], 1, 0)
                for micro in range(micros):
                    for tile in range(half // TILE):
                        wide_up[micro, h * (half // TILE) + tile, pl.ds(r, units, stride=3), :] = value[
                            micro * units : (micro + 1) * units, columns_at(tile)
                        ]
            if r == 2:
                for micro in range(micros):
                    for tile in tiles:
                        columns = columns_at(tile)
                        mixed[micro, :, columns] = tok[micro, :, columns].astype(WIDE) + wide_up[micro, tile]
                outs[0].start()

        return run

    plan.add("po", pool, ["pc", *have[0]], (), [shared("en", features)], 0.6, rank=3)
    plan.add("pr", project, ["po", *have[1]], (), spread_sends("q", 3 * units), 0.6, rank=3)
    plan.add("at", attend_now, ["pr"], spread_names("q"), spread_sends("a", units), 1.1, rank=3)
    plan.add("me", merge, ["at"], spread_names("a"), [shared("ea", features)], 0.15, rank=3)
    plan.add("ou", project_out, ["me", *have[2]], (), [shared("et", features)], 0.45, rank=3)
    for j in range(hidden_blocks):
        last = j == hidden_blocks - 1
        plan.add(
            ("wi", j), widen(j), ["ou", *have[3]] + ([("wi", i) for i in range(j)] if last else []), (),
            [shared("ec", hidden_width)] if last else (), 0.3, rank=3,
        )
    plan.add(
        "na", narrow, [("wi", j) for j in range(hidden_blocks)] + [*have[3]], (), [shared("es", features)], 0.5,
        rank=3,
    )
    for r in range(3):
        plan.add(
            ("li", r), lift(r), ["na", *have[5], "tok"] + ([("li", i) for i in range(r)]), (), (), 0.3, rank=8
        )

    def back_short():
        total = None
        for r in range(3):
            for h in range(2):
                begin = r * features + h * half
                term = contract(d_up[0:own, begin : begin + half], w[up_base + r, h], 1, 1)
                total = term if total is None else total + term
        short_grad[...] = total
        d_low[0:own] = total.astype(LOW)
        exchange("el", d_low)

    def back_widen(j):
        def run():
            total = contract(d_low[0:own, 0:half], w[back_base + j, 0], 1, 1)
            total = total + contract(d_low[0:own, half:features], w[back_base + j, 1], 1, 1)
            columns = slice(j * features, (j + 1) * features)
            value = hidden[:, columns]
            inner, slope = gelu_parts(value)
            factor = 0.5 * (1.0 + inner) + 0.5 * value * (1.0 - inner * inner) * slope
            d_inner[0:own, columns] = (total * factor).astype(LOW)
            if j == hidden_blocks - 1:
                exchange("ei", d_inner)

        return run

    def back_normal(value, which, hat, root):
        unit = hat[...]
        sums[which : which + 1, :] = jnp.sum(value * unit, axis=0, keepdims=True)
        sums[2 + which : 3 + which, :] = jnp.sum(value, axis=0, keepdims=True)
        scaled = value * gain[which : which + 1, :]
        return root[...] * (
            scaled - over_last(jnp.mean, scaled) - unit * over_last(jnp.mean, scaled * unit)
        )

    def back_two():
        total = None
        for j in range(hidden_blocks):
            for h in range(2):
                begin = j * features + h * half
                term = contract(d_inner[0:own, begin : begin + half], w[in_base + j, h], 1, 1)
                total = term if total is None else total + term
        value = short_grad[...] + back_normal(total, 1, hat_two, root_two)
        res_grad[...] = value
        d_res[0:own] = value.astype(LOW)
        exchange("er", d_res)

    def back_out():
        value = contract(d_res[0:own, 0:half], w[6, 0], 1, 1)
        value = value + contract(d_res[0:own, half:features], w[6, 1], 1, 1)
        for pair in range(heads // 2):
            to_heads(value[:, pair * pair_width : (pair + 1) * pair_width], da_out, pair, 0)
        spread("da", da_out, da_in)

    def back_attend():
        gather_up("da", da_in.at[0 : count - 1])
        queries, keys, values = (heads_of(q_in, part) for part in range(3))
        grads = da_in[...].reshape(lane_units, pair_width)
        totals = [None, None, None]
        slope_total = jnp.zeros((1, 1), WIDE)
        for micro in range(micros):
            mask = lanes_of(micro)
            own_grads = grads * mask
            probability = probs[micro]
            grad_prob = contract(own_grads, values, 1, 1)
            scaled = probability * grad_prob
            score = scaled - probability * over_last(jnp.sum, scaled)
            low_score = score.astype(LOW)
            gap = distances().astype(WIDE)
            slope_total = slope_total - jnp.sum(
                jnp.sum(low_score.astype(WIDE) * gap, axis=0, keepdims=True), axis=1, keepdims=True
            )
            terms = (
                contract(low_score, keys * mask, 1, 0) * 0.125,
                contract(low_score, queries * mask, 0, 0) * 0.125,
                contract(probability.astype(LOW), own_grads, 0, 0),
            )
            totals = [term if total is None else total + term for total, term in zip(totals, terms)]
        for part in range(3):
            dq_out[:, part * units : (part + 1) * units, :] = (
                totals[part].astype(LOW).reshape(count, units, pair_width)
            )
        spread("dq", dq_out, dq_in)
        places = lax.broadcasted_iota(jnp.int32, (1, features), 1)
        sums[4:5, :] = jnp.where(places == s, slope_total, 0.0)
        sums[5:8, :] = jnp.zeros((3, features), WIDE)

    def back_project():
        gather_up("dq", dq_in.at[0 : count - 1])
        for part in range(3):
            for pair in range(heads // 2):
                begin = part * features + pair * pair_width
                first, second = from_heads(dq_in, pair, part * units)
                d_qkv[0:units, begin : begin + pair_width] = first
                d_qkv[units:own, begin : begin + pair_width] = second
        exchange("eq", d_qkv)

    def back_one():
        total = None
        for part in range(3):
            for h in range(2):
                begin = part * features + h * half
                term = contract(d_qkv[0:own, begin : begin + half], w[3 + part, h], 1, 1)
                total = term if total is None else total + term
        value = res_grad[...] + back_normal(total, 0, hat_one, root_one)
        d_pool[0:own] = value.astype(LOW)
        exchange("ed1", d_pool)

    def back_pieces():
        for r in range(3):
            value = contract(d_pool[0:own, 0:half], w[r, 0], 1, 1)
            value = value + contract(d_pool[0:own, half:features], w[r, 1], 1, 1)
            for micro in range(micros):
                part = value[micro * units : (micro + 1) * units]
                if r < 2:
                    part = jnp.where(kept(micro), part, 0.0)
                for tile in tiles:
                    wide_grad[micro, tile, pl.ds(6 + r, units, stride=3), :] = part[:, columns_at(tile)]
        send("ed", wide_grad.at[:, :, 0:8], edge_in, (b, lax.rem(s + count - 1, count)))

    def finish_grad():
        flying["ed"].wait_recv()
        inside = (s < count - 1).astype(WIDE)
        for micro in range(micros):
            for tile in tiles:
                columns = columns_at(tile)
                wide_grad[micro, tile, 6 + tokens : 8 + tokens, :] = edge_in[micro, tile, 6:8, :] * inside
                grad[micro, :, columns] = cot[micro, :, columns].astype(WIDE) + wide_grad[micro, tile, 8 : 8 + tokens]
        outs[1].start()

    plan.add("bs", back_short, ["cot", *have[5]], (), [shared("el", features)], 0.65, rank=4)
    for j in range(hidden_blocks):
        last = j == hidden_blocks - 1
        plan.add(
            ("bw", j), back_widen(j),
            ["bs", *have[3], ("wi", j)] + ([("bw", i) for i in range(j)] if last else []), (),
            [shared("ei", hidden_width)] if last else (), 0.35, rank=4,
        )
    plan.add(
        "b2", back_two, [("bw", j) for j in range(hidden_blocks)] + [*have[3]], (),
        [shared("er", features)], 0.9, rank=4,
    )
    plan.add("bo", back_out, ["b2", *have[2]], (), spread_sends("da", units), 0.45, rank=4)
    plan.add("ba", back_attend, ["bo", "at"], spread_names("da"), spread_sends("dq", 3 * units), 1.4, rank=4)
    plan.add("bp", back_project, ["ba"], spread_names("dq"), [shared("eq", 3 * features)], 0.2, rank=4)
    plan.add("b1", back_one, ["bp"], (), [shared("ed1", features)], 0.75, rank=4)
    plan.add("bx", back_pieces, ["b1"], (), [("ed", "f", 2 * 8 * features * 4)], 0.65, rank=9)
    plan.add("fg", finish_grad, ["bx", "cot"], ["ed"], (), 0.3, rank=9)

    def add_pair(step, device):
        def run():
            if step > 0:
                flying[("s", step - 1)].wait_recv()
                sums[8 * step : 8 * step + 8] = sums[8 * step - 8 : 8 * step] + sums_in[8 * step - 8 : 8 * step]
            if device is not None:
                send(("s", step), sums.at[8 * step : 8 * step + 8], sums_in.at[8 * step : 8 * step + 8], device)
            else:
                small[...] = sums[8 * step : 8 * step + 8]

        return run

    partners = [
        core_peer,
        x_peer,
        (b, 2 * z + 1 - y),
        (b, 2 * (z + 1 - 2 * (z % 2)) + y),
        (b, 2 * lax.rem(z + 2, 4) + y),
        None,
    ]
    for step, device in enumerate(partners):
        plan.add(
            ("sum", step), add_pair(step, device), ["b1", "ba"] if step == 0 else [("sum", step - 1)],
            [("s", step - 1)] if step else (), [(("s", step), "f", 8 * features * 4)] if device is not None else (), 0.1,
            rank=0,
        )

    for name, columns in (
        ("ep", "pc"), ("en", "po"), ("ea", "me"), ("et", "ou"), ("ec", ("wi", hidden_blocks - 1)),
        ("es", "na"), ("eu", "cot"), ("el", "bs"), ("ei", ("bw", hidden_blocks - 1)),
        ("er", "b2"), ("eq", "bp"), ("ed1", "b1"),
    ):
        plan.add(("got", name), arrive(name), [columns], [name], cost=0.02)

    def columns_of(block):
        return pl.ds(pl.multiple_of(block * features + c * half, half), half)

    def outer(block, left, left_block, right, right_block):
        def run():
            rows = left[:, left_block * features : (left_block + 1) * features]
            g[block] = contract(rows, right[:, columns_of(right_block)], 0, 0).astype(LOW)

        return run

    def send_either(name, first_source, second_source, target):
        copies = [describe(source, target, x_peer, name) for source in (first_source, second_source)]
        launch(name, copies, [lambda plane=plane: pl.when(x == plane)(copies[plane].start) for plane in range(2)], name)

    def near_away():
        send_either("sn", d_low.at[0:own], x_two.at[0:own], x_near.at[0:own])

    def near_core():
        arrive("sn")()
        exchange("cn", x_near)

    def wide_away(j):
        columns = slice(j * features, (j + 1) * features)

        def run():
            source = (x_act.at[0:own, columns], d_inner.at[0:own, columns])
            send_either(("sw", j), *source, x_wide.at[0:own, columns])

        return run

    def wide_core(j):
        columns = slice(j * features, (j + 1) * features)

        def run():
            arrive(("sw", j))()
            send(("cw", j), x_wide.at[0:own, columns], x_wide.at[own : 2 * own, columns], core_peer)

        return run

    def outer_split(j):
        columns = slice(j * features, (j + 1) * features)

        def run():
            @pl.when(x == 0)
            def _():
                total = contract(x_two[...], d_inner[:, columns_of(j)], 0, 0)
                g[in_base + j] = (total + contract(x_near[...], x_wide[:, columns_of(j)], 0, 0)).astype(LOW)

            @pl.when(x == 1)
            def _():
                total = contract(x_act[:, columns], d_low[:, my_half], 0, 0)
                g[back_base + j] = (total + contract(x_wide[:, columns], x_near[:, my_half], 0, 0)).astype(LOW)

        return run

    lump = own * features * 2
    plan.add("sn", near_away, ["bs", "ou"], (), [("sn", "x", lump)], 0.05, 2)
    plan.add("nc", near_core, ["sn"], ["sn"], [("cn", "c", lump)], 0.05, 2)
    plan.add(("got", "cn"), arrive("cn"), ["nc"], ["cn"], (), 0.02, 2)
    for j in range(hidden_blocks):
        plan.add(("sw", j), wide_away(j), [("wi", j), ("bw", j)], (), [(("sw", j), "x", lump)], 0.05, 2)
        plan.add(("wc", j), wide_core(j), [("sw", j)], [("sw", j)], [(("cw", j), "c", lump)], 0.05, 2)
        plan.add(("got", "cw", j), arrive(("cw", j)), [("wc", j)], [("cw", j)], (), 0.02, 2)
        deps = [("got", e) for e in ("et", "ec", "el", "ei", "cn")] + [("got", "cw", j)]
        plan.add(("gr", j, "s"), outer_split(j), deps, cost=0.6, rank=4.5)
    quarter = half // 2
    quartered = {5: (x_short, d_up, "na", "cot", "es", "eu"), 1: (x_norm, d_qkv, "po", "bp", "en", "eq")}

    def left_away(k):
        def run():
            send(("tx", k), quartered[k][0].at[0:own], t_left.at[TURN[k], 0:own], x_peer)

        return run

    def left_core(k):
        def run():
            arrive(("tx", k))()
            send(("tc", k), t_left.at[TURN[k], 0:own], t_left.at[TURN[k], own : 2 * own], core_peer)

        return run

    def right_away(k, r):
        columns = slice(r * half, (r + 1) * half)

        def run():
            for core in range(2):
                begin = r * features + core * half + (1 - x) * quarter
                t_out[TURN[k], :, r * half + core * quarter : r * half + (core + 1) * quarter] = quartered[k][1][
                    0:own, pl.ds(pl.multiple_of(begin, quarter), quarter)
                ]
            send(("ty", k, r), t_out.at[TURN[k], :, columns], t_in.at[TURN[k], 0:own, columns], x_peer)

        return run

    def right_core(k, r):
        columns = slice(r * half, (r + 1) * half)

        def run():
            arrive(("ty", k, r))()
            send(("td", k, r), t_in.at[TURN[k], 0:own, columns], t_in.at[TURN[k], own : 2 * own, columns], core_peer)

        return run

    def outer_quarter(k, r):
        def run():
            left, right = quartered[k][:2]
            near = pl.ds(pl.multiple_of(r * features + c * half + x * quarter, quarter), quarter)
            away = pl.ds(pl.multiple_of(r * half + c * quarter, quarter), quarter)
            total = contract(left[...], right[:, near], 0, 0) + contract(t_left[TURN[k]], t_in[TURN[k], :, away], 0, 0)
            g[spans[k][0] + r, :, pl.ds(pl.multiple_of(x * quarter, quarter), quarter)] = total.astype(LOW)

        return run

    for k, (_, _, left_dep, right_dep, left_got, right_got) in quartered.items():
        plan.add(("tx", k), left_away(k), [left_dep], (), [(("tx", k), "x", lump)], 0.05, 2.5)
        plan.add(("tw", k), left_core(k), [("tx", k)], [("tx", k)], [(("tc", k), "c", lump)], 0.05, 2.5)
        plan.add(("got", "tc", k), arrive(("tc", k)), [("tw", k)], [("tc", k)], (), 0.02, 2.5)
        for r in range(3):
            plan.add(("ty", k, r), right_away(k, r), [right_dep], (), [(("ty", k, r), "x", lump // 2)], 0.05, 2.5)
            plan.add(("tz", k, r), right_core(k, r), [("ty", k, r)], [("ty", k, r)], [(("td", k, r), "c", lump // 2)], 0.05, 2.5)
            plan.add(("got", "td", k, r), arrive(("td", k, r)), [("tz", k, r)], [("td", k, r)], (), 0.02, 2.5)
            deps = [("got", left_got), ("got", right_got), ("got", "tc", k), ("got", "td", k, r)]
            plan.add(("gr", spans[k][0] + r), outer_quarter(k, r), deps, cost=0.4, rank=5)
    weight_grads = []
    for r in range(3):
        weight_grads.append((r, x_pool, r, d_pool, 0, [("got", "ep"), ("got", "ed1")]))
    weight_grads.append((6, x_att, 0, d_res, 0, [("got", "ea"), ("got", "er")]))
    for block, left, left_block, right, right_block, deps in weight_grads:
        plan.add(("gr", block), outer(block, left, left_block, right, right_block), deps, cost=0.3, rank=5)

    def scatter_chunk(rank, name, here, there, size, deps):
        split, quarters = there is not None, there is here
        blocks = pl.ds(here, size)
        load = size * piece_bytes // (2 if quarters else 1)
        away, span, away_span, length_out = blocks, slice(None), slice(None), half
        begin_out, away_out = c * half, c * half
        if quarters:
            span = pl.ds(pl.multiple_of(x * quarter, quarter), quarter)
            away_span = pl.ds(pl.multiple_of((1 - x) * quarter, quarter), quarter)
            length_out, begin_out, away_out = quarter, c * half + x * quarter, c * half + (1 - x) * quarter
        elif split:
            away = pl.ds(there, size)
        out_span = pl.ds(pl.multiple_of(begin_out, length_out), length_out)
        out_away = pl.ds(pl.multiple_of(away_out, length_out), length_out)

        half_rows = rows_of // 2
        sides = (("R", 0, right_in, right_peer), ("L", half_rows, left_in, left_peer))

        def first_step():
            for side, part, inbox, peer in sides:
                source = g.at[blocks, rows_at(4, part, half_rows), span]
                target = inbox.at[0, blocks, part : part + half_rows, span]
                send((side, "s", 1, name), source, target, peer, ("s", 1, name))

        def take(step):
            gather_up(("s", step, name), g.at[blocks, 0 : rows_of * (1 if step == 1 else 2), span])

        def next_step(step):
            def run():
                take(step - 1)
                for side, half_part, inbox, peer in sides:
                    offset = (5 - step) if side == "R" else (step - 5)
                    part, length = (half_part, half_rows) if step == 2 else (0, rows_of)
                    rows = rows_at(offset, part, length)
                    g[blocks, rows, span] = g[blocks, rows, span] + inbox[step - 2, blocks, part : part + length, span]
                    source = g.at[blocks, rows_at(offset), span]
                    send((side, "s", step, name), source, inbox.at[step - 1, blocks, :, span], peer, ("s", step, name))

            return run

        def finish():
            take(4)
            total = g[blocks, rows_at(0), span].astype(WIDE)
            total = total + right_in[3, blocks, :, span].astype(WIDE) + left_in[3, blocks, :, span].astype(WIDE)
            fin_out[blocks, :, span] = total.astype(LOW)
            send(("rx", name), fin_out.at[blocks, :, span], fin_in.at[blocks, :, span], x_peer)
            if split:
                red[blocks, :, out_span] = fin_out[blocks, :, span]
                send(("rc", name), fin_out.at[blocks, :, span], co_in.at[blocks, :, span], core_peer)

        def finish_x():
            arrive(("rx", name))()
            if split:
                red[away, :, out_away] = fin_in[away, :, away_span]
                send(("rd", name), fin_in.at[away, :, away_span], co_in.at[away, :, away_span], core_peer)
            else:
                total = (fin_out[blocks].astype(WIDE) + fin_in[blocks].astype(WIDE)).astype(LOW)
                co_out[blocks] = total
                red[blocks, :, my_half] = total
                send(("rc", name), co_out.at[blocks], co_in.at[blocks], core_peer)

        def finish_core():
            arrive(("rc", name), *([("rd", name)] if split else []))()
            red[blocks, :, other_half] = co_in[blocks]
            if split and not quarters:
                red[away, :, other_half] = co_in[away]

        links = (("R", "r"), ("L", "l"))
        out = [((side, "s", 1, name), link, load // 2) for side, link in links]
        plan.add(("r", 1, name), first_step, deps, (), out, 0.05, rank)
        for step in (2, 3, 4):
            waits = [(side, "s", step - 1, name) for side in "RL"]
            out = [((side, "s", step, name), link, load) for side, link in links]
            plan.add(("r", step, name), next_step(step), [("r", step - 1, name)], waits, out, 0.04 * size, rank)
        own_out = [(("rc", name), "c", load)]
        plan.add(
            ("fi", name), finish, [("r", 4, name)], [("R", "s", 4, name), ("L", "s", 4, name)],
            [(("rx", name), "x", load)] + (own_out if split else []), 0.02 * size, rank,
        )
        late_out = [(("rd", name), "c", load)] if split else own_out
        plan.add(("fx", name), finish_x, [("fi", name)], [("rx", name)], late_out, 0.02 * size, rank)
        plan.add(
            ("fc", name), finish_core, [("fx", name)], [("rc", name)] + ([("rd", name)] if split else []), (), 0.02 * size, rank
        )

    for k, offset, size, rank in SCATTERS:
        name = ("g", k, offset)
        if k == 3:
            deps = [("gr", j, "s") for j in range(offset, offset + size)]
            scatter_chunk(rank, name, ours + offset, theirs + offset, size, deps)
        else:
            begin = spans[k][0] + offset
            scatter_chunk(rank, name, begin, begin if k in quartered else None, size, [("gr", begin + j) for j in range(size)])

    for name, _ in plan.order():
        plan.tasks[name][0]()
    for copy in started[-SENDS:]:
        copy.wait_send()
    for copy in outs:
        copy.wait()


def adam_kernel(sizes, refs):
    owners, red, small, gain, bias, norm_m, norm_v, slope, slope_m, slope_v, master, first, second, mixed, grad = refs[:15]
    (
        new_w, new_m, new_v, new_low, norm_out, norm_m_out, norm_v_out, slope_out, slope_m_out, slope_v_out, mixed_out,
        grad_out,
    ) = refs[15:]
    step = pl.program_id(0)
    fix_first = 1.0 - beta_one**STEP
    fix_second = 1.0 - beta_two**STEP
    mixed_out[...] = mixed[...]
    grad_out[...] = grad[...]

    @pl.when(step == 0)
    def _():
        for begin, values in ((0, gain), (2, bias)):
            rows = slice(begin, begin + 2)
            norm_out[rows], norm_m_out[rows], norm_v_out[rows] = adam_update(
                values[...], small[rows], norm_m[rows], norm_v[rows], fix_first, fix_second, rate_norm, 0.0
            )
        heads = slope.shape[1]
        slope_out[...], slope_m_out[...], slope_v_out[...] = adam_update(
            slope[...], small[4:5, 0:heads], slope_m[...], slope_v[...], fix_first, fix_second, rate_slope, 0.0
        )

    me = lax.axis_index("batch")
    for place in range(master.shape[0]):
        slot = step * master.shape[0] + place
        block, held, base = jnp.int32(0), jnp.int32(0), 0
        for matrix_id, size in enumerate(sizes):
            begin = start_of(owners, matrix_id, sizes)
            inside = (owners[matrix_id] == me) & (slot >= begin) & (slot < begin + size)
            block = jnp.where(inside, base + slot - begin, block)
            held = jnp.where(inside, 1, held)
            base += size
        gradient = red[block].astype(WIDE)
        values = adam_update(
            master[place], gradient, first[place], second[place], fix_first, fix_second, rate_matrix, decay_rate
        )
        keep = jnp.full(gradient.shape, held, jnp.int32) > 0
        weight = jnp.where(keep, values[0], master[place])
        new_w[place] = weight
        new_m[place] = jnp.where(keep, values[1], first[place])
        new_v[place] = jnp.where(keep, values[2], second[place])
        new_low[place] = weight.astype(LOW)


def fused_body(tokens, cotangent, doc_lengths, owners, master, first_moment, second_moment, ln_gain, ln_bias, norm_m, norm_v, slopes, slope_m, slope_v):
    micros, _, tok_rows, features = tokens.shape
    units, heads, width = tok_rows // 3, slopes.shape[0], features // slopes.shape[0]
    sizes = tuple(block_counts(features, FF))
    blocks, own, half = sum(sizes), micros * units, features // 2
    slots, rows = master.shape[1], master.shape[2]
    lane_units = units * heads
    split = features // TILE
    hbm, vmem, smem = (pl.BlockSpec(memory_space=m) for m in (pl.ANY, pltpu.VMEM, pltpu.SMEM))
    low = lambda *shape: pltpu.VMEM(shape, LOW)
    wide = lambda *shape: pltpu.VMEM(shape, WIDE)
    pieces = lambda: low(blocks, rows, half)
    both = lambda columns: low(2 * own, columns)
    scratch = [
        low(blocks, 2, features, half), wide(slots, rows, features), pieces(), pieces(), pieces(), pieces(), pieces(),
        low(micros, tok_rows, features), low(micros, tok_rows, features), low(micros, 16, features),
        wide(micros, split, 16 + tok_rows, TILE), wide(micros, split, tok_rows, TILE),
        both(3 * features), both(features), both(features), both(features), both(FF), both(features),
        both(3 * features), both(features), both(FF), both(features), both(3 * features), both(features),
        wide(own, features), wide(own, features), wide(own, features), wide(own, 1), wide(own, 1),
        wide(own, features), wide(own, FF), wide(own, features), wide(own, features),
        low(heads, 3 * units, 2 * width), low(heads, 3 * units, 2 * width), low(heads, units, 2 * width),
        low(heads, units, 2 * width), low(heads, units, 2 * width), low(heads, units, 2 * width),
        low(heads, 3 * units, 2 * width), low(heads, 3 * units, 2 * width),
        wide(micros, lane_units, lane_units), wide(micros, tok_rows, features), wide(micros, tok_rows, features),
        wide(micros, split, tok_rows, TILE), wide(micros, split, 8 + tok_rows, TILE), wide(micros, split, 8, TILE),
        low(2 * own, features), low(2 * own, FF),
        low(2, 2 * own, features), low(2, own, 3 * half), low(2, 2 * own, 3 * half), low(blocks, features, half), low(4, blocks, rows, half), low(4, blocks, rows, half),
        pieces(), pieces(), pieces(), pieces(), wide(48, features), wide(40, features),
        pltpu.SemaphoreType.DMA((SENDS,)), pltpu.SemaphoreType.DMA((RECEIVES,)), pltpu.SemaphoreType.DMA((5,)),
    ]
    token_shape = (micros, tok_rows, features)
    dims = (units, features, FF, heads, micros, sizes)
    mixed, grad, red, small = pl.pallas_call(
        lambda *refs: main_kernel(dims, refs),
        out_shape=(
            jax.ShapeDtypeStruct(token_shape, WIDE),
            jax.ShapeDtypeStruct(token_shape, WIDE),
            jax.ShapeDtypeStruct((blocks, rows, features), LOW),
            jax.ShapeDtypeStruct((8, features), WIDE),
        ),
        in_specs=[smem, smem, smem, vmem, vmem, hbm, hbm, hbm],
        out_specs=(hbm, hbm, vmem, vmem),
        scratch_shapes=scratch,
        compiler_params=pltpu.CompilerParams(
            collective_id=0, has_side_effects=True, vmem_limit_bytes=60 * 2**20
        ),
        name="block",
    )(
        owners, doc_lengths[:, 0], slopes, ln_gain, ln_bias, tokens[:, 0], cotangent[:, 0], master[0]
    )
    steps = 4
    slot = pl.BlockSpec((slots // steps, rows, features), lambda j: (j, 0, 0))
    flat = (micros * tok_rows, features)
    some = pl.BlockSpec((flat[0] // steps, features), lambda j: (j, 0))
    moment_shape = jax.ShapeDtypeStruct((slots, rows, features), WIDE)
    norm_shape = jax.ShapeDtypeStruct((4, features), WIDE)
    slope_shape = jax.ShapeDtypeStruct((1, heads), WIDE)
    out = pl.pallas_call(
        lambda *refs: adam_kernel(sizes, refs),
        grid=(steps,),
        out_shape=(
            moment_shape, moment_shape, moment_shape, jax.ShapeDtypeStruct((slots, rows, features), LOW),
            norm_shape, norm_shape, norm_shape, slope_shape, slope_shape, slope_shape,
            jax.ShapeDtypeStruct(flat, WIDE), jax.ShapeDtypeStruct(flat, WIDE),
        ),
        in_specs=[smem] + [vmem] * 9 + [slot] * 3 + [some] * 2,
        out_specs=(slot, slot, slot, slot, vmem, vmem, vmem, vmem, vmem, vmem, some, some),
        compiler_params=pltpu.CompilerParams(dimension_semantics=("arbitrary",)),
        name="adam",
    )(
        owners, red, small, ln_gain, ln_bias, norm_m, norm_v, slopes[None], slope_m[None],
        slope_v[None], master[0], first_moment[0], second_moment[0],
        mixed.reshape(flat), grad.reshape(flat),
    )
    new_w, new_m, new_v, new_low, norm, norm_m, norm_v, slope, slope_m, slope_v, mixed, grad = out
    return (
        mixed.reshape(tokens.shape), grad.reshape(tokens.shape), new_w[None], new_m[None], new_v[None], new_low[None], norm, norm_m, norm_v,
        slope[0], slope_m[0], slope_v[0],
    )


def fits(mesh, shapes):
    return mesh.shape["batch"] == 4 and mesh.shape["seq"] == 8 and shapes[0].shape[1] == 1


def solution(mesh):
    in_specs = (
        P("batch", None, "seq", None),
        P("batch", None, "seq", None),
        P("batch", None, None),
        P(),
        P("batch", None, "seq", None),
        P("batch", None, "seq", None),
        P("batch", None, "seq", None),
        P(),
        P(),
        P(),
        P(),
        P(),
        P(),
        P(),
    )
    out_specs = (
        P("batch", None, "seq", None),
        P("batch", None, "seq", None),
        P("batch", None, "seq", None),
        P("batch", None, "seq", None),
        P("batch", None, "seq", None),
        P("batch", None, "seq", None),
        P(),
        P(),
        P(),
        P(),
        P(),
        P(),
    )

    def whole(*args):
        part = fused_body if fits(mesh, args) else body
        return jax.shard_map(
            part, mesh=mesh, in_specs=in_specs, out_specs=out_specs, check_vma=False
        )(*args)

    return whole
```

```python
import math

import jax
import jax.numpy as jnp
from jax import lax
from jax.experimental import pallas as pl
from jax.experimental.pallas import tpu as pltpu
from jax.sharding import PartitionSpec as P

FF = 2048
STEP = 10


beta_one = 0.9
beta_two = 0.95
adam_eps = 1e-08
decay_rate = 0.1
rate_matrix = 0.02
rate_norm = 0.2
rate_slope = 0.01
ln_eps = 1e-05
masked_score = -1000000000.0
row_kinds = (True, False, True, False, True, False)


def broadcast(value, axis, source):
    kept = jnp.where(lax.axis_index(axis) == source, value, 0).astype(value.dtype)
    return lax.psum(kept, axis)


def running_total(lengths):
    count = lengths.shape[-1]
    ends = [lengths[..., 0]]
    for index in range(1, count):
        ends.append(ends[-1] + lengths[..., index])
    return jnp.stack(ends, -1)


def for_sending(value):

    def short(part):
        return part.astype(jnp.bfloat16) if part.dtype == jnp.float32 else part

    return jax.tree.map(short, value)


def passed_along(value, axis, by):
    peers = lax.axis_size(axis)
    pairs = [(i, i + by) for i in range(peers) if 0 <= i + by < peers]
    return lax.ppermute(value, axis, pairs)


def layer_norm(values, gain, shift):
    center = jnp.mean(values, -1, keepdims=True)
    centred = values - center
    spread = jnp.mean(centred * centred, -1, keepdims=True)
    return centred * lax.rsqrt(spread + ln_eps) * gain + shift


def gelu_tanh(values):
    return jax.nn.gelu(values, approximate=True)


def block_counts(features, hidden):
    return [3, 3, 1, hidden // features, hidden // features, 3]


def block_starts(owners, sizes):
    starts_list = []
    for matrix_id in range(len(sizes)):
        shared = jnp.zeros((), jnp.int32)
        for earlier_id in range(matrix_id):
            shared = shared + jnp.where(
                owners[earlier_id] == owners[matrix_id], sizes[earlier_id], 0
            ).astype(jnp.int32)
        starts_list.append(shared)
    return starts_list


def slot_table(owners, device, sizes, slot_count):
    starts_list = block_starts(owners, sizes)
    slot_ids = jnp.arange(slot_count, dtype=jnp.int32)
    numbers = jnp.arange(sum(sizes), dtype=jnp.int32)
    slot_map = jnp.zeros((slot_count, sum(sizes)), jnp.float32)
    block_base = 0
    for matrix_id in range(len(sizes)):
        inside = (
            (owners[matrix_id] == device)
            & (slot_ids >= starts_list[matrix_id])
            & (slot_ids < starts_list[matrix_id] + sizes[matrix_id])
        )
        target = block_base + slot_ids - starts_list[matrix_id]
        slot_map = slot_map + (inside[:, None] & (target[:, None] == numbers[None, :])).astype(
            jnp.float32
        )
        block_base += sizes[matrix_id]
    return slot_map


def to_matrix(blocks, by_rows):
    if by_rows:
        return blocks.reshape(-1, blocks.shape[2])
    return blocks.transpose(1, 0, 2).reshape(blocks.shape[1], -1)


def to_blocks(matrix, by_rows, features):
    if by_rows:
        return matrix.reshape(-1, features, features)
    return matrix.reshape(features, -1, features).transpose(1, 0, 2)


def all_blocks(matrices, features):
    return jnp.concatenate(
        [to_blocks(matrices[matrix_id], row_kinds[matrix_id], features) for matrix_id in range(6)],
        0,
    )


def adam_update(weight, gradient, first_moment, second, fix_first, fix_second, rate, decay):
    first_new = beta_one * first_moment + (1.0 - beta_one) * gradient
    second_new = beta_two * second + (1.0 - beta_two) * gradient * gradient
    direction = first_new / fix_first / (jnp.sqrt(second_new / fix_second) + adam_eps)
    return (weight - rate * (direction + decay * weight), first_new, second_new)


def scores_for(query_block, key_rows, start_row, segment, head_slope):
    block_rows = query_block.shape[0]
    row_total = key_rows.shape[0]
    row_ids = start_row + jnp.arange(block_rows, dtype=jnp.int32)
    col_ids = jnp.arange(row_total, dtype=jnp.int32)
    distance = (row_ids[:, None] - col_ids[None, :]).astype(jnp.float32)
    seg_rows = lax.dynamic_slice_in_dim(segment, start_row, block_rows)
    allowed = (seg_rows[:, None] == segment[None, :]) & (col_ids[None, :] <= row_ids[:, None])
    raw_score = (
        jnp.dot(query_block, key_rows.T, preferred_element_type=jnp.float32) * 0.125
        - head_slope * distance
    )
    return (jnp.where(allowed, raw_score, masked_score), distance)


def attend(queries, key_rows, values, segment, head_slope, block_rows):
    row_total, head_width = queries.shape

    def per_block(start_row):
        query_block = lax.dynamic_slice_in_dim(queries, start_row, block_rows)
        scores, distance = scores_for(query_block, key_rows, start_row, segment, head_slope)
        largest = jnp.max(scores, -1, keepdims=True)
        log_total = largest + jnp.log(jnp.sum(jnp.exp(scores - largest), -1, keepdims=True))
        probability = jnp.exp(scores - log_total).astype(jnp.bfloat16)
        return (jnp.dot(probability, values, preferred_element_type=jnp.float32), log_total[:, 0])

    row_starts = jnp.arange(row_total // block_rows, dtype=jnp.int32) * block_rows
    attended, log_totals = lax.map(per_block, row_starts)
    return (attended.reshape(row_total, head_width), log_totals.reshape(row_total))


def attend_back(queries, key_rows, values, segment, head_slope, log_totals, grad_out, block_rows):
    row_total, head_width = queries.shape

    def per_block(carried, start_row):
        grad_keys, grad_values, grad_slope = carried
        query_block = lax.dynamic_slice_in_dim(queries, start_row, block_rows)
        grad_block = lax.dynamic_slice_in_dim(grad_out, start_row, block_rows)
        total_block = lax.dynamic_slice_in_dim(log_totals, start_row, block_rows)
        scores, distance = scores_for(query_block, key_rows, start_row, segment, head_slope)
        probability = jnp.exp(scores - total_block[:, None])
        grad_prob = jnp.dot(grad_block, values.T, preferred_element_type=jnp.float32)
        grad_score = (
            probability * (grad_prob - jnp.sum(probability * grad_prob, -1, keepdims=True))
        ).astype(jnp.bfloat16)
        grad_query = jnp.dot(grad_score, key_rows, preferred_element_type=jnp.float32) * 0.125
        grad_keys = (
            grad_keys
            + jnp.dot(grad_score.T, query_block, preferred_element_type=jnp.float32) * 0.125
        )
        grad_values = grad_values + jnp.dot(
            probability.astype(jnp.bfloat16).T, grad_block, preferred_element_type=jnp.float32
        )
        grad_slope = grad_slope - jnp.sum(grad_score.astype(jnp.float32) * distance)
        return ((grad_keys, grad_values, grad_slope), grad_query)

    row_starts = jnp.arange(row_total // block_rows, dtype=jnp.int32) * block_rows
    initial = (
        jnp.zeros((row_total, head_width), jnp.float32),
        jnp.zeros((row_total, head_width), jnp.float32),
        jnp.zeros((), jnp.float32),
    )
    (grad_keys, grad_values, grad_slope), grad_queries = lax.scan(per_block, initial, row_starts)
    return (grad_queries.reshape(row_total, head_width), grad_keys, grad_values, grad_slope)


def body(
    tokens,
    cotangent,
    doc_lengths,
    owners,
    master,
    first_moment,
    second_moment,
    ln_gain,
    ln_bias,
    norm_m,
    norm_v,
    slopes,
    slope_m,
    slope_v,
):
    micro_count, lane_count, tok_rows, features = tokens.shape
    unit_rows = tok_rows // 3
    seq_devices = lax.axis_size("seq")
    head_count = slopes.shape[0]
    head_width = features // head_count
    lane_units = unit_rows * seq_devices
    block_rows = min(512, lane_units)
    unit_total = lane_count * unit_rows
    slot_count = master.shape[1]
    sizes = block_counts(features, FF)
    starts_list = block_starts(owners, sizes)
    batch_rank = lax.axis_index("batch")
    seq_rank = lax.axis_index("seq")
    lane_rank = seq_rank // head_count
    head_rank = seq_rank % head_count
    low_slots = master[0].astype(jnp.bfloat16)
    fetched = []
    for matrix_id in range(6):
        owned_rows = lax.dynamic_slice_in_dim(
            low_slots, starts_list[matrix_id], sizes[matrix_id], 0
        )
        fetched.append(broadcast(owned_rows, "batch", owners[matrix_id]))
    gathered = lax.all_gather(for_sending(tuple(fetched)), "seq", axis=1, tiled=True)
    pool_weight, qkv_weight, out_weight, in_weight, back_weight, up_weight = [
        to_matrix(gathered[matrix_id], row_kinds[matrix_id]) for matrix_id in range(6)
    ]
    doc_ends = running_total(doc_lengths)
    doc_starts = jnp.concatenate(
        [jnp.zeros((micro_count, lane_count, 1), jnp.int32), doc_ends[..., :-1]], -1
    )
    unit_ids = seq_rank * unit_rows + jnp.arange(unit_rows, dtype=jnp.int32)
    keep_mask = 1.0 - jnp.any(
        unit_ids[None, None, :, None] == doc_starts[:, :, None, :], -1
    ).astype(jnp.float32)
    triples = tokens.reshape(micro_count, lane_count, unit_rows, 3, features)
    tail_tokens = triples[:, :, -1, 1:3]
    arrived = passed_along(tail_tokens, "seq", 1)
    lane_pick = jnp.arange(lane_count, dtype=jnp.int32) == lane_rank
    head_pick = jnp.arange(head_count, dtype=jnp.int32) == head_rank
    head_slope = jnp.sum(jnp.where(head_pick, slopes, 0.0))
    positions = jnp.arange(lane_units, dtype=jnp.int32)
    gain_grad = jnp.zeros((2, features), jnp.float32)
    bias_grad = jnp.zeros((2, features), jnp.float32)
    slope_grad = jnp.zeros((), jnp.float32)
    summed = None
    mixed_parts = []
    grad_parts = []
    outgoing = []
    for micro in range(micro_count):
        triple_now = triples[micro]
        keep_now = keep_mask[micro]
        earlier = jnp.concatenate([arrived[micro][:, None], triple_now[:, :-1, 1:3]], 1) * keep_now[
            :, :, None, None
        ].astype(jnp.bfloat16)
        pool_input = jnp.concatenate([earlier, triple_now[:, :, 0:1]], 2).reshape(
            unit_total, 3 * features
        )
        pooled = jnp.dot(pool_input, pool_weight, preferred_element_type=jnp.float32)
        normed = layer_norm(pooled, ln_gain[0], ln_bias[0]).astype(jnp.bfloat16)
        projected = jnp.dot(normed, qkv_weight, preferred_element_type=jnp.float32).astype(
            jnp.bfloat16
        )
        outbound = (
            projected.reshape(lane_count, unit_rows, 3, head_count, head_width)
            .transpose(0, 3, 1, 2, 4)
            .reshape(lane_count * head_count, unit_rows * 3 * head_width)
        )
        received = lax.all_to_all(outbound, "seq", split_axis=0, concat_axis=1, tiled=True).reshape(
            lane_units, 3, head_width
        )
        queries = received[:, 0]
        key_rows = received[:, 1]
        values = received[:, 2]
        lengths = jnp.sum(jnp.where(lane_pick[:, None], doc_lengths[micro], 0), 0)
        lane_ends = running_total(lengths)
        segment = jnp.sum((positions[:, None] >= lane_ends[None, :-1]).astype(jnp.int32), 1)
        attended, log_totals = attend(queries, key_rows, values, segment, head_slope, block_rows)
        returned = lax.all_to_all(
            attended.astype(jnp.bfloat16).reshape(1, lane_units * head_width),
            "seq",
            split_axis=1,
            concat_axis=0,
            tiled=True,
        )
        merged = (
            returned.reshape(lane_count, head_count, unit_rows, head_width)
            .transpose(0, 2, 1, 3)
            .reshape(unit_total, features)
        )
        residual = pooled + jnp.dot(merged, out_weight, preferred_element_type=jnp.float32)
        normed_two = layer_norm(residual, ln_gain[1], ln_bias[1]).astype(jnp.bfloat16)
        hidden = jnp.dot(normed_two, in_weight, preferred_element_type=jnp.float32)
        activated = gelu_tanh(hidden).astype(jnp.bfloat16)
        shortened = residual + jnp.dot(activated, back_weight, preferred_element_type=jnp.float32)
        short_low = shortened.astype(jnp.bfloat16)
        upward = jnp.dot(short_low, up_weight, preferred_element_type=jnp.float32).reshape(
            lane_count, unit_rows * 3, features
        )
        mixed_parts.append(tokens[micro].astype(jnp.float32) + upward)
        grad_upward = cotangent[micro].reshape(unit_total, 3 * features)
        sum_up = jnp.dot(short_low.T, grad_upward, preferred_element_type=jnp.float32)
        grad_short = jnp.dot(grad_upward, up_weight.T, preferred_element_type=jnp.float32)
        grad_short_low = grad_short.astype(jnp.bfloat16)
        sum_back = jnp.dot(activated.T, grad_short_low, preferred_element_type=jnp.float32)
        grad_activated = jnp.dot(grad_short_low, back_weight.T, preferred_element_type=jnp.float32)
        grad_hidden = jax.vjp(gelu_tanh, hidden)[1](grad_activated)[0].astype(jnp.bfloat16)
        sum_in = jnp.dot(normed_two.T, grad_hidden, preferred_element_type=jnp.float32)
        grad_normed_two = jnp.dot(grad_hidden, in_weight.T, preferred_element_type=jnp.float32)
        norm_two_back = jax.vjp(layer_norm, residual, ln_gain[1], ln_bias[1])[1]
        grad_resid_norm, grad_gain_two, grad_bias_two = norm_two_back(grad_normed_two)
        grad_residual = grad_short + grad_resid_norm
        grad_resid_low = grad_residual.astype(jnp.bfloat16)
        sum_out = jnp.dot(merged.T, grad_resid_low, preferred_element_type=jnp.float32)
        grad_merged = jnp.dot(
            grad_resid_low, out_weight.T, preferred_element_type=jnp.float32
        ).astype(jnp.bfloat16)
        back_outbound = (
            grad_merged.reshape(lane_count, unit_rows, head_count, head_width)
            .transpose(0, 2, 1, 3)
            .reshape(lane_count * head_count, unit_rows * head_width)
        )
        grad_attended = lax.all_to_all(
            back_outbound, "seq", split_axis=0, concat_axis=1, tiled=True
        ).reshape(lane_units, head_width)
        grad_queries, grad_keys, grad_values, grad_slope = attend_back(
            queries, key_rows, values, segment, head_slope, log_totals, grad_attended, block_rows
        )
        grad_heads = (
            jnp.stack([grad_queries, grad_keys, grad_values], 1)
            .astype(jnp.bfloat16)
            .reshape(1, lane_units * 3 * head_width)
        )
        grad_arrived = lax.all_to_all(grad_heads, "seq", split_axis=1, concat_axis=0, tiled=True)
        grad_projected = (
            grad_arrived.reshape(lane_count, head_count, unit_rows, 3, head_width)
            .transpose(0, 2, 3, 1, 4)
            .reshape(unit_total, 3 * features)
        )
        sum_qkv = jnp.dot(normed.T, grad_projected, preferred_element_type=jnp.float32)
        grad_normed = jnp.dot(grad_projected, qkv_weight.T, preferred_element_type=jnp.float32)
        norm_one_back = jax.vjp(layer_norm, pooled, ln_gain[0], ln_bias[0])[1]
        grad_pool_norm, grad_gain_one, grad_bias_one = norm_one_back(grad_normed)
        grad_pooled_low = (grad_residual + grad_pool_norm).astype(jnp.bfloat16)
        sum_pool = jnp.dot(pool_input.T, grad_pooled_low, preferred_element_type=jnp.float32)
        grad_pieces = jnp.dot(
            grad_pooled_low, pool_weight.T, preferred_element_type=jnp.float32
        ).reshape(lane_count, unit_rows, 3, features)
        grad_earlier = grad_pieces[:, :, 0:2] * keep_now[:, :, None, None]
        outgoing.append(grad_earlier[:, 0])
        following = jnp.concatenate(
            [grad_earlier[:, 1:], jnp.zeros((lane_count, 1, 2, features), jnp.float32)], 1
        )
        token_grad = jnp.concatenate([grad_pieces[:, :, 2:3], following], 2).reshape(
            lane_count, unit_rows * 3, features
        )
        grad_parts.append(cotangent[micro].astype(jnp.float32) + token_grad)
        gain_grad = gain_grad + jnp.stack([grad_gain_one, grad_gain_two])
        bias_grad = bias_grad + jnp.stack([grad_bias_one, grad_bias_two])
        slope_grad = slope_grad + grad_slope
        micro_grads = [sum_pool, sum_qkv, sum_out, sum_in, sum_back, sum_up]
        summed = (
            micro_grads
            if summed is None
            else [left + right for left, right in zip(summed, micro_grads)]
        )
    reduced = lax.psum_scatter(all_blocks(summed, features), "seq", scatter_dimension=1, tiled=True)
    incoming = passed_along(jnp.stack(outgoing).astype(jnp.bfloat16), "seq", -1).astype(jnp.float32)
    grad_tokens = jnp.stack(grad_parts).reshape(micro_count, lane_count, unit_rows, 3, features)
    grad_tokens = grad_tokens.at[:, :, -1, 1:3].add(incoming).reshape(tokens.shape)
    reduced_all = lax.psum(reduced, "batch")
    norm_grad, slopes_grad = lax.psum(
        (jnp.concatenate([gain_grad, bias_grad], 0), jnp.where(head_pick, slope_grad, 0.0)),
        ("batch", "seq"),
    )
    slot_map = slot_table(owners, batch_rank, sizes, slot_count)
    is_owned = jnp.sum(slot_map, -1)[:, None, None] > 0.5
    slot_grads = jnp.einsum("jb,brc->jrc", slot_map, reduced_all, precision=lax.Precision.HIGHEST)
    step_float = jnp.float32(STEP)
    fix_first = 1.0 - jnp.power(jnp.float32(beta_one), step_float)
    fix_second = 1.0 - jnp.power(jnp.float32(beta_two), step_float)
    new_weight, new_first, new_second = adam_update(
        master[0],
        slot_grads,
        first_moment[0],
        second_moment[0],
        fix_first,
        fix_second,
        rate_matrix,
        decay_rate,
    )
    new_weight = jnp.where(is_owned, new_weight, master[0])
    new_first = jnp.where(is_owned, new_first, first_moment[0])
    new_second = jnp.where(is_owned, new_second, second_moment[0])
    norm_now = jnp.concatenate([ln_gain, ln_bias], 0)
    new_norm, new_norm_m, new_norm_v = adam_update(
        norm_now, norm_grad, norm_m, norm_v, fix_first, fix_second, rate_norm, 0.0
    )
    new_slopes, new_slope_m, new_slope_v = adam_update(
        slopes, slopes_grad, slope_m, slope_v, fix_first, fix_second, rate_slope, 0.0
    )
    return (
        jnp.stack(mixed_parts),
        grad_tokens,
        new_weight[None],
        new_first[None],
        new_second[None],
        new_weight[None].astype(jnp.bfloat16),
        new_norm,
        new_norm_m,
        new_norm_v,
        new_slopes,
        new_slope_m,
        new_slope_v,
    )


MESH = pl.DeviceIdType.MESH
LOW = jnp.bfloat16
WIDE = jnp.float32
TILE = 128


class Plan:
    def __init__(self):
        self.tasks = {}

    def add(self, name, run, deps=(), waits=(), sends=(), cost=0.1, rank=0):
        assert name not in self.tasks
        self.tasks[name] = (run, tuple(deps), tuple(waits), tuple(sends), cost, rank)

    def order(self):
        now, done, arrival, free, listed = 0.0, set(), {}, {}, []
        left = list(self.tasks)
        while left:
            best = None
            for place, name in enumerate(left):
                run, deps, waits, sends, cost, rank = self.tasks[name]
                if any(d not in done for d in deps) or any(w not in arrival for w in waits):
                    continue
                begin = max([now] + [arrival[w] for w in waits] + [free.get(m[1], 0.0) - SLACK for m in sends])
                key = (begin, rank, place)
                if best is None or key < best[0]:
                    best = (key, name)
            name = best[1]
            run, deps, waits, sends, cost, rank = self.tasks[name]
            now = best[0][0] + cost
            for message, link, size in sends:
                rate, delay = LINKS[link]
                lanes = ("f", "r", "l") if link == "f" else (link,)
                end = max([now] + [free.get(lane, 0.0) for lane in lanes]) + size / rate
                free.update({lane: end for lane in lanes})
                arrival[message] = end + delay
            done.add(name)
            left.remove(name)
            listed.append((name, now))
        return listed


SLACK = 1.5
SENDS, RECEIVES = 32, 168
GATHERS = (
    (0, 0, 1, 0.0),
    (0, 1, 1, 0.01),
    (0, 2, 1, 0.02),
    (1, 0, 1, 0.1),
    (1, 1, 1, 0.11),
    (1, 2, 1, 0.12),
    (3, 0, 2, 0.2),
    (3, 2, 2, 0.22),
    (2, 0, 1, 0.3),
    (5, 0, 3, 0.4),
)
QUARTERS = {5: 0, 1: 3, 0: 6}
GATHER_QUARTERS = ()
AFTER = {}
SCATTERS = (
    (5, 0, 3, 1.0),
    (3, 0, 2, 1.1),
    (3, 2, 2, 1.2),
    (2, 0, 1, 1.3),
    (0, 0, 3, 0.7),
    (1, 0, 3, 0.8),
)
LINKS = {
    "c": (400e3, 1.0),
    "x": (52e3, 2.3),
    "r": (52e3, 2.3),
    "l": (52e3, 2.3),
    "f": (46e3, 3.3),
}


def start_of(owners, matrix_id, sizes):
    shared = jnp.int32(0)
    for earlier_id in range(matrix_id):
        shared = shared + jnp.where(owners[earlier_id] == owners[matrix_id], sizes[earlier_id], 0)
    return shared


def over_last(fn, value):
    return fn(value, axis=-1, keepdims=True)


def contract(left, right, left_dim, right_dim):
    return lax.dot_general(
        left, right, (((left_dim,), (right_dim,)), ((), ())), preferred_element_type=WIDE
    )


def gelu_parts(value):
    scale = math.sqrt(2.0 / math.pi)
    inner = jnp.tanh(scale * (value + 0.044715 * (value * value * value)))
    return inner, scale * (1.0 + 3 * 0.044715 * value * value)


def main_kernel(dims, refs):
    units, features, hidden_width, heads, micros, sizes = dims
    owners, docs, slopes, gain, bias, tok_hbm, cot_hbm, master_hbm = refs[:8]
    mixed_hbm, grad_hbm, red, small = refs[8:12]
    (
        w, masters, mine, other, core_in, both, x_in, tok, cot, tail_in, wide_tok, wide_cot, x_pool, x_norm, x_att,
        x_two, x_act, x_short, d_up, d_low, d_inner, d_res, d_qkv, d_pool, pooled, hat_one, hat_two, root_one, root_two,
        resid, hidden, short_grad, res_grad, q_out, q_in, a_out, a_in, da_out, da_in, dq_out, dq_in, probs, mixed, grad,
        wide_up, wide_grad, edge_in, x_near, x_wide, t_left, t_out, t_in, g, right_in, left_in, fin_out, fin_in, co_out, co_in, sums, sums_in, sends, recvs, local,
    ) = refs[12:]
    half = features // 2
    width = features // heads
    rows_of = masters.shape[1]
    count = heads
    tokens = 3 * units
    own = micros * units
    pair_width = 2 * width
    b, s = lax.axis_index("batch"), lax.axis_index("seq")
    x, c = b // 2, b % 2
    z, y = s // 2, s % 2
    spot = y * (7 - 2 * z) + z

    def seq_of(position):
        far = position // 4
        return 2 * (position + far * (7 - 2 * position)) + far

    def at(offset):
        return lax.rem(spot + offset + 2 * count, count)

    def rows_at(offset, part=0, length=rows_of):
        return pl.ds(pl.multiple_of(seq_of(at(offset)) * rows_of + part, 16), length)

    my_half = pl.ds(pl.multiple_of(c * half, half), half)
    other_half = pl.ds(pl.multiple_of((1 - c) * half, half), half)
    core_peer = (x * 2 + 1 - c, s)
    x_peer = ((1 - x) * 2 + c, s)
    right_peer = (b, seq_of(at(1)))
    left_peer = (b, seq_of(at(-1)))
    plan = Plan()
    flying, started, boxes = {}, [], {}

    def launch(name, copies, starts, group):
        if len(started) >= SENDS:
            started[len(started) - SENDS].wait_send()
        started.append(copies[0])
        flying[name] = copies[0]
        for start in starts:
            start()

    def describe(source, target, device, group):
        box = boxes.setdefault(group, len(boxes))
        return pltpu.make_async_remote_copy(
            src_ref=source,
            dst_ref=target,
            send_sem=sends.at[len(started) % SENDS],
            recv_sem=recvs.at[box],
            device_id=device,
            device_id_type=MESH,
        )

    def send(name, source, target, device, group=None):
        copy = describe(source, target, device, group or name)
        launch(name, [copy], [copy.start], group or name)

    def gather_up(group, whole):
        describe(whole, whole, core_peer, group).wait_recv()

    loads = [
        pltpu.make_async_copy(master_hbm, masters, local.at[0]),
        pltpu.make_async_copy(tok_hbm, tok, local.at[1]),
        pltpu.make_async_copy(cot_hbm, cot, local.at[2]),
    ]
    for copy in loads:
        copy.start()
    barrier = pltpu.get_barrier_semaphore()
    for step in range(1, count):
        pl.semaphore_signal(
            barrier, inc=1, device_id=(b, lax.rem(s + step, count)), device_id_type=MESH
        )
    for device in (core_peer, x_peer):
        pl.semaphore_signal(barrier, inc=1, device_id=device, device_id_type=MESH)
    pl.semaphore_wait(barrier, count + 1)

    spans, first = [], 0
    for size in sizes:
        spans.append((first, first + size))
        first += size
    in_base, back_base, up_base = spans[3][0], spans[4][0], spans[5][0]
    hidden_blocks = sizes[3]
    ours = in_base + x * hidden_blocks
    theirs = in_base + (1 - x) * hidden_blocks
    plan.add("ms", loads[0].wait, cost=0.5)

    def contribute(k):
        def run():
            lo, hi = spans[k]
            mask = (owners[k] == b).astype(WIDE)
            begin = start_of(owners, k, sizes)
            for block in range(lo, hi):
                slot = jnp.minimum(begin + (block - lo), masters.shape[0] - 1)
                mine[block] = (masters[slot, :, my_half] * mask).astype(LOW)
                other[block] = (masters[slot, :, other_half] * mask).astype(LOW)
            send(("g0", k), other.at[lo:hi], core_in.at[lo:hi], core_peer)

        return run

    def join_cores(k):
        def run():
            lo, hi = spans[k]
            flying[("g0", k)].wait_recv()
            both[lo:hi] = mine[lo:hi] + core_in[lo:hi]

        return run

    have = {k: [] for k in range(6)}
    gathers = []
    for k, offset, size, rank in GATHERS:
        name = ("w", k, offset)
        if k == 3:
            gathers.append((rank, name, (3, 4), ours + offset, theirs + offset, size))
            have[3] += [("h", name), ("hy", name)]
        else:
            begin = spans[k][0] + offset
            gathers.append((rank, name, (k,), begin, begin if k in GATHER_QUARTERS else None, size))
            have[k] += [("h", name)] + ([("hy", name)] if k in GATHER_QUARTERS else [])
    piece_bytes = rows_of * half * 2

    quarter = half // 2
    plane_span = pl.ds(pl.multiple_of(x * quarter, quarter), quarter)
    plane_away = pl.ds(pl.multiple_of((1 - x) * quarter, quarter), quarter)

    def gather_chunk(rank, name, parents, here, there, size):
        split, quarters = there is not None, there is here
        load = size * piece_bytes // (2 if quarters else 1)
        blocks = pl.ds(here, size)
        away = pl.ds(there, size) if split else blocks
        span, away_span = (plane_span, plane_away) if quarters else (slice(None), slice(None))

        def piece(offset, part=0, length=rows_of):
            return w.at[blocks, c, rows_at(offset, part, length), span]

        def join_here():
            send(("g1", name), both.at[away, :, away_span], x_in.at[away, :, away_span], x_peer)

        def join_x():
            flying[("g1", name)].wait_recv()
            w[blocks, c, rows_at(0), span] = both[blocks, :, span] + x_in[blocks, :, span]
            send(("R", 1, name), piece(0), piece(0), right_peer, (1, name))
            send(("L", 1, name), piece(0), piece(0), left_peer, (1, name))

        def onward(step):
            def run():
                gather_up((step - 1, name), w.at[blocks, c, 0 : rows_of * (2 if step < 5 else 1), span])
                if step == 5:
                    return
                for side, offset, peer in (("R", 1 - step, right_peer), ("L", step - 1, left_peer)):
                    part = piece(offset)
                    if step == 4:
                        part = piece(offset, 0 if side == "R" else rows_of // 2, rows_of // 2)
                    send((side, step, name), part, part, peer, (step, name))

            return run

        def across(step):
            def run():
                for side, offset in (("R", -step), ("L", step)):
                    part = piece(offset)
                    if step == 4:
                        part = piece(offset, 0 if side == "R" else rows_of // 2, rows_of // 2)
                    if step > 0 or side == "R":
                        send(("X", side, step, name), part, part, x_peer, ("X", name))

            return run

        def distribute(which, held, lanes):
            def run():
                send((which, name), w.at[held, c, :, lanes], w.at[held, c, :, lanes], core_peer)

            return run

        plan.add(("cx", name), join_here, [("cs", k) for k in parents], (), [(("g1", name), "x", load)], 0.05, rank)
        plan.add(
            ("x", name), join_x, [("cx", name)], [("g1", name)],
            [(("R", 1, name), "r", load), (("L", 1, name), "l", load)], 0.05, rank,
        )
        crossing = []

        def cross(step, after):
            messages = [("X", side, step, name) for side in ("RL" if step else "R")]
            size_of = load if step < 4 else load // 2
            plan.add(("X", step, name), across(step), [after], (), [(m, "x", size_of) for m in messages], 0.05, rank + 0.05)
            crossing.extend(messages)

        if split:
            cross(0, ("x", name))
        for step in (2, 3, 4, 5):
            size_of = load if step < 4 else load // 2
            out = [((side, step, name), link, size_of) for side, link in (("R", "r"), ("L", "l"))] if step < 5 else []
            before = ("x", name) if step == 2 else (step - 1, "f", name)
            waits = [(side, step - 1, name) for side in "RL"]
            plan.add((step, "f", name), onward(step), [before], waits, out, 0.05, rank)
            if split:
                cross(step - 1, (step, "f", name))
        plan.add(("di", name), distribute("D", blocks, span), [(5, "f", name)], (), [(("D", name), "c", 8 * load)], 0.05, rank)
        plan.add(("h", name), arrive(("D", name)), [("di", name)], [("D", name)], (), 0.02, rank)
        if split:
            whole = w.at[away, c, :, away_span]
            last = [("X", step, name) for step in range(5)]
            plan.add(("xw", name), lambda: gather_up(("X", name), whole), last, crossing, (), 0.05, rank)
            plan.add(("dy", name), distribute("E", away, away_span), [("xw", name)], (), [(("E", name), "c", 8 * load)], 0.05, rank)
            plan.add(("hy", name), arrive(("E", name)), [("dy", name)], [("E", name)], (), 0.02, rank)

    def arrive(*names):
        def run():
            for name in names:
                flying[name].wait_recv()

        return run

    for k in (0, 1, 3, 4, 2, 5):
        lo, hi = spans[k]
        load = (hi - lo) * piece_bytes
        plan.add(("co", k), contribute(k), ["ms"], (), [(("g0", k), "c", load)], 0.04 * (hi - lo), 0.1)
        plan.add(("cs", k), join_cores(k), [("co", k)], [("g0", k)], (), 0.02 * (hi - lo), 0.1)
    for chunk in gathers:
        gather_chunk(*chunk)

    def exchange(name, buffer):
        send(name, buffer.at[0:own], buffer.at[own : 2 * own], core_peer)

    def shared(name, columns):
        return (name, "c", own * columns * 2)

    lead = 16
    tiles = range(features // TILE)

    def columns_at(tile, base=0):
        return slice(base + tile * TILE, base + (tile + 1) * TILE)

    def ends_of(micro):
        ends = []
        total = jnp.int32(0)
        for index in range(docs.shape[1] - 1):
            total = total + docs[micro, index]
            ends.append(total)
        return ends

    def kept(micro):
        ids = s * units + lax.broadcasted_iota(jnp.int32, (units, 1), 0)
        starts = (ids == 0).astype(jnp.int32)
        for end in ends_of(micro):
            starts = starts | (ids == end).astype(jnp.int32)
        return starts == 0

    def load_tokens():
        loads[1].wait()
        send("tl", tok.at[:, tokens - lead :], tail_in, (b, lax.rem(s + 1, count)))
        for micro in range(micros):
            for tile in tiles:
                wide_tok[micro, tile, lead:] = tok[micro, :, columns_at(tile)].astype(WIDE)

    def load_cotangent():
        loads[2].wait()
        for micro in range(micros):
            for tile in tiles:
                wide_cot[micro, tile] = cot[micro, :, columns_at(tile)].astype(WIDE)
                for r in range(3):
                    d_up[micro * units : (micro + 1) * units, columns_at(tile, r * features)] = wide_cot[
                        micro, tile, pl.ds(r, units, stride=3), :
                    ].astype(LOW)
        exchange("eu", d_up)

    def make_pieces():
        flying["tl"].wait_recv()
        for micro in range(micros):
            keep = kept(micro)
            for tile in tiles:
                wide_tok[micro, tile, :lead] = tail_in[micro, :, columns_at(tile)].astype(WIDE)
                for r in range(3):
                    part = wide_tok[micro, tile, pl.ds(lead - 2 + r, units, stride=3), :]
                    if r < 2:
                        part = jnp.where(keep, part, 0.0)
                    x_pool[micro * units : (micro + 1) * units, columns_at(tile, r * features)] = part.astype(LOW)
        exchange("ep", x_pool)

    plan.add("tok", load_tokens, sends=[("tl", "f", 2 * lead * features * 2)], cost=0.3, rank=1)
    plan.add(
        "pc", make_pieces, ["tok"], ["tl"], [shared("ep", 3 * features)], 0.5, rank=1
    )
    plan.add("cot", load_cotangent, (), (), [shared("eu", 3 * features)], 0.5, rank=2)

    def normal(value, which, hat, root):
        centred = value - over_last(jnp.mean, value)
        scale = lax.rsqrt(over_last(jnp.mean, centred * centred) + ln_eps)
        unit = centred * scale
        hat[...] = unit
        root[...] = scale
        return (unit * gain[which : which + 1, :] + bias[which : which + 1, :]).astype(LOW)

    def both_halves(make):
        return jnp.concatenate([make(0), make(1)], axis=1)

    def pool():
        def side(h):
            total = None
            for r in range(3):
                term = contract(x_pool[0:own, r * features : (r + 1) * features], w[r, h], 1, 0)
                total = term if total is None else total + term
            return total

        value = both_halves(side)
        pooled[...] = value
        x_norm[0:own] = normal(value, 0, hat_one, root_one)
        exchange("en", x_norm)

    lane = lambda: lax.broadcasted_iota(jnp.int32, (1, pair_width), 1)

    def swap(value):
        return pltpu.roll(value, width, axis=1)

    def to_heads(tile, target, pair, row):
        low_lanes = lane() < width
        first, second = tile[:units], tile[units:]
        target[2 * pair, row : row + units] = jnp.where(low_lanes, first, swap(second)).astype(LOW)
        target[2 * pair + 1, row : row + units] = jnp.where(low_lanes, swap(first), second).astype(LOW)

    def from_heads(source, pair, row):
        low_lanes = lane() < width
        even = source[2 * pair, row : row + units].astype(WIDE)
        odd = source[2 * pair + 1, row : row + units].astype(WIDE)
        return jnp.where(low_lanes, even, swap(odd)).astype(LOW), jnp.where(low_lanes, swap(even), odd).astype(LOW)

    def spread(name, source, target):
        for step in range(1, count):
            there = lax.rem(s + step, count)
            send((name, step), source.at[there], target.at[s], (b, there), name)
        target[s] = source[s]

    def spread_names(name):
        return [(name, step) for step in range(1, count)]

    def spread_sends(name, rows):
        return [((name, step), "f", rows * pair_width * 2) for step in range(1, count)]

    def project():
        for part in range(3):
            for h in range(2):
                value = contract(x_norm[0:own], w[3 + part, h], 1, 0)
                for tile in range(half // pair_width):
                    to_heads(
                        value[:, tile * pair_width : (tile + 1) * pair_width],
                        q_out,
                        h * (half // pair_width) + tile,
                        part * units,
                    )
        spread("q", q_out, q_in)

    lane_units = units * count

    def heads_of(source, part):
        return source[:, part * units : (part + 1) * units, :].reshape(lane_units, pair_width)

    def lanes_of(micro):
        return (lane() // width == micro).astype(WIDE).astype(LOW)

    def distances():
        row_ids = lax.broadcasted_iota(jnp.int32, (lane_units, lane_units), 0)
        col_ids = lax.broadcasted_iota(jnp.int32, (lane_units, lane_units), 1)
        return row_ids - col_ids

    def attend_now():
        gather_up("q", q_in.at[0 : count - 1])
        queries, keys, values = (heads_of(q_in, part) for part in range(3))
        slope = slopes[s]
        total = None
        for micro in range(micros):
            gap = distances()
            row_seg = jnp.zeros((lane_units, 1), jnp.int32)
            col_seg = jnp.zeros((1, lane_units), jnp.int32)
            for end in ends_of(micro):
                row_seg += (lax.broadcasted_iota(jnp.int32, (lane_units, 1), 0) >= end).astype(jnp.int32)
                col_seg += (lax.broadcasted_iota(jnp.int32, (1, lane_units), 1) >= end).astype(jnp.int32)
            allowed = (row_seg == col_seg) & (gap >= 0)
            mask = lanes_of(micro)
            raw = contract(queries * mask, keys, 1, 1) * 0.125 - slope * gap.astype(WIDE)
            scores = jnp.where(allowed, raw, masked_score)
            raised = jnp.exp(scores - over_last(jnp.max, scores))
            probability = raised / over_last(jnp.sum, raised)
            probs[micro] = probability
            term = contract(probability.astype(LOW), values * mask, 1, 0)
            total = term if total is None else total + term
        a_out[...] = total.astype(LOW).reshape(count, units, pair_width)
        spread("a", a_out, a_in)

    def merge():
        gather_up("a", a_in.at[0 : count - 1])
        for pair in range(heads // 2):
            columns = slice(pair * pair_width, (pair + 1) * pair_width)
            first, second = from_heads(a_in, pair, 0)
            x_att[0:units, columns] = first
            x_att[units:own, columns] = second
        exchange("ea", x_att)

    def project_out():
        value = pooled[...] + both_halves(lambda h: contract(x_att[0:own], w[6, h], 1, 0))
        resid[...] = value
        x_two[0:own] = normal(value, 1, hat_two, root_two)
        exchange("et", x_two)


    def widen(j):
        def run():
            for h in range(2):
                columns = slice(j * features + h * half, j * features + (h + 1) * half)
                value = contract(x_two[0:own], w[in_base + j, h], 1, 0)
                hidden[:, columns] = value
                inner, _ = gelu_parts(value)
                x_act[0:own, columns] = (0.5 * value * (1.0 + inner)).astype(LOW)
            if j == hidden_blocks - 1:
                exchange("ec", x_act)

        return run

    def narrow():
        def side(h):
            total = resid[:, h * half : (h + 1) * half]
            for j in range(hidden_blocks):
                total = total + contract(
                    x_act[0:own, j * features : (j + 1) * features], w[back_base + j, h], 1, 0
                )
            return total

        x_short[0:own] = both_halves(side).astype(LOW)
        exchange("es", x_short)

    outs = [
        pltpu.make_async_copy(mixed, mixed_hbm, local.at[3]),
        pltpu.make_async_copy(grad, grad_hbm, local.at[4]),
    ]

    def lift(r):
        def run():
            for h in range(2):
                value = contract(x_short[0:own], w[up_base + r, h], 1, 0)
                for micro in range(micros):
                    for tile in range(half // TILE):
                        wide_up[micro, h * (half // TILE) + tile, pl.ds(r, units, stride=3), :] = value[
                            micro * units : (micro + 1) * units, columns_at(tile)
                        ]
            if r == 2:
                for micro in range(micros):
                    for tile in tiles:
                        columns = columns_at(tile)
                        mixed[micro, :, columns] = tok[micro, :, columns].astype(WIDE) + wide_up[micro, tile]
                outs[0].start()

        return run

    plan.add("po", pool, ["pc", *have[0]], (), [shared("en", features)], 0.6, rank=3)
    plan.add("pr", project, ["po", *have[1]], (), spread_sends("q", 3 * units), 0.6, rank=3)
    plan.add("at", attend_now, ["pr"], spread_names("q"), spread_sends("a", units), 1.1, rank=3)
    plan.add("me", merge, ["at"], spread_names("a"), [shared("ea", features)], 0.15, rank=3)
    plan.add("ou", project_out, ["me", *have[2]], (), [shared("et", features)], 0.45, rank=3)
    for j in range(hidden_blocks):
        last = j == hidden_blocks - 1
        plan.add(
            ("wi", j), widen(j), ["ou", *have[3]] + ([("wi", i) for i in range(j)] if last else []), (),
            [shared("ec", hidden_width)] if last else (), 0.3, rank=3,
        )
    plan.add(
        "na", narrow, [("wi", j) for j in range(hidden_blocks)] + [*have[3]], (), [shared("es", features)], 0.5,
        rank=3,
    )
    for r in range(3):
        plan.add(
            ("li", r), lift(r), ["na", *have[5], "tok"] + ([("li", i) for i in range(r)]), (), (), 0.3, rank=8
        )

    def back_short():
        total = None
        for r in range(3):
            for h in range(2):
                begin = r * features + h * half
                term = contract(d_up[0:own, begin : begin + half], w[up_base + r, h], 1, 1)
                total = term if total is None else total + term
        short_grad[...] = total
        d_low[0:own] = total.astype(LOW)
        exchange("el", d_low)

    def back_widen(j):
        def run():
            total = contract(d_low[0:own, 0:half], w[back_base + j, 0], 1, 1)
            total = total + contract(d_low[0:own, half:features], w[back_base + j, 1], 1, 1)
            columns = slice(j * features, (j + 1) * features)
            value = hidden[:, columns]
            inner, slope = gelu_parts(value)
            factor = 0.5 * (1.0 + inner) + 0.5 * value * (1.0 - inner * inner) * slope
            d_inner[0:own, columns] = (total * factor).astype(LOW)
            if j == hidden_blocks - 1:
                exchange("ei", d_inner)

        return run

    def back_normal(value, which, hat, root):
        unit = hat[...]
        sums[which : which + 1, :] = jnp.sum(value * unit, axis=0, keepdims=True)
        sums[2 + which : 3 + which, :] = jnp.sum(value, axis=0, keepdims=True)
        scaled = value * gain[which : which + 1, :]
        return root[...] * (
            scaled - over_last(jnp.mean, scaled) - unit * over_last(jnp.mean, scaled * unit)
        )

    def back_two():
        total = None
        for j in range(hidden_blocks):
            for h in range(2):
                begin = j * features + h * half
                term = contract(d_inner[0:own, begin : begin + half], w[in_base + j, h], 1, 1)
                total = term if total is None else total + term
        value = short_grad[...] + back_normal(total, 1, hat_two, root_two)
        res_grad[...] = value
        d_res[0:own] = value.astype(LOW)
        exchange("er", d_res)

    def back_out():
        value = contract(d_res[0:own, 0:half], w[6, 0], 1, 1)
        value = value + contract(d_res[0:own, half:features], w[6, 1], 1, 1)
        for pair in range(heads // 2):
            to_heads(value[:, pair * pair_width : (pair + 1) * pair_width], da_out, pair, 0)
        spread("da", da_out, da_in)

    def back_attend():
        gather_up("da", da_in.at[0 : count - 1])
        queries, keys, values = (heads_of(q_in, part) for part in range(3))
        grads = da_in[...].reshape(lane_units, pair_width)
        totals = [None, None, None]
        slope_total = jnp.zeros((1, 1), WIDE)
        for micro in range(micros):
            mask = lanes_of(micro)
            own_grads = grads * mask
            probability = probs[micro]
            grad_prob = contract(own_grads, values, 1, 1)
            scaled = probability * grad_prob
            score = scaled - probability * over_last(jnp.sum, scaled)
            low_score = score.astype(LOW)
            gap = distances().astype(WIDE)
            slope_total = slope_total - jnp.sum(
                jnp.sum(low_score.astype(WIDE) * gap, axis=0, keepdims=True), axis=1, keepdims=True
            )
            terms = (
                contract(low_score, keys * mask, 1, 0) * 0.125,
                contract(low_score, queries * mask, 0, 0) * 0.125,
                contract(probability.astype(LOW), own_grads, 0, 0),
            )
            totals = [term if total is None else total + term for total, term in zip(totals, terms)]
        for part in range(3):
            dq_out[:, part * units : (part + 1) * units, :] = (
                totals[part].astype(LOW).reshape(count, units, pair_width)
            )
        spread("dq", dq_out, dq_in)
        places = lax.broadcasted_iota(jnp.int32, (1, features), 1)
        sums[4:5, :] = jnp.where(places == s, slope_total, 0.0)
        sums[5:8, :] = jnp.zeros((3, features), WIDE)

    def back_project():
        gather_up("dq", dq_in.at[0 : count - 1])
        for part in range(3):
            for pair in range(heads // 2):
                begin = part * features + pair * pair_width
                first, second = from_heads(dq_in, pair, part * units)
                d_qkv[0:units, begin : begin + pair_width] = first
                d_qkv[units:own, begin : begin + pair_width] = second
        exchange("eq", d_qkv)

    def back_one():
        total = None
        for part in range(3):
            for h in range(2):
                begin = part * features + h * half
                term = contract(d_qkv[0:own, begin : begin + half], w[3 + part, h], 1, 1)
                total = term if total is None else total + term
        value = res_grad[...] + back_normal(total, 0, hat_one, root_one)
        d_pool[0:own] = value.astype(LOW)
        exchange("ed1", d_pool)

    def back_pieces():
        for r in range(3):
            value = contract(d_pool[0:own, 0:half], w[r, 0], 1, 1)
            value = value + contract(d_pool[0:own, half:features], w[r, 1], 1, 1)
            for micro in range(micros):
                part = value[micro * units : (micro + 1) * units]
                if r < 2:
                    part = jnp.where(kept(micro), part, 0.0)
                for tile in tiles:
                    wide_grad[micro, tile, pl.ds(6 + r, units, stride=3), :] = part[:, columns_at(tile)]
        send("ed", wide_grad.at[:, :, 0:8], edge_in, (b, lax.rem(s + count - 1, count)))

    def finish_grad():
        flying["ed"].wait_recv()
        inside = (s < count - 1).astype(WIDE)
        for micro in range(micros):
            for tile in tiles:
                columns = columns_at(tile)
                wide_grad[micro, tile, 6 + tokens : 8 + tokens, :] = edge_in[micro, tile, 6:8, :] * inside
                grad[micro, :, columns] = cot[micro, :, columns].astype(WIDE) + wide_grad[micro, tile, 8 : 8 + tokens]
        outs[1].start()

    plan.add("bs", back_short, ["cot", *have[5]], (), [shared("el", features)], 0.65, rank=4)
    for j in range(hidden_blocks):
        last = j == hidden_blocks - 1
        plan.add(
            ("bw", j), back_widen(j),
            ["bs", *have[3], ("wi", j)] + ([("bw", i) for i in range(j)] if last else []), (),
            [shared("ei", hidden_width)] if last else (), 0.35, rank=4,
        )
    plan.add(
        "b2", back_two, [("bw", j) for j in range(hidden_blocks)] + [*have[3]], (),
        [shared("er", features)], 0.9, rank=4,
    )
    plan.add("bo", back_out, ["b2", *have[2]], (), spread_sends("da", units), 0.45, rank=4)
    plan.add("ba", back_attend, ["bo", "at"], spread_names("da"), spread_sends("dq", 3 * units), 1.4, rank=4)
    plan.add("bp", back_project, ["ba"], spread_names("dq"), [shared("eq", 3 * features)], 0.2, rank=4)
    plan.add("b1", back_one, ["bp"], (), [shared("ed1", features)], 0.75, rank=4)
    plan.add("bx", back_pieces, ["b1"], (), [("ed", "f", 2 * 8 * features * 4)], 0.65, rank=9)
    plan.add("fg", finish_grad, ["bx", "cot"], ["ed"], (), 0.3, rank=9)

    def add_pair(step, device):
        def run():
            if step > 0:
                flying[("s", step - 1)].wait_recv()
                sums[8 * step : 8 * step + 8] = sums[8 * step - 8 : 8 * step] + sums_in[8 * step - 8 : 8 * step]
            if device is not None:
                send(("s", step), sums.at[8 * step : 8 * step + 8], sums_in.at[8 * step : 8 * step + 8], device)
            else:
                small[...] = sums[8 * step : 8 * step + 8]

        return run

    partners = [
        core_peer,
        x_peer,
        (b, 2 * z + 1 - y),
        (b, 2 * (z + 1 - 2 * (z % 2)) + y),
        (b, 2 * lax.rem(z + 2, 4) + y),
        None,
    ]
    for step, device in enumerate(partners):
        plan.add(
            ("sum", step), add_pair(step, device), ["b1", "ba"] if step == 0 else [("sum", step - 1)],
            [("s", step - 1)] if step else (), [(("s", step), "f", 8 * features * 4)] if device is not None else (), 0.1,
            rank=0,
        )

    for name, columns in (
        ("ep", "pc"), ("en", "po"), ("ea", "me"), ("et", "ou"), ("ec", ("wi", hidden_blocks - 1)),
        ("es", "na"), ("eu", "cot"), ("el", "bs"), ("ei", ("bw", hidden_blocks - 1)),
        ("er", "b2"), ("eq", "bp"), ("ed1", "b1"),
    ):
        plan.add(("got", name), arrive(name), [columns], [name], cost=0.02)

    def columns_of(block):
        return pl.ds(pl.multiple_of(block * features + c * half, half), half)

    def outer(block, left, left_block, right, right_block):
        def run():
            rows = left[:, left_block * features : (left_block + 1) * features]
            g[block] = contract(rows, right[:, columns_of(right_block)], 0, 0).astype(LOW)

        return run

    def send_either(name, first_source, second_source, target):
        copies = [describe(source, target, x_peer, name) for source in (first_source, second_source)]
        launch(name, copies, [lambda plane=plane: pl.when(x == plane)(copies[plane].start) for plane in range(2)], name)

    def near_away():
        send_either("sn", d_low.at[0:own], x_two.at[0:own], x_near.at[0:own])

    def near_core():
        arrive("sn")()
        exchange("cn", x_near)

    def wide_away(j):
        columns = slice(j * features, (j + 1) * features)

        def run():
            source = (x_act.at[0:own, columns], d_inner.at[0:own, columns])
            send_either(("sw", j), *source, x_wide.at[0:own, columns])

        return run

    def wide_core(j):
        columns = slice(j * features, (j + 1) * features)

        def run():
            arrive(("sw", j))()
            send(("cw", j), x_wide.at[0:own, columns], x_wide.at[own : 2 * own, columns], core_peer)

        return run

    def outer_split(j):
        columns = slice(j * features, (j + 1) * features)

        def run():
            @pl.when(x == 0)
            def _():
                total = contract(x_two[...], d_inner[:, columns_of(j)], 0, 0)
                g[in_base + j] = (total + contract(x_near[...], x_wide[:, columns_of(j)], 0, 0)).astype(LOW)

            @pl.when(x == 1)
            def _():
                total = contract(x_act[:, columns], d_low[:, my_half], 0, 0)
                g[back_base + j] = (total + contract(x_wide[:, columns], x_near[:, my_half], 0, 0)).astype(LOW)

        return run

    lump = own * features * 2
    plan.add("sn", near_away, ["bs", "ou"], (), [("sn", "x", lump)], 0.05, 2)
    plan.add("nc", near_core, ["sn"], ["sn"], [("cn", "c", lump)], 0.05, 2)
    plan.add(("got", "cn"), arrive("cn"), ["nc"], ["cn"], (), 0.02, 2)
    for j in range(hidden_blocks):
        plan.add(("sw", j), wide_away(j), [("wi", j), ("bw", j)], (), [(("sw", j), "x", lump)], 0.05, 2)
        plan.add(("wc", j), wide_core(j), [("sw", j)], [("sw", j)], [(("cw", j), "c", lump)], 0.05, 2)
        plan.add(("got", "cw", j), arrive(("cw", j)), [("wc", j)], [("cw", j)], (), 0.02, 2)
        deps = [("got", e) for e in ("et", "ec", "el", "ei", "cn")] + [("got", "cw", j)]
        plan.add(("gr", j, "s"), outer_split(j), deps, cost=0.6, rank=4.5)
    quartered = {
        0: (x_pool, 3, d_pool, 1, "pc", "b1", "ep", "ed1"),
        1: (x_norm, 1, d_qkv, 3, "po", "bp", "en", "eq"),
        2: (x_att, 1, d_res, 1, "me", "b2", "ea", "er"),
        5: (x_short, 1, d_up, 3, "na", "cot", "es", "eu"),
    }
    quartered = {k: quartered[k] for k in QUARTERS}

    def left_away(k, j):
        columns = slice(j * features, (j + 1) * features)

        def run():
            send(("tx", k, j), quartered[k][0].at[0:own, columns], t_left.at[QUARTERS[k] + j, 0:own], x_peer)

        return run

    def left_core(k, j):
        place = QUARTERS[k] + j

        def run():
            arrive(("tx", k, j))()
            send(("tc", k, j), t_left.at[place, 0:own], t_left.at[place, own : 2 * own], core_peer)

        return run

    def right_away(k, r):
        place = QUARTERS[k] + r

        def run():
            for core in range(2):
                begin = r * features + core * half + (1 - x) * quarter
                t_out[place, :, core * quarter : (core + 1) * quarter] = quartered[k][2][
                    0:own, pl.ds(pl.multiple_of(begin, quarter), quarter)
                ]
            send(("ty", k, r), t_out.at[place], t_in.at[place, 0:own], x_peer)

        return run

    def right_core(k, r):
        place = QUARTERS[k] + r

        def run():
            arrive(("ty", k, r))()
            send(("td", k, r), t_in.at[place, 0:own], t_in.at[place, own : 2 * own], core_peer)

        return run

    def outer_quarter(k, j, r):
        def run():
            left, _, right = quartered[k][:3]
            near = pl.ds(pl.multiple_of(r * features + c * half + x * quarter, quarter), quarter)
            away = pl.ds(pl.multiple_of(c * quarter, quarter), quarter)
            total = contract(left[:, j * features : (j + 1) * features], right[:, near], 0, 0)
            total = total + contract(t_left[QUARTERS[k] + j], t_in[QUARTERS[k] + r, :, away], 0, 0)
            g[spans[k][0] + j + r, :, plane_span] = total.astype(LOW)

        return run

    for k, (_, lefts, _, rights, left_dep, right_dep, left_got, right_got) in quartered.items():
        urgency = 2.6 if k == 0 else 2.5
        for j in range(lefts):
            plan.add(("tx", k, j), left_away(k, j), [left_dep] + list(AFTER.get(k, ())), (), [(("tx", k, j), "x", lump)], 0.05, urgency)
            plan.add(("tw", k, j), left_core(k, j), [("tx", k, j)], [("tx", k, j)], [(("tc", k, j), "c", lump)], 0.05, urgency)
            plan.add(("got", "tc", k, j), arrive(("tc", k, j)), [("tw", k, j)], [("tc", k, j)], (), 0.02, urgency)
        for r in range(rights):
            plan.add(("ty", k, r), right_away(k, r), [right_dep], (), [(("ty", k, r), "x", lump // 2)], 0.05, 2.5)
            plan.add(("tz", k, r), right_core(k, r), [("ty", k, r)], [("ty", k, r)], [(("td", k, r), "c", lump // 2)], 0.05, 2.5)
            plan.add(("got", "td", k, r), arrive(("td", k, r)), [("tz", k, r)], [("td", k, r)], (), 0.02, 2.5)
        for j in range(lefts):
            for r in range(rights):
                deps = [("got", left_got), ("got", right_got), ("got", "tc", k, j), ("got", "td", k, r)]
                plan.add(("gr", spans[k][0] + j + r), outer_quarter(k, j, r), deps, cost=0.4, rank=5)
    weight_grads = []
    for r in range(3):
        for k, left, left_block, right, right_block, deps in (
            (0, x_pool, r, d_pool, 0, ("ep", "ed1")), (1, x_norm, 0, d_qkv, r, ("en", "eq")),
            (2, x_att, 0, d_res, 0, ("ea", "er")), (5, x_short, 0, d_up, r, ("es", "eu")),
        ):
            if k not in QUARTERS and r < sizes[k]:
                deps = [("got", dep) for dep in deps]
                weight_grads.append((spans[k][0] + r, left, left_block, right, right_block, deps))
    for block, left, left_block, right, right_block, deps in weight_grads:
        plan.add(("gr", block), outer(block, left, left_block, right, right_block), deps, cost=0.3, rank=5)

    def scatter_chunk(rank, name, here, there, size, deps):
        split, quarters = there is not None, there is here
        blocks = pl.ds(here, size)
        load = size * piece_bytes // (2 if quarters else 1)
        away, span, away_span, length_out = blocks, slice(None), slice(None), half
        begin_out, away_out = c * half, c * half
        if quarters:
            span, away_span = plane_span, plane_away
            length_out, begin_out, away_out = quarter, c * half + x * quarter, c * half + (1 - x) * quarter
        elif split:
            away = pl.ds(there, size)
        out_span = pl.ds(pl.multiple_of(begin_out, length_out), length_out)
        out_away = pl.ds(pl.multiple_of(away_out, length_out), length_out)

        half_rows = rows_of // 2
        sides = (("R", 0, right_in, right_peer), ("L", half_rows, left_in, left_peer))

        def first_step():
            for side, part, inbox, peer in sides:
                source = g.at[blocks, rows_at(4, part, half_rows), span]
                target = inbox.at[0, blocks, part : part + half_rows, span]
                send((side, "s", 1, name), source, target, peer, ("s", 1, name))

        def take(step):
            gather_up(("s", step, name), g.at[blocks, 0 : rows_of * (1 if step == 1 else 2), span])

        def next_step(step):
            def run():
                take(step - 1)
                for side, half_part, inbox, peer in sides:
                    offset = (5 - step) if side == "R" else (step - 5)
                    part, length = (half_part, half_rows) if step == 2 else (0, rows_of)
                    rows = rows_at(offset, part, length)
                    g[blocks, rows, span] = g[blocks, rows, span] + inbox[step - 2, blocks, part : part + length, span]
                    source = g.at[blocks, rows_at(offset), span]
                    send((side, "s", step, name), source, inbox.at[step - 1, blocks, :, span], peer, ("s", step, name))

            return run

        def finish():
            take(4)
            total = g[blocks, rows_at(0), span].astype(WIDE)
            total = total + right_in[3, blocks, :, span].astype(WIDE) + left_in[3, blocks, :, span].astype(WIDE)
            fin_out[blocks, :, span] = total.astype(LOW)
            send(("rx", name), fin_out.at[blocks, :, span], fin_in.at[blocks, :, span], x_peer)
            if split:
                red[blocks, :, out_span] = fin_out[blocks, :, span]
                send(("rc", name), fin_out.at[blocks, :, span], co_in.at[blocks, :, span], core_peer)

        def finish_x():
            arrive(("rx", name))()
            if split:
                red[away, :, out_away] = fin_in[away, :, away_span]
                send(("rd", name), fin_in.at[away, :, away_span], co_in.at[away, :, away_span], core_peer)
            else:
                total = (fin_out[blocks].astype(WIDE) + fin_in[blocks].astype(WIDE)).astype(LOW)
                co_out[blocks] = total
                red[blocks, :, my_half] = total
                send(("rc", name), co_out.at[blocks], co_in.at[blocks], core_peer)

        def finish_core():
            arrive(("rc", name), *([("rd", name)] if split else []))()
            red[blocks, :, other_half] = co_in[blocks]
            if split and not quarters:
                red[away, :, other_half] = co_in[away]

        links = (("R", "r"), ("L", "l"))
        out = [((side, "s", 1, name), link, load // 2) for side, link in links]
        plan.add(("r", 1, name), first_step, deps, (), out, 0.05, rank)
        for step in (2, 3, 4):
            waits = [(side, "s", step - 1, name) for side in "RL"]
            out = [((side, "s", step, name), link, load) for side, link in links]
            plan.add(("r", step, name), next_step(step), [("r", step - 1, name)], waits, out, 0.04 * size, rank)
        own_out = [(("rc", name), "c", load)]
        plan.add(
            ("fi", name), finish, [("r", 4, name)], [("R", "s", 4, name), ("L", "s", 4, name)],
            [(("rx", name), "x", load)] + (own_out if split else []), 0.02 * size, rank,
        )
        late_out = [(("rd", name), "c", load)] if split else own_out
        plan.add(("fx", name), finish_x, [("fi", name)], [("rx", name)], late_out, 0.02 * size, rank)
        plan.add(
            ("fc", name), finish_core, [("fx", name)], [("rc", name)] + ([("rd", name)] if split else []), (), 0.02 * size, rank
        )

    for k, offset, size, rank in SCATTERS:
        name = ("g", k, offset)
        if k == 3:
            deps = [("gr", j, "s") for j in range(offset, offset + size)]
            scatter_chunk(rank, name, ours + offset, theirs + offset, size, deps)
        else:
            begin = spans[k][0] + offset
            scatter_chunk(rank, name, begin, begin if k in QUARTERS else None, size, [("gr", begin + j) for j in range(size)])

    for name, _ in plan.order():
        plan.tasks[name][0]()
    assert len(boxes) <= RECEIVES
    for copy in started[-SENDS:]:
        copy.wait_send()
    for copy in outs:
        copy.wait()


def adam_kernel(sizes, refs):
    owners, red, small, gain, bias, norm_m, norm_v, slope, slope_m, slope_v, master, first, second, mixed, grad = refs[:15]
    (
        new_w, new_m, new_v, new_low, norm_out, norm_m_out, norm_v_out, slope_out, slope_m_out, slope_v_out, mixed_out,
        grad_out,
    ) = refs[15:]
    step = pl.program_id(0)
    fix_first = 1.0 - beta_one**STEP
    fix_second = 1.0 - beta_two**STEP
    mixed_out[...] = mixed[...]
    grad_out[...] = grad[...]

    @pl.when(step == 0)
    def _():
        for begin, values in ((0, gain), (2, bias)):
            rows = slice(begin, begin + 2)
            norm_out[rows], norm_m_out[rows], norm_v_out[rows] = adam_update(
                values[...], small[rows], norm_m[rows], norm_v[rows], fix_first, fix_second, rate_norm, 0.0
            )
        heads = slope.shape[1]
        slope_out[...], slope_m_out[...], slope_v_out[...] = adam_update(
            slope[...], small[4:5, 0:heads], slope_m[...], slope_v[...], fix_first, fix_second, rate_slope, 0.0
        )

    me = lax.axis_index("batch")
    for place in range(master.shape[0]):
        slot = step * master.shape[0] + place
        block, held, base = jnp.int32(0), jnp.int32(0), 0
        for matrix_id, size in enumerate(sizes):
            begin = start_of(owners, matrix_id, sizes)
            inside = (owners[matrix_id] == me) & (slot >= begin) & (slot < begin + size)
            block = jnp.where(inside, base + slot - begin, block)
            held = jnp.where(inside, 1, held)
            base += size
        gradient = red[block].astype(WIDE)
        values = adam_update(
            master[place], gradient, first[place], second[place], fix_first, fix_second, rate_matrix, decay_rate
        )
        keep = jnp.full(gradient.shape, held, jnp.int32) > 0
        weight = jnp.where(keep, values[0], master[place])
        new_w[place] = weight
        new_m[place] = jnp.where(keep, values[1], first[place])
        new_v[place] = jnp.where(keep, values[2], second[place])
        new_low[place] = weight.astype(LOW)


def fused_body(tokens, cotangent, doc_lengths, owners, master, first_moment, second_moment, ln_gain, ln_bias, norm_m, norm_v, slopes, slope_m, slope_v):
    micros, _, tok_rows, features = tokens.shape
    units, heads, width = tok_rows // 3, slopes.shape[0], features // slopes.shape[0]
    sizes = tuple(block_counts(features, FF))
    blocks, own, half = sum(sizes), micros * units, features // 2
    slots, rows = master.shape[1], master.shape[2]
    lane_units = units * heads
    split = features // TILE
    hbm, vmem, smem = (pl.BlockSpec(memory_space=m) for m in (pl.ANY, pltpu.VMEM, pltpu.SMEM))
    low = lambda *shape: pltpu.VMEM(shape, LOW)
    wide = lambda *shape: pltpu.VMEM(shape, WIDE)
    pieces = lambda: low(blocks, rows, half)
    both = lambda columns: low(2 * own, columns)
    scratch = [
        low(blocks, 2, features, half), wide(slots, rows, features), pieces(), pieces(), pieces(), pieces(), pieces(),
        low(micros, tok_rows, features), low(micros, tok_rows, features), low(micros, 16, features),
        wide(micros, split, 16 + tok_rows, TILE), wide(micros, split, tok_rows, TILE),
        both(3 * features), both(features), both(features), both(features), both(FF), both(features),
        both(3 * features), both(features), both(FF), both(features), both(3 * features), both(features),
        wide(own, features), wide(own, features), wide(own, features), wide(own, 1), wide(own, 1),
        wide(own, features), wide(own, FF), wide(own, features), wide(own, features),
        low(heads, 3 * units, 2 * width), low(heads, 3 * units, 2 * width), low(heads, units, 2 * width),
        low(heads, units, 2 * width), low(heads, units, 2 * width), low(heads, units, 2 * width),
        low(heads, 3 * units, 2 * width), low(heads, 3 * units, 2 * width),
        wide(micros, lane_units, lane_units), wide(micros, tok_rows, features), wide(micros, tok_rows, features),
        wide(micros, split, tok_rows, TILE), wide(micros, split, 8 + tok_rows, TILE), wide(micros, split, 8, TILE),
        low(2 * own, features), low(2 * own, FF),
        low(10, 2 * own, features), low(10, own, half), low(10, 2 * own, half), low(blocks, features, half), low(4, blocks, rows, half), low(4, blocks, rows, half),
        pieces(), pieces(), pieces(), pieces(), wide(48, features), wide(40, features),
        pltpu.SemaphoreType.DMA((SENDS,)), pltpu.SemaphoreType.DMA((RECEIVES,)), pltpu.SemaphoreType.DMA((5,)),
    ]
    token_shape = (micros, tok_rows, features)
    dims = (units, features, FF, heads, micros, sizes)
    mixed, grad, red, small = pl.pallas_call(
        lambda *refs: main_kernel(dims, refs),
        out_shape=(
            jax.ShapeDtypeStruct(token_shape, WIDE),
            jax.ShapeDtypeStruct(token_shape, WIDE),
            jax.ShapeDtypeStruct((blocks, rows, features), LOW),
            jax.ShapeDtypeStruct((8, features), WIDE),
        ),
        in_specs=[smem, smem, smem, vmem, vmem, hbm, hbm, hbm],
        out_specs=(hbm, hbm, vmem, vmem),
        scratch_shapes=scratch,
        compiler_params=pltpu.CompilerParams(
            collective_id=0, has_side_effects=True, vmem_limit_bytes=60 * 2**20
        ),
        name="block",
    )(
        owners, doc_lengths[:, 0], slopes, ln_gain, ln_bias, tokens[:, 0], cotangent[:, 0], master[0]
    )
    steps = 2
    slot = pl.BlockSpec((slots // steps, rows, features), lambda j: (j, 0, 0))
    flat = (micros * tok_rows, features)
    some = pl.BlockSpec((flat[0] // steps, features), lambda j: (j, 0))
    moment_shape = jax.ShapeDtypeStruct((slots, rows, features), WIDE)
    norm_shape = jax.ShapeDtypeStruct((4, features), WIDE)
    slope_shape = jax.ShapeDtypeStruct((1, heads), WIDE)
    out = pl.pallas_call(
        lambda *refs: adam_kernel(sizes, refs),
        grid=(steps,),
        out_shape=(
            moment_shape, moment_shape, moment_shape, jax.ShapeDtypeStruct((slots, rows, features), LOW),
            norm_shape, norm_shape, norm_shape, slope_shape, slope_shape, slope_shape,
            jax.ShapeDtypeStruct(flat, WIDE), jax.ShapeDtypeStruct(flat, WIDE),
        ),
        in_specs=[smem] + [vmem] * 9 + [slot] * 3 + [some] * 2,
        out_specs=(slot, slot, slot, slot, vmem, vmem, vmem, vmem, vmem, vmem, some, some),
        compiler_params=pltpu.CompilerParams(dimension_semantics=("arbitrary",)),
        name="adam",
    )(
        owners, red, small, ln_gain, ln_bias, norm_m, norm_v, slopes[None], slope_m[None],
        slope_v[None], master[0], first_moment[0], second_moment[0],
        mixed.reshape(flat), grad.reshape(flat),
    )
    new_w, new_m, new_v, new_low, norm, norm_m, norm_v, slope, slope_m, slope_v, mixed, grad = out
    return (
        mixed.reshape(tokens.shape), grad.reshape(tokens.shape), new_w[None], new_m[None], new_v[None], new_low[None], norm, norm_m, norm_v,
        slope[0], slope_m[0], slope_v[0],
    )


def fits(mesh, shapes):
    return mesh.shape["batch"] == 4 and mesh.shape["seq"] == 8 and shapes[0].shape[1] == 1


def solution(mesh):
    in_specs = (
        P("batch", None, "seq", None),
        P("batch", None, "seq", None),
        P("batch", None, None),
        P(),
        P("batch", None, "seq", None),
        P("batch", None, "seq", None),
        P("batch", None, "seq", None),
        P(),
        P(),
        P(),
        P(),
        P(),
        P(),
        P(),
    )
    out_specs = (
        P("batch", None, "seq", None),
        P("batch", None, "seq", None),
        P("batch", None, "seq", None),
        P("batch", None, "seq", None),
        P("batch", None, "seq", None),
        P("batch", None, "seq", None),
        P(),
        P(),
        P(),
        P(),
        P(),
        P(),
    )

    def whole(*args):
        part = fused_body if fits(mesh, args) else body
        return jax.shard_map(
            part, mesh=mesh, in_specs=in_specs, out_specs=out_specs, check_vma=False
        )(*args)

    return whole
```

```python
import math

import jax
import jax.numpy as jnp
from jax import lax
from jax.experimental import pallas as pl
from jax.experimental.pallas import tpu as pltpu
from jax.sharding import PartitionSpec as P

FF = 2048
STEP = 10


beta_one = 0.9
beta_two = 0.95
adam_eps = 1e-08
decay_rate = 0.1
rate_matrix = 0.02
rate_norm = 0.2
rate_slope = 0.01
ln_eps = 1e-05
masked_score = -1000000000.0
row_kinds = (True, False, True, False, True, False)


def broadcast(value, axis, source):
    kept = jnp.where(lax.axis_index(axis) == source, value, 0).astype(value.dtype)
    return lax.psum(kept, axis)


def running_total(lengths):
    count = lengths.shape[-1]
    ends = [lengths[..., 0]]
    for index in range(1, count):
        ends.append(ends[-1] + lengths[..., index])
    return jnp.stack(ends, -1)


def for_sending(value):

    def short(part):
        return part.astype(jnp.bfloat16) if part.dtype == jnp.float32 else part

    return jax.tree.map(short, value)


def passed_along(value, axis, by):
    peers = lax.axis_size(axis)
    pairs = [(i, i + by) for i in range(peers) if 0 <= i + by < peers]
    return lax.ppermute(value, axis, pairs)


def layer_norm(values, gain, shift):
    center = jnp.mean(values, -1, keepdims=True)
    centred = values - center
    spread = jnp.mean(centred * centred, -1, keepdims=True)
    return centred * lax.rsqrt(spread + ln_eps) * gain + shift


def gelu_tanh(values):
    return jax.nn.gelu(values, approximate=True)


def block_counts(features, hidden):
    return [3, 3, 1, hidden // features, hidden // features, 3]


def block_starts(owners, sizes):
    starts_list = []
    for matrix_id in range(len(sizes)):
        shared = jnp.zeros((), jnp.int32)
        for earlier_id in range(matrix_id):
            shared = shared + jnp.where(
                owners[earlier_id] == owners[matrix_id], sizes[earlier_id], 0
            ).astype(jnp.int32)
        starts_list.append(shared)
    return starts_list


def slot_table(owners, device, sizes, slot_count):
    starts_list = block_starts(owners, sizes)
    slot_ids = jnp.arange(slot_count, dtype=jnp.int32)
    numbers = jnp.arange(sum(sizes), dtype=jnp.int32)
    slot_map = jnp.zeros((slot_count, sum(sizes)), jnp.float32)
    block_base = 0
    for matrix_id in range(len(sizes)):
        inside = (
            (owners[matrix_id] == device)
            & (slot_ids >= starts_list[matrix_id])
            & (slot_ids < starts_list[matrix_id] + sizes[matrix_id])
        )
        target = block_base + slot_ids - starts_list[matrix_id]
        slot_map = slot_map + (inside[:, None] & (target[:, None] == numbers[None, :])).astype(
            jnp.float32
        )
        block_base += sizes[matrix_id]
    return slot_map


def to_matrix(blocks, by_rows):
    if by_rows:
        return blocks.reshape(-1, blocks.shape[2])
    return blocks.transpose(1, 0, 2).reshape(blocks.shape[1], -1)


def to_blocks(matrix, by_rows, features):
    if by_rows:
        return matrix.reshape(-1, features, features)
    return matrix.reshape(features, -1, features).transpose(1, 0, 2)


def all_blocks(matrices, features):
    return jnp.concatenate(
        [to_blocks(matrices[matrix_id], row_kinds[matrix_id], features) for matrix_id in range(6)],
        0,
    )


def adam_update(weight, gradient, first_moment, second, fix_first, fix_second, rate, decay):
    first_new = beta_one * first_moment + (1.0 - beta_one) * gradient
    second_new = beta_two * second + (1.0 - beta_two) * gradient * gradient
    direction = first_new / fix_first / (jnp.sqrt(second_new / fix_second) + adam_eps)
    return (weight - rate * (direction + decay * weight), first_new, second_new)


def scores_for(query_block, key_rows, start_row, segment, head_slope):
    block_rows = query_block.shape[0]
    row_total = key_rows.shape[0]
    row_ids = start_row + jnp.arange(block_rows, dtype=jnp.int32)
    col_ids = jnp.arange(row_total, dtype=jnp.int32)
    distance = (row_ids[:, None] - col_ids[None, :]).astype(jnp.float32)
    seg_rows = lax.dynamic_slice_in_dim(segment, start_row, block_rows)
    allowed = (seg_rows[:, None] == segment[None, :]) & (col_ids[None, :] <= row_ids[:, None])
    raw_score = (
        jnp.dot(query_block, key_rows.T, preferred_element_type=jnp.float32) * 0.125
        - head_slope * distance
    )
    return (jnp.where(allowed, raw_score, masked_score), distance)


def attend(queries, key_rows, values, segment, head_slope, block_rows):
    row_total, head_width = queries.shape

    def per_block(start_row):
        query_block = lax.dynamic_slice_in_dim(queries, start_row, block_rows)
        scores, distance = scores_for(query_block, key_rows, start_row, segment, head_slope)
        largest = jnp.max(scores, -1, keepdims=True)
        log_total = largest + jnp.log(jnp.sum(jnp.exp(scores - largest), -1, keepdims=True))
        probability = jnp.exp(scores - log_total).astype(jnp.bfloat16)
        return (jnp.dot(probability, values, preferred_element_type=jnp.float32), log_total[:, 0])

    row_starts = jnp.arange(row_total // block_rows, dtype=jnp.int32) * block_rows
    attended, log_totals = lax.map(per_block, row_starts)
    return (attended.reshape(row_total, head_width), log_totals.reshape(row_total))


def attend_back(queries, key_rows, values, segment, head_slope, log_totals, grad_out, block_rows):
    row_total, head_width = queries.shape

    def per_block(carried, start_row):
        grad_keys, grad_values, grad_slope = carried
        query_block = lax.dynamic_slice_in_dim(queries, start_row, block_rows)
        grad_block = lax.dynamic_slice_in_dim(grad_out, start_row, block_rows)
        total_block = lax.dynamic_slice_in_dim(log_totals, start_row, block_rows)
        scores, distance = scores_for(query_block, key_rows, start_row, segment, head_slope)
        probability = jnp.exp(scores - total_block[:, None])
        grad_prob = jnp.dot(grad_block, values.T, preferred_element_type=jnp.float32)
        grad_score = (
            probability * (grad_prob - jnp.sum(probability * grad_prob, -1, keepdims=True))
        ).astype(jnp.bfloat16)
        grad_query = jnp.dot(grad_score, key_rows, preferred_element_type=jnp.float32) * 0.125
        grad_keys = (
            grad_keys
            + jnp.dot(grad_score.T, query_block, preferred_element_type=jnp.float32) * 0.125
        )
        grad_values = grad_values + jnp.dot(
            probability.astype(jnp.bfloat16).T, grad_block, preferred_element_type=jnp.float32
        )
        grad_slope = grad_slope - jnp.sum(grad_score.astype(jnp.float32) * distance)
        return ((grad_keys, grad_values, grad_slope), grad_query)

    row_starts = jnp.arange(row_total // block_rows, dtype=jnp.int32) * block_rows
    initial = (
        jnp.zeros((row_total, head_width), jnp.float32),
        jnp.zeros((row_total, head_width), jnp.float32),
        jnp.zeros((), jnp.float32),
    )
    (grad_keys, grad_values, grad_slope), grad_queries = lax.scan(per_block, initial, row_starts)
    return (grad_queries.reshape(row_total, head_width), grad_keys, grad_values, grad_slope)


def body(
    tokens,
    cotangent,
    doc_lengths,
    owners,
    master,
    first_moment,
    second_moment,
    ln_gain,
    ln_bias,
    norm_m,
    norm_v,
    slopes,
    slope_m,
    slope_v,
):
    micro_count, lane_count, tok_rows, features = tokens.shape
    unit_rows = tok_rows // 3
    seq_devices = lax.axis_size("seq")
    head_count = slopes.shape[0]
    head_width = features // head_count
    lane_units = unit_rows * seq_devices
    block_rows = min(512, lane_units)
    unit_total = lane_count * unit_rows
    slot_count = master.shape[1]
    sizes = block_counts(features, FF)
    starts_list = block_starts(owners, sizes)
    batch_rank = lax.axis_index("batch")
    seq_rank = lax.axis_index("seq")
    lane_rank = seq_rank // head_count
    head_rank = seq_rank % head_count
    low_slots = master[0].astype(jnp.bfloat16)
    fetched = []
    for matrix_id in range(6):
        owned_rows = lax.dynamic_slice_in_dim(
            low_slots, starts_list[matrix_id], sizes[matrix_id], 0
        )
        fetched.append(broadcast(owned_rows, "batch", owners[matrix_id]))
    gathered = lax.all_gather(for_sending(tuple(fetched)), "seq", axis=1, tiled=True)
    pool_weight, qkv_weight, out_weight, in_weight, back_weight, up_weight = [
        to_matrix(gathered[matrix_id], row_kinds[matrix_id]) for matrix_id in range(6)
    ]
    doc_ends = running_total(doc_lengths)
    doc_starts = jnp.concatenate(
        [jnp.zeros((micro_count, lane_count, 1), jnp.int32), doc_ends[..., :-1]], -1
    )
    unit_ids = seq_rank * unit_rows + jnp.arange(unit_rows, dtype=jnp.int32)
    keep_mask = 1.0 - jnp.any(
        unit_ids[None, None, :, None] == doc_starts[:, :, None, :], -1
    ).astype(jnp.float32)
    triples = tokens.reshape(micro_count, lane_count, unit_rows, 3, features)
    tail_tokens = triples[:, :, -1, 1:3]
    arrived = passed_along(tail_tokens, "seq", 1)
    lane_pick = jnp.arange(lane_count, dtype=jnp.int32) == lane_rank
    head_pick = jnp.arange(head_count, dtype=jnp.int32) == head_rank
    head_slope = jnp.sum(jnp.where(head_pick, slopes, 0.0))
    positions = jnp.arange(lane_units, dtype=jnp.int32)
    gain_grad = jnp.zeros((2, features), jnp.float32)
    bias_grad = jnp.zeros((2, features), jnp.float32)
    slope_grad = jnp.zeros((), jnp.float32)
    summed = None
    mixed_parts = []
    grad_parts = []
    outgoing = []
    for micro in range(micro_count):
        triple_now = triples[micro]
        keep_now = keep_mask[micro]
        earlier = jnp.concatenate([arrived[micro][:, None], triple_now[:, :-1, 1:3]], 1) * keep_now[
            :, :, None, None
        ].astype(jnp.bfloat16)
        pool_input = jnp.concatenate([earlier, triple_now[:, :, 0:1]], 2).reshape(
            unit_total, 3 * features
        )
        pooled = jnp.dot(pool_input, pool_weight, preferred_element_type=jnp.float32)
        normed = layer_norm(pooled, ln_gain[0], ln_bias[0]).astype(jnp.bfloat16)
        projected = jnp.dot(normed, qkv_weight, preferred_element_type=jnp.float32).astype(
            jnp.bfloat16
        )
        outbound = (
            projected.reshape(lane_count, unit_rows, 3, head_count, head_width)
            .transpose(0, 3, 1, 2, 4)
            .reshape(lane_count * head_count, unit_rows * 3 * head_width)
        )
        received = lax.all_to_all(outbound, "seq", split_axis=0, concat_axis=1, tiled=True).reshape(
            lane_units, 3, head_width
        )
        queries = received[:, 0]
        key_rows = received[:, 1]
        values = received[:, 2]
        lengths = jnp.sum(jnp.where(lane_pick[:, None], doc_lengths[micro], 0), 0)
        lane_ends = running_total(lengths)
        segment = jnp.sum((positions[:, None] >= lane_ends[None, :-1]).astype(jnp.int32), 1)
        attended, log_totals = attend(queries, key_rows, values, segment, head_slope, block_rows)
        returned = lax.all_to_all(
            attended.astype(jnp.bfloat16).reshape(1, lane_units * head_width),
            "seq",
            split_axis=1,
            concat_axis=0,
            tiled=True,
        )
        merged = (
            returned.reshape(lane_count, head_count, unit_rows, head_width)
            .transpose(0, 2, 1, 3)
            .reshape(unit_total, features)
        )
        residual = pooled + jnp.dot(merged, out_weight, preferred_element_type=jnp.float32)
        normed_two = layer_norm(residual, ln_gain[1], ln_bias[1]).astype(jnp.bfloat16)
        hidden = jnp.dot(normed_two, in_weight, preferred_element_type=jnp.float32)
        activated = gelu_tanh(hidden).astype(jnp.bfloat16)
        shortened = residual + jnp.dot(activated, back_weight, preferred_element_type=jnp.float32)
        short_low = shortened.astype(jnp.bfloat16)
        upward = jnp.dot(short_low, up_weight, preferred_element_type=jnp.float32).reshape(
            lane_count, unit_rows * 3, features
        )
        mixed_parts.append(tokens[micro].astype(jnp.float32) + upward)
        grad_upward = cotangent[micro].reshape(unit_total, 3 * features)
        sum_up = jnp.dot(short_low.T, grad_upward, preferred_element_type=jnp.float32)
        grad_short = jnp.dot(grad_upward, up_weight.T, preferred_element_type=jnp.float32)
        grad_short_low = grad_short.astype(jnp.bfloat16)
        sum_back = jnp.dot(activated.T, grad_short_low, preferred_element_type=jnp.float32)
        grad_activated = jnp.dot(grad_short_low, back_weight.T, preferred_element_type=jnp.float32)
        grad_hidden = jax.vjp(gelu_tanh, hidden)[1](grad_activated)[0].astype(jnp.bfloat16)
        sum_in = jnp.dot(normed_two.T, grad_hidden, preferred_element_type=jnp.float32)
        grad_normed_two = jnp.dot(grad_hidden, in_weight.T, preferred_element_type=jnp.float32)
        norm_two_back = jax.vjp(layer_norm, residual, ln_gain[1], ln_bias[1])[1]
        grad_resid_norm, grad_gain_two, grad_bias_two = norm_two_back(grad_normed_two)
        grad_residual = grad_short + grad_resid_norm
        grad_resid_low = grad_residual.astype(jnp.bfloat16)
        sum_out = jnp.dot(merged.T, grad_resid_low, preferred_element_type=jnp.float32)
        grad_merged = jnp.dot(
            grad_resid_low, out_weight.T, preferred_element_type=jnp.float32
        ).astype(jnp.bfloat16)
        back_outbound = (
            grad_merged.reshape(lane_count, unit_rows, head_count, head_width)
            .transpose(0, 2, 1, 3)
            .reshape(lane_count * head_count, unit_rows * head_width)
        )
        grad_attended = lax.all_to_all(
            back_outbound, "seq", split_axis=0, concat_axis=1, tiled=True
        ).reshape(lane_units, head_width)
        grad_queries, grad_keys, grad_values, grad_slope = attend_back(
            queries, key_rows, values, segment, head_slope, log_totals, grad_attended, block_rows
        )
        grad_heads = (
            jnp.stack([grad_queries, grad_keys, grad_values], 1)
            .astype(jnp.bfloat16)
            .reshape(1, lane_units * 3 * head_width)
        )
        grad_arrived = lax.all_to_all(grad_heads, "seq", split_axis=1, concat_axis=0, tiled=True)
        grad_projected = (
            grad_arrived.reshape(lane_count, head_count, unit_rows, 3, head_width)
            .transpose(0, 2, 3, 1, 4)
            .reshape(unit_total, 3 * features)
        )
        sum_qkv = jnp.dot(normed.T, grad_projected, preferred_element_type=jnp.float32)
        grad_normed = jnp.dot(grad_projected, qkv_weight.T, preferred_element_type=jnp.float32)
        norm_one_back = jax.vjp(layer_norm, pooled, ln_gain[0], ln_bias[0])[1]
        grad_pool_norm, grad_gain_one, grad_bias_one = norm_one_back(grad_normed)
        grad_pooled_low = (grad_residual + grad_pool_norm).astype(jnp.bfloat16)
        sum_pool = jnp.dot(pool_input.T, grad_pooled_low, preferred_element_type=jnp.float32)
        grad_pieces = jnp.dot(
            grad_pooled_low, pool_weight.T, preferred_element_type=jnp.float32
        ).reshape(lane_count, unit_rows, 3, features)
        grad_earlier = grad_pieces[:, :, 0:2] * keep_now[:, :, None, None]
        outgoing.append(grad_earlier[:, 0])
        following = jnp.concatenate(
            [grad_earlier[:, 1:], jnp.zeros((lane_count, 1, 2, features), jnp.float32)], 1
        )
        token_grad = jnp.concatenate([grad_pieces[:, :, 2:3], following], 2).reshape(
            lane_count, unit_rows * 3, features
        )
        grad_parts.append(cotangent[micro].astype(jnp.float32) + token_grad)
        gain_grad = gain_grad + jnp.stack([grad_gain_one, grad_gain_two])
        bias_grad = bias_grad + jnp.stack([grad_bias_one, grad_bias_two])
        slope_grad = slope_grad + grad_slope
        micro_grads = [sum_pool, sum_qkv, sum_out, sum_in, sum_back, sum_up]
        summed = (
            micro_grads
            if summed is None
            else [left + right for left, right in zip(summed, micro_grads)]
        )
    reduced = lax.psum_scatter(all_blocks(summed, features), "seq", scatter_dimension=1, tiled=True)
    incoming = passed_along(jnp.stack(outgoing).astype(jnp.bfloat16), "seq", -1).astype(jnp.float32)
    grad_tokens = jnp.stack(grad_parts).reshape(micro_count, lane_count, unit_rows, 3, features)
    grad_tokens = grad_tokens.at[:, :, -1, 1:3].add(incoming).reshape(tokens.shape)
    reduced_all = lax.psum(reduced, "batch")
    norm_grad, slopes_grad = lax.psum(
        (jnp.concatenate([gain_grad, bias_grad], 0), jnp.where(head_pick, slope_grad, 0.0)),
        ("batch", "seq"),
    )
    slot_map = slot_table(owners, batch_rank, sizes, slot_count)
    is_owned = jnp.sum(slot_map, -1)[:, None, None] > 0.5
    slot_grads = jnp.einsum("jb,brc->jrc", slot_map, reduced_all, precision=lax.Precision.HIGHEST)
    step_float = jnp.float32(STEP)
    fix_first = 1.0 - jnp.power(jnp.float32(beta_one), step_float)
    fix_second = 1.0 - jnp.power(jnp.float32(beta_two), step_float)
    new_weight, new_first, new_second = adam_update(
        master[0],
        slot_grads,
        first_moment[0],
        second_moment[0],
        fix_first,
        fix_second,
        rate_matrix,
        decay_rate,
    )
    new_weight = jnp.where(is_owned, new_weight, master[0])
    new_first = jnp.where(is_owned, new_first, first_moment[0])
    new_second = jnp.where(is_owned, new_second, second_moment[0])
    norm_now = jnp.concatenate([ln_gain, ln_bias], 0)
    new_norm, new_norm_m, new_norm_v = adam_update(
        norm_now, norm_grad, norm_m, norm_v, fix_first, fix_second, rate_norm, 0.0
    )
    new_slopes, new_slope_m, new_slope_v = adam_update(
        slopes, slopes_grad, slope_m, slope_v, fix_first, fix_second, rate_slope, 0.0
    )
    return (
        jnp.stack(mixed_parts),
        grad_tokens,
        new_weight[None],
        new_first[None],
        new_second[None],
        new_weight[None].astype(jnp.bfloat16),
        new_norm,
        new_norm_m,
        new_norm_v,
        new_slopes,
        new_slope_m,
        new_slope_v,
    )


MESH = pl.DeviceIdType.MESH
LOW = jnp.bfloat16
WIDE = jnp.float32
TILE = 128


class Plan:
    def __init__(self):
        self.tasks = {}

    def add(self, name, run, deps=(), waits=(), sends=(), cost=0.1, rank=0):
        assert name not in self.tasks
        self.tasks[name] = (run, tuple(deps), tuple(waits), tuple(sends), cost, rank)

    def order(self):
        now, done, arrival, free, listed = 0.0, set(), {}, {}, []
        left = list(self.tasks)
        while left:
            best = None
            for place, name in enumerate(left):
                run, deps, waits, sends, cost, rank = self.tasks[name]
                if any(d not in done for d in deps) or any(w not in arrival for w in waits):
                    continue
                begin = max([now] + [arrival[w] for w in waits] + [free.get(m[1], 0.0) - SLACK for m in sends])
                key = (begin, rank, place)
                if best is None or key < best[0]:
                    best = (key, name)
            name = best[1]
            run, deps, waits, sends, cost, rank = self.tasks[name]
            now = best[0][0] + cost
            for message, link, size in sends:
                rate, delay = LINKS[link]
                lanes = ("f", "r", "l") if link == "f" else (link,)
                end = max([now] + [free.get(lane, 0.0) for lane in lanes]) + size / rate
                free.update({lane: end for lane in lanes})
                arrival[message] = end + delay
            done.add(name)
            left.remove(name)
            listed.append((name, now))
        return listed


SLACK = 2.0
SENDS, RECEIVES = 32, 180
GATHERS = (
    (0, 0, 1, 0.0),
    (0, 1, 1, 0.07),
    (0, 2, 1, 0.08),
    (1, 0, 1, 0.21),
    (1, 1, 1, 0.21),
    (1, 2, 1, 0.21),
    (3, 0, 2, 0.31),
    (3, 2, 2, 0.33),
    (2, 0, 1, 0.43),
    (5, 0, 3, 0.37),
)
QUARTERS = {5: 0, 1: 3, 0: 6}
AFTER = {}
WHOLE = ()
SCATTERS = (
    (5, 0, 3, 0.93),
    (3, 0, 2, 1.01),
    (3, 2, 2, 0.93),
    (2, 0, 1, 1.26),
    (0, 0, 1, 0.43),
    (0, 1, 1, 0.43),
    (0, 2, 1, 0.43),
    (1, 0, 3, 0.6),
)
LINKS = {
    "c": (400e3, 1.0),
    "x": (52e3, 2.3),
    "r": (52e3, 2.3),
    "l": (52e3, 2.3),
    "f": (46e3, 3.3),
}


def start_of(owners, matrix_id, sizes):
    shared = jnp.int32(0)
    for earlier_id in range(matrix_id):
        shared = shared + jnp.where(owners[earlier_id] == owners[matrix_id], sizes[earlier_id], 0)
    return shared


def over_last(fn, value):
    return fn(value, axis=-1, keepdims=True)


def contract(left, right, left_dim, right_dim):
    return lax.dot_general(
        left, right, (((left_dim,), (right_dim,)), ((), ())), preferred_element_type=WIDE
    )


def gelu_parts(value):
    scale = math.sqrt(2.0 / math.pi)
    inner = jnp.tanh(scale * (value + 0.044715 * (value * value * value)))
    return inner, scale * (1.0 + 3 * 0.044715 * value * value)


def main_kernel(dims, refs):
    units, features, hidden_width, heads, micros, sizes = dims
    owners, docs, slopes, gain, bias, tok_hbm, cot_hbm, master_hbm = refs[:8]
    mixed_hbm, grad_hbm, red, small = refs[8:12]
    (
        w, masters, mine, other, core_in, both, x_in, tok, cot, tail_in, wide_tok, wide_cot, x_pool, x_norm, x_att,
        x_two, x_act, x_short, d_up, d_low, d_inner, d_res, d_qkv, d_pool, pooled, hat_one, hat_two, root_one, root_two,
        resid, hidden, short_grad, res_grad, q_out, q_in, a_out, a_in, da_out, da_in, dq_out, dq_in, probs, mixed, grad,
        wide_up, wide_grad, edge_in, x_near, x_wide, t_left, t_out, t_in, u_out, u_in, dx_out, dx_in, g, right_in, left_in, fin_out, fin_in, co_out, co_in, sums, sums_in, sends, recvs, local,
    ) = refs[12:]
    half = features // 2
    width = features // heads
    rows_of = masters.shape[1]
    count = heads
    tokens = 3 * units
    own = micros * units
    pair_width = 2 * width
    b, s = lax.axis_index("batch"), lax.axis_index("seq")
    x, c = b // 2, b % 2
    z, y = s // 2, s % 2
    spot = y * (7 - 2 * z) + z

    def seq_of(position):
        far = position // 4
        return 2 * (position + far * (7 - 2 * position)) + far

    def at(offset):
        return lax.rem(spot + offset + 2 * count, count)

    def rows_at(offset, part=0, length=rows_of):
        return pl.ds(pl.multiple_of(seq_of(at(offset)) * rows_of + part, 16), length)

    my_half = pl.ds(pl.multiple_of(c * half, half), half)
    other_half = pl.ds(pl.multiple_of((1 - c) * half, half), half)
    core_peer = (x * 2 + 1 - c, s)
    x_peer = ((1 - x) * 2 + c, s)
    cross_peer = ((1 - x) * 2 + 1 - c, s)
    right_peer = (b, seq_of(at(1)))
    left_peer = (b, seq_of(at(-1)))
    plan = Plan()
    flying, started, boxes = {}, [], {}

    def launch(name, copies, starts, group):
        if len(started) >= SENDS:
            started[len(started) - SENDS].wait_send()
        started.append(copies[0])
        flying[name] = copies[0]
        for start in starts:
            start()

    def describe(source, target, device, group):
        box = boxes.setdefault(group, len(boxes))
        return pltpu.make_async_remote_copy(
            src_ref=source,
            dst_ref=target,
            send_sem=sends.at[len(started) % SENDS],
            recv_sem=recvs.at[box],
            device_id=device,
            device_id_type=MESH,
        )

    def send(name, source, target, device, group=None):
        copy = describe(source, target, device, group or name)
        launch(name, [copy], [copy.start], group or name)

    def gather_up(group, whole):
        describe(whole, whole, core_peer, group).wait_recv()

    loads = [
        pltpu.make_async_copy(master_hbm, masters, local.at[0]),
        pltpu.make_async_copy(tok_hbm, tok, local.at[1]),
        pltpu.make_async_copy(cot_hbm, cot, local.at[2]),
    ]
    for copy in loads:
        copy.start()
    barrier = pltpu.get_barrier_semaphore()
    for step in range(1, count):
        pl.semaphore_signal(
            barrier, inc=1, device_id=(b, lax.rem(s + step, count)), device_id_type=MESH
        )
    for device in (core_peer, x_peer, cross_peer):
        pl.semaphore_signal(barrier, inc=1, device_id=device, device_id_type=MESH)
    pl.semaphore_wait(barrier, count + 2)

    spans, first = [], 0
    for size in sizes:
        spans.append((first, first + size))
        first += size
    in_base, back_base, up_base = spans[3][0], spans[4][0], spans[5][0]
    hidden_blocks = sizes[3]
    ours = in_base + x * hidden_blocks
    theirs = in_base + (1 - x) * hidden_blocks
    plan.add("ms", loads[0].wait, cost=0.5)

    def contribute(k):
        def run():
            lo, hi = spans[k]
            mask = (owners[k] == b).astype(WIDE)
            begin = start_of(owners, k, sizes)
            for block in range(lo, hi):
                slot = jnp.minimum(begin + (block - lo), masters.shape[0] - 1)
                mine[block] = (masters[slot, :, my_half] * mask).astype(LOW)
                other[block] = (masters[slot, :, other_half] * mask).astype(LOW)
            send(("g0", k), other.at[lo:hi], core_in.at[lo:hi], core_peer)

        return run

    def join_cores(k):
        def run():
            lo, hi = spans[k]
            flying[("g0", k)].wait_recv()
            both[lo:hi] = mine[lo:hi] + core_in[lo:hi]

        return run

    have = {k: [] for k in range(6)}
    gathers = []
    for k, offset, size, rank in GATHERS:
        name = ("w", k, offset)
        if k == 3:
            gathers.append((rank, name, (3, 4), ours + offset, theirs + offset, size))
            have[3] += [("h", name), ("hy", name)]
        else:
            begin = spans[k][0] + offset
            gathers.append((rank, name, (k,), begin, begin if k == 5 else None, size))
            have[k] += [("h", name)]
    piece_bytes = rows_of * half * 2

    quarter = half // 2
    plane_span = pl.ds(pl.multiple_of(x * quarter, quarter), quarter)
    plane_away = pl.ds(pl.multiple_of((1 - x) * quarter, quarter), quarter)

    def gather_chunk(rank, name, parents, here, there, size):
        quarters = there is here
        split = there is not None and not quarters
        load = size * piece_bytes // (2 if quarters else 1)
        blocks = pl.ds(here, size)
        away = pl.ds(there, size) if split else blocks
        span, away_span = (plane_span, plane_away) if quarters else (slice(None), slice(None))

        def piece(offset, part=0, length=rows_of):
            return w.at[blocks, c, rows_at(offset, part, length), span]

        def join_here():
            send(("g1", name), both.at[away, :, away_span], x_in.at[away, :, away_span], x_peer)

        def join_x():
            flying[("g1", name)].wait_recv()
            w[blocks, c, rows_at(0), span] = both[blocks, :, span] + x_in[blocks, :, span]
            send(("R", 1, name), piece(0), piece(0), right_peer, (1, name))
            send(("L", 1, name), piece(0), piece(0), left_peer, (1, name))

        def onward(step):
            def run():
                gather_up((step - 1, name), w.at[blocks, c, 0 : rows_of * (2 if step < 5 else 1), span])
                if step == 5:
                    return
                for side, offset, peer in (("R", 1 - step, right_peer), ("L", step - 1, left_peer)):
                    part = piece(offset)
                    if step == 4:
                        part = piece(offset, 0 if side == "R" else rows_of // 2, rows_of // 2)
                    send((side, step, name), part, part, peer, (step, name))

            return run

        def across(step):
            def run():
                for side, offset in (("R", -step), ("L", step)):
                    part = piece(offset)
                    if step == 4:
                        part = piece(offset, 0 if side == "R" else rows_of // 2, rows_of // 2)
                    if step > 0 or side == "R":
                        send(("X", side, step, name), part, part, x_peer, ("X", name))

            return run

        def distribute(which, held, lanes):
            def run():
                send((which, name), w.at[held, c, :, lanes], w.at[held, c, :, lanes], core_peer)

            return run

        plan.add(("cx", name), join_here, [("cs", k) for k in parents], (), [(("g1", name), "x", load)], 0.05, rank)
        plan.add(
            ("x", name), join_x, [("cx", name)], [("g1", name)],
            [(("R", 1, name), "r", load), (("L", 1, name), "l", load)], 0.05, rank,
        )
        crossing = []

        def cross(step, after):
            messages = [("X", side, step, name) for side in ("RL" if step else "R")]
            size_of = load if step < 4 else load // 2
            plan.add(("X", step, name), across(step), [after], (), [(m, "x", size_of) for m in messages], 0.05, rank + 0.05)
            crossing.extend(messages)

        if split:
            cross(0, ("x", name))
        for step in (2, 3, 4, 5):
            size_of = load if step < 4 else load // 2
            out = [((side, step, name), link, size_of) for side, link in (("R", "r"), ("L", "l"))] if step < 5 else []
            before = ("x", name) if step == 2 else (step - 1, "f", name)
            waits = [(side, step - 1, name) for side in "RL"]
            plan.add((step, "f", name), onward(step), [before], waits, out, 0.05, rank)
            if split:
                cross(step - 1, (step, "f", name))
        plan.add(("di", name), distribute("D", blocks, span), [(5, "f", name)], (), [(("D", name), "c", 8 * load)], 0.05, rank)
        plan.add(("h", name), arrive(("D", name)), [("di", name)], [("D", name)], (), 0.02, rank)
        if split:
            whole = w.at[away, c, :, away_span]
            last = [("X", step, name) for step in range(5)]
            plan.add(("xw", name), lambda: gather_up(("X", name), whole), last, crossing, (), 0.05, rank)
            plan.add(("dy", name), distribute("E", away, away_span), [("xw", name)], (), [(("E", name), "c", 8 * load)], 0.05, rank)
            plan.add(("hy", name), arrive(("E", name)), [("dy", name)], [("E", name)], (), 0.02, rank)

    def arrive(*names):
        def run():
            for name in names:
                flying[name].wait_recv()

        return run

    for k in (0, 1, 3, 4, 2, 5):
        lo, hi = spans[k]
        load = (hi - lo) * piece_bytes
        plan.add(("co", k), contribute(k), ["ms"], (), [(("g0", k), "c", load)], 0.04 * (hi - lo), 0.1)
        plan.add(("cs", k), join_cores(k), [("co", k)], [("g0", k)], (), 0.02 * (hi - lo), 0.1)
    for chunk in gathers:
        gather_chunk(*chunk)

    def exchange(name, buffer):
        send(name, buffer.at[0:own], buffer.at[own : 2 * own], core_peer)

    def shared(name, columns):
        return (name, "c", own * columns * 2)

    lead = 16
    tiles = range(features // TILE)

    def columns_at(tile, base=0):
        return slice(base + tile * TILE, base + (tile + 1) * TILE)

    def ends_of(micro):
        ends = []
        total = jnp.int32(0)
        for index in range(docs.shape[1] - 1):
            total = total + docs[micro, index]
            ends.append(total)
        return ends

    def kept(micro):
        ids = s * units + lax.broadcasted_iota(jnp.int32, (units, 1), 0)
        starts = (ids == 0).astype(jnp.int32)
        for end in ends_of(micro):
            starts = starts | (ids == end).astype(jnp.int32)
        return starts == 0

    def load_tokens():
        loads[1].wait()
        send("tl", tok.at[:, tokens - lead :], tail_in, (b, lax.rem(s + 1, count)))
        for micro in range(micros):
            for tile in tiles:
                wide_tok[micro, tile, lead:] = tok[micro, :, columns_at(tile)].astype(WIDE)

    def load_cotangent():
        loads[2].wait()
        for micro in range(micros):
            for tile in tiles:
                wide_cot[micro, tile] = cot[micro, :, columns_at(tile)].astype(WIDE)
                for r in range(3):
                    d_up[micro * units : (micro + 1) * units, columns_at(tile, r * features)] = wide_cot[
                        micro, tile, pl.ds(r, units, stride=3), :
                    ].astype(LOW)
        exchange("eu", d_up)

    def make_pieces():
        flying["tl"].wait_recv()
        for micro in range(micros):
            keep = kept(micro)
            for tile in tiles:
                wide_tok[micro, tile, :lead] = tail_in[micro, :, columns_at(tile)].astype(WIDE)
                for r in range(3):
                    part = wide_tok[micro, tile, pl.ds(lead - 2 + r, units, stride=3), :]
                    if r < 2:
                        part = jnp.where(keep, part, 0.0)
                    x_pool[micro * units : (micro + 1) * units, columns_at(tile, r * features)] = part.astype(LOW)
        exchange("ep", x_pool)

    plan.add("tok", load_tokens, sends=[("tl", "f", 2 * lead * features * 2)], cost=0.3, rank=1)
    plan.add(
        "pc", make_pieces, ["tok"], ["tl"], [shared("ep", 3 * features)], 0.5, rank=1
    )
    plan.add("cot", load_cotangent, (), (), [shared("eu", 3 * features)], 0.5, rank=2)

    def normal(value, which, hat, root):
        centred = value - over_last(jnp.mean, value)
        scale = lax.rsqrt(over_last(jnp.mean, centred * centred) + ln_eps)
        unit = centred * scale
        hat[...] = unit
        root[...] = scale
        return (unit * gain[which : which + 1, :] + bias[which : which + 1, :]).astype(LOW)

    def both_halves(make):
        return jnp.concatenate([make(0), make(1)], axis=1)

    def pool():
        def side(h):
            total = None
            for r in range(3):
                term = contract(x_pool[0:own, r * features : (r + 1) * features], w[r, h], 1, 0)
                total = term if total is None else total + term
            return total

        value = both_halves(side)
        pooled[...] = value
        x_norm[0:own] = normal(value, 0, hat_one, root_one)
        exchange("en", x_norm)

    lane = lambda: lax.broadcasted_iota(jnp.int32, (1, pair_width), 1)

    def swap(value):
        return pltpu.roll(value, width, axis=1)

    def to_heads(tile, target, pair, row):
        low_lanes = lane() < width
        first, second = tile[:units], tile[units:]
        target[2 * pair, row : row + units] = jnp.where(low_lanes, first, swap(second)).astype(LOW)
        target[2 * pair + 1, row : row + units] = jnp.where(low_lanes, swap(first), second).astype(LOW)

    def from_heads(source, pair, row):
        low_lanes = lane() < width
        even = source[2 * pair, row : row + units].astype(WIDE)
        odd = source[2 * pair + 1, row : row + units].astype(WIDE)
        return jnp.where(low_lanes, even, swap(odd)).astype(LOW), jnp.where(low_lanes, swap(even), odd).astype(LOW)

    def spread(name, source, target):
        for step in range(1, count):
            there = lax.rem(s + step, count)
            send((name, step), source.at[there], target.at[s], (b, there), name)
        target[s] = source[s]

    def spread_names(name):
        return [(name, step) for step in range(1, count)]

    def spread_sends(name, rows):
        return [((name, step), "f", rows * pair_width * 2) for step in range(1, count)]

    def project():
        for part in range(3):
            for h in range(2):
                value = contract(x_norm[0:own], w[3 + part, h], 1, 0)
                for tile in range(half // pair_width):
                    to_heads(
                        value[:, tile * pair_width : (tile + 1) * pair_width],
                        q_out,
                        h * (half // pair_width) + tile,
                        part * units,
                    )
        spread("q", q_out, q_in)

    lane_units = units * count

    def heads_of(source, part):
        return source[:, part * units : (part + 1) * units, :].reshape(lane_units, pair_width)

    def lanes_of(micro):
        return (lane() // width == micro).astype(WIDE).astype(LOW)

    def distances():
        row_ids = lax.broadcasted_iota(jnp.int32, (lane_units, lane_units), 0)
        col_ids = lax.broadcasted_iota(jnp.int32, (lane_units, lane_units), 1)
        return row_ids - col_ids

    def attend_now():
        gather_up("q", q_in.at[0 : count - 1])
        queries, keys, values = (heads_of(q_in, part) for part in range(3))
        slope = slopes[s]
        total = None
        for micro in range(micros):
            gap = distances()
            row_seg = jnp.zeros((lane_units, 1), jnp.int32)
            col_seg = jnp.zeros((1, lane_units), jnp.int32)
            for end in ends_of(micro):
                row_seg += (lax.broadcasted_iota(jnp.int32, (lane_units, 1), 0) >= end).astype(jnp.int32)
                col_seg += (lax.broadcasted_iota(jnp.int32, (1, lane_units), 1) >= end).astype(jnp.int32)
            allowed = (row_seg == col_seg) & (gap >= 0)
            mask = lanes_of(micro)
            raw = contract(queries * mask, keys, 1, 1) * 0.125 - slope * gap.astype(WIDE)
            scores = jnp.where(allowed, raw, masked_score)
            raised = jnp.exp(scores - over_last(jnp.max, scores))
            probability = raised / over_last(jnp.sum, raised)
            probs[micro] = probability
            term = contract(probability.astype(LOW), values * mask, 1, 0)
            total = term if total is None else total + term
        a_out[...] = total.astype(LOW).reshape(count, units, pair_width)
        spread("a", a_out, a_in)

    def merge():
        gather_up("a", a_in.at[0 : count - 1])
        for pair in range(heads // 2):
            columns = slice(pair * pair_width, (pair + 1) * pair_width)
            first, second = from_heads(a_in, pair, 0)
            x_att[0:units, columns] = first
            x_att[units:own, columns] = second
        exchange("ea", x_att)

    def project_out():
        value = pooled[...] + both_halves(lambda h: contract(x_att[0:own], w[6, h], 1, 0))
        resid[...] = value
        x_two[0:own] = normal(value, 1, hat_two, root_two)
        exchange("et", x_two)


    def widen(j):
        def run():
            for h in range(2):
                columns = slice(j * features + h * half, j * features + (h + 1) * half)
                value = contract(x_two[0:own], w[in_base + j, h], 1, 0)
                hidden[:, columns] = value
                inner, _ = gelu_parts(value)
                x_act[0:own, columns] = (0.5 * value * (1.0 + inner)).astype(LOW)
            if j == hidden_blocks - 1:
                exchange("ec", x_act)

        return run

    def narrow():
        def side(h):
            total = resid[:, h * half : (h + 1) * half]
            for j in range(hidden_blocks):
                total = total + contract(
                    x_act[0:own, j * features : (j + 1) * features], w[back_base + j, h], 1, 0
                )
            return total

        x_short[0:own] = both_halves(side).astype(LOW)
        exchange("es", x_short)

    outs = [
        pltpu.make_async_copy(mixed, mixed_hbm, local.at[3]),
        pltpu.make_async_copy(grad, grad_hbm, local.at[4]),
    ]

    def place_up(r, value, core, plane):
        for micro in range(micros):
            wide_up[micro, 2 * core + plane, pl.ds(r, units, stride=3), :] = value[micro * units : (micro + 1) * units]

    def lift_away():
        for r in range(3):
            for core in range(2):
                value = contract(t_left[QUARTERS[5], 0:own], w[up_base + r, core, :, plane_span], 1, 0)
                u_out[:, (2 * r + core) * quarter : (2 * r + core + 1) * quarter] = value.astype(LOW)
        send("ux", u_out, u_in, x_peer)

    def lift(r):
        def run():
            for core in range(2):
                place_up(r, contract(x_short[0:own], w[up_base + r, core, :, plane_span], 1, 0), core, x)

        return run

    def finish_mixed():
        arrive("ux")()
        for r in range(3):
            for core in range(2):
                begin = (2 * r + core) * quarter
                place_up(r, u_in[:, begin : begin + quarter].astype(WIDE), core, 1 - x)
        for micro in range(micros):
            for tile in tiles:
                columns = columns_at(tile)
                mixed[micro, :, columns] = tok[micro, :, columns].astype(WIDE) + wide_up[micro, tile]
        outs[0].start()

    plan.add("po", pool, ["pc", *have[0]], (), [shared("en", features)], 0.6, rank=3)
    plan.add("pr", project, ["po", *have[1]], (), spread_sends("q", 3 * units), 0.6, rank=3)
    plan.add("at", attend_now, ["pr"], spread_names("q"), spread_sends("a", units), 1.1, rank=3)
    plan.add("me", merge, ["at"], spread_names("a"), [shared("ea", features)], 0.15, rank=3)
    plan.add("ou", project_out, ["me", *have[2]], (), [shared("et", features)], 0.45, rank=3)
    for j in range(hidden_blocks):
        last = j == hidden_blocks - 1
        plan.add(
            ("wi", j), widen(j), ["ou", *have[3]] + ([("wi", i) for i in range(j)] if last else []), (),
            [shared("ec", hidden_width)] if last else (), 0.3, rank=3,
        )
    plan.add(
        "na", narrow, [("wi", j) for j in range(hidden_blocks)] + [*have[3]], (), [shared("es", features)], 0.5,
        rank=3,
    )
    for r in range(3):
        plan.add(("li", r), lift(r), ["na", *have[5]], (), (), 0.2, rank=8)
    quarter_lump = own * 3 * half * 2
    plan.add("lq", lift_away, [("tw", 5, 0), *have[5]], (), [("ux", "x", quarter_lump)], 0.6, rank=8)
    plan.add("lf", finish_mixed, ["lq", "tok"] + [("li", r) for r in range(3)], ["ux"], (), 0.4, rank=8)

    def back_short_away():
        total = None
        for r in range(3):
            for core in range(2):
                columns = slice(core * quarter, (core + 1) * quarter)
                term = contract(t_in[QUARTERS[5] + r, 0:own, columns], w[up_base + r, core, :, plane_span], 1, 1)
                total = term if total is None else total + term
        dx_out[...] = total.astype(LOW)
        send("dx", dx_out, dx_in, x_peer)

    def back_short_here():
        total = None
        for r in range(3):
            for core in range(2):
                columns = pl.ds(pl.multiple_of(r * features + core * half + x * quarter, quarter), quarter)
                term = contract(d_up[0:own, columns], w[up_base + r, core, :, plane_span], 1, 1)
                total = term if total is None else total + term
        short_grad[...] = total

    def back_short():
        arrive("dx")()
        total = short_grad[...] + dx_in[...].astype(WIDE)
        short_grad[...] = total
        d_low[0:own] = total.astype(LOW)
        exchange("el", d_low)

    def back_widen(j):
        def run():
            total = contract(d_low[0:own, 0:half], w[back_base + j, 0], 1, 1)
            total = total + contract(d_low[0:own, half:features], w[back_base + j, 1], 1, 1)
            columns = slice(j * features, (j + 1) * features)
            value = hidden[:, columns]
            inner, slope = gelu_parts(value)
            factor = 0.5 * (1.0 + inner) + 0.5 * value * (1.0 - inner * inner) * slope
            d_inner[0:own, columns] = (total * factor).astype(LOW)
            if j == hidden_blocks - 1:
                exchange("ei", d_inner)

        return run

    def back_normal(value, which, hat, root):
        unit = hat[...]
        sums[which : which + 1, :] = jnp.sum(value * unit, axis=0, keepdims=True)
        sums[2 + which : 3 + which, :] = jnp.sum(value, axis=0, keepdims=True)
        scaled = value * gain[which : which + 1, :]
        return root[...] * (
            scaled - over_last(jnp.mean, scaled) - unit * over_last(jnp.mean, scaled * unit)
        )

    def back_two():
        total = None
        for j in range(hidden_blocks):
            for h in range(2):
                begin = j * features + h * half
                term = contract(d_inner[0:own, begin : begin + half], w[in_base + j, h], 1, 1)
                total = term if total is None else total + term
        value = short_grad[...] + back_normal(total, 1, hat_two, root_two)
        res_grad[...] = value
        d_res[0:own] = value.astype(LOW)
        exchange("er", d_res)

    def back_out():
        value = contract(d_res[0:own, 0:half], w[6, 0], 1, 1)
        value = value + contract(d_res[0:own, half:features], w[6, 1], 1, 1)
        for pair in range(heads // 2):
            to_heads(value[:, pair * pair_width : (pair + 1) * pair_width], da_out, pair, 0)
        spread("da", da_out, da_in)

    def back_attend():
        gather_up("da", da_in.at[0 : count - 1])
        queries, keys, values = (heads_of(q_in, part) for part in range(3))
        grads = da_in[...].reshape(lane_units, pair_width)
        totals = [None, None, None]
        slope_total = jnp.zeros((1, 1), WIDE)
        for micro in range(micros):
            mask = lanes_of(micro)
            own_grads = grads * mask
            probability = probs[micro]
            grad_prob = contract(own_grads, values, 1, 1)
            scaled = probability * grad_prob
            score = scaled - probability * over_last(jnp.sum, scaled)
            low_score = score.astype(LOW)
            gap = distances().astype(WIDE)
            slope_total = slope_total - jnp.sum(
                jnp.sum(low_score.astype(WIDE) * gap, axis=0, keepdims=True), axis=1, keepdims=True
            )
            terms = (
                contract(low_score, keys * mask, 1, 0) * 0.125,
                contract(low_score, queries * mask, 0, 0) * 0.125,
                contract(probability.astype(LOW), own_grads, 0, 0),
            )
            totals = [term if total is None else total + term for total, term in zip(totals, terms)]
        for part in range(3):
            dq_out[:, part * units : (part + 1) * units, :] = (
                totals[part].astype(LOW).reshape(count, units, pair_width)
            )
        spread("dq", dq_out, dq_in)
        places = lax.broadcasted_iota(jnp.int32, (1, features), 1)
        sums[4:5, :] = jnp.where(places == s, slope_total, 0.0)
        sums[5:8, :] = jnp.zeros((3, features), WIDE)

    def back_project():
        gather_up("dq", dq_in.at[0 : count - 1])
        for part in range(3):
            for pair in range(heads // 2):
                begin = part * features + pair * pair_width
                first, second = from_heads(dq_in, pair, part * units)
                d_qkv[0:units, begin : begin + pair_width] = first
                d_qkv[units:own, begin : begin + pair_width] = second
        exchange("eq", d_qkv)

    def back_one():
        total = None
        for part in range(3):
            for h in range(2):
                begin = part * features + h * half
                term = contract(d_qkv[0:own, begin : begin + half], w[3 + part, h], 1, 1)
                total = term if total is None else total + term
        value = res_grad[...] + back_normal(total, 0, hat_one, root_one)
        d_pool[0:own] = value.astype(LOW)
        exchange("ed1", d_pool)

    def back_pieces():
        for r in range(3):
            value = contract(d_pool[0:own, 0:half], w[r, 0], 1, 1)
            value = value + contract(d_pool[0:own, half:features], w[r, 1], 1, 1)
            for micro in range(micros):
                part = value[micro * units : (micro + 1) * units]
                if r < 2:
                    part = jnp.where(kept(micro), part, 0.0)
                for tile in tiles:
                    wide_grad[micro, tile, pl.ds(6 + r, units, stride=3), :] = part[:, columns_at(tile)]
        send("ed", wide_grad.at[:, :, 0:8], edge_in, (b, lax.rem(s + count - 1, count)))

    def finish_grad():
        flying["ed"].wait_recv()
        inside = (s < count - 1).astype(WIDE)
        for micro in range(micros):
            for tile in tiles:
                columns = columns_at(tile)
                wide_grad[micro, tile, 6 + tokens : 8 + tokens, :] = edge_in[micro, tile, 6:8, :] * inside
                grad[micro, :, columns] = cot[micro, :, columns].astype(WIDE) + wide_grad[micro, tile, 8 : 8 + tokens]
        outs[1].start()

    plan.add(
        "bq", back_short_away, [("tz", 5, r) for r in range(3)] + have[5], (), [("dx", "x", own * features * 2)], 0.6, rank=2
    )
    plan.add("bh", back_short_here, ["cot", *have[5]], (), (), 0.6, rank=3)
    plan.add("bs", back_short, ["bq", "bh"], ["dx"], [shared("el", features)], 0.1, rank=3)
    for j in range(hidden_blocks):
        last = j == hidden_blocks - 1
        plan.add(
            ("bw", j), back_widen(j),
            ["bs", *have[3], ("wi", j)] + ([("bw", i) for i in range(j)] if last else []), (),
            [shared("ei", hidden_width)] if last else (), 0.35, rank=4,
        )
    plan.add(
        "b2", back_two, [("bw", j) for j in range(hidden_blocks)] + [*have[3]], (),
        [shared("er", features)], 0.9, rank=4,
    )
    plan.add("bo", back_out, ["b2", *have[2]], (), spread_sends("da", units), 0.45, rank=4)
    plan.add("ba", back_attend, ["bo", "at"], spread_names("da"), spread_sends("dq", 3 * units), 1.4, rank=4)
    plan.add("bp", back_project, ["ba"], spread_names("dq"), [shared("eq", 3 * features)], 0.2, rank=4)
    plan.add("b1", back_one, ["bp"], (), [shared("ed1", features)], 0.75, rank=4)
    plan.add("bx", back_pieces, ["b1"], (), [("ed", "f", 2 * 8 * features * 4)], 0.65, rank=9)
    plan.add("fg", finish_grad, ["bx", "cot"], ["ed"], (), 0.3, rank=9)

    def add_pair(step, device):
        def run():
            if step > 0:
                flying[("s", step - 1)].wait_recv()
                sums[8 * step : 8 * step + 8] = sums[8 * step - 8 : 8 * step] + sums_in[8 * step - 8 : 8 * step]
            if device is not None:
                send(("s", step), sums.at[8 * step : 8 * step + 8], sums_in.at[8 * step : 8 * step + 8], device)
            else:
                small[...] = sums[8 * step : 8 * step + 8]

        return run

    partners = [
        core_peer,
        x_peer,
        (b, 2 * z + 1 - y),
        (b, 2 * (z + 1 - 2 * (z % 2)) + y),
        (b, 2 * lax.rem(z + 2, 4) + y),
        None,
    ]
    for step, device in enumerate(partners):
        plan.add(
            ("sum", step), add_pair(step, device), ["b1", "ba"] if step == 0 else [("sum", step - 1)],
            [("s", step - 1)] if step else (), [(("s", step), "f", 8 * features * 4)] if device is not None else (), 0.1,
            rank=0,
        )

    for name, columns in (
        ("ep", "pc"), ("en", "po"), ("ea", "me"), ("et", "ou"), ("ec", ("wi", hidden_blocks - 1)),
        ("es", "na"), ("eu", "cot"), ("el", "bs"), ("ei", ("bw", hidden_blocks - 1)),
        ("er", "b2"), ("eq", "bp"), ("ed1", "b1"),
    ):
        plan.add(("got", name), arrive(name), [columns], [name], cost=0.02)

    def columns_of(block):
        return pl.ds(pl.multiple_of(block * features + c * half, half), half)

    def outer(block, left, left_block, right, right_block):
        def run():
            rows = left[:, left_block * features : (left_block + 1) * features]
            g[block] = contract(rows, right[:, columns_of(right_block)], 0, 0).astype(LOW)

        return run

    def send_either(name, first_source, second_source, target):
        copies = [describe(source, target, x_peer, name) for source in (first_source, second_source)]
        launch(name, copies, [lambda plane=plane: pl.when(x == plane)(copies[plane].start) for plane in range(2)], name)

    def near_away():
        send_either("sn", d_low.at[0:own], x_two.at[0:own], x_near.at[0:own])

    def near_core():
        arrive("sn")()
        exchange("cn", x_near)

    def wide_away(j):
        columns = slice(j * features, (j + 1) * features)

        def run():
            source = (x_act.at[0:own, columns], d_inner.at[0:own, columns])
            send_either(("sw", j), *source, x_wide.at[0:own, columns])

        return run

    def wide_core(j):
        columns = slice(j * features, (j + 1) * features)

        def run():
            arrive(("sw", j))()
            send(("cw", j), x_wide.at[0:own, columns], x_wide.at[own : 2 * own, columns], core_peer)

        return run

    def outer_split(j):
        columns = slice(j * features, (j + 1) * features)

        def run():
            @pl.when(x == 0)
            def _():
                total = contract(x_two[...], d_inner[:, columns_of(j)], 0, 0)
                g[in_base + j] = (total + contract(x_near[...], x_wide[:, columns_of(j)], 0, 0)).astype(LOW)

            @pl.when(x == 1)
            def _():
                total = contract(x_act[:, columns], d_low[:, my_half], 0, 0)
                g[back_base + j] = (total + contract(x_wide[:, columns], x_near[:, my_half], 0, 0)).astype(LOW)

        return run

    lump = own * features * 2
    plan.add("sn", near_away, ["bs", "ou"], (), [("sn", "x", lump)], 0.05, 2)
    plan.add("nc", near_core, ["sn"], ["sn"], [("cn", "c", lump)], 0.05, 2)
    plan.add(("got", "cn"), arrive("cn"), ["nc"], ["cn"], (), 0.02, 2)
    for j in range(hidden_blocks):
        plan.add(("sw", j), wide_away(j), [("wi", j), ("bw", j)], (), [(("sw", j), "x", lump)], 0.05, 2)
        plan.add(("wc", j), wide_core(j), [("sw", j)], [("sw", j)], [(("cw", j), "c", lump)], 0.05, 2)
        plan.add(("got", "cw", j), arrive(("cw", j)), [("wc", j)], [("cw", j)], (), 0.02, 2)
        deps = [("got", e) for e in ("et", "ec", "el", "ei", "cn")] + [("got", "cw", j)]
        plan.add(("gr", j, "s"), outer_split(j), deps, cost=0.6, rank=4.5)
    quartered = {
        0: (x_pool, 3, d_pool, 1, "pc", "b1", "ep", "ed1"),
        1: (x_norm, 1, d_qkv, 3, "po", "bp", "en", "eq"),
        2: (x_att, 1, d_res, 1, "me", "b2", "ea", "er"),
        5: (x_short, 1, d_up, 3, "na", "cot", "es", "eu"),
    }
    quartered = {k: quartered[k] for k in QUARTERS}

    def left_away(k, j):
        columns = slice(j * features, (j + 1) * features)

        def run():
            send(("tx", k, j), quartered[k][0].at[0:own, columns], t_left.at[QUARTERS[k] + j, 0:own], x_peer)

        return run

    def left_core(k, j):
        place = QUARTERS[k] + j

        def run():
            arrive(("tx", k, j))()
            send(("tc", k, j), t_left.at[place, 0:own], t_left.at[place, own : 2 * own], core_peer)

        return run

    def right_away(k, r):
        place = QUARTERS[k] + r

        def run():
            for core in range(2):
                begin = r * features + core * half + (1 - x) * quarter
                t_out[place, :, core * quarter : (core + 1) * quarter] = quartered[k][2][
                    0:own, pl.ds(pl.multiple_of(begin, quarter), quarter)
                ]
            if k == 5:
                send(("ty", k, r), t_out.at[place], t_in.at[place, 0:own], x_peer)
                return
            lanes = [pl.ds(pl.multiple_of(core * quarter, quarter), quarter) for core in (c, 1 - c)]
            send(("ty", k, r), t_out.at[place, :, lanes[0]], t_in.at[place, 0:own, 0:quarter], x_peer, ("ty", k, r))
            send(("tu", k, r), t_out.at[place, :, lanes[1]], t_in.at[place, own : 2 * own, 0:quarter], cross_peer, ("ty", k, r))

        return run

    def right_core(k, r):
        place = QUARTERS[k] + r

        def run():
            arrive(("ty", k, r))()
            send(("td", k, r), t_in.at[place, 0:own], t_in.at[place, own : 2 * own], core_peer)

        return run

    def outer_quarter(k, j, r):
        def run():
            left, _, right = quartered[k][:3]
            near = pl.ds(pl.multiple_of(r * features + c * half + x * quarter, quarter), quarter)
            away = pl.ds(pl.multiple_of(c * quarter, quarter), quarter) if k == 5 else slice(0, quarter)
            total = contract(left[:, j * features : (j + 1) * features], right[:, near], 0, 0)
            total = total + contract(t_left[QUARTERS[k] + j], t_in[QUARTERS[k] + r, :, away], 0, 0)
            g[spans[k][0] + j + r, :, plane_span] = total.astype(LOW)

        return run

    for k, (_, lefts, _, rights, left_dep, right_dep, left_got, right_got) in quartered.items():
        urgency = 3.5 if k == 0 else 2.5
        for j in range(lefts):
            plan.add(("tx", k, j), left_away(k, j), [left_dep] + list(AFTER.get(k, ())), (), [(("tx", k, j), "x", lump)], 0.05, urgency)
            plan.add(("tw", k, j), left_core(k, j), [("tx", k, j)], [("tx", k, j)], [(("tc", k, j), "c", lump)], 0.05, urgency)
            plan.add(("got", "tc", k, j), arrive(("tc", k, j)), [("tw", k, j)], [("tc", k, j)], (), 0.02, urgency)
        for r in range(rights):
            if k != 5:
                parts = [("ty", k, r), ("tu", k, r)]
                whole = t_in.at[QUARTERS[k] + r, :, 0:quarter]
                plan.add(parts[0], right_away(k, r), [right_dep], (), [(p, "x", lump // 4) for p in parts], 0.1, 2.5)
                take = lambda k=k, r=r, whole=whole: gather_up(("ty", k, r), whole)
                plan.add(("got", "td", k, r), take, parts[:1], parts, (), 0.02, 2.5)
                continue
            plan.add(("ty", k, r), right_away(k, r), [right_dep], (), [(("ty", k, r), "x", lump // 2)], 0.05, 2.5)
            plan.add(("tz", k, r), right_core(k, r), [("ty", k, r)], [("ty", k, r)], [(("td", k, r), "c", lump // 2)], 0.05, 2.5)
            plan.add(("got", "td", k, r), arrive(("td", k, r)), [("tz", k, r)], [("td", k, r)], (), 0.02, 2.5)
        for j in range(lefts if k not in WHOLE else 0):
            for r in range(rights):
                deps = [("got", left_got), ("got", right_got), ("got", "tc", k, j), ("got", "td", k, r)]
                plan.add(("gr", spans[k][0] + j + r), outer_quarter(k, j, r), deps, cost=0.4, rank=5)
    weight_grads = []
    for r in range(3):
        for k, left, left_block, right, right_block, deps in (
            (0, x_pool, r, d_pool, 0, ("ep", "ed1")), (1, x_norm, 0, d_qkv, r, ("en", "eq")),
            (2, x_att, 0, d_res, 0, ("ea", "er")), (5, x_short, 0, d_up, r, ("es", "eu")),
        ):
            if (k in WHOLE or k not in QUARTERS) and r < sizes[k]:
                deps = [("got", dep) for dep in deps]
                weight_grads.append((spans[k][0] + r, left, left_block, right, right_block, deps))
    for block, left, left_block, right, right_block, deps in weight_grads:
        plan.add(("gr", block), outer(block, left, left_block, right, right_block), deps, cost=0.3, rank=5)

    def scatter_chunk(rank, name, here, there, size, deps):
        split, quarters = there is not None, there is here
        blocks = pl.ds(here, size)
        load = size * piece_bytes // (2 if quarters else 1)
        away, span, away_span, length_out = blocks, slice(None), slice(None), half
        begin_out, away_out = c * half, c * half
        if quarters:
            span, away_span = plane_span, plane_away
            length_out, begin_out, away_out = quarter, c * half + x * quarter, c * half + (1 - x) * quarter
        elif split:
            away = pl.ds(there, size)
        out_span = pl.ds(pl.multiple_of(begin_out, length_out), length_out)
        out_away = pl.ds(pl.multiple_of(away_out, length_out), length_out)

        half_rows = rows_of // 2
        sides = (("R", 0, right_in, right_peer), ("L", half_rows, left_in, left_peer))

        def first_step():
            for side, part, inbox, peer in sides:
                source = g.at[blocks, rows_at(4, part, half_rows), span]
                target = inbox.at[0, blocks, part : part + half_rows, span]
                send((side, "s", 1, name), source, target, peer, ("s", 1, name))

        def take(step):
            gather_up(("s", step, name), g.at[blocks, 0 : rows_of * (1 if step == 1 else 2), span])

        def next_step(step):
            def run():
                take(step - 1)
                for side, half_part, inbox, peer in sides:
                    offset = (5 - step) if side == "R" else (step - 5)
                    part, length = (half_part, half_rows) if step == 2 else (0, rows_of)
                    rows = rows_at(offset, part, length)
                    g[blocks, rows, span] = g[blocks, rows, span] + inbox[step - 2, blocks, part : part + length, span]
                    source = g.at[blocks, rows_at(offset), span]
                    send((side, "s", step, name), source, inbox.at[step - 1, blocks, :, span], peer, ("s", step, name))

            return run

        def finish():
            take(4)
            total = g[blocks, rows_at(0), span].astype(WIDE)
            total = total + right_in[3, blocks, :, span].astype(WIDE) + left_in[3, blocks, :, span].astype(WIDE)
            fin_out[blocks, :, span] = total.astype(LOW)
            send(("rx", name), fin_out.at[blocks, :, span], fin_in.at[blocks, :, span], x_peer)
            if quarters:
                send(("rd", name), fin_out.at[blocks, :, span], co_in.at[blocks, :, span], cross_peer)
            if split:
                send(("rc", name), fin_out.at[blocks, :, span], co_in.at[blocks, :, span], core_peer)
                red[blocks, :, out_span] = fin_out[blocks, :, span]

        def finish_x():
            arrive(("rx", name))()
            if split:
                red[away, :, out_away] = fin_in[away, :, away_span]
                if not quarters:
                    send(("rd", name), fin_in.at[away, :, away_span], co_in.at[away, :, away_span], core_peer)
            else:
                total = (fin_out[blocks].astype(WIDE) + fin_in[blocks].astype(WIDE)).astype(LOW)
                co_out[blocks] = total
                red[blocks, :, my_half] = total
                send(("rc", name), co_out.at[blocks], co_in.at[blocks], core_peer)

        def finish_core():
            arrive(("rc", name), *([("rd", name)] if split else []))()
            red[blocks, :, other_half] = co_in[blocks]
            if split and not quarters:
                red[away, :, other_half] = co_in[away]

        links = (("R", "r"), ("L", "l"))
        out = [((side, "s", 1, name), link, load // 2) for side, link in links]
        plan.add(("r", 1, name), first_step, deps, (), out, 0.05, rank)
        for step in (2, 3, 4):
            waits = [(side, "s", step - 1, name) for side in "RL"]
            out = [((side, "s", step, name), link, load) for side, link in links]
            plan.add(("r", step, name), next_step(step), [("r", step - 1, name)], waits, out, 0.04 * size, rank)
        own_out = [(("rc", name), "c", load)]
        plan.add(
            ("fi", name), finish, [("r", 4, name)], [("R", "s", 4, name), ("L", "s", 4, name)],
            [(("rx", name), "x", load)] + (own_out if split else []) + ([(("rd", name), "x", load)] if quarters else []),
            0.02 * size, rank,
        )
        late_out = ([] if quarters else [(("rd", name), "c", load)]) if split else own_out
        plan.add(("fx", name), finish_x, [("fi", name)], [("rx", name)], late_out, 0.02 * size, rank)
        plan.add(
            ("fc", name), finish_core, [("fx", name)], [("rc", name)] + ([("rd", name)] if split else []), (), 0.02 * size, rank
        )

    for k, offset, size, rank in SCATTERS:
        name = ("g", k, offset)
        if k == 3:
            deps = [("gr", j, "s") for j in range(offset, offset + size)]
            scatter_chunk(rank, name, ours + offset, theirs + offset, size, deps)
        else:
            begin = spans[k][0] + offset
            scatter_chunk(rank, name, begin, begin if k in QUARTERS and k not in WHOLE else None, size, [("gr", begin + j) for j in range(size)])

    for name, _ in plan.order():
        plan.tasks[name][0]()
    assert len(boxes) <= RECEIVES
    for copy in started[-SENDS:]:
        copy.wait_send()
    for copy in outs:
        copy.wait()


def adam_kernel(sizes, refs):
    owners, red, small, gain, bias, norm_m, norm_v, slope, slope_m, slope_v, master, first, second, mixed, grad = refs[:15]
    (
        new_w, new_m, new_v, new_low, norm_out, norm_m_out, norm_v_out, slope_out, slope_m_out, slope_v_out, mixed_out,
        grad_out,
    ) = refs[15:]
    step = pl.program_id(0)
    fix_first = 1.0 - beta_one**STEP
    fix_second = 1.0 - beta_two**STEP
    mixed_out[...] = mixed[...]
    grad_out[...] = grad[...]

    @pl.when(step == 0)
    def _():
        for begin, values in ((0, gain), (2, bias)):
            rows = slice(begin, begin + 2)
            norm_out[rows], norm_m_out[rows], norm_v_out[rows] = adam_update(
                values[...], small[rows], norm_m[rows], norm_v[rows], fix_first, fix_second, rate_norm, 0.0
            )
        heads = slope.shape[1]
        slope_out[...], slope_m_out[...], slope_v_out[...] = adam_update(
            slope[...], small[4:5, 0:heads], slope_m[...], slope_v[...], fix_first, fix_second, rate_slope, 0.0
        )

    me = lax.axis_index("batch")
    for place in range(master.shape[0]):
        slot = step * master.shape[0] + place
        block, held, base = jnp.int32(0), jnp.int32(0), 0
        for matrix_id, size in enumerate(sizes):
            begin = start_of(owners, matrix_id, sizes)
            inside = (owners[matrix_id] == me) & (slot >= begin) & (slot < begin + size)
            block = jnp.where(inside, base + slot - begin, block)
            held = jnp.where(inside, 1, held)
            base += size
        gradient = red[block].astype(WIDE)
        values = adam_update(
            master[place], gradient, first[place], second[place], fix_first, fix_second, rate_matrix, decay_rate
        )
        keep = jnp.full(gradient.shape, held, jnp.int32) > 0
        weight = jnp.where(keep, values[0], master[place])
        new_w[place] = weight
        new_m[place] = jnp.where(keep, values[1], first[place])
        new_v[place] = jnp.where(keep, values[2], second[place])
        new_low[place] = weight.astype(LOW)


def fused_body(tokens, cotangent, doc_lengths, owners, master, first_moment, second_moment, ln_gain, ln_bias, norm_m, norm_v, slopes, slope_m, slope_v):
    micros, _, tok_rows, features = tokens.shape
    units, heads, width = tok_rows // 3, slopes.shape[0], features // slopes.shape[0]
    sizes = tuple(block_counts(features, FF))
    blocks, own, half = sum(sizes), micros * units, features // 2
    slots, rows = master.shape[1], master.shape[2]
    lane_units = units * heads
    split = features // TILE
    hbm, vmem, smem = (pl.BlockSpec(memory_space=m) for m in (pl.ANY, pltpu.VMEM, pltpu.SMEM))
    low = lambda *shape: pltpu.VMEM(shape, LOW)
    wide = lambda *shape: pltpu.VMEM(shape, WIDE)
    pieces = lambda: low(blocks, rows, half)
    both = lambda columns: low(2 * own, columns)
    scratch = [
        low(blocks, 2, features, half), wide(slots, rows, features), pieces(), pieces(), pieces(), pieces(), pieces(),
        low(micros, tok_rows, features), low(micros, tok_rows, features), low(micros, 16, features),
        wide(micros, split, 16 + tok_rows, TILE), wide(micros, split, tok_rows, TILE),
        both(3 * features), both(features), both(features), both(features), both(FF), both(features),
        both(3 * features), both(features), both(FF), both(features), both(3 * features), both(features),
        wide(own, features), wide(own, features), wide(own, features), wide(own, 1), wide(own, 1),
        wide(own, features), wide(own, FF), wide(own, features), wide(own, features),
        low(heads, 3 * units, 2 * width), low(heads, 3 * units, 2 * width), low(heads, units, 2 * width),
        low(heads, units, 2 * width), low(heads, units, 2 * width), low(heads, units, 2 * width),
        low(heads, 3 * units, 2 * width), low(heads, 3 * units, 2 * width),
        wide(micros, lane_units, lane_units), wide(micros, tok_rows, features), wide(micros, tok_rows, features),
        wide(micros, split, tok_rows, TILE), wide(micros, split, 8 + tok_rows, TILE), wide(micros, split, 8, TILE),
        low(2 * own, features), low(2 * own, FF),
        low(10, 2 * own, features), low(10, own, half), low(10, 2 * own, half),
        low(own, 3 * half), low(own, 3 * half), low(own, features), low(own, features), low(blocks, features, half), low(4, blocks, rows, half), low(4, blocks, rows, half),
        pieces(), pieces(), pieces(), pieces(), wide(48, features), wide(40, features),
        pltpu.SemaphoreType.DMA((SENDS,)), pltpu.SemaphoreType.DMA((RECEIVES,)), pltpu.SemaphoreType.DMA((5,)),
    ]
    token_shape = (micros, tok_rows, features)
    dims = (units, features, FF, heads, micros, sizes)
    mixed, grad, red, small = pl.pallas_call(
        lambda *refs: main_kernel(dims, refs),
        out_shape=(
            jax.ShapeDtypeStruct(token_shape, WIDE),
            jax.ShapeDtypeStruct(token_shape, WIDE),
            jax.ShapeDtypeStruct((blocks, rows, features), LOW),
            jax.ShapeDtypeStruct((8, features), WIDE),
        ),
        in_specs=[smem, smem, smem, vmem, vmem, hbm, hbm, hbm],
        out_specs=(hbm, hbm, vmem, vmem),
        scratch_shapes=scratch,
        compiler_params=pltpu.CompilerParams(
            collective_id=0, has_side_effects=True, vmem_limit_bytes=60 * 2**20
        ),
        name="block",
    )(
        owners, doc_lengths[:, 0], slopes, ln_gain, ln_bias, tokens[:, 0], cotangent[:, 0], master[0]
    )
    steps = 2
    slot = pl.BlockSpec((slots // steps, rows, features), lambda j: (j, 0, 0))
    flat = (micros * tok_rows, features)
    some = pl.BlockSpec((flat[0] // steps, features), lambda j: (j, 0))
    moment_shape = jax.ShapeDtypeStruct((slots, rows, features), WIDE)
    norm_shape = jax.ShapeDtypeStruct((4, features), WIDE)
    slope_shape = jax.ShapeDtypeStruct((1, heads), WIDE)
    out = pl.pallas_call(
        lambda *refs: adam_kernel(sizes, refs),
        grid=(steps,),
        out_shape=(
            moment_shape, moment_shape, moment_shape, jax.ShapeDtypeStruct((slots, rows, features), LOW),
            norm_shape, norm_shape, norm_shape, slope_shape, slope_shape, slope_shape,
            jax.ShapeDtypeStruct(flat, WIDE), jax.ShapeDtypeStruct(flat, WIDE),
        ),
        in_specs=[smem] + [vmem] * 9 + [slot] * 3 + [some] * 2,
        out_specs=(slot, slot, slot, slot, vmem, vmem, vmem, vmem, vmem, vmem, some, some),
        compiler_params=pltpu.CompilerParams(dimension_semantics=("arbitrary",)),
        name="adam",
    )(
        owners, red, small, ln_gain, ln_bias, norm_m, norm_v, slopes[None], slope_m[None],
        slope_v[None], master[0], first_moment[0], second_moment[0],
        mixed.reshape(flat), grad.reshape(flat),
    )
    new_w, new_m, new_v, new_low, norm, norm_m, norm_v, slope, slope_m, slope_v, mixed, grad = out
    return (
        mixed.reshape(tokens.shape), grad.reshape(tokens.shape), new_w[None], new_m[None], new_v[None], new_low[None], norm, norm_m, norm_v,
        slope[0], slope_m[0], slope_v[0],
    )


def fits(mesh, shapes):
    return mesh.shape["batch"] == 4 and mesh.shape["seq"] == 8 and shapes[0].shape[1] == 1


def solution(mesh):
    in_specs = (
        P("batch", None, "seq", None),
        P("batch", None, "seq", None),
        P("batch", None, None),
        P(),
        P("batch", None, "seq", None),
        P("batch", None, "seq", None),
        P("batch", None, "seq", None),
        P(),
        P(),
        P(),
        P(),
        P(),
        P(),
        P(),
    )
    out_specs = (
        P("batch", None, "seq", None),
        P("batch", None, "seq", None),
        P("batch", None, "seq", None),
        P("batch", None, "seq", None),
        P("batch", None, "seq", None),
        P("batch", None, "seq", None),
        P(),
        P(),
        P(),
        P(),
        P(),
        P(),
    )

    def whole(*args):
        part = fused_body if fits(mesh, args) else body
        return jax.shard_map(
            part, mesh=mesh, in_specs=in_specs, out_specs=out_specs, check_vma=False
        )(*args)

    return whole
```

```python
import math

import jax
import jax.numpy as jnp
from jax import lax
from jax.experimental import pallas as pl
from jax.experimental.pallas import tpu as pltpu
from jax.sharding import PartitionSpec as P

FF = 2048
STEP = 10


beta_one = 0.9
beta_two = 0.95
adam_eps = 1e-08
decay_rate = 0.1
rate_matrix = 0.02
rate_norm = 0.2
rate_slope = 0.01
ln_eps = 1e-05
masked_score = -1000000000.0
row_kinds = (True, False, True, False, True, False)


def broadcast(value, axis, source):
    kept = jnp.where(lax.axis_index(axis) == source, value, 0).astype(value.dtype)
    return lax.psum(kept, axis)


def running_total(lengths):
    count = lengths.shape[-1]
    ends = [lengths[..., 0]]
    for index in range(1, count):
        ends.append(ends[-1] + lengths[..., index])
    return jnp.stack(ends, -1)


def for_sending(value):

    def short(part):
        return part.astype(jnp.bfloat16) if part.dtype == jnp.float32 else part

    return jax.tree.map(short, value)


def passed_along(value, axis, by):
    peers = lax.axis_size(axis)
    pairs = [(i, i + by) for i in range(peers) if 0 <= i + by < peers]
    return lax.ppermute(value, axis, pairs)


def layer_norm(values, gain, shift):
    center = jnp.mean(values, -1, keepdims=True)
    centred = values - center
    spread = jnp.mean(centred * centred, -1, keepdims=True)
    return centred * lax.rsqrt(spread + ln_eps) * gain + shift


def gelu_tanh(values):
    return jax.nn.gelu(values, approximate=True)


def block_counts(features, hidden):
    return [3, 3, 1, hidden // features, hidden // features, 3]


def block_starts(owners, sizes):
    starts_list = []
    for matrix_id in range(len(sizes)):
        shared = jnp.zeros((), jnp.int32)
        for earlier_id in range(matrix_id):
            shared = shared + jnp.where(
                owners[earlier_id] == owners[matrix_id], sizes[earlier_id], 0
            ).astype(jnp.int32)
        starts_list.append(shared)
    return starts_list


def slot_table(owners, device, sizes, slot_count):
    starts_list = block_starts(owners, sizes)
    slot_ids = jnp.arange(slot_count, dtype=jnp.int32)
    numbers = jnp.arange(sum(sizes), dtype=jnp.int32)
    slot_map = jnp.zeros((slot_count, sum(sizes)), jnp.float32)
    block_base = 0
    for matrix_id in range(len(sizes)):
        inside = (
            (owners[matrix_id] == device)
            & (slot_ids >= starts_list[matrix_id])
            & (slot_ids < starts_list[matrix_id] + sizes[matrix_id])
        )
        target = block_base + slot_ids - starts_list[matrix_id]
        slot_map = slot_map + (inside[:, None] & (target[:, None] == numbers[None, :])).astype(
            jnp.float32
        )
        block_base += sizes[matrix_id]
    return slot_map


def to_matrix(blocks, by_rows):
    if by_rows:
        return blocks.reshape(-1, blocks.shape[2])
    return blocks.transpose(1, 0, 2).reshape(blocks.shape[1], -1)


def to_blocks(matrix, by_rows, features):
    if by_rows:
        return matrix.reshape(-1, features, features)
    return matrix.reshape(features, -1, features).transpose(1, 0, 2)


def all_blocks(matrices, features):
    return jnp.concatenate(
        [to_blocks(matrices[matrix_id], row_kinds[matrix_id], features) for matrix_id in range(6)],
        0,
    )


def adam_update(weight, gradient, first_moment, second, fix_first, fix_second, rate, decay):
    first_new = beta_one * first_moment + (1.0 - beta_one) * gradient
    second_new = beta_two * second + (1.0 - beta_two) * gradient * gradient
    direction = first_new / fix_first / (jnp.sqrt(second_new / fix_second) + adam_eps)
    return (weight - rate * (direction + decay * weight), first_new, second_new)


def scores_for(query_block, key_rows, start_row, segment, head_slope):
    block_rows = query_block.shape[0]
    row_total = key_rows.shape[0]
    row_ids = start_row + jnp.arange(block_rows, dtype=jnp.int32)
    col_ids = jnp.arange(row_total, dtype=jnp.int32)
    distance = (row_ids[:, None] - col_ids[None, :]).astype(jnp.float32)
    seg_rows = lax.dynamic_slice_in_dim(segment, start_row, block_rows)
    allowed = (seg_rows[:, None] == segment[None, :]) & (col_ids[None, :] <= row_ids[:, None])
    raw_score = (
        jnp.dot(query_block, key_rows.T, preferred_element_type=jnp.float32) * 0.125
        - head_slope * distance
    )
    return (jnp.where(allowed, raw_score, masked_score), distance)


def attend(queries, key_rows, values, segment, head_slope, block_rows):
    row_total, head_width = queries.shape

    def per_block(start_row):
        query_block = lax.dynamic_slice_in_dim(queries, start_row, block_rows)
        scores, distance = scores_for(query_block, key_rows, start_row, segment, head_slope)
        largest = jnp.max(scores, -1, keepdims=True)
        log_total = largest + jnp.log(jnp.sum(jnp.exp(scores - largest), -1, keepdims=True))
        probability = jnp.exp(scores - log_total).astype(jnp.bfloat16)
        return (jnp.dot(probability, values, preferred_element_type=jnp.float32), log_total[:, 0])

    row_starts = jnp.arange(row_total // block_rows, dtype=jnp.int32) * block_rows
    attended, log_totals = lax.map(per_block, row_starts)
    return (attended.reshape(row_total, head_width), log_totals.reshape(row_total))


def attend_back(queries, key_rows, values, segment, head_slope, log_totals, grad_out, block_rows):
    row_total, head_width = queries.shape

    def per_block(carried, start_row):
        grad_keys, grad_values, grad_slope = carried
        query_block = lax.dynamic_slice_in_dim(queries, start_row, block_rows)
        grad_block = lax.dynamic_slice_in_dim(grad_out, start_row, block_rows)
        total_block = lax.dynamic_slice_in_dim(log_totals, start_row, block_rows)
        scores, distance = scores_for(query_block, key_rows, start_row, segment, head_slope)
        probability = jnp.exp(scores - total_block[:, None])
        grad_prob = jnp.dot(grad_block, values.T, preferred_element_type=jnp.float32)
        grad_score = (
            probability * (grad_prob - jnp.sum(probability * grad_prob, -1, keepdims=True))
        ).astype(jnp.bfloat16)
        grad_query = jnp.dot(grad_score, key_rows, preferred_element_type=jnp.float32) * 0.125
        grad_keys = (
            grad_keys
            + jnp.dot(grad_score.T, query_block, preferred_element_type=jnp.float32) * 0.125
        )
        grad_values = grad_values + jnp.dot(
            probability.astype(jnp.bfloat16).T, grad_block, preferred_element_type=jnp.float32
        )
        grad_slope = grad_slope - jnp.sum(grad_score.astype(jnp.float32) * distance)
        return ((grad_keys, grad_values, grad_slope), grad_query)

    row_starts = jnp.arange(row_total // block_rows, dtype=jnp.int32) * block_rows
    initial = (
        jnp.zeros((row_total, head_width), jnp.float32),
        jnp.zeros((row_total, head_width), jnp.float32),
        jnp.zeros((), jnp.float32),
    )
    (grad_keys, grad_values, grad_slope), grad_queries = lax.scan(per_block, initial, row_starts)
    return (grad_queries.reshape(row_total, head_width), grad_keys, grad_values, grad_slope)


def body(
    tokens,
    cotangent,
    doc_lengths,
    owners,
    master,
    first_moment,
    second_moment,
    ln_gain,
    ln_bias,
    norm_m,
    norm_v,
    slopes,
    slope_m,
    slope_v,
):
    micro_count, lane_count, tok_rows, features = tokens.shape
    unit_rows = tok_rows // 3
    seq_devices = lax.axis_size("seq")
    head_count = slopes.shape[0]
    head_width = features // head_count
    lane_units = unit_rows * seq_devices
    block_rows = min(512, lane_units)
    unit_total = lane_count * unit_rows
    slot_count = master.shape[1]
    sizes = block_counts(features, FF)
    starts_list = block_starts(owners, sizes)
    batch_rank = lax.axis_index("batch")
    seq_rank = lax.axis_index("seq")
    lane_rank = seq_rank // head_count
    head_rank = seq_rank % head_count
    low_slots = master[0].astype(jnp.bfloat16)
    fetched = []
    for matrix_id in range(6):
        owned_rows = lax.dynamic_slice_in_dim(
            low_slots, starts_list[matrix_id], sizes[matrix_id], 0
        )
        fetched.append(broadcast(owned_rows, "batch", owners[matrix_id]))
    gathered = lax.all_gather(for_sending(tuple(fetched)), "seq", axis=1, tiled=True)
    pool_weight, qkv_weight, out_weight, in_weight, back_weight, up_weight = [
        to_matrix(gathered[matrix_id], row_kinds[matrix_id]) for matrix_id in range(6)
    ]
    doc_ends = running_total(doc_lengths)
    doc_starts = jnp.concatenate(
        [jnp.zeros((micro_count, lane_count, 1), jnp.int32), doc_ends[..., :-1]], -1
    )
    unit_ids = seq_rank * unit_rows + jnp.arange(unit_rows, dtype=jnp.int32)
    keep_mask = 1.0 - jnp.any(
        unit_ids[None, None, :, None] == doc_starts[:, :, None, :], -1
    ).astype(jnp.float32)
    triples = tokens.reshape(micro_count, lane_count, unit_rows, 3, features)
    tail_tokens = triples[:, :, -1, 1:3]
    arrived = passed_along(tail_tokens, "seq", 1)
    lane_pick = jnp.arange(lane_count, dtype=jnp.int32) == lane_rank
    head_pick = jnp.arange(head_count, dtype=jnp.int32) == head_rank
    head_slope = jnp.sum(jnp.where(head_pick, slopes, 0.0))
    positions = jnp.arange(lane_units, dtype=jnp.int32)
    gain_grad = jnp.zeros((2, features), jnp.float32)
    bias_grad = jnp.zeros((2, features), jnp.float32)
    slope_grad = jnp.zeros((), jnp.float32)
    summed = None
    mixed_parts = []
    grad_parts = []
    outgoing = []
    for micro in range(micro_count):
        triple_now = triples[micro]
        keep_now = keep_mask[micro]
        earlier = jnp.concatenate([arrived[micro][:, None], triple_now[:, :-1, 1:3]], 1) * keep_now[
            :, :, None, None
        ].astype(jnp.bfloat16)
        pool_input = jnp.concatenate([earlier, triple_now[:, :, 0:1]], 2).reshape(
            unit_total, 3 * features
        )
        pooled = jnp.dot(pool_input, pool_weight, preferred_element_type=jnp.float32)
        normed = layer_norm(pooled, ln_gain[0], ln_bias[0]).astype(jnp.bfloat16)
        projected = jnp.dot(normed, qkv_weight, preferred_element_type=jnp.float32).astype(
            jnp.bfloat16
        )
        outbound = (
            projected.reshape(lane_count, unit_rows, 3, head_count, head_width)
            .transpose(0, 3, 1, 2, 4)
            .reshape(lane_count * head_count, unit_rows * 3 * head_width)
        )
        received = lax.all_to_all(outbound, "seq", split_axis=0, concat_axis=1, tiled=True).reshape(
            lane_units, 3, head_width
        )
        queries = received[:, 0]
        key_rows = received[:, 1]
        values = received[:, 2]
        lengths = jnp.sum(jnp.where(lane_pick[:, None], doc_lengths[micro], 0), 0)
        lane_ends = running_total(lengths)
        segment = jnp.sum((positions[:, None] >= lane_ends[None, :-1]).astype(jnp.int32), 1)
        attended, log_totals = attend(queries, key_rows, values, segment, head_slope, block_rows)
        returned = lax.all_to_all(
            attended.astype(jnp.bfloat16).reshape(1, lane_units * head_width),
            "seq",
            split_axis=1,
            concat_axis=0,
            tiled=True,
        )
        merged = (
            returned.reshape(lane_count, head_count, unit_rows, head_width)
            .transpose(0, 2, 1, 3)
            .reshape(unit_total, features)
        )
        residual = pooled + jnp.dot(merged, out_weight, preferred_element_type=jnp.float32)
        normed_two = layer_norm(residual, ln_gain[1], ln_bias[1]).astype(jnp.bfloat16)
        hidden = jnp.dot(normed_two, in_weight, preferred_element_type=jnp.float32)
        activated = gelu_tanh(hidden).astype(jnp.bfloat16)
        shortened = residual + jnp.dot(activated, back_weight, preferred_element_type=jnp.float32)
        short_low = shortened.astype(jnp.bfloat16)
        upward = jnp.dot(short_low, up_weight, preferred_element_type=jnp.float32).reshape(
            lane_count, unit_rows * 3, features
        )
        mixed_parts.append(tokens[micro].astype(jnp.float32) + upward)
        grad_upward = cotangent[micro].reshape(unit_total, 3 * features)
        sum_up = jnp.dot(short_low.T, grad_upward, preferred_element_type=jnp.float32)
        grad_short = jnp.dot(grad_upward, up_weight.T, preferred_element_type=jnp.float32)
        grad_short_low = grad_short.astype(jnp.bfloat16)
        sum_back = jnp.dot(activated.T, grad_short_low, preferred_element_type=jnp.float32)
        grad_activated = jnp.dot(grad_short_low, back_weight.T, preferred_element_type=jnp.float32)
        grad_hidden = jax.vjp(gelu_tanh, hidden)[1](grad_activated)[0].astype(jnp.bfloat16)
        sum_in = jnp.dot(normed_two.T, grad_hidden, preferred_element_type=jnp.float32)
        grad_normed_two = jnp.dot(grad_hidden, in_weight.T, preferred_element_type=jnp.float32)
        norm_two_back = jax.vjp(layer_norm, residual, ln_gain[1], ln_bias[1])[1]
        grad_resid_norm, grad_gain_two, grad_bias_two = norm_two_back(grad_normed_two)
        grad_residual = grad_short + grad_resid_norm
        grad_resid_low = grad_residual.astype(jnp.bfloat16)
        sum_out = jnp.dot(merged.T, grad_resid_low, preferred_element_type=jnp.float32)
        grad_merged = jnp.dot(
            grad_resid_low, out_weight.T, preferred_element_type=jnp.float32
        ).astype(jnp.bfloat16)
        back_outbound = (
            grad_merged.reshape(lane_count, unit_rows, head_count, head_width)
            .transpose(0, 2, 1, 3)
            .reshape(lane_count * head_count, unit_rows * head_width)
        )
        grad_attended = lax.all_to_all(
            back_outbound, "seq", split_axis=0, concat_axis=1, tiled=True
        ).reshape(lane_units, head_width)
        grad_queries, grad_keys, grad_values, grad_slope = attend_back(
            queries, key_rows, values, segment, head_slope, log_totals, grad_attended, block_rows
        )
        grad_heads = (
            jnp.stack([grad_queries, grad_keys, grad_values], 1)
            .astype(jnp.bfloat16)
            .reshape(1, lane_units * 3 * head_width)
        )
        grad_arrived = lax.all_to_all(grad_heads, "seq", split_axis=1, concat_axis=0, tiled=True)
        grad_projected = (
            grad_arrived.reshape(lane_count, head_count, unit_rows, 3, head_width)
            .transpose(0, 2, 3, 1, 4)
            .reshape(unit_total, 3 * features)
        )
        sum_qkv = jnp.dot(normed.T, grad_projected, preferred_element_type=jnp.float32)
        grad_normed = jnp.dot(grad_projected, qkv_weight.T, preferred_element_type=jnp.float32)
        norm_one_back = jax.vjp(layer_norm, pooled, ln_gain[0], ln_bias[0])[1]
        grad_pool_norm, grad_gain_one, grad_bias_one = norm_one_back(grad_normed)
        grad_pooled_low = (grad_residual + grad_pool_norm).astype(jnp.bfloat16)
        sum_pool = jnp.dot(pool_input.T, grad_pooled_low, preferred_element_type=jnp.float32)
        grad_pieces = jnp.dot(
            grad_pooled_low, pool_weight.T, preferred_element_type=jnp.float32
        ).reshape(lane_count, unit_rows, 3, features)
        grad_earlier = grad_pieces[:, :, 0:2] * keep_now[:, :, None, None]
        outgoing.append(grad_earlier[:, 0])
        following = jnp.concatenate(
            [grad_earlier[:, 1:], jnp.zeros((lane_count, 1, 2, features), jnp.float32)], 1
        )
        token_grad = jnp.concatenate([grad_pieces[:, :, 2:3], following], 2).reshape(
            lane_count, unit_rows * 3, features
        )
        grad_parts.append(cotangent[micro].astype(jnp.float32) + token_grad)
        gain_grad = gain_grad + jnp.stack([grad_gain_one, grad_gain_two])
        bias_grad = bias_grad + jnp.stack([grad_bias_one, grad_bias_two])
        slope_grad = slope_grad + grad_slope
        micro_grads = [sum_pool, sum_qkv, sum_out, sum_in, sum_back, sum_up]
        summed = (
            micro_grads
            if summed is None
            else [left + right for left, right in zip(summed, micro_grads)]
        )
    reduced = lax.psum_scatter(all_blocks(summed, features), "seq", scatter_dimension=1, tiled=True)
    incoming = passed_along(jnp.stack(outgoing).astype(jnp.bfloat16), "seq", -1).astype(jnp.float32)
    grad_tokens = jnp.stack(grad_parts).reshape(micro_count, lane_count, unit_rows, 3, features)
    grad_tokens = grad_tokens.at[:, :, -1, 1:3].add(incoming).reshape(tokens.shape)
    reduced_all = lax.psum(reduced, "batch")
    norm_grad, slopes_grad = lax.psum(
        (jnp.concatenate([gain_grad, bias_grad], 0), jnp.where(head_pick, slope_grad, 0.0)),
        ("batch", "seq"),
    )
    slot_map = slot_table(owners, batch_rank, sizes, slot_count)
    is_owned = jnp.sum(slot_map, -1)[:, None, None] > 0.5
    slot_grads = jnp.einsum("jb,brc->jrc", slot_map, reduced_all, precision=lax.Precision.HIGHEST)
    step_float = jnp.float32(STEP)
    fix_first = 1.0 - jnp.power(jnp.float32(beta_one), step_float)
    fix_second = 1.0 - jnp.power(jnp.float32(beta_two), step_float)
    new_weight, new_first, new_second = adam_update(
        master[0],
        slot_grads,
        first_moment[0],
        second_moment[0],
        fix_first,
        fix_second,
        rate_matrix,
        decay_rate,
    )
    new_weight = jnp.where(is_owned, new_weight, master[0])
    new_first = jnp.where(is_owned, new_first, first_moment[0])
    new_second = jnp.where(is_owned, new_second, second_moment[0])
    norm_now = jnp.concatenate([ln_gain, ln_bias], 0)
    new_norm, new_norm_m, new_norm_v = adam_update(
        norm_now, norm_grad, norm_m, norm_v, fix_first, fix_second, rate_norm, 0.0
    )
    new_slopes, new_slope_m, new_slope_v = adam_update(
        slopes, slopes_grad, slope_m, slope_v, fix_first, fix_second, rate_slope, 0.0
    )
    return (
        jnp.stack(mixed_parts),
        grad_tokens,
        new_weight[None],
        new_first[None],
        new_second[None],
        new_weight[None].astype(jnp.bfloat16),
        new_norm,
        new_norm_m,
        new_norm_v,
        new_slopes,
        new_slope_m,
        new_slope_v,
    )


MESH = pl.DeviceIdType.MESH
LOW = jnp.bfloat16
WIDE = jnp.float32
TILE = 128


class Plan:
    def __init__(self):
        self.tasks = {}

    def add(self, name, run, deps=(), waits=(), sends=(), cost=0.1, rank=0):
        assert name not in self.tasks
        self.tasks[name] = (run, tuple(deps), tuple(waits), tuple(sends), cost, rank)

    def order(self):
        now, done, arrival, free, listed = 0.0, set(), {}, {}, []
        left = list(self.tasks)
        while left:
            best = None
            for place, name in enumerate(left):
                run, deps, waits, sends, cost, rank = self.tasks[name]
                if any(d not in done for d in deps) or any(w not in arrival for w in waits):
                    continue
                begin = max([now] + [arrival[w] for w in waits] + [free.get(m[1], 0.0) - SLACK for m in sends])
                key = (begin, rank, place)
                if best is None or key < best[0]:
                    best = (key, name)
            name = best[1]
            run, deps, waits, sends, cost, rank = self.tasks[name]
            now = best[0][0] + cost
            for message, link, size in sends:
                rate, delay = LINKS[link]
                lanes = ("f", "r", "l") if link == "f" else (link,)
                end = max([now] + [free.get(lane, 0.0) for lane in lanes]) + size / rate
                free.update({lane: end for lane in lanes})
                arrival[message] = end + delay
            done.add(name)
            left.remove(name)
            listed.append((name, now))
        return listed


SLACK = 2.0
SENDS, RECEIVES = 32, 180
GATHERS = (
    (0, 0, 1, 0.0),
    (0, 1, 1, 0.07),
    (0, 2, 1, 0.08),
    (1, 0, 1, 0.21),
    (1, 1, 1, 0.21),
    (1, 2, 1, 0.21),
    (3, 0, 2, 0.31),
    (3, 2, 2, 0.33),
    (2, 0, 1, 0.43),
    (5, 0, 3, 0.37),
)
QUARTERS = {5: 0, 1: 3, 0: 6}
AFTER = {}
WHOLE = ()
SCATTERS = (
    (5, 0, 3, 0.93),
    (3, 0, 2, 1.01),
    (3, 2, 2, 0.93),
    (2, 0, 1, 1.26),
    (0, 0, 1, 0.43),
    (0, 1, 1, 0.43),
    (0, 2, 1, 0.43),
    (1, 0, 3, 0.6),
)
LINKS = {
    "c": (400e3, 1.0),
    "x": (52e3, 2.3),
    "r": (52e3, 2.3),
    "l": (52e3, 2.3),
    "f": (46e3, 3.3),
}


def start_of(owners, matrix_id, sizes):
    shared = jnp.int32(0)
    for earlier_id in range(matrix_id):
        shared = shared + jnp.where(owners[earlier_id] == owners[matrix_id], sizes[earlier_id], 0)
    return shared


def over_last(fn, value):
    return fn(value, axis=-1, keepdims=True)


def contract(left, right, left_dim, right_dim):
    return lax.dot_general(
        left, right, (((left_dim,), (right_dim,)), ((), ())), preferred_element_type=WIDE
    )


def gelu_parts(value):
    scale = math.sqrt(2.0 / math.pi)
    inner = jnp.tanh(scale * (value + 0.044715 * (value * value * value)))
    return inner, scale * (1.0 + 3 * 0.044715 * value * value)


def main_kernel(dims, refs):
    units, features, hidden_width, heads, micros, sizes = dims
    tables, (tok_hbm, cot_hbm, master_hbm, first_hbm, second_hbm) = refs[:10], refs[10:15]
    mixed_hbm, grad_hbm, slot_grads, small, masters, firsts, seconds = refs[15:22]
    held = refs[22:32]
    owners, docs, slopes, gain, bias, norm_m, norm_v, slope_row, slope_m, slope_v = held
    (
        w, red, mine, other, core_in, both, x_in, tok, cot, tail_in, wide_tok, wide_cot, x_pool, x_norm, x_att,
        x_two, x_act, x_short, d_up, d_low, d_inner, d_res, d_qkv, d_pool, pooled, hat_one, hat_two, root_one, root_two,
        resid, hidden, short_grad, res_grad, q_out, q_in, a_out, a_in, da_out, da_in, dq_out, dq_in, probs, mixed, grad,
        wide_up, wide_grad, edge_in, x_near, x_wide, t_left, t_out, t_in, u_out, u_in, dx_out, dx_in, g, right_in, left_in, fin_out, fin_in, co_out, co_in, sums, sums_in, sends, recvs, local,
    ) = refs[32:]
    half = features // 2
    width = features // heads
    rows_of = masters.shape[1]
    count = heads
    tokens = 3 * units
    own = micros * units
    pair_width = 2 * width
    b, s = lax.axis_index("batch"), lax.axis_index("seq")
    x, c = b // 2, b % 2
    z, y = s // 2, s % 2
    spot = y * (7 - 2 * z) + z

    def seq_of(position):
        far = position // 4
        return 2 * (position + far * (7 - 2 * position)) + far

    def at(offset):
        return lax.rem(spot + offset + 2 * count, count)

    def rows_at(offset, part=0, length=rows_of):
        return pl.ds(pl.multiple_of(seq_of(at(offset)) * rows_of + part, 16), length)

    my_half = pl.ds(pl.multiple_of(c * half, half), half)
    other_half = pl.ds(pl.multiple_of((1 - c) * half, half), half)
    core_peer = (x * 2 + 1 - c, s)
    x_peer = ((1 - x) * 2 + c, s)
    cross_peer = ((1 - x) * 2 + 1 - c, s)
    right_peer = (b, seq_of(at(1)))
    left_peer = (b, seq_of(at(-1)))
    plan = Plan()
    flying, started, boxes = {}, [], {}

    def launch(name, copies, starts, group):
        if len(started) >= SENDS:
            started[len(started) - SENDS].wait_send()
        started.append(copies[0])
        flying[name] = copies[0]
        for start in starts:
            start()

    def describe(source, target, device, group):
        box = boxes.setdefault(group, len(boxes))
        return pltpu.make_async_remote_copy(
            src_ref=source,
            dst_ref=target,
            send_sem=sends.at[len(started) % SENDS],
            recv_sem=recvs.at[box],
            device_id=device,
            device_id_type=MESH,
        )

    def send(name, source, target, device, group=None):
        copy = describe(source, target, device, group or name)
        launch(name, [copy], [copy.start], group or name)

    def gather_up(group, whole):
        describe(whole, whole, core_peer, group).wait_recv()

    loads = [
        pltpu.make_async_copy(master_hbm, masters, local.at[0]),
        pltpu.make_async_copy(tok_hbm, tok, local.at[1]),
        pltpu.make_async_copy(cot_hbm, cot, local.at[2]),
    ]
    for table, place in zip(tables, held):
        loads.append(pltpu.make_async_copy(table, place, local.at[len(loads) + 2]))
    for copy in loads:
        copy.start()
    moments = [
        pltpu.make_async_copy(first_hbm, firsts, local.at[15]),
        pltpu.make_async_copy(second_hbm, seconds, local.at[16]),
    ]
    barrier = pltpu.get_barrier_semaphore()
    for step in range(1, count):
        pl.semaphore_signal(
            barrier, inc=1, device_id=(b, lax.rem(s + step, count)), device_id_type=MESH
        )
    for device in (core_peer, x_peer, cross_peer):
        pl.semaphore_signal(barrier, inc=1, device_id=device, device_id_type=MESH)
    pl.semaphore_wait(barrier, count + 2)
    for copy in loads[3:]:
        copy.wait()

    spans, first = [], 0
    for size in sizes:
        spans.append((first, first + size))
        first += size
    in_base, back_base, up_base = spans[3][0], spans[4][0], spans[5][0]
    hidden_blocks = sizes[3]
    ours = in_base + x * hidden_blocks
    theirs = in_base + (1 - x) * hidden_blocks
    plan.add("ms", loads[0].wait, cost=0.5)

    def contribute(k):
        def run():
            lo, hi = spans[k]
            mask = (owners[k] == b).astype(WIDE)
            begin = start_of(owners, k, sizes)
            for block in range(lo, hi):
                slot = jnp.minimum(begin + (block - lo), masters.shape[0] - 1)
                mine[block] = (masters[slot, :, my_half] * mask).astype(LOW)
                other[block] = (masters[slot, :, other_half] * mask).astype(LOW)
            send(("g0", k), other.at[lo:hi], core_in.at[lo:hi], core_peer)

        return run

    def join_cores(k):
        def run():
            lo, hi = spans[k]
            flying[("g0", k)].wait_recv()
            both[lo:hi] = mine[lo:hi] + core_in[lo:hi]

        return run

    have = {k: [] for k in range(6)}
    gathers = []
    for k, offset, size, rank in GATHERS:
        name = ("w", k, offset)
        if k == 3:
            gathers.append((rank, name, (3, 4), ours + offset, theirs + offset, size))
            have[3] += [("h", name), ("hy", name)]
        else:
            begin = spans[k][0] + offset
            gathers.append((rank, name, (k,), begin, begin if k == 5 else None, size))
            have[k] += [("h", name)]
    piece_bytes = rows_of * half * 2

    quarter = half // 2
    plane_span = pl.ds(pl.multiple_of(x * quarter, quarter), quarter)
    plane_away = pl.ds(pl.multiple_of((1 - x) * quarter, quarter), quarter)

    def gather_chunk(rank, name, parents, here, there, size):
        quarters = there is here
        split = there is not None and not quarters
        load = size * piece_bytes // (2 if quarters else 1)
        blocks = pl.ds(here, size)
        away = pl.ds(there, size) if split else blocks
        span, away_span = (plane_span, plane_away) if quarters else (slice(None), slice(None))

        def piece(offset, part=0, length=rows_of):
            return w.at[blocks, c, rows_at(offset, part, length), span]

        def join_here():
            send(("g1", name), both.at[away, :, away_span], x_in.at[away, :, away_span], x_peer)

        def join_x():
            flying[("g1", name)].wait_recv()
            w[blocks, c, rows_at(0), span] = both[blocks, :, span] + x_in[blocks, :, span]
            send(("R", 1, name), piece(0), piece(0), right_peer, (1, name))
            send(("L", 1, name), piece(0), piece(0), left_peer, (1, name))

        def onward(step):
            def run():
                gather_up((step - 1, name), w.at[blocks, c, 0 : rows_of * (2 if step < 5 else 1), span])
                if step == 5:
                    return
                for side, offset, peer in (("R", 1 - step, right_peer), ("L", step - 1, left_peer)):
                    part = piece(offset)
                    if step == 4:
                        part = piece(offset, 0 if side == "R" else rows_of // 2, rows_of // 2)
                    send((side, step, name), part, part, peer, (step, name))

            return run

        def across(step):
            def run():
                for side, offset in (("R", -step), ("L", step)):
                    part = piece(offset)
                    if step == 4:
                        part = piece(offset, 0 if side == "R" else rows_of // 2, rows_of // 2)
                    if step > 0 or side == "R":
                        send(("X", side, step, name), part, part, x_peer, ("X", name))

            return run

        def distribute(which, held, lanes):
            def run():
                send((which, name), w.at[held, c, :, lanes], w.at[held, c, :, lanes], core_peer)

            return run

        plan.add(("cx", name), join_here, [("cs", k) for k in parents], (), [(("g1", name), "x", load)], 0.05, rank)
        plan.add(
            ("x", name), join_x, [("cx", name)], [("g1", name)],
            [(("R", 1, name), "r", load), (("L", 1, name), "l", load)], 0.05, rank,
        )
        crossing = []

        def cross(step, after):
            messages = [("X", side, step, name) for side in ("RL" if step else "R")]
            size_of = load if step < 4 else load // 2
            plan.add(("X", step, name), across(step), [after], (), [(m, "x", size_of) for m in messages], 0.05, rank + 0.05)
            crossing.extend(messages)

        if split:
            cross(0, ("x", name))
        for step in (2, 3, 4, 5):
            size_of = load if step < 4 else load // 2
            out = [((side, step, name), link, size_of) for side, link in (("R", "r"), ("L", "l"))] if step < 5 else []
            before = ("x", name) if step == 2 else (step - 1, "f", name)
            waits = [(side, step - 1, name) for side in "RL"]
            plan.add((step, "f", name), onward(step), [before], waits, out, 0.05, rank)
            if split:
                cross(step - 1, (step, "f", name))
        plan.add(("di", name), distribute("D", blocks, span), [(5, "f", name)], (), [(("D", name), "c", 8 * load)], 0.05, rank)
        plan.add(("h", name), arrive(("D", name)), [("di", name)], [("D", name)], (), 0.02, rank)
        if split:
            whole = w.at[away, c, :, away_span]
            last = [("X", step, name) for step in range(5)]
            plan.add(("xw", name), lambda: gather_up(("X", name), whole), last, crossing, (), 0.05, rank)
            plan.add(("dy", name), distribute("E", away, away_span), [("xw", name)], (), [(("E", name), "c", 8 * load)], 0.05, rank)
            plan.add(("hy", name), arrive(("E", name)), [("dy", name)], [("E", name)], (), 0.02, rank)

    def arrive(*names):
        def run():
            for name in names:
                flying[name].wait_recv()

        return run

    for k in (0, 1, 3, 4, 2, 5):
        lo, hi = spans[k]
        load = (hi - lo) * piece_bytes
        plan.add(("co", k), contribute(k), ["ms"], (), [(("g0", k), "c", load)], 0.04 * (hi - lo), 0.1)
        plan.add(("cs", k), join_cores(k), [("co", k)], [("g0", k)], (), 0.02 * (hi - lo), 0.1)
    for chunk in gathers:
        gather_chunk(*chunk)

    def exchange(name, buffer):
        send(name, buffer.at[0:own], buffer.at[own : 2 * own], core_peer)

    def shared(name, columns):
        return (name, "c", own * columns * 2)

    lead = 16
    tiles = range(features // TILE)

    def columns_at(tile, base=0):
        return slice(base + tile * TILE, base + (tile + 1) * TILE)

    def ends_of(micro):
        ends = []
        total = jnp.int32(0)
        for index in range(docs.shape[1] - 1):
            total = total + docs[micro, index]
            ends.append(total)
        return ends

    def kept(micro):
        ids = s * units + lax.broadcasted_iota(jnp.int32, (units, 1), 0)
        starts = (ids == 0).astype(jnp.int32)
        for end in ends_of(micro):
            starts = starts | (ids == end).astype(jnp.int32)
        return starts == 0

    def load_tokens():
        loads[1].wait()
        send("tl", tok.at[:, tokens - lead :], tail_in, (b, lax.rem(s + 1, count)))
        for micro in range(micros):
            for tile in tiles:
                wide_tok[micro, tile, lead:] = tok[micro, :, columns_at(tile)].astype(WIDE)

    def load_cotangent():
        loads[2].wait()
        for micro in range(micros):
            for tile in tiles:
                wide_cot[micro, tile] = cot[micro, :, columns_at(tile)].astype(WIDE)
                for r in range(3):
                    d_up[micro * units : (micro + 1) * units, columns_at(tile, r * features)] = wide_cot[
                        micro, tile, pl.ds(r, units, stride=3), :
                    ].astype(LOW)
        exchange("eu", d_up)

    def make_pieces():
        flying["tl"].wait_recv()
        for micro in range(micros):
            keep = kept(micro)
            for tile in tiles:
                wide_tok[micro, tile, :lead] = tail_in[micro, :, columns_at(tile)].astype(WIDE)
                for r in range(3):
                    part = wide_tok[micro, tile, pl.ds(lead - 2 + r, units, stride=3), :]
                    if r < 2:
                        part = jnp.where(keep, part, 0.0)
                    x_pool[micro * units : (micro + 1) * units, columns_at(tile, r * features)] = part.astype(LOW)
        exchange("ep", x_pool)

    plan.add("tok", load_tokens, sends=[("tl", "f", 2 * lead * features * 2)], cost=0.3, rank=1)
    plan.add(
        "pc", make_pieces, ["tok"], ["tl"], [shared("ep", 3 * features)], 0.5, rank=1
    )
    plan.add("cot", load_cotangent, (), (), [shared("eu", 3 * features)], 0.5, rank=2)

    def normal(value, which, hat, root):
        centred = value - over_last(jnp.mean, value)
        scale = lax.rsqrt(over_last(jnp.mean, centred * centred) + ln_eps)
        unit = centred * scale
        hat[...] = unit
        root[...] = scale
        return (unit * gain[which : which + 1, :] + bias[which : which + 1, :]).astype(LOW)

    def both_halves(make):
        return jnp.concatenate([make(0), make(1)], axis=1)

    def pool():
        def side(h):
            total = None
            for r in range(3):
                term = contract(x_pool[0:own, r * features : (r + 1) * features], w[r, h], 1, 0)
                total = term if total is None else total + term
            return total

        value = both_halves(side)
        pooled[...] = value
        x_norm[0:own] = normal(value, 0, hat_one, root_one)
        exchange("en", x_norm)

    lane = lambda: lax.broadcasted_iota(jnp.int32, (1, pair_width), 1)

    def swap(value):
        return pltpu.roll(value, width, axis=1)

    def to_heads(tile, target, pair, row):
        low_lanes = lane() < width
        first, second = tile[:units], tile[units:]
        target[2 * pair, row : row + units] = jnp.where(low_lanes, first, swap(second)).astype(LOW)
        target[2 * pair + 1, row : row + units] = jnp.where(low_lanes, swap(first), second).astype(LOW)

    def from_heads(source, pair, row):
        low_lanes = lane() < width
        even = source[2 * pair, row : row + units].astype(WIDE)
        odd = source[2 * pair + 1, row : row + units].astype(WIDE)
        return jnp.where(low_lanes, even, swap(odd)).astype(LOW), jnp.where(low_lanes, swap(even), odd).astype(LOW)

    def spread(name, source, target):
        for step in range(1, count):
            there = lax.rem(s + step, count)
            send((name, step), source.at[there], target.at[s], (b, there), name)
        target[s] = source[s]

    def spread_names(name):
        return [(name, step) for step in range(1, count)]

    def spread_sends(name, rows):
        return [((name, step), "f", rows * pair_width * 2) for step in range(1, count)]

    def project():
        for part in range(3):
            for h in range(2):
                value = contract(x_norm[0:own], w[3 + part, h], 1, 0)
                for tile in range(half // pair_width):
                    to_heads(
                        value[:, tile * pair_width : (tile + 1) * pair_width],
                        q_out,
                        h * (half // pair_width) + tile,
                        part * units,
                    )
        spread("q", q_out, q_in)

    lane_units = units * count

    def heads_of(source, part):
        return source[:, part * units : (part + 1) * units, :].reshape(lane_units, pair_width)

    def lanes_of(micro):
        return (lane() // width == micro).astype(WIDE).astype(LOW)

    def distances():
        row_ids = lax.broadcasted_iota(jnp.int32, (lane_units, lane_units), 0)
        col_ids = lax.broadcasted_iota(jnp.int32, (lane_units, lane_units), 1)
        return row_ids - col_ids

    def attend_now():
        gather_up("q", q_in.at[0 : count - 1])
        queries, keys, values = (heads_of(q_in, part) for part in range(3))
        slope = slopes[s]
        total = None
        for micro in range(micros):
            gap = distances()
            row_seg = jnp.zeros((lane_units, 1), jnp.int32)
            col_seg = jnp.zeros((1, lane_units), jnp.int32)
            for end in ends_of(micro):
                row_seg += (lax.broadcasted_iota(jnp.int32, (lane_units, 1), 0) >= end).astype(jnp.int32)
                col_seg += (lax.broadcasted_iota(jnp.int32, (1, lane_units), 1) >= end).astype(jnp.int32)
            allowed = (row_seg == col_seg) & (gap >= 0)
            mask = lanes_of(micro)
            raw = contract(queries * mask, keys, 1, 1) * 0.125 - slope * gap.astype(WIDE)
            scores = jnp.where(allowed, raw, masked_score)
            raised = jnp.exp(scores - over_last(jnp.max, scores))
            probability = raised / over_last(jnp.sum, raised)
            probs[micro] = probability
            term = contract(probability.astype(LOW), values * mask, 1, 0)
            total = term if total is None else total + term
        a_out[...] = total.astype(LOW).reshape(count, units, pair_width)
        spread("a", a_out, a_in)

    def merge():
        gather_up("a", a_in.at[0 : count - 1])
        for pair in range(heads // 2):
            columns = slice(pair * pair_width, (pair + 1) * pair_width)
            first, second = from_heads(a_in, pair, 0)
            x_att[0:units, columns] = first
            x_att[units:own, columns] = second
        exchange("ea", x_att)

    def project_out():
        value = pooled[...] + both_halves(lambda h: contract(x_att[0:own], w[6, h], 1, 0))
        resid[...] = value
        x_two[0:own] = normal(value, 1, hat_two, root_two)
        exchange("et", x_two)


    def widen(j):
        def run():
            for h in range(2):
                columns = slice(j * features + h * half, j * features + (h + 1) * half)
                value = contract(x_two[0:own], w[in_base + j, h], 1, 0)
                hidden[:, columns] = value
                inner, _ = gelu_parts(value)
                x_act[0:own, columns] = (0.5 * value * (1.0 + inner)).astype(LOW)
            if j == hidden_blocks - 1:
                exchange("ec", x_act)

        return run

    def narrow():
        def side(h):
            total = resid[:, h * half : (h + 1) * half]
            for j in range(hidden_blocks):
                total = total + contract(
                    x_act[0:own, j * features : (j + 1) * features], w[back_base + j, h], 1, 0
                )
            return total

        x_short[0:own] = both_halves(side).astype(LOW)
        exchange("es", x_short)

    outs = [
        pltpu.make_async_copy(mixed, mixed_hbm, local.at[3]),
        pltpu.make_async_copy(grad, grad_hbm, local.at[4]),
    ]

    def place_up(r, value, core, plane):
        for micro in range(micros):
            wide_up[micro, 2 * core + plane, pl.ds(r, units, stride=3), :] = value[micro * units : (micro + 1) * units]

    def lift_away():
        for r in range(3):
            for core in range(2):
                value = contract(t_left[QUARTERS[5], 0:own], w[up_base + r, core, :, plane_span], 1, 0)
                u_out[:, (2 * r + core) * quarter : (2 * r + core + 1) * quarter] = value.astype(LOW)
        send("ux", u_out, u_in, x_peer)

    def lift(r):
        def run():
            for core in range(2):
                place_up(r, contract(x_short[0:own], w[up_base + r, core, :, plane_span], 1, 0), core, x)

        return run

    def finish_mixed():
        arrive("ux")()
        for r in range(3):
            for core in range(2):
                begin = (2 * r + core) * quarter
                place_up(r, u_in[:, begin : begin + quarter].astype(WIDE), core, 1 - x)
        for micro in range(micros):
            for tile in tiles:
                columns = columns_at(tile)
                mixed[micro, :, columns] = tok[micro, :, columns].astype(WIDE) + wide_up[micro, tile]
        outs[0].start()

    plan.add("po", pool, ["pc", *have[0]], (), [shared("en", features)], 0.6, rank=3)
    plan.add("pr", project, ["po", *have[1]], (), spread_sends("q", 3 * units), 0.6, rank=3)
    plan.add("at", attend_now, ["pr"], spread_names("q"), spread_sends("a", units), 1.1, rank=3)
    plan.add("me", merge, ["at"], spread_names("a"), [shared("ea", features)], 0.15, rank=3)
    plan.add("ou", project_out, ["me", *have[2]], (), [shared("et", features)], 0.45, rank=3)
    for j in range(hidden_blocks):
        last = j == hidden_blocks - 1
        plan.add(
            ("wi", j), widen(j), ["ou", *have[3]] + ([("wi", i) for i in range(j)] if last else []), (),
            [shared("ec", hidden_width)] if last else (), 0.3, rank=3,
        )
    plan.add(
        "na", narrow, [("wi", j) for j in range(hidden_blocks)] + [*have[3]], (), [shared("es", features)], 0.5,
        rank=3,
    )
    for r in range(3):
        plan.add(("li", r), lift(r), ["na", *have[5]], (), (), 0.2, rank=8)
    quarter_lump = own * 3 * half * 2
    plan.add("lq", lift_away, [("tw", 5, 0), *have[5]], (), [("ux", "x", quarter_lump)], 0.6, rank=8)
    plan.add("lf", finish_mixed, ["lq", "tok"] + [("li", r) for r in range(3)], ["ux"], (), 0.4, rank=8)

    def back_short_away():
        total = None
        for r in range(3):
            for core in range(2):
                columns = slice(core * quarter, (core + 1) * quarter)
                term = contract(t_in[QUARTERS[5] + r, 0:own, columns], w[up_base + r, core, :, plane_span], 1, 1)
                total = term if total is None else total + term
        dx_out[...] = total.astype(LOW)
        send("dx", dx_out, dx_in, x_peer)

    def back_short_here():
        total = None
        for r in range(3):
            for core in range(2):
                columns = pl.ds(pl.multiple_of(r * features + core * half + x * quarter, quarter), quarter)
                term = contract(d_up[0:own, columns], w[up_base + r, core, :, plane_span], 1, 1)
                total = term if total is None else total + term
        short_grad[...] = total

    def back_short():
        arrive("dx")()
        total = short_grad[...] + dx_in[...].astype(WIDE)
        short_grad[...] = total
        d_low[0:own] = total.astype(LOW)
        exchange("el", d_low)

    def back_widen(j):
        def run():
            total = contract(d_low[0:own, 0:half], w[back_base + j, 0], 1, 1)
            total = total + contract(d_low[0:own, half:features], w[back_base + j, 1], 1, 1)
            columns = slice(j * features, (j + 1) * features)
            value = hidden[:, columns]
            inner, slope = gelu_parts(value)
            factor = 0.5 * (1.0 + inner) + 0.5 * value * (1.0 - inner * inner) * slope
            d_inner[0:own, columns] = (total * factor).astype(LOW)
            if j == hidden_blocks - 1:
                exchange("ei", d_inner)

        return run

    def back_normal(value, which, hat, root):
        unit = hat[...]
        sums[which : which + 1, :] = jnp.sum(value * unit, axis=0, keepdims=True)
        sums[2 + which : 3 + which, :] = jnp.sum(value, axis=0, keepdims=True)
        scaled = value * gain[which : which + 1, :]
        return root[...] * (
            scaled - over_last(jnp.mean, scaled) - unit * over_last(jnp.mean, scaled * unit)
        )

    def back_two():
        total = None
        for j in range(hidden_blocks):
            for h in range(2):
                begin = j * features + h * half
                term = contract(d_inner[0:own, begin : begin + half], w[in_base + j, h], 1, 1)
                total = term if total is None else total + term
        value = short_grad[...] + back_normal(total, 1, hat_two, root_two)
        res_grad[...] = value
        d_res[0:own] = value.astype(LOW)
        exchange("er", d_res)

    def back_out():
        value = contract(d_res[0:own, 0:half], w[6, 0], 1, 1)
        value = value + contract(d_res[0:own, half:features], w[6, 1], 1, 1)
        for pair in range(heads // 2):
            to_heads(value[:, pair * pair_width : (pair + 1) * pair_width], da_out, pair, 0)
        spread("da", da_out, da_in)

    def back_attend():
        gather_up("da", da_in.at[0 : count - 1])
        queries, keys, values = (heads_of(q_in, part) for part in range(3))
        grads = da_in[...].reshape(lane_units, pair_width)
        totals = [None, None, None]
        slope_total = jnp.zeros((1, 1), WIDE)
        for micro in range(micros):
            mask = lanes_of(micro)
            own_grads = grads * mask
            probability = probs[micro]
            grad_prob = contract(own_grads, values, 1, 1)
            scaled = probability * grad_prob
            score = scaled - probability * over_last(jnp.sum, scaled)
            low_score = score.astype(LOW)
            gap = distances().astype(WIDE)
            slope_total = slope_total - jnp.sum(
                jnp.sum(low_score.astype(WIDE) * gap, axis=0, keepdims=True), axis=1, keepdims=True
            )
            terms = (
                contract(low_score, keys * mask, 1, 0) * 0.125,
                contract(low_score, queries * mask, 0, 0) * 0.125,
                contract(probability.astype(LOW), own_grads, 0, 0),
            )
            totals = [term if total is None else total + term for total, term in zip(totals, terms)]
        for part in range(3):
            dq_out[:, part * units : (part + 1) * units, :] = (
                totals[part].astype(LOW).reshape(count, units, pair_width)
            )
        spread("dq", dq_out, dq_in)
        places = lax.broadcasted_iota(jnp.int32, (1, features), 1)
        sums[4:5, :] = jnp.where(places == s, slope_total, 0.0)
        sums[5:8, :] = jnp.zeros((3, features), WIDE)

    def back_project():
        gather_up("dq", dq_in.at[0 : count - 1])
        for part in range(3):
            for pair in range(heads // 2):
                begin = part * features + pair * pair_width
                first, second = from_heads(dq_in, pair, part * units)
                d_qkv[0:units, begin : begin + pair_width] = first
                d_qkv[units:own, begin : begin + pair_width] = second
        exchange("eq", d_qkv)

    def back_one():
        total = None
        for part in range(3):
            for h in range(2):
                begin = part * features + h * half
                term = contract(d_qkv[0:own, begin : begin + half], w[3 + part, h], 1, 1)
                total = term if total is None else total + term
        value = res_grad[...] + back_normal(total, 0, hat_one, root_one)
        d_pool[0:own] = value.astype(LOW)
        exchange("ed1", d_pool)

    def back_pieces():
        for r in range(3):
            value = contract(d_pool[0:own, 0:half], w[r, 0], 1, 1)
            value = value + contract(d_pool[0:own, half:features], w[r, 1], 1, 1)
            for micro in range(micros):
                part = value[micro * units : (micro + 1) * units]
                if r < 2:
                    part = jnp.where(kept(micro), part, 0.0)
                for tile in tiles:
                    wide_grad[micro, tile, pl.ds(6 + r, units, stride=3), :] = part[:, columns_at(tile)]
        send("ed", wide_grad.at[:, :, 0:8], edge_in, (b, lax.rem(s + count - 1, count)))

    def finish_grad():
        flying["ed"].wait_recv()
        inside = (s < count - 1).astype(WIDE)
        for micro in range(micros):
            for tile in tiles:
                columns = columns_at(tile)
                wide_grad[micro, tile, 6 + tokens : 8 + tokens, :] = edge_in[micro, tile, 6:8, :] * inside
                grad[micro, :, columns] = cot[micro, :, columns].astype(WIDE) + wide_grad[micro, tile, 8 : 8 + tokens]
        outs[1].start()

    plan.add(
        "bq", back_short_away, [("tz", 5, r) for r in range(3)] + have[5], (), [("dx", "x", own * features * 2)], 0.6, rank=2
    )
    plan.add("bh", back_short_here, ["cot", *have[5]], (), (), 0.6, rank=3)
    plan.add("bs", back_short, ["bq", "bh"], ["dx"], [shared("el", features)], 0.1, rank=3)
    for j in range(hidden_blocks):
        last = j == hidden_blocks - 1
        plan.add(
            ("bw", j), back_widen(j),
            ["bs", *have[3], ("wi", j)] + ([("bw", i) for i in range(j)] if last else []), (),
            [shared("ei", hidden_width)] if last else (), 0.35, rank=4,
        )
    plan.add(
        "b2", back_two, [("bw", j) for j in range(hidden_blocks)] + [*have[3]], (),
        [shared("er", features)], 0.9, rank=4,
    )
    plan.add("bo", back_out, ["b2", *have[2]], (), spread_sends("da", units), 0.45, rank=4)
    plan.add("ba", back_attend, ["bo", "at"], spread_names("da"), spread_sends("dq", 3 * units), 1.4, rank=4)
    plan.add("bp", back_project, ["ba"], spread_names("dq"), [shared("eq", 3 * features)], 0.2, rank=4)
    plan.add("b1", back_one, ["bp"], (), [shared("ed1", features)], 0.75, rank=4)
    plan.add("bx", back_pieces, ["b1"], (), [("ed", "f", 2 * 8 * features * 4)], 0.65, rank=9)
    plan.add("fg", finish_grad, ["bx", "cot"], ["ed"], (), 0.3, rank=9)

    fixes = (1.0 - beta_one**STEP, 1.0 - beta_two**STEP)

    def finish_small(total):
        for begin, values in ((0, gain), (2, bias)):
            rows = slice(begin, begin + 2)
            new = adam_update(values[...], total[rows], norm_m[rows], norm_v[rows], *fixes, rate_norm, 0.0)
            for place, value in enumerate(new):
                small[4 * place + begin : 4 * place + begin + 2] = value
        new = adam_update(slope_row[...], total[4:5, 0:heads], slope_m[...], slope_v[...], *fixes, rate_slope, 0.0)
        for place, value in enumerate(new):
            small[12 + place : 13 + place, 0:heads] = value

    def fill_slots():
        lanes = lax.broadcasted_iota(jnp.int32, (1, features), 1)
        marks = jnp.zeros((1, features), WIDE)
        for slot in range(masters.shape[0]):
            block, mark, base = jnp.int32(0), jnp.float32(0), 0
            for matrix_id, size in enumerate(sizes):
                begin = start_of(owners, matrix_id, sizes)
                inside = (owners[matrix_id] == b) & (slot >= begin) & (slot < begin + size)
                block = jnp.where(inside, base + slot - begin, block)
                mark = jnp.where(inside, 1.0, mark)
                base += size
            slot_grads[slot] = red[block]
            marks = jnp.where(lanes == slot, mark, marks)
        small[15:16, :] = marks

    def add_pair(step, device):
        def run():
            if step > 0:
                flying[("s", step - 1)].wait_recv()
                sums[8 * step : 8 * step + 8] = sums[8 * step - 8 : 8 * step] + sums_in[8 * step - 8 : 8 * step]
            if device is not None:
                send(("s", step), sums.at[8 * step : 8 * step + 8], sums_in.at[8 * step : 8 * step + 8], device)
            else:
                finish_small(sums[8 * step : 8 * step + 8])

        return run

    partners = [
        core_peer,
        x_peer,
        (b, 2 * z + 1 - y),
        (b, 2 * (z + 1 - 2 * (z % 2)) + y),
        (b, 2 * lax.rem(z + 2, 4) + y),
        None,
    ]
    for step, device in enumerate(partners):
        plan.add(
            ("sum", step), add_pair(step, device), ["b1", "ba"] if step == 0 else [("sum", step - 1)],
            [("s", step - 1)] if step else (), [(("s", step), "f", 8 * features * 4)] if device is not None else (), 0.1,
            rank=0,
        )

    for name, columns in (
        ("ep", "pc"), ("en", "po"), ("ea", "me"), ("et", "ou"), ("ec", ("wi", hidden_blocks - 1)),
        ("es", "na"), ("eu", "cot"), ("el", "bs"), ("ei", ("bw", hidden_blocks - 1)),
        ("er", "b2"), ("eq", "bp"), ("ed1", "b1"),
    ):
        plan.add(("got", name), arrive(name), [columns], [name], cost=0.02)

    def columns_of(block):
        return pl.ds(pl.multiple_of(block * features + c * half, half), half)

    def outer(block, left, left_block, right, right_block):
        def run():
            rows = left[:, left_block * features : (left_block + 1) * features]
            g[block] = contract(rows, right[:, columns_of(right_block)], 0, 0).astype(LOW)

        return run

    def send_either(name, first_source, second_source, target):
        copies = [describe(source, target, x_peer, name) for source in (first_source, second_source)]
        launch(name, copies, [lambda plane=plane: pl.when(x == plane)(copies[plane].start) for plane in range(2)], name)

    def near_away():
        send_either("sn", d_low.at[0:own], x_two.at[0:own], x_near.at[0:own])

    def near_core():
        arrive("sn")()
        exchange("cn", x_near)

    def wide_away(j):
        columns = slice(j * features, (j + 1) * features)

        def run():
            source = (x_act.at[0:own, columns], d_inner.at[0:own, columns])
            send_either(("sw", j), *source, x_wide.at[0:own, columns])

        return run

    def wide_core(j):
        columns = slice(j * features, (j + 1) * features)

        def run():
            arrive(("sw", j))()
            send(("cw", j), x_wide.at[0:own, columns], x_wide.at[own : 2 * own, columns], core_peer)

        return run

    def outer_split(j):
        columns = slice(j * features, (j + 1) * features)

        def run():
            @pl.when(x == 0)
            def _():
                total = contract(x_two[...], d_inner[:, columns_of(j)], 0, 0)
                g[in_base + j] = (total + contract(x_near[...], x_wide[:, columns_of(j)], 0, 0)).astype(LOW)

            @pl.when(x == 1)
            def _():
                total = contract(x_act[:, columns], d_low[:, my_half], 0, 0)
                g[back_base + j] = (total + contract(x_wide[:, columns], x_near[:, my_half], 0, 0)).astype(LOW)

        return run

    lump = own * features * 2
    plan.add("sn", near_away, ["bs", "ou"], (), [("sn", "x", lump)], 0.05, 2)
    plan.add("nc", near_core, ["sn"], ["sn"], [("cn", "c", lump)], 0.05, 2)
    plan.add(("got", "cn"), arrive("cn"), ["nc"], ["cn"], (), 0.02, 2)
    for j in range(hidden_blocks):
        plan.add(("sw", j), wide_away(j), [("wi", j), ("bw", j)], (), [(("sw", j), "x", lump)], 0.05, 2)
        plan.add(("wc", j), wide_core(j), [("sw", j)], [("sw", j)], [(("cw", j), "c", lump)], 0.05, 2)
        plan.add(("got", "cw", j), arrive(("cw", j)), [("wc", j)], [("cw", j)], (), 0.02, 2)
        deps = [("got", e) for e in ("et", "ec", "el", "ei", "cn")] + [("got", "cw", j)]
        plan.add(("gr", j, "s"), outer_split(j), deps, cost=0.6, rank=4.5)
    quartered = {
        0: (x_pool, 3, d_pool, 1, "pc", "b1", "ep", "ed1"),
        1: (x_norm, 1, d_qkv, 3, "po", "bp", "en", "eq"),
        2: (x_att, 1, d_res, 1, "me", "b2", "ea", "er"),
        5: (x_short, 1, d_up, 3, "na", "cot", "es", "eu"),
    }
    quartered = {k: quartered[k] for k in QUARTERS}

    def left_away(k, j):
        columns = slice(j * features, (j + 1) * features)

        def run():
            send(("tx", k, j), quartered[k][0].at[0:own, columns], t_left.at[QUARTERS[k] + j, 0:own], x_peer)

        return run

    def left_core(k, j):
        place = QUARTERS[k] + j

        def run():
            arrive(("tx", k, j))()
            send(("tc", k, j), t_left.at[place, 0:own], t_left.at[place, own : 2 * own], core_peer)

        return run

    def right_away(k, r):
        place = QUARTERS[k] + r

        def run():
            for core in range(2):
                begin = r * features + core * half + (1 - x) * quarter
                t_out[place, :, core * quarter : (core + 1) * quarter] = quartered[k][2][
                    0:own, pl.ds(pl.multiple_of(begin, quarter), quarter)
                ]
            if k == 5:
                send(("ty", k, r), t_out.at[place], t_in.at[place, 0:own], x_peer)
                return
            lanes = [pl.ds(pl.multiple_of(core * quarter, quarter), quarter) for core in (c, 1 - c)]
            send(("ty", k, r), t_out.at[place, :, lanes[0]], t_in.at[place, 0:own, 0:quarter], x_peer, ("ty", k, r))
            send(("tu", k, r), t_out.at[place, :, lanes[1]], t_in.at[place, own : 2 * own, 0:quarter], cross_peer, ("ty", k, r))

        return run

    def right_core(k, r):
        place = QUARTERS[k] + r

        def run():
            arrive(("ty", k, r))()
            send(("td", k, r), t_in.at[place, 0:own], t_in.at[place, own : 2 * own], core_peer)

        return run

    def outer_quarter(k, j, r):
        def run():
            left, _, right = quartered[k][:3]
            near = pl.ds(pl.multiple_of(r * features + c * half + x * quarter, quarter), quarter)
            away = pl.ds(pl.multiple_of(c * quarter, quarter), quarter) if k == 5 else slice(0, quarter)
            total = contract(left[:, j * features : (j + 1) * features], right[:, near], 0, 0)
            total = total + contract(t_left[QUARTERS[k] + j], t_in[QUARTERS[k] + r, :, away], 0, 0)
            g[spans[k][0] + j + r, :, plane_span] = total.astype(LOW)

        return run

    for k, (_, lefts, _, rights, left_dep, right_dep, left_got, right_got) in quartered.items():
        urgency = 3.5 if k == 0 else 2.5
        for j in range(lefts):
            plan.add(("tx", k, j), left_away(k, j), [left_dep] + list(AFTER.get(k, ())), (), [(("tx", k, j), "x", lump)], 0.05, urgency)
            plan.add(("tw", k, j), left_core(k, j), [("tx", k, j)], [("tx", k, j)], [(("tc", k, j), "c", lump)], 0.05, urgency)
            plan.add(("got", "tc", k, j), arrive(("tc", k, j)), [("tw", k, j)], [("tc", k, j)], (), 0.02, urgency)
        for r in range(rights):
            if k != 5:
                parts = [("ty", k, r), ("tu", k, r)]
                whole = t_in.at[QUARTERS[k] + r, :, 0:quarter]
                plan.add(parts[0], right_away(k, r), [right_dep], (), [(p, "x", lump // 4) for p in parts], 0.1, 2.5)
                take = lambda k=k, r=r, whole=whole: gather_up(("ty", k, r), whole)
                plan.add(("got", "td", k, r), take, parts[:1], parts, (), 0.02, 2.5)
                continue
            plan.add(("ty", k, r), right_away(k, r), [right_dep], (), [(("ty", k, r), "x", lump // 2)], 0.05, 2.5)
            plan.add(("tz", k, r), right_core(k, r), [("ty", k, r)], [("ty", k, r)], [(("td", k, r), "c", lump // 2)], 0.05, 2.5)
            plan.add(("got", "td", k, r), arrive(("td", k, r)), [("tz", k, r)], [("td", k, r)], (), 0.02, 2.5)
        for j in range(lefts if k not in WHOLE else 0):
            for r in range(rights):
                deps = [("got", left_got), ("got", right_got), ("got", "tc", k, j), ("got", "td", k, r)]
                plan.add(("gr", spans[k][0] + j + r), outer_quarter(k, j, r), deps, cost=0.4, rank=5)
    weight_grads = []
    for r in range(3):
        for k, left, left_block, right, right_block, deps in (
            (0, x_pool, r, d_pool, 0, ("ep", "ed1")), (1, x_norm, 0, d_qkv, r, ("en", "eq")),
            (2, x_att, 0, d_res, 0, ("ea", "er")), (5, x_short, 0, d_up, r, ("es", "eu")),
        ):
            if (k in WHOLE or k not in QUARTERS) and r < sizes[k]:
                deps = [("got", dep) for dep in deps]
                weight_grads.append((spans[k][0] + r, left, left_block, right, right_block, deps))
    for block, left, left_block, right, right_block, deps in weight_grads:
        plan.add(("gr", block), outer(block, left, left_block, right, right_block), deps, cost=0.3, rank=5)

    def scatter_chunk(rank, name, here, there, size, deps):
        split, quarters = there is not None, there is here
        blocks = pl.ds(here, size)
        load = size * piece_bytes // (2 if quarters else 1)
        away, span, away_span, length_out = blocks, slice(None), slice(None), half
        begin_out, away_out = c * half, c * half
        if quarters:
            span, away_span = plane_span, plane_away
            length_out, begin_out, away_out = quarter, c * half + x * quarter, c * half + (1 - x) * quarter
        elif split:
            away = pl.ds(there, size)
        out_span = pl.ds(pl.multiple_of(begin_out, length_out), length_out)
        out_away = pl.ds(pl.multiple_of(away_out, length_out), length_out)

        half_rows = rows_of // 2
        sides = (("R", 0, right_in, right_peer), ("L", half_rows, left_in, left_peer))

        def first_step():
            for side, part, inbox, peer in sides:
                source = g.at[blocks, rows_at(4, part, half_rows), span]
                target = inbox.at[0, blocks, part : part + half_rows, span]
                send((side, "s", 1, name), source, target, peer, ("s", 1, name))

        def take(step):
            gather_up(("s", step, name), g.at[blocks, 0 : rows_of * (1 if step == 1 else 2), span])

        def next_step(step):
            def run():
                take(step - 1)
                for side, half_part, inbox, peer in sides:
                    offset = (5 - step) if side == "R" else (step - 5)
                    part, length = (half_part, half_rows) if step == 2 else (0, rows_of)
                    rows = rows_at(offset, part, length)
                    g[blocks, rows, span] = g[blocks, rows, span] + inbox[step - 2, blocks, part : part + length, span]
                    source = g.at[blocks, rows_at(offset), span]
                    send((side, "s", step, name), source, inbox.at[step - 1, blocks, :, span], peer, ("s", step, name))

            return run

        def finish():
            take(4)
            total = g[blocks, rows_at(0), span].astype(WIDE)
            total = total + right_in[3, blocks, :, span].astype(WIDE) + left_in[3, blocks, :, span].astype(WIDE)
            fin_out[blocks, :, span] = total.astype(LOW)
            send(("rx", name), fin_out.at[blocks, :, span], fin_in.at[blocks, :, span], x_peer)
            if quarters:
                send(("rd", name), fin_out.at[blocks, :, span], co_in.at[blocks, :, span], cross_peer)
            if split:
                send(("rc", name), fin_out.at[blocks, :, span], co_in.at[blocks, :, span], core_peer)
                red[blocks, :, out_span] = fin_out[blocks, :, span]

        def finish_x():
            arrive(("rx", name))()
            if split:
                red[away, :, out_away] = fin_in[away, :, away_span]
                if not quarters:
                    send(("rd", name), fin_in.at[away, :, away_span], co_in.at[away, :, away_span], core_peer)
            else:
                total = (fin_out[blocks].astype(WIDE) + fin_in[blocks].astype(WIDE)).astype(LOW)
                co_out[blocks] = total
                red[blocks, :, my_half] = total
                send(("rc", name), co_out.at[blocks], co_in.at[blocks], core_peer)

        def finish_core():
            arrive(("rc", name), *([("rd", name)] if split else []))()
            red[blocks, :, other_half] = co_in[blocks]
            if split and not quarters:
                red[away, :, other_half] = co_in[away]

        links = (("R", "r"), ("L", "l"))
        out = [((side, "s", 1, name), link, load // 2) for side, link in links]
        plan.add(("r", 1, name), first_step, deps, (), out, 0.05, rank)
        for step in (2, 3, 4):
            waits = [(side, "s", step - 1, name) for side in "RL"]
            out = [((side, "s", step, name), link, load) for side, link in links]
            plan.add(("r", step, name), next_step(step), [("r", step - 1, name)], waits, out, 0.04 * size, rank)
        own_out = [(("rc", name), "c", load)]
        plan.add(
            ("fi", name), finish, [("r", 4, name)], [("R", "s", 4, name), ("L", "s", 4, name)],
            [(("rx", name), "x", load)] + (own_out if split else []) + ([(("rd", name), "x", load)] if quarters else []),
            0.02 * size, rank,
        )
        late_out = ([] if quarters else [(("rd", name), "c", load)]) if split else own_out
        plan.add(("fx", name), finish_x, [("fi", name)], [("rx", name)], late_out, 0.02 * size, rank)
        plan.add(
            ("fc", name), finish_core, [("fx", name)], [("rc", name)] + ([("rd", name)] if split else []), (), 0.02 * size, rank
        )

    for k, offset, size, rank in SCATTERS:
        name = ("g", k, offset)
        if k == 3:
            deps = [("gr", j, "s") for j in range(offset, offset + size)]
            scatter_chunk(rank, name, ours + offset, theirs + offset, size, deps)
        else:
            begin = spans[k][0] + offset
            scatter_chunk(rank, name, begin, begin if k in QUARTERS and k not in WHOLE else None, size, [("gr", begin + j) for j in range(size)])

    plan.add("mo", lambda: [copy.start() for copy in moments], ["pc"], (), (), 0.02, rank=8)
    plan.add("sl", fill_slots, ["mo"] + [("fc", ("g", k, offset)) for k, offset, _, _ in SCATTERS], (), (), 0.2, rank=9)
    for name, _ in plan.order():
        plan.tasks[name][0]()
    assert len(boxes) <= RECEIVES
    for copy in started[-SENDS:]:
        copy.wait_send()
    for copy in outs + moments:
        copy.wait()


def adam_kernel(refs):
    grads, small, master, first, second, mixed, grad = refs[:7]
    new_w, new_m, new_v, new_low, mixed_out, grad_out = refs[7:13]
    norm_outs, slope_outs = refs[13:16], refs[16:19]
    step = pl.program_id(0)
    fixes = (1.0 - beta_one**STEP, 1.0 - beta_two**STEP)
    rows = mixed_out.shape[0]
    part = pl.ds(pl.multiple_of(step * rows, 8), rows)
    mixed_out[...] = mixed[part]
    grad_out[...] = grad[part]

    @pl.when(step == 0)
    def _():
        heads = slope_outs[0].shape[1]
        for place in range(3):
            norm_outs[place][...] = small[4 * place : 4 * place + 4]
            slope_outs[place][...] = small[12 + place : 13 + place, 0:heads]

    count = new_w.shape[0]
    lanes = lax.broadcasted_iota(jnp.int32, (1, small.shape[1]), 1)
    for place in range(count):
        slot = step * count + place
        old = (master[slot], first[slot], second[slot])
        values = adam_update(old[0], grads[slot].astype(WIDE), old[1], old[2], *fixes, rate_matrix, decay_rate)
        mark = jnp.sum(jnp.where(lanes == slot, small[15:16, :], 0.0), axis=1, keepdims=True)
        keep = jnp.broadcast_to(mark, old[0].shape) > 0.5
        weight, new_m[place], new_v[place] = (jnp.where(keep, new, was) for new, was in zip(values, old))
        new_w[place] = weight
        new_low[place] = weight.astype(LOW)


def fused_body(tokens, cotangent, doc_lengths, owners, master, first_moment, second_moment, ln_gain, ln_bias, norm_m, norm_v, slopes, slope_m, slope_v):
    micros, _, tok_rows, features = tokens.shape
    units, heads, width = tok_rows // 3, slopes.shape[0], features // slopes.shape[0]
    sizes = tuple(block_counts(features, FF))
    blocks, own, half = sum(sizes), micros * units, features // 2
    slots, rows = master.shape[1], master.shape[2]
    lane_units = units * heads
    split = features // TILE
    hbm, vmem, anywhere = (pl.BlockSpec(memory_space=m) for m in (pltpu.HBM, pltpu.VMEM, pl.ANY))
    low = lambda *shape: pltpu.VMEM(shape, LOW)
    wide = lambda *shape: pltpu.VMEM(shape, WIDE)
    pieces = lambda: low(blocks, rows, half)
    both = lambda columns: low(2 * own, columns)
    scratch = [
        pltpu.SMEM(owners.shape, jnp.int32), pltpu.SMEM((micros, doc_lengths.shape[2]), jnp.int32),
        pltpu.SMEM(slopes.shape, WIDE), wide(2, features), wide(2, features), wide(4, features), wide(4, features),
        wide(1, heads), wide(1, heads), wide(1, heads),
        low(blocks, 2, features, half), low(blocks, rows, features), pieces(), pieces(), pieces(), pieces(), pieces(),
        low(micros, tok_rows, features), low(micros, tok_rows, features), low(micros, 16, features),
        wide(micros, split, 16 + tok_rows, TILE), wide(micros, split, tok_rows, TILE),
        both(3 * features), both(features), both(features), both(features), both(FF), both(features),
        both(3 * features), both(features), both(FF), both(features), both(3 * features), both(features),
        wide(own, features), wide(own, features), wide(own, features), wide(own, 1), wide(own, 1),
        wide(own, features), wide(own, FF), wide(own, features), wide(own, features),
        low(heads, 3 * units, 2 * width), low(heads, 3 * units, 2 * width), low(heads, units, 2 * width),
        low(heads, units, 2 * width), low(heads, units, 2 * width), low(heads, units, 2 * width),
        low(heads, 3 * units, 2 * width), low(heads, 3 * units, 2 * width),
        wide(micros, lane_units, lane_units), wide(micros, tok_rows, features), wide(micros, tok_rows, features),
        wide(micros, split, tok_rows, TILE), wide(micros, split, 8 + tok_rows, TILE), wide(micros, split, 8, TILE),
        low(2 * own, features), low(2 * own, FF),
        low(10, 2 * own, features), low(10, own, half), low(10, 2 * own, half),
        low(own, 3 * half), low(own, 3 * half), low(own, features), low(own, features), low(blocks, features, half), low(4, blocks, rows, half), low(4, blocks, rows, half),
        pieces(), pieces(), pieces(), pieces(), wide(48, features), wide(40, features),
        pltpu.SemaphoreType.DMA((SENDS,)), pltpu.SemaphoreType.DMA((RECEIVES,)), pltpu.SemaphoreType.DMA((17,)),
    ]
    token_shape = (micros, tok_rows, features)
    dims = (units, features, FF, heads, micros, sizes)
    moment_shape = jax.ShapeDtypeStruct((slots, rows, features), WIDE)
    mixed, grad, grads, small, weights, firsts, seconds = pl.pallas_call(
        lambda *refs: main_kernel(dims, refs),
        out_shape=(
            jax.ShapeDtypeStruct(token_shape, WIDE),
            jax.ShapeDtypeStruct(token_shape, WIDE),
            jax.ShapeDtypeStruct((slots, rows, features), LOW),
            jax.ShapeDtypeStruct((16, features), WIDE),
            moment_shape, moment_shape, moment_shape,
        ),
        in_specs=[hbm] * 15,
        out_specs=(anywhere, anywhere) + (vmem,) * 5,
        scratch_shapes=scratch,
        compiler_params=pltpu.CompilerParams(
            collective_id=0, has_side_effects=True, vmem_limit_bytes=47 * 2**20
        ),
        name="block",
    )(*[pltpu.with_memory_space_constraint(value, pltpu.HBM) for value in (
        owners, doc_lengths[:, 0], slopes, ln_gain, ln_bias, norm_m, norm_v, slopes[None], slope_m[None], slope_v[None],
        tokens[:, 0], cotangent[:, 0], master[0], first_moment[0], second_moment[0],
    )])
    steps = 2
    flat = (micros * tok_rows, features)
    slot = pl.BlockSpec((slots // steps, rows, features), lambda j: (j, 0, 0))
    some = pl.BlockSpec((flat[0] // steps, features), lambda j: (j, 0))
    norm_shape = jax.ShapeDtypeStruct((4, features), WIDE)
    slope_shape = jax.ShapeDtypeStruct((1, heads), WIDE)
    out = pl.pallas_call(
        lambda *refs: adam_kernel(refs),
        grid=(steps,),
        out_shape=(
            moment_shape, moment_shape, moment_shape, jax.ShapeDtypeStruct((slots, rows, features), LOW),
            jax.ShapeDtypeStruct(flat, WIDE), jax.ShapeDtypeStruct(flat, WIDE),
            norm_shape, norm_shape, norm_shape, slope_shape, slope_shape, slope_shape,
        ),
        in_specs=[vmem] * 7,
        out_specs=(slot, slot, slot, slot, some, some) + (vmem,) * 6,
        compiler_params=pltpu.CompilerParams(dimension_semantics=("arbitrary",), vmem_limit_bytes=12 * 2**20),
        name="adam",
    )(grads, small, weights, firsts, seconds, mixed.reshape(flat), grad.reshape(flat))
    new_w, new_m, new_v, new_low, mixed, grad, norm, norm_m, norm_v, slope, slope_m, slope_v = out
    return (
        mixed.reshape(tokens.shape), grad.reshape(tokens.shape), new_w[None], new_m[None], new_v[None], new_low[None], norm, norm_m, norm_v,
        slope[0], slope_m[0], slope_v[0],
    )


def fits(mesh, shapes):
    return mesh.shape["batch"] == 4 and mesh.shape["seq"] == 8 and shapes[0].shape[1] == 1


def solution(mesh):
    in_specs = (
        P("batch", None, "seq", None),
        P("batch", None, "seq", None),
        P("batch", None, None),
        P(),
        P("batch", None, "seq", None),
        P("batch", None, "seq", None),
        P("batch", None, "seq", None),
        P(),
        P(),
        P(),
        P(),
        P(),
        P(),
        P(),
    )
    out_specs = (
        P("batch", None, "seq", None),
        P("batch", None, "seq", None),
        P("batch", None, "seq", None),
        P("batch", None, "seq", None),
        P("batch", None, "seq", None),
        P("batch", None, "seq", None),
        P(),
        P(),
        P(),
        P(),
        P(),
        P(),
    )

    def whole(*args):
        part = fused_body if fits(mesh, args) else body
        return jax.shard_map(
            part, mesh=mesh, in_specs=in_specs, out_specs=out_specs, check_vma=False
        )(*args)

    return whole
```

```python
import math

import jax
import jax.numpy as jnp
from jax import lax
from jax.experimental import pallas as pl
from jax.experimental.pallas import tpu as pltpu
from jax.sharding import PartitionSpec as P

FF = 2048
STEP = 10


beta_one = 0.9
beta_two = 0.95
adam_eps = 1e-08
decay_rate = 0.1
rate_matrix = 0.02
rate_norm = 0.2
rate_slope = 0.01
ln_eps = 1e-05
masked_score = -1000000000.0
row_kinds = (True, False, True, False, True, False)


def broadcast(value, axis, source):
    kept = jnp.where(lax.axis_index(axis) == source, value, 0).astype(value.dtype)
    return lax.psum(kept, axis)


def running_total(lengths):
    count = lengths.shape[-1]
    ends = [lengths[..., 0]]
    for index in range(1, count):
        ends.append(ends[-1] + lengths[..., index])
    return jnp.stack(ends, -1)


def for_sending(value):

    def short(part):
        return part.astype(jnp.bfloat16) if part.dtype == jnp.float32 else part

    return jax.tree.map(short, value)


def passed_along(value, axis, by):
    peers = lax.axis_size(axis)
    pairs = [(i, i + by) for i in range(peers) if 0 <= i + by < peers]
    return lax.ppermute(value, axis, pairs)


def layer_norm(values, gain, shift):
    center = jnp.mean(values, -1, keepdims=True)
    centred = values - center
    spread = jnp.mean(centred * centred, -1, keepdims=True)
    return centred * lax.rsqrt(spread + ln_eps) * gain + shift


def gelu_tanh(values):
    return jax.nn.gelu(values, approximate=True)


def block_counts(features, hidden):
    return [3, 3, 1, hidden // features, hidden // features, 3]


def block_starts(owners, sizes):
    starts_list = []
    for matrix_id in range(len(sizes)):
        shared = jnp.zeros((), jnp.int32)
        for earlier_id in range(matrix_id):
            shared = shared + jnp.where(
                owners[earlier_id] == owners[matrix_id], sizes[earlier_id], 0
            ).astype(jnp.int32)
        starts_list.append(shared)
    return starts_list


def slot_table(owners, device, sizes, slot_count):
    starts_list = block_starts(owners, sizes)
    slot_ids = jnp.arange(slot_count, dtype=jnp.int32)
    numbers = jnp.arange(sum(sizes), dtype=jnp.int32)
    slot_map = jnp.zeros((slot_count, sum(sizes)), jnp.float32)
    block_base = 0
    for matrix_id in range(len(sizes)):
        inside = (
            (owners[matrix_id] == device)
            & (slot_ids >= starts_list[matrix_id])
            & (slot_ids < starts_list[matrix_id] + sizes[matrix_id])
        )
        target = block_base + slot_ids - starts_list[matrix_id]
        slot_map = slot_map + (inside[:, None] & (target[:, None] == numbers[None, :])).astype(
            jnp.float32
        )
        block_base += sizes[matrix_id]
    return slot_map


def to_matrix(blocks, by_rows):
    if by_rows:
        return blocks.reshape(-1, blocks.shape[2])
    return blocks.transpose(1, 0, 2).reshape(blocks.shape[1], -1)


def to_blocks(matrix, by_rows, features):
    if by_rows:
        return matrix.reshape(-1, features, features)
    return matrix.reshape(features, -1, features).transpose(1, 0, 2)


def all_blocks(matrices, features):
    return jnp.concatenate(
        [to_blocks(matrices[matrix_id], row_kinds[matrix_id], features) for matrix_id in range(6)],
        0,
    )


def adam_update(weight, gradient, first_moment, second, fix_first, fix_second, rate, decay):
    first_new = beta_one * first_moment + (1.0 - beta_one) * gradient
    second_new = beta_two * second + (1.0 - beta_two) * gradient * gradient
    direction = first_new / fix_first / (jnp.sqrt(second_new / fix_second) + adam_eps)
    return (weight - rate * (direction + decay * weight), first_new, second_new)


def scores_for(query_block, key_rows, start_row, segment, head_slope):
    block_rows = query_block.shape[0]
    row_total = key_rows.shape[0]
    row_ids = start_row + jnp.arange(block_rows, dtype=jnp.int32)
    col_ids = jnp.arange(row_total, dtype=jnp.int32)
    distance = (row_ids[:, None] - col_ids[None, :]).astype(jnp.float32)
    seg_rows = lax.dynamic_slice_in_dim(segment, start_row, block_rows)
    allowed = (seg_rows[:, None] == segment[None, :]) & (col_ids[None, :] <= row_ids[:, None])
    raw_score = (
        jnp.dot(query_block, key_rows.T, preferred_element_type=jnp.float32) * 0.125
        - head_slope * distance
    )
    return (jnp.where(allowed, raw_score, masked_score), distance)


def attend(queries, key_rows, values, segment, head_slope, block_rows):
    row_total, head_width = queries.shape

    def per_block(start_row):
        query_block = lax.dynamic_slice_in_dim(queries, start_row, block_rows)
        scores, distance = scores_for(query_block, key_rows, start_row, segment, head_slope)
        largest = jnp.max(scores, -1, keepdims=True)
        log_total = largest + jnp.log(jnp.sum(jnp.exp(scores - largest), -1, keepdims=True))
        probability = jnp.exp(scores - log_total).astype(jnp.bfloat16)
        return (jnp.dot(probability, values, preferred_element_type=jnp.float32), log_total[:, 0])

    row_starts = jnp.arange(row_total // block_rows, dtype=jnp.int32) * block_rows
    attended, log_totals = lax.map(per_block, row_starts)
    return (attended.reshape(row_total, head_width), log_totals.reshape(row_total))


def attend_back(queries, key_rows, values, segment, head_slope, log_totals, grad_out, block_rows):
    row_total, head_width = queries.shape

    def per_block(carried, start_row):
        grad_keys, grad_values, grad_slope = carried
        query_block = lax.dynamic_slice_in_dim(queries, start_row, block_rows)
        grad_block = lax.dynamic_slice_in_dim(grad_out, start_row, block_rows)
        total_block = lax.dynamic_slice_in_dim(log_totals, start_row, block_rows)
        scores, distance = scores_for(query_block, key_rows, start_row, segment, head_slope)
        probability = jnp.exp(scores - total_block[:, None])
        grad_prob = jnp.dot(grad_block, values.T, preferred_element_type=jnp.float32)
        grad_score = (
            probability * (grad_prob - jnp.sum(probability * grad_prob, -1, keepdims=True))
        ).astype(jnp.bfloat16)
        grad_query = jnp.dot(grad_score, key_rows, preferred_element_type=jnp.float32) * 0.125
        grad_keys = (
            grad_keys
            + jnp.dot(grad_score.T, query_block, preferred_element_type=jnp.float32) * 0.125
        )
        grad_values = grad_values + jnp.dot(
            probability.astype(jnp.bfloat16).T, grad_block, preferred_element_type=jnp.float32
        )
        grad_slope = grad_slope - jnp.sum(grad_score.astype(jnp.float32) * distance)
        return ((grad_keys, grad_values, grad_slope), grad_query)

    row_starts = jnp.arange(row_total // block_rows, dtype=jnp.int32) * block_rows
    initial = (
        jnp.zeros((row_total, head_width), jnp.float32),
        jnp.zeros((row_total, head_width), jnp.float32),
        jnp.zeros((), jnp.float32),
    )
    (grad_keys, grad_values, grad_slope), grad_queries = lax.scan(per_block, initial, row_starts)
    return (grad_queries.reshape(row_total, head_width), grad_keys, grad_values, grad_slope)


def body(
    tokens,
    cotangent,
    doc_lengths,
    owners,
    master,
    first_moment,
    second_moment,
    ln_gain,
    ln_bias,
    norm_m,
    norm_v,
    slopes,
    slope_m,
    slope_v,
):
    micro_count, lane_count, tok_rows, features = tokens.shape
    unit_rows = tok_rows // 3
    seq_devices = lax.axis_size("seq")
    head_count = slopes.shape[0]
    head_width = features // head_count
    lane_units = unit_rows * seq_devices
    block_rows = min(512, lane_units)
    unit_total = lane_count * unit_rows
    slot_count = master.shape[1]
    sizes = block_counts(features, FF)
    starts_list = block_starts(owners, sizes)
    batch_rank = lax.axis_index("batch")
    seq_rank = lax.axis_index("seq")
    lane_rank = seq_rank // head_count
    head_rank = seq_rank % head_count
    low_slots = master[0].astype(jnp.bfloat16)
    fetched = []
    for matrix_id in range(6):
        owned_rows = lax.dynamic_slice_in_dim(
            low_slots, starts_list[matrix_id], sizes[matrix_id], 0
        )
        fetched.append(broadcast(owned_rows, "batch", owners[matrix_id]))
    gathered = lax.all_gather(for_sending(tuple(fetched)), "seq", axis=1, tiled=True)
    pool_weight, qkv_weight, out_weight, in_weight, back_weight, up_weight = [
        to_matrix(gathered[matrix_id], row_kinds[matrix_id]) for matrix_id in range(6)
    ]
    doc_ends = running_total(doc_lengths)
    doc_starts = jnp.concatenate(
        [jnp.zeros((micro_count, lane_count, 1), jnp.int32), doc_ends[..., :-1]], -1
    )
    unit_ids = seq_rank * unit_rows + jnp.arange(unit_rows, dtype=jnp.int32)
    keep_mask = 1.0 - jnp.any(
        unit_ids[None, None, :, None] == doc_starts[:, :, None, :], -1
    ).astype(jnp.float32)
    triples = tokens.reshape(micro_count, lane_count, unit_rows, 3, features)
    tail_tokens = triples[:, :, -1, 1:3]
    arrived = passed_along(tail_tokens, "seq", 1)
    lane_pick = jnp.arange(lane_count, dtype=jnp.int32) == lane_rank
    head_pick = jnp.arange(head_count, dtype=jnp.int32) == head_rank
    head_slope = jnp.sum(jnp.where(head_pick, slopes, 0.0))
    positions = jnp.arange(lane_units, dtype=jnp.int32)
    gain_grad = jnp.zeros((2, features), jnp.float32)
    bias_grad = jnp.zeros((2, features), jnp.float32)
    slope_grad = jnp.zeros((), jnp.float32)
    summed = None
    mixed_parts = []
    grad_parts = []
    outgoing = []
    for micro in range(micro_count):
        triple_now = triples[micro]
        keep_now = keep_mask[micro]
        earlier = jnp.concatenate([arrived[micro][:, None], triple_now[:, :-1, 1:3]], 1) * keep_now[
            :, :, None, None
        ].astype(jnp.bfloat16)
        pool_input = jnp.concatenate([earlier, triple_now[:, :, 0:1]], 2).reshape(
            unit_total, 3 * features
        )
        pooled = jnp.dot(pool_input, pool_weight, preferred_element_type=jnp.float32)
        normed = layer_norm(pooled, ln_gain[0], ln_bias[0]).astype(jnp.bfloat16)
        projected = jnp.dot(normed, qkv_weight, preferred_element_type=jnp.float32).astype(
            jnp.bfloat16
        )
        outbound = (
            projected.reshape(lane_count, unit_rows, 3, head_count, head_width)
            .transpose(0, 3, 1, 2, 4)
            .reshape(lane_count * head_count, unit_rows * 3 * head_width)
        )
        received = lax.all_to_all(outbound, "seq", split_axis=0, concat_axis=1, tiled=True).reshape(
            lane_units, 3, head_width
        )
        queries = received[:, 0]
        key_rows = received[:, 1]
        values = received[:, 2]
        lengths = jnp.sum(jnp.where(lane_pick[:, None], doc_lengths[micro], 0), 0)
        lane_ends = running_total(lengths)
        segment = jnp.sum((positions[:, None] >= lane_ends[None, :-1]).astype(jnp.int32), 1)
        attended, log_totals = attend(queries, key_rows, values, segment, head_slope, block_rows)
        returned = lax.all_to_all(
            attended.astype(jnp.bfloat16).reshape(1, lane_units * head_width),
            "seq",
            split_axis=1,
            concat_axis=0,
            tiled=True,
        )
        merged = (
            returned.reshape(lane_count, head_count, unit_rows, head_width)
            .transpose(0, 2, 1, 3)
            .reshape(unit_total, features)
        )
        residual = pooled + jnp.dot(merged, out_weight, preferred_element_type=jnp.float32)
        normed_two = layer_norm(residual, ln_gain[1], ln_bias[1]).astype(jnp.bfloat16)
        hidden = jnp.dot(normed_two, in_weight, preferred_element_type=jnp.float32)
        activated = gelu_tanh(hidden).astype(jnp.bfloat16)
        shortened = residual + jnp.dot(activated, back_weight, preferred_element_type=jnp.float32)
        short_low = shortened.astype(jnp.bfloat16)
        upward = jnp.dot(short_low, up_weight, preferred_element_type=jnp.float32).reshape(
            lane_count, unit_rows * 3, features
        )
        mixed_parts.append(tokens[micro].astype(jnp.float32) + upward)
        grad_upward = cotangent[micro].reshape(unit_total, 3 * features)
        sum_up = jnp.dot(short_low.T, grad_upward, preferred_element_type=jnp.float32)
        grad_short = jnp.dot(grad_upward, up_weight.T, preferred_element_type=jnp.float32)
        grad_short_low = grad_short.astype(jnp.bfloat16)
        sum_back = jnp.dot(activated.T, grad_short_low, preferred_element_type=jnp.float32)
        grad_activated = jnp.dot(grad_short_low, back_weight.T, preferred_element_type=jnp.float32)
        grad_hidden = jax.vjp(gelu_tanh, hidden)[1](grad_activated)[0].astype(jnp.bfloat16)
        sum_in = jnp.dot(normed_two.T, grad_hidden, preferred_element_type=jnp.float32)
        grad_normed_two = jnp.dot(grad_hidden, in_weight.T, preferred_element_type=jnp.float32)
        norm_two_back = jax.vjp(layer_norm, residual, ln_gain[1], ln_bias[1])[1]
        grad_resid_norm, grad_gain_two, grad_bias_two = norm_two_back(grad_normed_two)
        grad_residual = grad_short + grad_resid_norm
        grad_resid_low = grad_residual.astype(jnp.bfloat16)
        sum_out = jnp.dot(merged.T, grad_resid_low, preferred_element_type=jnp.float32)
        grad_merged = jnp.dot(
            grad_resid_low, out_weight.T, preferred_element_type=jnp.float32
        ).astype(jnp.bfloat16)
        back_outbound = (
            grad_merged.reshape(lane_count, unit_rows, head_count, head_width)
            .transpose(0, 2, 1, 3)
            .reshape(lane_count * head_count, unit_rows * head_width)
        )
        grad_attended = lax.all_to_all(
            back_outbound, "seq", split_axis=0, concat_axis=1, tiled=True
        ).reshape(lane_units, head_width)
        grad_queries, grad_keys, grad_values, grad_slope = attend_back(
            queries, key_rows, values, segment, head_slope, log_totals, grad_attended, block_rows
        )
        grad_heads = (
            jnp.stack([grad_queries, grad_keys, grad_values], 1)
            .astype(jnp.bfloat16)
            .reshape(1, lane_units * 3 * head_width)
        )
        grad_arrived = lax.all_to_all(grad_heads, "seq", split_axis=1, concat_axis=0, tiled=True)
        grad_projected = (
            grad_arrived.reshape(lane_count, head_count, unit_rows, 3, head_width)
            .transpose(0, 2, 3, 1, 4)
            .reshape(unit_total, 3 * features)
        )
        sum_qkv = jnp.dot(normed.T, grad_projected, preferred_element_type=jnp.float32)
        grad_normed = jnp.dot(grad_projected, qkv_weight.T, preferred_element_type=jnp.float32)
        norm_one_back = jax.vjp(layer_norm, pooled, ln_gain[0], ln_bias[0])[1]
        grad_pool_norm, grad_gain_one, grad_bias_one = norm_one_back(grad_normed)
        grad_pooled_low = (grad_residual + grad_pool_norm).astype(jnp.bfloat16)
        sum_pool = jnp.dot(pool_input.T, grad_pooled_low, preferred_element_type=jnp.float32)
        grad_pieces = jnp.dot(
            grad_pooled_low, pool_weight.T, preferred_element_type=jnp.float32
        ).reshape(lane_count, unit_rows, 3, features)
        grad_earlier = grad_pieces[:, :, 0:2] * keep_now[:, :, None, None]
        outgoing.append(grad_earlier[:, 0])
        following = jnp.concatenate(
            [grad_earlier[:, 1:], jnp.zeros((lane_count, 1, 2, features), jnp.float32)], 1
        )
        token_grad = jnp.concatenate([grad_pieces[:, :, 2:3], following], 2).reshape(
            lane_count, unit_rows * 3, features
        )
        grad_parts.append(cotangent[micro].astype(jnp.float32) + token_grad)
        gain_grad = gain_grad + jnp.stack([grad_gain_one, grad_gain_two])
        bias_grad = bias_grad + jnp.stack([grad_bias_one, grad_bias_two])
        slope_grad = slope_grad + grad_slope
        micro_grads = [sum_pool, sum_qkv, sum_out, sum_in, sum_back, sum_up]
        summed = (
            micro_grads
            if summed is None
            else [left + right for left, right in zip(summed, micro_grads)]
        )
    reduced = lax.psum_scatter(all_blocks(summed, features), "seq", scatter_dimension=1, tiled=True)
    incoming = passed_along(jnp.stack(outgoing).astype(jnp.bfloat16), "seq", -1).astype(jnp.float32)
    grad_tokens = jnp.stack(grad_parts).reshape(micro_count, lane_count, unit_rows, 3, features)
    grad_tokens = grad_tokens.at[:, :, -1, 1:3].add(incoming).reshape(tokens.shape)
    reduced_all = lax.psum(reduced, "batch")
    norm_grad, slopes_grad = lax.psum(
        (jnp.concatenate([gain_grad, bias_grad], 0), jnp.where(head_pick, slope_grad, 0.0)),
        ("batch", "seq"),
    )
    slot_map = slot_table(owners, batch_rank, sizes, slot_count)
    is_owned = jnp.sum(slot_map, -1)[:, None, None] > 0.5
    slot_grads = jnp.einsum("jb,brc->jrc", slot_map, reduced_all, precision=lax.Precision.HIGHEST)
    step_float = jnp.float32(STEP)
    fix_first = 1.0 - jnp.power(jnp.float32(beta_one), step_float)
    fix_second = 1.0 - jnp.power(jnp.float32(beta_two), step_float)
    new_weight, new_first, new_second = adam_update(
        master[0],
        slot_grads,
        first_moment[0],
        second_moment[0],
        fix_first,
        fix_second,
        rate_matrix,
        decay_rate,
    )
    new_weight = jnp.where(is_owned, new_weight, master[0])
    new_first = jnp.where(is_owned, new_first, first_moment[0])
    new_second = jnp.where(is_owned, new_second, second_moment[0])
    norm_now = jnp.concatenate([ln_gain, ln_bias], 0)
    new_norm, new_norm_m, new_norm_v = adam_update(
        norm_now, norm_grad, norm_m, norm_v, fix_first, fix_second, rate_norm, 0.0
    )
    new_slopes, new_slope_m, new_slope_v = adam_update(
        slopes, slopes_grad, slope_m, slope_v, fix_first, fix_second, rate_slope, 0.0
    )
    return (
        jnp.stack(mixed_parts),
        grad_tokens,
        new_weight[None],
        new_first[None],
        new_second[None],
        new_weight[None].astype(jnp.bfloat16),
        new_norm,
        new_norm_m,
        new_norm_v,
        new_slopes,
        new_slope_m,
        new_slope_v,
    )


MESH = pl.DeviceIdType.MESH
LOW = jnp.bfloat16
WIDE = jnp.float32
TILE = 128


class Plan:
    def __init__(self):
        self.tasks = {}

    def add(self, name, run, deps=(), waits=(), sends=(), cost=0.1, rank=0):
        assert name not in self.tasks
        self.tasks[name] = (run, tuple(deps), tuple(waits), tuple(sends), cost, rank)

    def order(self):
        now, done, arrival, free, listed = 0.0, set(), {}, {}, []
        left = list(self.tasks)
        while left:
            best = None
            for place, name in enumerate(left):
                run, deps, waits, sends, cost, rank = self.tasks[name]
                if any(d not in done for d in deps) or any(w not in arrival for w in waits):
                    continue
                begin = max([now] + [arrival[w] for w in waits] + [free.get(m[1], 0.0) - SLACK for m in sends])
                key = (begin, rank, place)
                if best is None or key < best[0]:
                    best = (key, name)
            name = best[1]
            run, deps, waits, sends, cost, rank = self.tasks[name]
            now = best[0][0] + cost
            for message, link, size in sends:
                rate, delay = LINKS[link]
                lanes = ("f", "r", "l") if link == "f" else (link,)
                end = max([now] + [free.get(lane, 0.0) for lane in lanes]) + size / rate
                free.update({lane: end for lane in lanes})
                arrival[message] = end + delay
            done.add(name)
            left.remove(name)
            listed.append((name, now))
        return listed


SLACK = 2.0
SENDS, RECEIVES = 24, 180
GATHERS = (
    (0, 0, 1, 0.0),
    (0, 1, 1, 0.07),
    (0, 2, 1, 0.08),
    (1, 0, 1, 0.21),
    (1, 1, 1, 0.21),
    (1, 2, 1, 0.21),
    (3, 0, 2, 0.31),
    (3, 2, 2, 0.33),
    (2, 0, 1, 0.43),
    (5, 0, 3, 0.37),
)
QUARTERS = {5: 0, 1: 3, 0: 6}
AFTER = {}
WHOLE = ()
FIRST = ("w", 0, 0)
SCATTERS = (
    (5, 0, 3, 0.93),
    (3, 0, 2, 1.01),
    (3, 2, 2, 0.93),
    (2, 0, 1, 1.26),
    (0, 0, 1, 0.43),
    (0, 1, 1, 0.43),
    (0, 2, 1, 0.43),
    (1, 0, 3, 0.6),
)
LINKS = {
    "c": (400e3, 1.0),
    "x": (52e3, 2.3),
    "r": (52e3, 2.3),
    "l": (52e3, 2.3),
    "f": (46e3, 3.3),
}


def start_of(owners, matrix_id, sizes):
    shared = jnp.int32(0)
    for earlier_id in range(matrix_id):
        shared = shared + jnp.where(owners[earlier_id] == owners[matrix_id], sizes[earlier_id], 0)
    return shared


def over_last(fn, value):
    return fn(value, axis=-1, keepdims=True)


def contract(left, right, left_dim, right_dim):
    return lax.dot_general(
        left, right, (((left_dim,), (right_dim,)), ((), ())), preferred_element_type=WIDE
    )


def gelu_parts(value):
    scale = math.sqrt(2.0 / math.pi)
    inner = jnp.tanh(scale * (value + 0.044715 * (value * value * value)))
    return inner, scale * (1.0 + 3 * 0.044715 * value * value)


def main_kernel(dims, refs):
    units, features, hidden_width, heads, micros, sizes = dims
    tables, (tok_hbm, cot_hbm, master_hbm, first_hbm, second_hbm) = refs[:10], refs[10:15]
    mixed_hbm, grad_hbm, slot_grads, small, masters, firsts, seconds = refs[15:22]
    held = refs[22:32]
    owners, docs, slopes, gain, bias, norm_m, norm_v, slope_row, slope_m, slope_v = held
    (
        w, red, cross_in, mine, other, core_in, both, x_in, tok, cot, tail_in, wide_tok, wide_cot, x_pool, x_norm, x_att,
        x_two, x_act, x_short, d_up, d_low, d_inner, d_res, d_qkv, d_pool, pooled, hat_one, hat_two, root_one, root_two,
        resid, hidden, short_grad, res_grad, q_out, q_in, a_out, a_in, da_out, da_in, dq_out, dq_in, probs, mixed, grad,
        wide_up, wide_grad, edge_in, x_near, x_wide, t_left, t_out, t_in, u_out, u_in, dx_out, dx_in, g, right_in, left_in, fin_out, fin_in, co_out, co_in, sums, sums_in, sends, recvs, local,
    ) = refs[32:]
    half = features // 2
    width = features // heads
    rows_of = masters.shape[1]
    count = heads
    tokens = 3 * units
    own = micros * units
    pair_width = 2 * width
    b, s = lax.axis_index("batch"), lax.axis_index("seq")
    x, c = b // 2, b % 2
    z, y = s // 2, s % 2
    spot = y * (7 - 2 * z) + z

    def seq_of(position):
        far = position // 4
        return 2 * (position + far * (7 - 2 * position)) + far

    def at(offset):
        return lax.rem(spot + offset + 2 * count, count)

    def rows_at(offset, part=0, length=rows_of):
        return pl.ds(pl.multiple_of(seq_of(at(offset)) * rows_of + part, 16), length)

    my_half = pl.ds(pl.multiple_of(c * half, half), half)
    other_half = pl.ds(pl.multiple_of((1 - c) * half, half), half)
    core_peer = (x * 2 + 1 - c, s)
    x_peer = ((1 - x) * 2 + c, s)
    cross_peer = ((1 - x) * 2 + 1 - c, s)
    right_peer = (b, seq_of(at(1)))
    left_peer = (b, seq_of(at(-1)))
    plan = Plan()
    flying, started, boxes = {}, [], {}

    def launch(name, copies, starts, group):
        if len(started) >= SENDS:
            started[len(started) - SENDS].wait_send()
        started.append(copies[0])
        flying[name] = copies[0]
        for start in starts:
            start()

    def describe(source, target, device, group):
        box = boxes.setdefault(group, len(boxes))
        return pltpu.make_async_remote_copy(
            src_ref=source,
            dst_ref=target,
            send_sem=sends.at[len(started) % SENDS],
            recv_sem=recvs.at[box],
            device_id=device,
            device_id_type=MESH,
        )

    def send(name, source, target, device, group=None):
        copy = describe(source, target, device, group or name)
        launch(name, [copy], [copy.start], group or name)

    def gather_up(group, whole):
        describe(whole, whole, core_peer, group).wait_recv()

    loads = [
        pltpu.make_async_copy(master_hbm, masters, local.at[0]),
        pltpu.make_async_copy(tok_hbm, tok, local.at[1]),
        pltpu.make_async_copy(cot_hbm, cot, local.at[2]),
    ]
    for table, place in zip(tables, held):
        loads.append(pltpu.make_async_copy(table, place, local.at[len(loads) + 2]))
    for copy in loads:
        copy.start()
    moments = [
        pltpu.make_async_copy(first_hbm, firsts, local.at[15]),
        pltpu.make_async_copy(second_hbm, seconds, local.at[16]),
    ]
    barrier = pltpu.get_barrier_semaphore()
    for step in range(1, count):
        pl.semaphore_signal(
            barrier, inc=1, device_id=(b, lax.rem(s + step, count)), device_id_type=MESH
        )
    for device in (core_peer, x_peer, cross_peer):
        pl.semaphore_signal(barrier, inc=1, device_id=device, device_id_type=MESH)
    pl.semaphore_wait(barrier, count + 2)
    for copy in loads[3:]:
        copy.wait()

    spans, first = [], 0
    for size in sizes:
        spans.append((first, first + size))
        first += size
    in_base, back_base, up_base = spans[3][0], spans[4][0], spans[5][0]
    hidden_blocks = sizes[3]
    ours = in_base + x * hidden_blocks
    theirs = in_base + (1 - x) * hidden_blocks
    plan.add("ms", loads[0].wait, cost=0.5)

    def contribute(k):
        def run():
            lo, hi = spans[k]
            mask = (owners[k] == b).astype(WIDE)
            begin = start_of(owners, k, sizes)
            for block in range(lo, hi):
                slot = jnp.minimum(begin + (block - lo), masters.shape[0] - 1)
                mine[block] = (masters[slot, :, my_half] * mask).astype(LOW)
                other[block] = (masters[slot, :, other_half] * mask).astype(LOW)
                if block == 0:
                    send(("g1", FIRST), mine.at[0], x_in.at[0], x_peer, ("g1", FIRST))
                    send(("g2", FIRST), other.at[0], cross_in, cross_peer, ("g1", FIRST))
            send(("g0", k), other.at[lo:hi], core_in.at[lo:hi], core_peer)

        return run

    def join_cores(k):
        def run():
            lo, hi = spans[k]
            flying[("g0", k)].wait_recv()
            both[lo:hi] = mine[lo:hi] + core_in[lo:hi]

        return run

    have = {k: [] for k in range(6)}
    gathers = []
    for k, offset, size, rank in GATHERS:
        name = ("w", k, offset)
        if k == 3:
            gathers.append((rank, name, (3, 4), ours + offset, theirs + offset, size))
            have[3] += [("h", name), ("hy", name)]
        else:
            begin = spans[k][0] + offset
            gathers.append((rank, name, (k,), begin, begin if k == 5 else None, size))
            have[k] += [("h", name)]
    piece_bytes = rows_of * half * 2

    quarter = half // 2
    plane_span = pl.ds(pl.multiple_of(x * quarter, quarter), quarter)
    plane_away = pl.ds(pl.multiple_of((1 - x) * quarter, quarter), quarter)

    def gather_chunk(rank, name, parents, here, there, size):
        quarters = there is here
        split = there is not None and not quarters
        load = size * piece_bytes // (2 if quarters else 1)
        blocks = pl.ds(here, size)
        away = pl.ds(there, size) if split else blocks
        span, away_span = (plane_span, plane_away) if quarters else (slice(None), slice(None))

        def piece(offset, part=0, length=rows_of):
            return w.at[blocks, c, rows_at(offset, part, length), span]

        def join_here():
            send(("g1", name), both.at[away, :, away_span], x_in.at[away, :, away_span], x_peer)

        def join_x():
            if name == FIRST:
                gather_up(("g1", FIRST), w.at[0:2, c, 0:rows_of])
                w[0, c, rows_at(0)] = both[0] + (x_in[0] + cross_in[...])
            else:
                flying[("g1", name)].wait_recv()
                w[blocks, c, rows_at(0), span] = both[blocks, :, span] + x_in[blocks, :, span]
            send(("R", 1, name), piece(0), piece(0), right_peer, (1, name))
            send(("L", 1, name), piece(0), piece(0), left_peer, (1, name))

        def onward(step):
            def run():
                gather_up((step - 1, name), w.at[blocks, c, 0 : rows_of * (2 if step < 5 else 1), span])
                if step == 5:
                    return
                for side, offset, peer in (("R", 1 - step, right_peer), ("L", step - 1, left_peer)):
                    part = piece(offset)
                    if step == 4:
                        part = piece(offset, 0 if side == "R" else rows_of // 2, rows_of // 2)
                    send((side, step, name), part, part, peer, (step, name))

            return run

        def across(step):
            def run():
                for side, offset in (("R", -step), ("L", step)):
                    part = piece(offset)
                    if step == 4:
                        part = piece(offset, 0 if side == "R" else rows_of // 2, rows_of // 2)
                    if step > 0 or side == "R":
                        send(("X", side, step, name), part, part, x_peer, ("X", name))

            return run

        def distribute(which, held, lanes):
            def run():
                send((which, name), w.at[held, c, :, lanes], w.at[held, c, :, lanes], core_peer)

            return run

        before = ("cs", 0)
        if name != FIRST:
            before = ("cx", name)
            plan.add(before, join_here, [("cs", k) for k in parents], (), [(("g1", name), "x", load)], 0.05, rank)
        plan.add(
            ("x", name), join_x, [before], [("g1", name)] + ([("g2", name)] if name == FIRST else []),
            [(("R", 1, name), "r", load), (("L", 1, name), "l", load)], 0.05, rank,
        )
        crossing = []

        def cross(step, after):
            messages = [("X", side, step, name) for side in ("RL" if step else "R")]
            size_of = load if step < 4 else load // 2
            plan.add(("X", step, name), across(step), [after], (), [(m, "x", size_of) for m in messages], 0.05, rank + 0.05)
            crossing.extend(messages)

        if split:
            cross(0, ("x", name))
        for step in (2, 3, 4, 5):
            size_of = load if step < 4 else load // 2
            out = [((side, step, name), link, size_of) for side, link in (("R", "r"), ("L", "l"))] if step < 5 else []
            before = ("x", name) if step == 2 else (step - 1, "f", name)
            waits = [(side, step - 1, name) for side in "RL"]
            plan.add((step, "f", name), onward(step), [before], waits, out, 0.05, rank)
            if split:
                cross(step - 1, (step, "f", name))
        plan.add(("di", name), distribute("D", blocks, span), [(5, "f", name)], (), [(("D", name), "c", 8 * load)], 0.05, rank)
        plan.add(("h", name), arrive(("D", name)), [("di", name)], [("D", name)], (), 0.02, rank)
        if split:
            whole = w.at[away, c, :, away_span]
            last = [("X", step, name) for step in range(5)]
            plan.add(("xw", name), lambda: gather_up(("X", name), whole), last, crossing, (), 0.05, rank)
            plan.add(("dy", name), distribute("E", away, away_span), [("xw", name)], (), [(("E", name), "c", 8 * load)], 0.05, rank)
            plan.add(("hy", name), arrive(("E", name)), [("dy", name)], [("E", name)], (), 0.02, rank)

    def arrive(*names):
        def run():
            for name in names:
                flying[name].wait_recv()

        return run

    for k in (0, 1, 3, 4, 2, 5):
        lo, hi = spans[k]
        load = (hi - lo) * piece_bytes
        early = [((which, FIRST), "x", piece_bytes) for which in ("g1", "g2")] if k == 0 else []
        plan.add(("co", k), contribute(k), ["ms"], (), early + [(("g0", k), "c", load)], 0.04 * (hi - lo), 0.1)
        plan.add(("cs", k), join_cores(k), [("co", k)], [("g0", k)], (), 0.02 * (hi - lo), 0.1)
    for chunk in gathers:
        gather_chunk(*chunk)

    def exchange(name, buffer):
        send(name, buffer.at[0:own], buffer.at[own : 2 * own], core_peer)

    def shared(name, columns):
        return (name, "c", own * columns * 2)

    lead = 16
    tiles = range(features // TILE)

    def columns_at(tile, base=0):
        return slice(base + tile * TILE, base + (tile + 1) * TILE)

    def ends_of(micro):
        ends = []
        total = jnp.int32(0)
        for index in range(docs.shape[1] - 1):
            total = total + docs[micro, index]
            ends.append(total)
        return ends

    def kept(micro):
        ids = s * units + lax.broadcasted_iota(jnp.int32, (units, 1), 0)
        starts = (ids == 0).astype(jnp.int32)
        for end in ends_of(micro):
            starts = starts | (ids == end).astype(jnp.int32)
        return starts == 0

    def load_tokens():
        loads[1].wait()
        send("tl", tok.at[:, tokens - lead :], tail_in, (b, lax.rem(s + 1, count)))
        for micro in range(micros):
            for tile in tiles:
                wide_tok[micro, tile, lead:] = tok[micro, :, columns_at(tile)].astype(WIDE)

    def load_cotangent():
        loads[2].wait()
        for micro in range(micros):
            for tile in tiles:
                wide_cot[micro, tile] = cot[micro, :, columns_at(tile)].astype(WIDE)
                for r in range(3):
                    d_up[micro * units : (micro + 1) * units, columns_at(tile, r * features)] = wide_cot[
                        micro, tile, pl.ds(r, units, stride=3), :
                    ].astype(LOW)
        exchange("eu", d_up)

    def make_pieces():
        flying["tl"].wait_recv()
        for micro in range(micros):
            keep = kept(micro)
            for tile in tiles:
                wide_tok[micro, tile, :lead] = tail_in[micro, :, columns_at(tile)].astype(WIDE)
                for r in range(3):
                    part = wide_tok[micro, tile, pl.ds(lead - 2 + r, units, stride=3), :]
                    if r < 2:
                        part = jnp.where(keep, part, 0.0)
                    x_pool[micro * units : (micro + 1) * units, columns_at(tile, r * features)] = part.astype(LOW)
        exchange("ep", x_pool)

    plan.add("tok", load_tokens, sends=[("tl", "f", 2 * lead * features * 2)], cost=0.3, rank=1)
    plan.add(
        "pc", make_pieces, ["tok"], ["tl"], [shared("ep", 3 * features)], 0.5, rank=1
    )
    plan.add("cot", load_cotangent, (), (), [shared("eu", 3 * features)], 0.5, rank=2)

    def normal(value, which, hat, root):
        centred = value - over_last(jnp.mean, value)
        scale = lax.rsqrt(over_last(jnp.mean, centred * centred) + ln_eps)
        unit = centred * scale
        hat[...] = unit
        root[...] = scale
        return (unit * gain[which : which + 1, :] + bias[which : which + 1, :]).astype(LOW)

    def both_halves(make):
        return jnp.concatenate([make(0), make(1)], axis=1)

    def pool():
        def side(h):
            total = None
            for r in range(3):
                term = contract(x_pool[0:own, r * features : (r + 1) * features], w[r, h], 1, 0)
                total = term if total is None else total + term
            return total

        value = both_halves(side)
        pooled[...] = value
        x_norm[0:own] = normal(value, 0, hat_one, root_one)
        exchange("en", x_norm)

    lane = lambda: lax.broadcasted_iota(jnp.int32, (1, pair_width), 1)

    def swap(value):
        return pltpu.roll(value, width, axis=1)

    def to_heads(tile, target, pair, row):
        low_lanes = lane() < width
        first, second = tile[:units], tile[units:]
        target[2 * pair, row : row + units] = jnp.where(low_lanes, first, swap(second)).astype(LOW)
        target[2 * pair + 1, row : row + units] = jnp.where(low_lanes, swap(first), second).astype(LOW)

    def from_heads(source, pair, row):
        low_lanes = lane() < width
        even = source[2 * pair, row : row + units].astype(WIDE)
        odd = source[2 * pair + 1, row : row + units].astype(WIDE)
        return jnp.where(low_lanes, even, swap(odd)).astype(LOW), jnp.where(low_lanes, swap(even), odd).astype(LOW)

    def spread(name, source, target):
        for step in range(1, count):
            there = lax.rem(s + step, count)
            send((name, step), source.at[there], target.at[s], (b, there), name)
        target[s] = source[s]

    def spread_names(name):
        return [(name, step) for step in range(1, count)]

    def spread_sends(name, rows):
        return [((name, step), "f", rows * pair_width * 2) for step in range(1, count)]

    def project():
        for part in range(3):
            for h in range(2):
                value = contract(x_norm[0:own], w[3 + part, h], 1, 0)
                for tile in range(half // pair_width):
                    to_heads(
                        value[:, tile * pair_width : (tile + 1) * pair_width],
                        q_out,
                        h * (half // pair_width) + tile,
                        part * units,
                    )
        spread("q", q_out, q_in)

    lane_units = units * count

    def heads_of(source, part):
        return source[:, part * units : (part + 1) * units, :].reshape(lane_units, pair_width)

    def lanes_of(micro):
        return (lane() // width == micro).astype(WIDE).astype(LOW)

    def distances():
        row_ids = lax.broadcasted_iota(jnp.int32, (lane_units, lane_units), 0)
        col_ids = lax.broadcasted_iota(jnp.int32, (lane_units, lane_units), 1)
        return row_ids - col_ids

    def attend_now():
        gather_up("q", q_in.at[0 : count - 1])
        queries, keys, values = (heads_of(q_in, part) for part in range(3))
        slope = slopes[s]
        total = None
        for micro in range(micros):
            gap = distances()
            row_seg = jnp.zeros((lane_units, 1), jnp.int32)
            col_seg = jnp.zeros((1, lane_units), jnp.int32)
            for end in ends_of(micro):
                row_seg += (lax.broadcasted_iota(jnp.int32, (lane_units, 1), 0) >= end).astype(jnp.int32)
                col_seg += (lax.broadcasted_iota(jnp.int32, (1, lane_units), 1) >= end).astype(jnp.int32)
            allowed = (row_seg == col_seg) & (gap >= 0)
            mask = lanes_of(micro)
            raw = contract(queries * mask, keys, 1, 1) * 0.125 - slope * gap.astype(WIDE)
            scores = jnp.where(allowed, raw, masked_score)
            raised = jnp.exp(scores - over_last(jnp.max, scores))
            probability = raised / over_last(jnp.sum, raised)
            probs[micro] = probability
            term = contract(probability.astype(LOW), values * mask, 1, 0)
            total = term if total is None else total + term
        a_out[...] = total.astype(LOW).reshape(count, units, pair_width)
        spread("a", a_out, a_in)

    def merge():
        gather_up("a", a_in.at[0 : count - 1])
        for pair in range(heads // 2):
            columns = slice(pair * pair_width, (pair + 1) * pair_width)
            first, second = from_heads(a_in, pair, 0)
            x_att[0:units, columns] = first
            x_att[units:own, columns] = second
        exchange("ea", x_att)

    def project_out():
        value = pooled[...] + both_halves(lambda h: contract(x_att[0:own], w[6, h], 1, 0))
        resid[...] = value
        x_two[0:own] = normal(value, 1, hat_two, root_two)
        exchange("et", x_two)


    def widen(j):
        def run():
            for h in range(2):
                columns = slice(j * features + h * half, j * features + (h + 1) * half)
                value = contract(x_two[0:own], w[in_base + j, h], 1, 0)
                hidden[:, columns] = value
                inner, _ = gelu_parts(value)
                x_act[0:own, columns] = (0.5 * value * (1.0 + inner)).astype(LOW)
            if j == hidden_blocks - 1:
                exchange("ec", x_act)

        return run

    def narrow():
        def side(h):
            total = resid[:, h * half : (h + 1) * half]
            for j in range(hidden_blocks):
                total = total + contract(
                    x_act[0:own, j * features : (j + 1) * features], w[back_base + j, h], 1, 0
                )
            return total

        x_short[0:own] = both_halves(side).astype(LOW)
        exchange("es", x_short)

    outs = [
        pltpu.make_async_copy(mixed, mixed_hbm, local.at[3]),
        pltpu.make_async_copy(grad, grad_hbm, local.at[4]),
    ]

    def place_up(r, value, core, plane):
        for micro in range(micros):
            wide_up[micro, 2 * core + plane, pl.ds(r, units, stride=3), :] = value[micro * units : (micro + 1) * units]

    def lift_away():
        for r in range(3):
            for core in range(2):
                value = contract(t_left[QUARTERS[5], 0:own], w[up_base + r, core, :, plane_span], 1, 0)
                u_out[:, (2 * r + core) * quarter : (2 * r + core + 1) * quarter] = value.astype(LOW)
        send("ux", u_out, u_in, x_peer)

    def lift(r):
        def run():
            for core in range(2):
                place_up(r, contract(x_short[0:own], w[up_base + r, core, :, plane_span], 1, 0), core, x)

        return run

    def finish_mixed():
        arrive("ux")()
        for r in range(3):
            for core in range(2):
                begin = (2 * r + core) * quarter
                place_up(r, u_in[:, begin : begin + quarter].astype(WIDE), core, 1 - x)
        for micro in range(micros):
            for tile in tiles:
                columns = columns_at(tile)
                mixed[micro, :, columns] = tok[micro, :, columns].astype(WIDE) + wide_up[micro, tile]
        outs[0].start()

    plan.add("po", pool, ["pc", *have[0]], (), [shared("en", features)], 0.6, rank=3)
    plan.add("pr", project, ["po", *have[1]], (), spread_sends("q", 3 * units), 0.6, rank=3)
    plan.add("at", attend_now, ["pr"], spread_names("q"), spread_sends("a", units), 1.1, rank=3)
    plan.add("me", merge, ["at"], spread_names("a"), [shared("ea", features)], 0.15, rank=3)
    plan.add("ou", project_out, ["me", *have[2]], (), [shared("et", features)], 0.45, rank=3)
    for j in range(hidden_blocks):
        last = j == hidden_blocks - 1
        plan.add(
            ("wi", j), widen(j), ["ou", *have[3]] + ([("wi", i) for i in range(j)] if last else []), (),
            [shared("ec", hidden_width)] if last else (), 0.3, rank=3,
        )
    plan.add(
        "na", narrow, [("wi", j) for j in range(hidden_blocks)] + [*have[3]], (), [shared("es", features)], 0.5,
        rank=3,
    )
    for r in range(3):
        plan.add(("li", r), lift(r), ["na", *have[5]], (), (), 0.2, rank=8)
    quarter_lump = own * 3 * half * 2
    plan.add("lq", lift_away, [("tw", 5, 0), *have[5]], (), [("ux", "x", quarter_lump)], 0.6, rank=8)
    plan.add("lf", finish_mixed, ["lq", "tok"] + [("li", r) for r in range(3)], ["ux"], (), 0.4, rank=8)

    def back_short_away():
        total = None
        for r in range(3):
            for core in range(2):
                columns = slice(core * quarter, (core + 1) * quarter)
                term = contract(t_in[QUARTERS[5] + r, 0:own, columns], w[up_base + r, core, :, plane_span], 1, 1)
                total = term if total is None else total + term
        dx_out[...] = total.astype(LOW)
        send("dx", dx_out, dx_in, x_peer)

    def back_short_here():
        total = None
        for r in range(3):
            for core in range(2):
                columns = pl.ds(pl.multiple_of(r * features + core * half + x * quarter, quarter), quarter)
                term = contract(d_up[0:own, columns], w[up_base + r, core, :, plane_span], 1, 1)
                total = term if total is None else total + term
        short_grad[...] = total

    def back_short():
        arrive("dx")()
        total = short_grad[...] + dx_in[...].astype(WIDE)
        short_grad[...] = total
        d_low[0:own] = total.astype(LOW)
        exchange("el", d_low)

    def back_widen(j):
        def run():
            total = contract(d_low[0:own, 0:half], w[back_base + j, 0], 1, 1)
            total = total + contract(d_low[0:own, half:features], w[back_base + j, 1], 1, 1)
            columns = slice(j * features, (j + 1) * features)
            value = hidden[:, columns]
            inner, slope = gelu_parts(value)
            factor = 0.5 * (1.0 + inner) + 0.5 * value * (1.0 - inner * inner) * slope
            d_inner[0:own, columns] = (total * factor).astype(LOW)
            if j == hidden_blocks - 1:
                exchange("ei", d_inner)

        return run

    def back_normal(value, which, hat, root):
        unit = hat[...]
        sums[which : which + 1, :] = jnp.sum(value * unit, axis=0, keepdims=True)
        sums[2 + which : 3 + which, :] = jnp.sum(value, axis=0, keepdims=True)
        scaled = value * gain[which : which + 1, :]
        return root[...] * (
            scaled - over_last(jnp.mean, scaled) - unit * over_last(jnp.mean, scaled * unit)
        )

    def back_two():
        total = None
        for j in range(hidden_blocks):
            for h in range(2):
                begin = j * features + h * half
                term = contract(d_inner[0:own, begin : begin + half], w[in_base + j, h], 1, 1)
                total = term if total is None else total + term
        value = short_grad[...] + back_normal(total, 1, hat_two, root_two)
        res_grad[...] = value
        d_res[0:own] = value.astype(LOW)
        exchange("er", d_res)

    def back_out():
        value = contract(d_res[0:own, 0:half], w[6, 0], 1, 1)
        value = value + contract(d_res[0:own, half:features], w[6, 1], 1, 1)
        for pair in range(heads // 2):
            to_heads(value[:, pair * pair_width : (pair + 1) * pair_width], da_out, pair, 0)
        spread("da", da_out, da_in)

    def back_attend():
        gather_up("da", da_in.at[0 : count - 1])
        queries, keys, values = (heads_of(q_in, part) for part in range(3))
        grads = da_in[...].reshape(lane_units, pair_width)
        totals = [None, None, None]
        slope_total = jnp.zeros((1, 1), WIDE)
        for micro in range(micros):
            mask = lanes_of(micro)
            own_grads = grads * mask
            probability = probs[micro]
            grad_prob = contract(own_grads, values, 1, 1)
            scaled = probability * grad_prob
            score = scaled - probability * over_last(jnp.sum, scaled)
            low_score = score.astype(LOW)
            gap = distances().astype(WIDE)
            slope_total = slope_total - jnp.sum(
                jnp.sum(low_score.astype(WIDE) * gap, axis=0, keepdims=True), axis=1, keepdims=True
            )
            terms = (
                contract(low_score, keys * mask, 1, 0) * 0.125,
                contract(low_score, queries * mask, 0, 0) * 0.125,
                contract(probability.astype(LOW), own_grads, 0, 0),
            )
            totals = [term if total is None else total + term for total, term in zip(totals, terms)]
        for part in range(3):
            dq_out[:, part * units : (part + 1) * units, :] = (
                totals[part].astype(LOW).reshape(count, units, pair_width)
            )
        spread("dq", dq_out, dq_in)
        places = lax.broadcasted_iota(jnp.int32, (1, features), 1)
        sums[4:5, :] = jnp.where(places == s, slope_total, 0.0)
        sums[5:8, :] = jnp.zeros((3, features), WIDE)

    def back_project():
        gather_up("dq", dq_in.at[0 : count - 1])
        for part in range(3):
            for pair in range(heads // 2):
                begin = part * features + pair * pair_width
                first, second = from_heads(dq_in, pair, part * units)
                d_qkv[0:units, begin : begin + pair_width] = first
                d_qkv[units:own, begin : begin + pair_width] = second
        exchange("eq", d_qkv)

    def back_one():
        total = None
        for part in range(3):
            for h in range(2):
                begin = part * features + h * half
                term = contract(d_qkv[0:own, begin : begin + half], w[3 + part, h], 1, 1)
                total = term if total is None else total + term
        value = res_grad[...] + back_normal(total, 0, hat_one, root_one)
        d_pool[0:own] = value.astype(LOW)
        exchange("ed1", d_pool)

    def back_pieces():
        for r in range(3):
            value = contract(d_pool[0:own, 0:half], w[r, 0], 1, 1)
            value = value + contract(d_pool[0:own, half:features], w[r, 1], 1, 1)
            for micro in range(micros):
                part = value[micro * units : (micro + 1) * units]
                if r < 2:
                    part = jnp.where(kept(micro), part, 0.0)
                for tile in tiles:
                    wide_grad[micro, tile, pl.ds(6 + r, units, stride=3), :] = part[:, columns_at(tile)]
        send("ed", wide_grad.at[:, :, 0:8], edge_in, (b, lax.rem(s + count - 1, count)))

    def finish_grad():
        flying["ed"].wait_recv()
        inside = (s < count - 1).astype(WIDE)
        for micro in range(micros):
            for tile in tiles:
                columns = columns_at(tile)
                wide_grad[micro, tile, 6 + tokens : 8 + tokens, :] = edge_in[micro, tile, 6:8, :] * inside
                grad[micro, :, columns] = cot[micro, :, columns].astype(WIDE) + wide_grad[micro, tile, 8 : 8 + tokens]
        outs[1].start()

    plan.add(
        "bq", back_short_away, [("tz", 5, r) for r in range(3)] + have[5], (), [("dx", "x", own * features * 2)], 0.6, rank=2
    )
    plan.add("bh", back_short_here, ["cot", *have[5]], (), (), 0.6, rank=3)
    plan.add("bs", back_short, ["bq", "bh"], ["dx"], [shared("el", features)], 0.1, rank=3)
    for j in range(hidden_blocks):
        last = j == hidden_blocks - 1
        plan.add(
            ("bw", j), back_widen(j),
            ["bs", *have[3], ("wi", j)] + ([("bw", i) for i in range(j)] if last else []), (),
            [shared("ei", hidden_width)] if last else (), 0.35, rank=4,
        )
    plan.add(
        "b2", back_two, [("bw", j) for j in range(hidden_blocks)] + [*have[3]], (),
        [shared("er", features)], 0.9, rank=4,
    )
    plan.add("bo", back_out, ["b2", *have[2]], (), spread_sends("da", units), 0.45, rank=4)
    plan.add("ba", back_attend, ["bo", "at"], spread_names("da"), spread_sends("dq", 3 * units), 1.4, rank=4)
    plan.add("bp", back_project, ["ba"], spread_names("dq"), [shared("eq", 3 * features)], 0.2, rank=4)
    plan.add("b1", back_one, ["bp"], (), [shared("ed1", features)], 0.75, rank=4)
    plan.add("bx", back_pieces, ["b1"], (), [("ed", "f", 2 * 8 * features * 4)], 0.65, rank=9)
    plan.add("fg", finish_grad, ["bx", "cot"], ["ed"], (), 0.3, rank=9)

    fixes = (1.0 - beta_one**STEP, 1.0 - beta_two**STEP)

    def finish_small(total):
        for begin, values in ((0, gain), (2, bias)):
            rows = slice(begin, begin + 2)
            new = adam_update(values[...], total[rows], norm_m[rows], norm_v[rows], *fixes, rate_norm, 0.0)
            for place, value in enumerate(new):
                small[4 * place + begin : 4 * place + begin + 2] = value
        new = adam_update(slope_row[...], total[4:5, 0:heads], slope_m[...], slope_v[...], *fixes, rate_slope, 0.0)
        for place, value in enumerate(new):
            small[12 + place : 13 + place, 0:heads] = value

    def fill_slots():
        lanes = lax.broadcasted_iota(jnp.int32, (1, features), 1)
        marks = jnp.zeros((1, features), WIDE)
        for slot in range(masters.shape[0]):
            block, mark, base = jnp.int32(0), jnp.float32(0), 0
            for matrix_id, size in enumerate(sizes):
                begin = start_of(owners, matrix_id, sizes)
                inside = (owners[matrix_id] == b) & (slot >= begin) & (slot < begin + size)
                block = jnp.where(inside, base + slot - begin, block)
                mark = jnp.where(inside, 1.0, mark)
                base += size
            slot_grads[slot] = red[block]
            marks = jnp.where(lanes == slot, mark, marks)
        small[15:16, :] = marks

    def add_pair(step, device):
        def run():
            if step > 0:
                flying[("s", step - 1)].wait_recv()
                sums[8 * step : 8 * step + 8] = sums[8 * step - 8 : 8 * step] + sums_in[8 * step - 8 : 8 * step]
            if device is not None:
                send(("s", step), sums.at[8 * step : 8 * step + 8], sums_in.at[8 * step : 8 * step + 8], device)
            else:
                finish_small(sums[8 * step : 8 * step + 8])

        return run

    partners = [
        core_peer,
        x_peer,
        (b, 2 * z + 1 - y),
        (b, 2 * (z + 1 - 2 * (z % 2)) + y),
        (b, 2 * lax.rem(z + 2, 4) + y),
        None,
    ]
    for step, device in enumerate(partners):
        plan.add(
            ("sum", step), add_pair(step, device), ["b1", "ba"] if step == 0 else [("sum", step - 1)],
            [("s", step - 1)] if step else (), [(("s", step), "f", 8 * features * 4)] if device is not None else (), 0.1,
            rank=0,
        )

    for name, columns in (
        ("ep", "pc"), ("en", "po"), ("ea", "me"), ("et", "ou"), ("ec", ("wi", hidden_blocks - 1)),
        ("es", "na"), ("eu", "cot"), ("el", "bs"), ("ei", ("bw", hidden_blocks - 1)),
        ("er", "b2"), ("eq", "bp"), ("ed1", "b1"),
    ):
        plan.add(("got", name), arrive(name), [columns], [name], cost=0.02)

    def columns_of(block):
        return pl.ds(pl.multiple_of(block * features + c * half, half), half)

    def outer(block, left, left_block, right, right_block):
        def run():
            rows = left[:, left_block * features : (left_block + 1) * features]
            g[block] = contract(rows, right[:, columns_of(right_block)], 0, 0).astype(LOW)

        return run

    def send_either(name, first_source, second_source, target):
        copies = [describe(source, target, x_peer, name) for source in (first_source, second_source)]
        launch(name, copies, [lambda plane=plane: pl.when(x == plane)(copies[plane].start) for plane in range(2)], name)

    def near_away():
        send_either("sn", d_low.at[0:own], x_two.at[0:own], x_near.at[0:own])

    def near_core():
        arrive("sn")()
        exchange("cn", x_near)

    def wide_away(j):
        columns = slice(j * features, (j + 1) * features)

        def run():
            source = (x_act.at[0:own, columns], d_inner.at[0:own, columns])
            send_either(("sw", j), *source, x_wide.at[0:own, columns])

        return run

    def wide_core(j):
        columns = slice(j * features, (j + 1) * features)

        def run():
            arrive(("sw", j))()
            send(("cw", j), x_wide.at[0:own, columns], x_wide.at[own : 2 * own, columns], core_peer)

        return run

    def outer_split(j):
        columns = slice(j * features, (j + 1) * features)

        def run():
            @pl.when(x == 0)
            def _():
                total = contract(x_two[...], d_inner[:, columns_of(j)], 0, 0)
                g[in_base + j] = (total + contract(x_near[...], x_wide[:, columns_of(j)], 0, 0)).astype(LOW)

            @pl.when(x == 1)
            def _():
                total = contract(x_act[:, columns], d_low[:, my_half], 0, 0)
                g[back_base + j] = (total + contract(x_wide[:, columns], x_near[:, my_half], 0, 0)).astype(LOW)

        return run

    lump = own * features * 2
    plan.add("sn", near_away, ["bs", "ou"], (), [("sn", "x", lump)], 0.05, 2)
    plan.add("nc", near_core, ["sn"], ["sn"], [("cn", "c", lump)], 0.05, 2)
    plan.add(("got", "cn"), arrive("cn"), ["nc"], ["cn"], (), 0.02, 2)
    for j in range(hidden_blocks):
        plan.add(("sw", j), wide_away(j), [("wi", j), ("bw", j)], (), [(("sw", j), "x", lump)], 0.05, 2)
        plan.add(("wc", j), wide_core(j), [("sw", j)], [("sw", j)], [(("cw", j), "c", lump)], 0.05, 2)
        plan.add(("got", "cw", j), arrive(("cw", j)), [("wc", j)], [("cw", j)], (), 0.02, 2)
        deps = [("got", e) for e in ("et", "ec", "el", "ei", "cn")] + [("got", "cw", j)]
        plan.add(("gr", j, "s"), outer_split(j), deps, cost=0.6, rank=4.5)
    quartered = {
        0: (x_pool, 3, d_pool, 1, "pc", "b1", "ep", "ed1"),
        1: (x_norm, 1, d_qkv, 3, "po", "bp", "en", "eq"),
        2: (x_att, 1, d_res, 1, "me", "b2", "ea", "er"),
        5: (x_short, 1, d_up, 3, "na", "cot", "es", "eu"),
    }
    quartered = {k: quartered[k] for k in QUARTERS}

    def left_away(k, j):
        columns = slice(j * features, (j + 1) * features)

        def run():
            send(("tx", k, j), quartered[k][0].at[0:own, columns], t_left.at[QUARTERS[k] + j, 0:own], x_peer)

        return run

    def left_core(k, j):
        place = QUARTERS[k] + j

        def run():
            arrive(("tx", k, j))()
            send(("tc", k, j), t_left.at[place, 0:own], t_left.at[place, own : 2 * own], core_peer)

        return run

    def right_away(k, r):
        place = QUARTERS[k] + r

        def run():
            for core in range(2):
                begin = r * features + core * half + (1 - x) * quarter
                t_out[place, :, core * quarter : (core + 1) * quarter] = quartered[k][2][
                    0:own, pl.ds(pl.multiple_of(begin, quarter), quarter)
                ]
            if k == 5:
                send(("ty", k, r), t_out.at[place], t_in.at[place, 0:own], x_peer)
                return
            lanes = [pl.ds(pl.multiple_of(core * quarter, quarter), quarter) for core in (c, 1 - c)]
            send(("ty", k, r), t_out.at[place, :, lanes[0]], t_in.at[place, 0:own, 0:quarter], x_peer, ("ty", k, r))
            send(("tu", k, r), t_out.at[place, :, lanes[1]], t_in.at[place, own : 2 * own, 0:quarter], cross_peer, ("ty", k, r))

        return run

    def right_core(k, r):
        place = QUARTERS[k] + r

        def run():
            arrive(("ty", k, r))()
            send(("td", k, r), t_in.at[place, 0:own], t_in.at[place, own : 2 * own], core_peer)

        return run

    def outer_quarter(k, j, r):
        def run():
            left, _, right = quartered[k][:3]
            near = pl.ds(pl.multiple_of(r * features + c * half + x * quarter, quarter), quarter)
            away = pl.ds(pl.multiple_of(c * quarter, quarter), quarter) if k == 5 else slice(0, quarter)
            total = contract(left[:, j * features : (j + 1) * features], right[:, near], 0, 0)
            total = total + contract(t_left[QUARTERS[k] + j], t_in[QUARTERS[k] + r, :, away], 0, 0)
            g[spans[k][0] + j + r, :, plane_span] = total.astype(LOW)

        return run

    for k, (_, lefts, _, rights, left_dep, right_dep, left_got, right_got) in quartered.items():
        urgency = 3.5 if k == 0 else 2.5
        for j in range(lefts):
            plan.add(("tx", k, j), left_away(k, j), [left_dep] + list(AFTER.get(k, ())), (), [(("tx", k, j), "x", lump)], 0.05, urgency)
            plan.add(("tw", k, j), left_core(k, j), [("tx", k, j)], [("tx", k, j)], [(("tc", k, j), "c", lump)], 0.05, urgency)
            plan.add(("got", "tc", k, j), arrive(("tc", k, j)), [("tw", k, j)], [("tc", k, j)], (), 0.02, urgency)
        for r in range(rights):
            if k != 5:
                parts = [("ty", k, r), ("tu", k, r)]
                whole = t_in.at[QUARTERS[k] + r, :, 0:quarter]
                plan.add(parts[0], right_away(k, r), [right_dep], (), [(p, "x", lump // 4) for p in parts], 0.1, 2.5)
                take = lambda k=k, r=r, whole=whole: gather_up(("ty", k, r), whole)
                plan.add(("got", "td", k, r), take, parts[:1], parts, (), 0.02, 2.5)
                continue
            plan.add(("ty", k, r), right_away(k, r), [right_dep], (), [(("ty", k, r), "x", lump // 2)], 0.05, 2.5)
            plan.add(("tz", k, r), right_core(k, r), [("ty", k, r)], [("ty", k, r)], [(("td", k, r), "c", lump // 2)], 0.05, 2.5)
            plan.add(("got", "td", k, r), arrive(("td", k, r)), [("tz", k, r)], [("td", k, r)], (), 0.02, 2.5)
        for j in range(lefts if k not in WHOLE else 0):
            for r in range(rights):
                deps = [("got", left_got), ("got", right_got), ("got", "tc", k, j), ("got", "td", k, r)]
                plan.add(("gr", spans[k][0] + j + r), outer_quarter(k, j, r), deps, cost=0.4, rank=5)
    weight_grads = []
    for r in range(3):
        for k, left, left_block, right, right_block, deps in (
            (0, x_pool, r, d_pool, 0, ("ep", "ed1")), (1, x_norm, 0, d_qkv, r, ("en", "eq")),
            (2, x_att, 0, d_res, 0, ("ea", "er")), (5, x_short, 0, d_up, r, ("es", "eu")),
        ):
            if (k in WHOLE or k not in QUARTERS) and r < sizes[k]:
                deps = [("got", dep) for dep in deps]
                weight_grads.append((spans[k][0] + r, left, left_block, right, right_block, deps))
    for block, left, left_block, right, right_block, deps in weight_grads:
        plan.add(("gr", block), outer(block, left, left_block, right, right_block), deps, cost=0.3, rank=5)

    def scatter_chunk(rank, name, here, there, size, deps):
        split, quarters = there is not None, there is here
        blocks = pl.ds(here, size)
        load = size * piece_bytes // (2 if quarters else 1)
        away, span, away_span, length_out = blocks, slice(None), slice(None), half
        begin_out, away_out = c * half, c * half
        if quarters:
            span, away_span = plane_span, plane_away
            length_out, begin_out, away_out = quarter, c * half + x * quarter, c * half + (1 - x) * quarter
        elif split:
            away = pl.ds(there, size)
        out_span = pl.ds(pl.multiple_of(begin_out, length_out), length_out)
        out_away = pl.ds(pl.multiple_of(away_out, length_out), length_out)

        half_rows = rows_of // 2
        sides = (("R", 0, right_in, right_peer), ("L", half_rows, left_in, left_peer))

        def first_step():
            for side, part, inbox, peer in sides:
                source = g.at[blocks, rows_at(4, part, half_rows), span]
                target = inbox.at[0, blocks, part : part + half_rows, span]
                send((side, "s", 1, name), source, target, peer, ("s", 1, name))

        def take(step):
            gather_up(("s", step, name), g.at[blocks, 0 : rows_of * (1 if step == 1 else 2), span])

        def next_step(step):
            def run():
                take(step - 1)
                for side, half_part, inbox, peer in sides:
                    offset = (5 - step) if side == "R" else (step - 5)
                    part, length = (half_part, half_rows) if step == 2 else (0, rows_of)
                    rows = rows_at(offset, part, length)
                    g[blocks, rows, span] = g[blocks, rows, span] + inbox[step - 2, blocks, part : part + length, span]
                    source = g.at[blocks, rows_at(offset), span]
                    send((side, "s", step, name), source, inbox.at[step - 1, blocks, :, span], peer, ("s", step, name))

            return run

        def finish():
            take(4)
            total = g[blocks, rows_at(0), span].astype(WIDE)
            total = total + right_in[3, blocks, :, span].astype(WIDE) + left_in[3, blocks, :, span].astype(WIDE)
            fin_out[blocks, :, span] = total.astype(LOW)
            send(("rx", name), fin_out.at[blocks, :, span], fin_in.at[blocks, :, span], x_peer)
            if quarters:
                send(("rd", name), fin_out.at[blocks, :, span], co_in.at[blocks, :, span], cross_peer)
            if split:
                send(("rc", name), fin_out.at[blocks, :, span], co_in.at[blocks, :, span], core_peer)
                red[blocks, :, out_span] = fin_out[blocks, :, span]

        def finish_x():
            arrive(("rx", name))()
            if split:
                red[away, :, out_away] = fin_in[away, :, away_span]
                if not quarters:
                    send(("rd", name), fin_in.at[away, :, away_span], co_in.at[away, :, away_span], core_peer)
            else:
                total = (fin_out[blocks].astype(WIDE) + fin_in[blocks].astype(WIDE)).astype(LOW)
                co_out[blocks] = total
                red[blocks, :, my_half] = total
                send(("rc", name), co_out.at[blocks], co_in.at[blocks], core_peer)

        def finish_core():
            arrive(("rc", name), *([("rd", name)] if split else []))()
            red[blocks, :, other_half] = co_in[blocks]
            if split and not quarters:
                red[away, :, other_half] = co_in[away]

        links = (("R", "r"), ("L", "l"))
        out = [((side, "s", 1, name), link, load // 2) for side, link in links]
        plan.add(("r", 1, name), first_step, deps, (), out, 0.05, rank)
        for step in (2, 3, 4):
            waits = [(side, "s", step - 1, name) for side in "RL"]
            out = [((side, "s", step, name), link, load) for side, link in links]
            plan.add(("r", step, name), next_step(step), [("r", step - 1, name)], waits, out, 0.04 * size, rank)
        own_out = [(("rc", name), "c", load)]
        plan.add(
            ("fi", name), finish, [("r", 4, name)], [("R", "s", 4, name), ("L", "s", 4, name)],
            [(("rx", name), "x", load)] + (own_out if split else []) + ([(("rd", name), "x", load)] if quarters else []),
            0.02 * size, rank,
        )
        late_out = ([] if quarters else [(("rd", name), "c", load)]) if split else own_out
        plan.add(("fx", name), finish_x, [("fi", name)], [("rx", name)], late_out, 0.02 * size, rank)
        plan.add(
            ("fc", name), finish_core, [("fx", name)], [("rc", name)] + ([("rd", name)] if split else []), (), 0.02 * size, rank
        )

    for k, offset, size, rank in SCATTERS:
        name = ("g", k, offset)
        if k == 3:
            deps = [("gr", j, "s") for j in range(offset, offset + size)]
            scatter_chunk(rank, name, ours + offset, theirs + offset, size, deps)
        else:
            begin = spans[k][0] + offset
            scatter_chunk(rank, name, begin, begin if k in QUARTERS and k not in WHOLE else None, size, [("gr", begin + j) for j in range(size)])

    plan.add("mo", lambda: [copy.start() for copy in moments], ["pc"], (), (), 0.02, rank=8)
    plan.add("sl", fill_slots, ["mo"] + [("fc", ("g", k, offset)) for k, offset, _, _ in SCATTERS], (), (), 0.2, rank=9)
    for name, _ in plan.order():
        plan.tasks[name][0]()
    assert len(boxes) <= RECEIVES
    for copy in started[-SENDS:]:
        copy.wait_send()
    for copy in outs + moments:
        copy.wait()


def adam_kernel(refs):
    grads, small, master, first, second, mixed, grad = refs[:7]
    new_w, new_m, new_v, new_low, mixed_out, grad_out = refs[7:13]
    norm_outs, slope_outs = refs[13:16], refs[16:19]
    step = pl.program_id(0)
    fixes = (1.0 - beta_one**STEP, 1.0 - beta_two**STEP)
    rows = mixed_out.shape[0]
    part = pl.ds(pl.multiple_of(step * rows, 8), rows)
    mixed_out[...] = mixed[part]
    grad_out[...] = grad[part]

    @pl.when(step == 0)
    def _():
        heads = slope_outs[0].shape[1]
        for place in range(3):
            norm_outs[place][...] = small[4 * place : 4 * place + 4]
            slope_outs[place][...] = small[12 + place : 13 + place, 0:heads]

    count = new_w.shape[0]
    lanes = lax.broadcasted_iota(jnp.int32, (1, small.shape[1]), 1)
    for place in range(count):
        slot = step * count + place
        old = (master[slot], first[slot], second[slot])
        values = adam_update(old[0], grads[slot].astype(WIDE), old[1], old[2], *fixes, rate_matrix, decay_rate)
        mark = jnp.sum(jnp.where(lanes == slot, small[15:16, :], 0.0), axis=1, keepdims=True)
        keep = jnp.broadcast_to(mark, old[0].shape) > 0.5
        weight, new_m[place], new_v[place] = (jnp.where(keep, new, was) for new, was in zip(values, old))
        new_w[place] = weight
        new_low[place] = weight.astype(LOW)


def fused_body(tokens, cotangent, doc_lengths, owners, master, first_moment, second_moment, ln_gain, ln_bias, norm_m, norm_v, slopes, slope_m, slope_v):
    micros, _, tok_rows, features = tokens.shape
    units, heads, width = tok_rows // 3, slopes.shape[0], features // slopes.shape[0]
    sizes = tuple(block_counts(features, FF))
    blocks, own, half = sum(sizes), micros * units, features // 2
    slots, rows = master.shape[1], master.shape[2]
    lane_units = units * heads
    split = features // TILE
    hbm, vmem, anywhere = (pl.BlockSpec(memory_space=m) for m in (pltpu.HBM, pltpu.VMEM, pl.ANY))
    low = lambda *shape: pltpu.VMEM(shape, LOW)
    wide = lambda *shape: pltpu.VMEM(shape, WIDE)
    pieces = lambda: low(blocks, rows, half)
    both = lambda columns: low(2 * own, columns)
    scratch = [
        pltpu.SMEM(owners.shape, jnp.int32), pltpu.SMEM((micros, doc_lengths.shape[2]), jnp.int32),
        pltpu.SMEM(slopes.shape, WIDE), wide(2, features), wide(2, features), wide(4, features), wide(4, features),
        wide(1, heads), wide(1, heads), wide(1, heads),
        low(blocks, 2, features, half), low(blocks, rows, features), low(rows, half), pieces(), pieces(), pieces(), pieces(), pieces(),
        low(micros, tok_rows, features), low(micros, tok_rows, features), low(micros, 16, features),
        wide(micros, split, 16 + tok_rows, TILE), wide(micros, split, tok_rows, TILE),
        both(3 * features), both(features), both(features), both(features), both(FF), both(features),
        both(3 * features), both(features), both(FF), both(features), both(3 * features), both(features),
        wide(own, features), wide(own, features), wide(own, features), wide(own, 1), wide(own, 1),
        wide(own, features), wide(own, FF), wide(own, features), wide(own, features),
        low(heads, 3 * units, 2 * width), low(heads, 3 * units, 2 * width), low(heads, units, 2 * width),
        low(heads, units, 2 * width), low(heads, units, 2 * width), low(heads, units, 2 * width),
        low(heads, 3 * units, 2 * width), low(heads, 3 * units, 2 * width),
        wide(micros, lane_units, lane_units), wide(micros, tok_rows, features), wide(micros, tok_rows, features),
        wide(micros, split, tok_rows, TILE), wide(micros, split, 8 + tok_rows, TILE), wide(micros, split, 8, TILE),
        low(2 * own, features), low(2 * own, FF),
        low(10, 2 * own, features), low(10, own, half), low(10, 2 * own, half),
        low(own, 3 * half), low(own, 3 * half), low(own, features), low(own, features), low(blocks, features, half), low(4, blocks, rows, half), low(4, blocks, rows, half),
        pieces(), pieces(), pieces(), pieces(), wide(48, features), wide(40, features),
        pltpu.SemaphoreType.DMA((SENDS,)), pltpu.SemaphoreType.DMA((RECEIVES,)), pltpu.SemaphoreType.DMA((17,)),
    ]
    token_shape = (micros, tok_rows, features)
    dims = (units, features, FF, heads, micros, sizes)
    moment_shape = jax.ShapeDtypeStruct((slots, rows, features), WIDE)
    mixed, grad, grads, small, weights, firsts, seconds = pl.pallas_call(
        lambda *refs: main_kernel(dims, refs),
        out_shape=(
            jax.ShapeDtypeStruct(token_shape, WIDE),
            jax.ShapeDtypeStruct(token_shape, WIDE),
            jax.ShapeDtypeStruct((slots, rows, features), LOW),
            jax.ShapeDtypeStruct((16, features), WIDE),
            moment_shape, moment_shape, moment_shape,
        ),
        in_specs=[hbm] * 15,
        out_specs=(anywhere, anywhere) + (vmem,) * 5,
        scratch_shapes=scratch,
        compiler_params=pltpu.CompilerParams(
            collective_id=0, has_side_effects=True, vmem_limit_bytes=47 * 2**20
        ),
        name="block",
    )(*[pltpu.with_memory_space_constraint(value, pltpu.HBM) for value in (
        owners, doc_lengths[:, 0], slopes, ln_gain, ln_bias, norm_m, norm_v, slopes[None], slope_m[None], slope_v[None],
        tokens[:, 0], cotangent[:, 0], master[0], first_moment[0], second_moment[0],
    )])
    steps = 2
    flat = (micros * tok_rows, features)
    slot = pl.BlockSpec((slots // steps, rows, features), lambda j: (j, 0, 0))
    some = pl.BlockSpec((flat[0] // steps, features), lambda j: (j, 0))
    norm_shape = jax.ShapeDtypeStruct((4, features), WIDE)
    slope_shape = jax.ShapeDtypeStruct((1, heads), WIDE)
    out = pl.pallas_call(
        lambda *refs: adam_kernel(refs),
        grid=(steps,),
        out_shape=(
            moment_shape, moment_shape, moment_shape, jax.ShapeDtypeStruct((slots, rows, features), LOW),
            jax.ShapeDtypeStruct(flat, WIDE), jax.ShapeDtypeStruct(flat, WIDE),
            norm_shape, norm_shape, norm_shape, slope_shape, slope_shape, slope_shape,
        ),
        in_specs=[vmem] * 7,
        out_specs=(slot, slot, slot, slot, some, some) + (vmem,) * 6,
        compiler_params=pltpu.CompilerParams(dimension_semantics=("arbitrary",), vmem_limit_bytes=12 * 2**20),
        name="adam",
    )(grads, small, weights, firsts, seconds, mixed.reshape(flat), grad.reshape(flat))
    new_w, new_m, new_v, new_low, mixed, grad, norm, norm_m, norm_v, slope, slope_m, slope_v = out
    return (
        mixed.reshape(tokens.shape), grad.reshape(tokens.shape), new_w[None], new_m[None], new_v[None], new_low[None], norm, norm_m, norm_v,
        slope[0], slope_m[0], slope_v[0],
    )


def fits(mesh, shapes):
    return mesh.shape["batch"] == 4 and mesh.shape["seq"] == 8 and shapes[0].shape[1] == 1


def solution(mesh):
    in_specs = (
        P("batch", None, "seq", None),
        P("batch", None, "seq", None),
        P("batch", None, None),
        P(),
        P("batch", None, "seq", None),
        P("batch", None, "seq", None),
        P("batch", None, "seq", None),
        P(),
        P(),
        P(),
        P(),
        P(),
        P(),
        P(),
    )
    out_specs = (
        P("batch", None, "seq", None),
        P("batch", None, "seq", None),
        P("batch", None, "seq", None),
        P("batch", None, "seq", None),
        P("batch", None, "seq", None),
        P("batch", None, "seq", None),
        P(),
        P(),
        P(),
        P(),
        P(),
        P(),
    )

    def whole(*args):
        part = fused_body if fits(mesh, args) else body
        return jax.shard_map(
            part, mesh=mesh, in_specs=in_specs, out_specs=out_specs, check_vma=False
        )(*args)

    return whole
```

```python
import math

import jax
import jax.numpy as jnp
from jax import lax
from jax.experimental import pallas as pl
from jax.experimental.pallas import tpu as pltpu
from jax.sharding import PartitionSpec as P

FF = 2048
STEP = 10


beta_one = 0.9
beta_two = 0.95
adam_eps = 1e-08
decay_rate = 0.1
rate_matrix = 0.02
rate_norm = 0.2
rate_slope = 0.01
ln_eps = 1e-05
masked_score = -1000000000.0
row_kinds = (True, False, True, False, True, False)


def broadcast(value, axis, source):
    kept = jnp.where(lax.axis_index(axis) == source, value, 0).astype(value.dtype)
    return lax.psum(kept, axis)


def running_total(lengths):
    count = lengths.shape[-1]
    ends = [lengths[..., 0]]
    for index in range(1, count):
        ends.append(ends[-1] + lengths[..., index])
    return jnp.stack(ends, -1)


def for_sending(value):

    def short(part):
        return part.astype(jnp.bfloat16) if part.dtype == jnp.float32 else part

    return jax.tree.map(short, value)


def passed_along(value, axis, by):
    peers = lax.axis_size(axis)
    pairs = [(i, i + by) for i in range(peers) if 0 <= i + by < peers]
    return lax.ppermute(value, axis, pairs)


def layer_norm(values, gain, shift):
    center = jnp.mean(values, -1, keepdims=True)
    centred = values - center
    spread = jnp.mean(centred * centred, -1, keepdims=True)
    return centred * lax.rsqrt(spread + ln_eps) * gain + shift


def gelu_tanh(values):
    return jax.nn.gelu(values, approximate=True)


def block_counts(features, hidden):
    return [3, 3, 1, hidden // features, hidden // features, 3]


def block_starts(owners, sizes):
    starts_list = []
    for matrix_id in range(len(sizes)):
        shared = jnp.zeros((), jnp.int32)
        for earlier_id in range(matrix_id):
            shared = shared + jnp.where(
                owners[earlier_id] == owners[matrix_id], sizes[earlier_id], 0
            ).astype(jnp.int32)
        starts_list.append(shared)
    return starts_list


def slot_table(owners, device, sizes, slot_count):
    starts_list = block_starts(owners, sizes)
    slot_ids = jnp.arange(slot_count, dtype=jnp.int32)
    numbers = jnp.arange(sum(sizes), dtype=jnp.int32)
    slot_map = jnp.zeros((slot_count, sum(sizes)), jnp.float32)
    block_base = 0
    for matrix_id in range(len(sizes)):
        inside = (
            (owners[matrix_id] == device)
            & (slot_ids >= starts_list[matrix_id])
            & (slot_ids < starts_list[matrix_id] + sizes[matrix_id])
        )
        target = block_base + slot_ids - starts_list[matrix_id]
        slot_map = slot_map + (inside[:, None] & (target[:, None] == numbers[None, :])).astype(
            jnp.float32
        )
        block_base += sizes[matrix_id]
    return slot_map


def to_matrix(blocks, by_rows):
    if by_rows:
        return blocks.reshape(-1, blocks.shape[2])
    return blocks.transpose(1, 0, 2).reshape(blocks.shape[1], -1)


def to_blocks(matrix, by_rows, features):
    if by_rows:
        return matrix.reshape(-1, features, features)
    return matrix.reshape(features, -1, features).transpose(1, 0, 2)


def all_blocks(matrices, features):
    return jnp.concatenate(
        [to_blocks(matrices[matrix_id], row_kinds[matrix_id], features) for matrix_id in range(6)],
        0,
    )


def adam_update(weight, gradient, first_moment, second, fix_first, fix_second, rate, decay):
    first_new = beta_one * first_moment + (1.0 - beta_one) * gradient
    second_new = beta_two * second + (1.0 - beta_two) * gradient * gradient
    direction = first_new / fix_first / (jnp.sqrt(second_new / fix_second) + adam_eps)
    return (weight - rate * (direction + decay * weight), first_new, second_new)


def scores_for(query_block, key_rows, start_row, segment, head_slope):
    block_rows = query_block.shape[0]
    row_total = key_rows.shape[0]
    row_ids = start_row + jnp.arange(block_rows, dtype=jnp.int32)
    col_ids = jnp.arange(row_total, dtype=jnp.int32)
    distance = (row_ids[:, None] - col_ids[None, :]).astype(jnp.float32)
    seg_rows = lax.dynamic_slice_in_dim(segment, start_row, block_rows)
    allowed = (seg_rows[:, None] == segment[None, :]) & (col_ids[None, :] <= row_ids[:, None])
    raw_score = (
        jnp.dot(query_block, key_rows.T, preferred_element_type=jnp.float32) * 0.125
        - head_slope * distance
    )
    return (jnp.where(allowed, raw_score, masked_score), distance)


def attend(queries, key_rows, values, segment, head_slope, block_rows):
    row_total, head_width = queries.shape

    def per_block(start_row):
        query_block = lax.dynamic_slice_in_dim(queries, start_row, block_rows)
        scores, distance = scores_for(query_block, key_rows, start_row, segment, head_slope)
        largest = jnp.max(scores, -1, keepdims=True)
        log_total = largest + jnp.log(jnp.sum(jnp.exp(scores - largest), -1, keepdims=True))
        probability = jnp.exp(scores - log_total).astype(jnp.bfloat16)
        return (jnp.dot(probability, values, preferred_element_type=jnp.float32), log_total[:, 0])

    row_starts = jnp.arange(row_total // block_rows, dtype=jnp.int32) * block_rows
    attended, log_totals = lax.map(per_block, row_starts)
    return (attended.reshape(row_total, head_width), log_totals.reshape(row_total))


def attend_back(queries, key_rows, values, segment, head_slope, log_totals, grad_out, block_rows):
    row_total, head_width = queries.shape

    def per_block(carried, start_row):
        grad_keys, grad_values, grad_slope = carried
        query_block = lax.dynamic_slice_in_dim(queries, start_row, block_rows)
        grad_block = lax.dynamic_slice_in_dim(grad_out, start_row, block_rows)
        total_block = lax.dynamic_slice_in_dim(log_totals, start_row, block_rows)
        scores, distance = scores_for(query_block, key_rows, start_row, segment, head_slope)
        probability = jnp.exp(scores - total_block[:, None])
        grad_prob = jnp.dot(grad_block, values.T, preferred_element_type=jnp.float32)
        grad_score = (
            probability * (grad_prob - jnp.sum(probability * grad_prob, -1, keepdims=True))
        ).astype(jnp.bfloat16)
        grad_query = jnp.dot(grad_score, key_rows, preferred_element_type=jnp.float32) * 0.125
        grad_keys = (
            grad_keys
            + jnp.dot(grad_score.T, query_block, preferred_element_type=jnp.float32) * 0.125
        )
        grad_values = grad_values + jnp.dot(
            probability.astype(jnp.bfloat16).T, grad_block, preferred_element_type=jnp.float32
        )
        grad_slope = grad_slope - jnp.sum(grad_score.astype(jnp.float32) * distance)
        return ((grad_keys, grad_values, grad_slope), grad_query)

    row_starts = jnp.arange(row_total // block_rows, dtype=jnp.int32) * block_rows
    initial = (
        jnp.zeros((row_total, head_width), jnp.float32),
        jnp.zeros((row_total, head_width), jnp.float32),
        jnp.zeros((), jnp.float32),
    )
    (grad_keys, grad_values, grad_slope), grad_queries = lax.scan(per_block, initial, row_starts)
    return (grad_queries.reshape(row_total, head_width), grad_keys, grad_values, grad_slope)


def body(
    tokens,
    cotangent,
    doc_lengths,
    owners,
    master,
    first_moment,
    second_moment,
    ln_gain,
    ln_bias,
    norm_m,
    norm_v,
    slopes,
    slope_m,
    slope_v,
):
    micro_count, lane_count, tok_rows, features = tokens.shape
    unit_rows = tok_rows // 3
    seq_devices = lax.axis_size("seq")
    head_count = slopes.shape[0]
    head_width = features // head_count
    lane_units = unit_rows * seq_devices
    block_rows = min(512, lane_units)
    unit_total = lane_count * unit_rows
    slot_count = master.shape[1]
    sizes = block_counts(features, FF)
    starts_list = block_starts(owners, sizes)
    batch_rank = lax.axis_index("batch")
    seq_rank = lax.axis_index("seq")
    lane_rank = seq_rank // head_count
    head_rank = seq_rank % head_count
    low_slots = master[0].astype(jnp.bfloat16)
    fetched = []
    for matrix_id in range(6):
        owned_rows = lax.dynamic_slice_in_dim(
            low_slots, starts_list[matrix_id], sizes[matrix_id], 0
        )
        fetched.append(broadcast(owned_rows, "batch", owners[matrix_id]))
    gathered = lax.all_gather(for_sending(tuple(fetched)), "seq", axis=1, tiled=True)
    pool_weight, qkv_weight, out_weight, in_weight, back_weight, up_weight = [
        to_matrix(gathered[matrix_id], row_kinds[matrix_id]) for matrix_id in range(6)
    ]
    doc_ends = running_total(doc_lengths)
    doc_starts = jnp.concatenate(
        [jnp.zeros((micro_count, lane_count, 1), jnp.int32), doc_ends[..., :-1]], -1
    )
    unit_ids = seq_rank * unit_rows + jnp.arange(unit_rows, dtype=jnp.int32)
    keep_mask = 1.0 - jnp.any(
        unit_ids[None, None, :, None] == doc_starts[:, :, None, :], -1
    ).astype(jnp.float32)
    triples = tokens.reshape(micro_count, lane_count, unit_rows, 3, features)
    tail_tokens = triples[:, :, -1, 1:3]
    arrived = passed_along(tail_tokens, "seq", 1)
    lane_pick = jnp.arange(lane_count, dtype=jnp.int32) == lane_rank
    head_pick = jnp.arange(head_count, dtype=jnp.int32) == head_rank
    head_slope = jnp.sum(jnp.where(head_pick, slopes, 0.0))
    positions = jnp.arange(lane_units, dtype=jnp.int32)
    gain_grad = jnp.zeros((2, features), jnp.float32)
    bias_grad = jnp.zeros((2, features), jnp.float32)
    slope_grad = jnp.zeros((), jnp.float32)
    summed = None
    mixed_parts = []
    grad_parts = []
    outgoing = []
    for micro in range(micro_count):
        triple_now = triples[micro]
        keep_now = keep_mask[micro]
        earlier = jnp.concatenate([arrived[micro][:, None], triple_now[:, :-1, 1:3]], 1) * keep_now[
            :, :, None, None
        ].astype(jnp.bfloat16)
        pool_input = jnp.concatenate([earlier, triple_now[:, :, 0:1]], 2).reshape(
            unit_total, 3 * features
        )
        pooled = jnp.dot(pool_input, pool_weight, preferred_element_type=jnp.float32)
        normed = layer_norm(pooled, ln_gain[0], ln_bias[0]).astype(jnp.bfloat16)
        projected = jnp.dot(normed, qkv_weight, preferred_element_type=jnp.float32).astype(
            jnp.bfloat16
        )
        outbound = (
            projected.reshape(lane_count, unit_rows, 3, head_count, head_width)
            .transpose(0, 3, 1, 2, 4)
            .reshape(lane_count * head_count, unit_rows * 3 * head_width)
        )
        received = lax.all_to_all(outbound, "seq", split_axis=0, concat_axis=1, tiled=True).reshape(
            lane_units, 3, head_width
        )
        queries = received[:, 0]
        key_rows = received[:, 1]
        values = received[:, 2]
        lengths = jnp.sum(jnp.where(lane_pick[:, None], doc_lengths[micro], 0), 0)
        lane_ends = running_total(lengths)
        segment = jnp.sum((positions[:, None] >= lane_ends[None, :-1]).astype(jnp.int32), 1)
        attended, log_totals = attend(queries, key_rows, values, segment, head_slope, block_rows)
        returned = lax.all_to_all(
            attended.astype(jnp.bfloat16).reshape(1, lane_units * head_width),
            "seq",
            split_axis=1,
            concat_axis=0,
            tiled=True,
        )
        merged = (
            returned.reshape(lane_count, head_count, unit_rows, head_width)
            .transpose(0, 2, 1, 3)
            .reshape(unit_total, features)
        )
        residual = pooled + jnp.dot(merged, out_weight, preferred_element_type=jnp.float32)
        normed_two = layer_norm(residual, ln_gain[1], ln_bias[1]).astype(jnp.bfloat16)
        hidden = jnp.dot(normed_two, in_weight, preferred_element_type=jnp.float32)
        activated = gelu_tanh(hidden).astype(jnp.bfloat16)
        shortened = residual + jnp.dot(activated, back_weight, preferred_element_type=jnp.float32)
        short_low = shortened.astype(jnp.bfloat16)
        upward = jnp.dot(short_low, up_weight, preferred_element_type=jnp.float32).reshape(
            lane_count, unit_rows * 3, features
        )
        mixed_parts.append(tokens[micro].astype(jnp.float32) + upward)
        grad_upward = cotangent[micro].reshape(unit_total, 3 * features)
        sum_up = jnp.dot(short_low.T, grad_upward, preferred_element_type=jnp.float32)
        grad_short = jnp.dot(grad_upward, up_weight.T, preferred_element_type=jnp.float32)
        grad_short_low = grad_short.astype(jnp.bfloat16)
        sum_back = jnp.dot(activated.T, grad_short_low, preferred_element_type=jnp.float32)
        grad_activated = jnp.dot(grad_short_low, back_weight.T, preferred_element_type=jnp.float32)
        grad_hidden = jax.vjp(gelu_tanh, hidden)[1](grad_activated)[0].astype(jnp.bfloat16)
        sum_in = jnp.dot(normed_two.T, grad_hidden, preferred_element_type=jnp.float32)
        grad_normed_two = jnp.dot(grad_hidden, in_weight.T, preferred_element_type=jnp.float32)
        norm_two_back = jax.vjp(layer_norm, residual, ln_gain[1], ln_bias[1])[1]
        grad_resid_norm, grad_gain_two, grad_bias_two = norm_two_back(grad_normed_two)
        grad_residual = grad_short + grad_resid_norm
        grad_resid_low = grad_residual.astype(jnp.bfloat16)
        sum_out = jnp.dot(merged.T, grad_resid_low, preferred_element_type=jnp.float32)
        grad_merged = jnp.dot(
            grad_resid_low, out_weight.T, preferred_element_type=jnp.float32
        ).astype(jnp.bfloat16)
        back_outbound = (
            grad_merged.reshape(lane_count, unit_rows, head_count, head_width)
            .transpose(0, 2, 1, 3)
            .reshape(lane_count * head_count, unit_rows * head_width)
        )
        grad_attended = lax.all_to_all(
            back_outbound, "seq", split_axis=0, concat_axis=1, tiled=True
        ).reshape(lane_units, head_width)
        grad_queries, grad_keys, grad_values, grad_slope = attend_back(
            queries, key_rows, values, segment, head_slope, log_totals, grad_attended, block_rows
        )
        grad_heads = (
            jnp.stack([grad_queries, grad_keys, grad_values], 1)
            .astype(jnp.bfloat16)
            .reshape(1, lane_units * 3 * head_width)
        )
        grad_arrived = lax.all_to_all(grad_heads, "seq", split_axis=1, concat_axis=0, tiled=True)
        grad_projected = (
            grad_arrived.reshape(lane_count, head_count, unit_rows, 3, head_width)
            .transpose(0, 2, 3, 1, 4)
            .reshape(unit_total, 3 * features)
        )
        sum_qkv = jnp.dot(normed.T, grad_projected, preferred_element_type=jnp.float32)
        grad_normed = jnp.dot(grad_projected, qkv_weight.T, preferred_element_type=jnp.float32)
        norm_one_back = jax.vjp(layer_norm, pooled, ln_gain[0], ln_bias[0])[1]
        grad_pool_norm, grad_gain_one, grad_bias_one = norm_one_back(grad_normed)
        grad_pooled_low = (grad_residual + grad_pool_norm).astype(jnp.bfloat16)
        sum_pool = jnp.dot(pool_input.T, grad_pooled_low, preferred_element_type=jnp.float32)
        grad_pieces = jnp.dot(
            grad_pooled_low, pool_weight.T, preferred_element_type=jnp.float32
        ).reshape(lane_count, unit_rows, 3, features)
        grad_earlier = grad_pieces[:, :, 0:2] * keep_now[:, :, None, None]
        outgoing.append(grad_earlier[:, 0])
        following = jnp.concatenate(
            [grad_earlier[:, 1:], jnp.zeros((lane_count, 1, 2, features), jnp.float32)], 1
        )
        token_grad = jnp.concatenate([grad_pieces[:, :, 2:3], following], 2).reshape(
            lane_count, unit_rows * 3, features
        )
        grad_parts.append(cotangent[micro].astype(jnp.float32) + token_grad)
        gain_grad = gain_grad + jnp.stack([grad_gain_one, grad_gain_two])
        bias_grad = bias_grad + jnp.stack([grad_bias_one, grad_bias_two])
        slope_grad = slope_grad + grad_slope
        micro_grads = [sum_pool, sum_qkv, sum_out, sum_in, sum_back, sum_up]
        summed = (
            micro_grads
            if summed is None
            else [left + right for left, right in zip(summed, micro_grads)]
        )
    reduced = lax.psum_scatter(all_blocks(summed, features), "seq", scatter_dimension=1, tiled=True)
    incoming = passed_along(jnp.stack(outgoing).astype(jnp.bfloat16), "seq", -1).astype(jnp.float32)
    grad_tokens = jnp.stack(grad_parts).reshape(micro_count, lane_count, unit_rows, 3, features)
    grad_tokens = grad_tokens.at[:, :, -1, 1:3].add(incoming).reshape(tokens.shape)
    reduced_all = lax.psum(reduced, "batch")
    norm_grad, slopes_grad = lax.psum(
        (jnp.concatenate([gain_grad, bias_grad], 0), jnp.where(head_pick, slope_grad, 0.0)),
        ("batch", "seq"),
    )
    slot_map = slot_table(owners, batch_rank, sizes, slot_count)
    is_owned = jnp.sum(slot_map, -1)[:, None, None] > 0.5
    slot_grads = jnp.einsum("jb,brc->jrc", slot_map, reduced_all, precision=lax.Precision.HIGHEST)
    step_float = jnp.float32(STEP)
    fix_first = 1.0 - jnp.power(jnp.float32(beta_one), step_float)
    fix_second = 1.0 - jnp.power(jnp.float32(beta_two), step_float)
    new_weight, new_first, new_second = adam_update(
        master[0],
        slot_grads,
        first_moment[0],
        second_moment[0],
        fix_first,
        fix_second,
        rate_matrix,
        decay_rate,
    )
    new_weight = jnp.where(is_owned, new_weight, master[0])
    new_first = jnp.where(is_owned, new_first, first_moment[0])
    new_second = jnp.where(is_owned, new_second, second_moment[0])
    norm_now = jnp.concatenate([ln_gain, ln_bias], 0)
    new_norm, new_norm_m, new_norm_v = adam_update(
        norm_now, norm_grad, norm_m, norm_v, fix_first, fix_second, rate_norm, 0.0
    )
    new_slopes, new_slope_m, new_slope_v = adam_update(
        slopes, slopes_grad, slope_m, slope_v, fix_first, fix_second, rate_slope, 0.0
    )
    return (
        jnp.stack(mixed_parts),
        grad_tokens,
        new_weight[None],
        new_first[None],
        new_second[None],
        new_weight[None].astype(jnp.bfloat16),
        new_norm,
        new_norm_m,
        new_norm_v,
        new_slopes,
        new_slope_m,
        new_slope_v,
    )


MESH = pl.DeviceIdType.MESH
LOW = jnp.bfloat16
WIDE = jnp.float32
TILE = 128


class Plan:
    def __init__(self):
        self.tasks = {}

    def add(self, name, run, deps=(), waits=(), sends=(), cost=0.1, rank=0):
        assert name not in self.tasks
        self.tasks[name] = (run, tuple(deps), tuple(waits), tuple(sends), cost, rank)

    def order(self):
        now, done, arrival, free, listed = 0.0, set(), {}, {}, []
        left = list(self.tasks)
        while left:
            best = None
            for place, name in enumerate(left):
                run, deps, waits, sends, cost, rank = self.tasks[name]
                if any(d not in done for d in deps) or any(w not in arrival for w in waits):
                    continue
                begin = max([now] + [arrival[w] for w in waits] + [free.get(m[1], 0.0) - SLACK for m in sends])
                key = (begin, rank, place)
                if best is None or key < best[0]:
                    best = (key, name)
            name = best[1]
            run, deps, waits, sends, cost, rank = self.tasks[name]
            now = best[0][0] + cost
            for message, link, size in sends:
                rate, delay = LINKS[link]
                lanes = ("f", "r", "l") if link == "f" else (link,)
                end = max([now] + [free.get(lane, 0.0) for lane in lanes]) + size / rate
                free.update({lane: end for lane in lanes})
                arrival[message] = end + delay
            done.add(name)
            left.remove(name)
            listed.append((name, now))
        return listed


SLACK = 2.0
SENDS, RECEIVES = 24, 175
GATHERS = (
    (0, 0, 1, 0.0),
    (0, 1, 1, 0.07),
    (0, 2, 1, 0.08),
    (1, 0, 1, 0.21),
    (1, 1, 1, 0.21),
    (1, 2, 1, 0.21),
    (3, 0, 2, 0.31),
    (3, 2, 2, 0.33),
    (2, 0, 1, 0.43),
    (5, 0, 3, 0.37),
)
QUARTERS = {5: 0, 1: 3, 0: 6}
AFTER = {}
WHOLE = ()
FIRST = ("w", 0, 0)
SCATTERS = (
    (5, 0, 3, 0.93),
    (3, 0, 2, 1.01),
    (3, 2, 2, 0.93),
    (2, 0, 1, 1.26),
    (0, 0, 1, 0.43),
    (0, 1, 1, 0.43),
    (0, 2, 1, 0.43),
    (1, 0, 3, 0.6),
)
LINKS = {
    "c": (400e3, 1.0),
    "x": (52e3, 2.3),
    "r": (52e3, 2.3),
    "l": (52e3, 2.3),
    "f": (46e3, 3.3),
}


def start_of(owners, matrix_id, sizes):
    shared = jnp.int32(0)
    for earlier_id in range(matrix_id):
        shared = shared + jnp.where(owners[earlier_id] == owners[matrix_id], sizes[earlier_id], 0)
    return shared


def over_last(fn, value):
    return fn(value, axis=-1, keepdims=True)


def contract(left, right, left_dim, right_dim):
    return lax.dot_general(
        left, right, (((left_dim,), (right_dim,)), ((), ())), preferred_element_type=WIDE
    )


def gelu_parts(value):
    scale = math.sqrt(2.0 / math.pi)
    inner = jnp.tanh(scale * (value + 0.044715 * (value * value * value)))
    return inner, scale * (1.0 + 3 * 0.044715 * value * value)


def main_kernel(dims, refs):
    units, features, hidden_width, heads, micros, sizes = dims
    tables, (tok_hbm, cot_hbm, master_hbm, first_hbm, second_hbm) = refs[:10], refs[10:15]
    mixed_hbm, grad_hbm, slot_grads, small, masters, firsts, seconds = refs[15:22]
    held = refs[22:32]
    owners, docs, slopes, gain, bias, norm_m, norm_v, slope_row, slope_m, slope_v = held
    (
        w, red, cross_in, mine, other, core_in, both, x_in, tok, cot, tail_in, wide_tok, wide_cot, x_pool, x_norm, x_att,
        x_two, x_act, x_short, d_up, d_low, d_inner, d_res, d_qkv, d_pool, pooled, hat_one, hat_two, root_one, root_two,
        resid, hidden, short_grad, res_grad, q_out, q_in, a_out, a_in, da_out, da_in, dq_out, dq_in, probs, mixed, grad,
        wide_up, wide_grad, edge_in, x_near, x_wide, t_left, t_out, t_in, u_out, u_in, dx_out, dx_in, g, right_in, left_in, fin_out, fin_in, co_out, co_in, sums, sums_in, sends, recvs, local,
    ) = refs[32:]
    half = features // 2
    width = features // heads
    rows_of = masters.shape[1]
    count = heads
    tokens = 3 * units
    own = micros * units
    pair_width = 2 * width
    b, s = lax.axis_index("batch"), lax.axis_index("seq")
    x, c = b // 2, b % 2
    z, y = s // 2, s % 2
    spot = y * (7 - 2 * z) + z

    def seq_of(position):
        far = position // 4
        return 2 * (position + far * (7 - 2 * position)) + far

    def at(offset):
        return lax.rem(spot + offset + 2 * count, count)

    def rows_at(offset, part=0, length=rows_of):
        return pl.ds(pl.multiple_of(seq_of(at(offset)) * rows_of + part, 16), length)

    my_half = pl.ds(pl.multiple_of(c * half, half), half)
    other_half = pl.ds(pl.multiple_of((1 - c) * half, half), half)
    core_peer = (x * 2 + 1 - c, s)
    x_peer = ((1 - x) * 2 + c, s)
    cross_peer = ((1 - x) * 2 + 1 - c, s)
    right_peer = (b, seq_of(at(1)))
    left_peer = (b, seq_of(at(-1)))
    plan = Plan()
    flying, started, boxes = {}, [], {}

    def launch(name, copies, starts, group):
        if len(started) >= SENDS:
            started[len(started) - SENDS].wait_send()
        started.append(copies[0])
        flying[name] = copies[0]
        for start in starts:
            start()

    def describe(source, target, device, group):
        box = boxes.setdefault(group, len(boxes))
        return pltpu.make_async_remote_copy(
            src_ref=source,
            dst_ref=target,
            send_sem=sends.at[len(started) % SENDS],
            recv_sem=recvs.at[box],
            device_id=device,
            device_id_type=MESH,
        )

    def send(name, source, target, device, group=None):
        copy = describe(source, target, device, group or name)
        launch(name, [copy], [copy.start], group or name)

    def gather_up(group, whole):
        describe(whole, whole, core_peer, group).wait_recv()

    loads = [
        pltpu.make_async_copy(master_hbm, masters, local.at[0]),
        pltpu.make_async_copy(tok_hbm, tok, local.at[1]),
        pltpu.make_async_copy(cot_hbm, cot, local.at[2]),
    ]
    for table, place in zip(tables, held):
        loads.append(pltpu.make_async_copy(table, place, local.at[len(loads) + 2]))
    for copy in loads:
        copy.start()
    moments = [
        pltpu.make_async_copy(first_hbm, firsts, local.at[15]),
        pltpu.make_async_copy(second_hbm, seconds, local.at[16]),
    ]
    barrier = pltpu.get_barrier_semaphore()
    for step in range(1, count):
        pl.semaphore_signal(
            barrier, inc=1, device_id=(b, lax.rem(s + step, count)), device_id_type=MESH
        )
    for device in (core_peer, x_peer, cross_peer):
        pl.semaphore_signal(barrier, inc=1, device_id=device, device_id_type=MESH)
    pl.semaphore_wait(barrier, count + 2)
    for copy in loads[3:]:
        copy.wait()

    spans, first = [], 0
    for size in sizes:
        spans.append((first, first + size))
        first += size
    in_base, back_base, up_base = spans[3][0], spans[4][0], spans[5][0]
    hidden_blocks = sizes[3]
    ours = in_base + x * hidden_blocks
    theirs = in_base + (1 - x) * hidden_blocks
    plan.add("ms", loads[0].wait, cost=0.5)

    def contribute(k):
        def run():
            lo, hi = spans[k]
            mask = (owners[k] == b).astype(WIDE)
            begin = start_of(owners, k, sizes)
            for block in range(lo, hi):
                slot = jnp.minimum(begin + (block - lo), masters.shape[0] - 1)
                mine[block] = (masters[slot, :, my_half] * mask).astype(LOW)
                other[block] = (masters[slot, :, other_half] * mask).astype(LOW)
                if block == 0:
                    send(("g1", FIRST), mine.at[0], x_in.at[0], x_peer, ("g1", FIRST))
                    send(("g2", FIRST), other.at[0], cross_in, cross_peer, ("g1", FIRST))
            send(("g0", k), other.at[lo:hi], core_in.at[lo:hi], core_peer)

        return run

    def join_cores(k):
        def run():
            lo, hi = spans[k]
            flying[("g0", k)].wait_recv()
            both[lo:hi] = mine[lo:hi] + core_in[lo:hi]

        return run

    have = {k: [] for k in range(6)}
    gathers = []
    for k, offset, size, rank in GATHERS:
        name = ("w", k, offset)
        if k == 3:
            gathers.append((rank, name, (3, 4), ours + offset, theirs + offset, size))
            have[3] += [("h", name), ("hy", name)]
        else:
            begin = spans[k][0] + offset
            gathers.append((rank, name, (k,), begin, begin if k == 5 else None, size))
            have[k] += [("h", name)]
    piece_bytes = rows_of * half * 2

    quarter = half // 2
    plane_span = pl.ds(pl.multiple_of(x * quarter, quarter), quarter)
    plane_away = pl.ds(pl.multiple_of((1 - x) * quarter, quarter), quarter)

    def gather_chunk(rank, name, parents, here, there, size):
        quarters = there is here
        split = there is not None and not quarters
        load = size * piece_bytes // (2 if quarters else 1)
        blocks = pl.ds(here, size)
        away = pl.ds(there, size) if split else blocks
        span, away_span = (plane_span, plane_away) if quarters else (slice(None), slice(None))

        def piece(offset, part=0, length=rows_of):
            return w.at[blocks, c, rows_at(offset, part, length), span]

        def join_here():
            send(("g1", name), both.at[away, :, away_span], x_in.at[away, :, away_span], x_peer)

        def join_x():
            if name == FIRST:
                gather_up(("g1", FIRST), w.at[0:2, c, 0:rows_of])
                w[0, c, rows_at(0)] = both[0] + (x_in[0] + cross_in[...])
            else:
                flying[("g1", name)].wait_recv()
                w[blocks, c, rows_at(0), span] = both[blocks, :, span] + x_in[blocks, :, span]
            send(("R", 1, name), piece(0), piece(0), right_peer, (1, name))
            send(("L", 1, name), piece(0), piece(0), left_peer, (1, name))

        def onward(step):
            def run():
                gather_up((step - 1, name), w.at[blocks, c, 0 : rows_of * (2 if step < 5 else 1), span])
                if step == 5:
                    return
                for side, offset, peer in (("R", 1 - step, right_peer), ("L", step - 1, left_peer)):
                    part = piece(offset)
                    if step == 4:
                        part = piece(offset, 0 if side == "R" else rows_of // 2, rows_of // 2)
                    send((side, step, name), part, part, peer, (step, name))

            return run

        def across(step):
            def run():
                for side, offset in (("R", -step), ("L", step)):
                    part = piece(offset)
                    if step == 4:
                        part = piece(offset, 0 if side == "R" else rows_of // 2, rows_of // 2)
                    if step > 0 or side == "R":
                        send(("X", side, step, name), part, part, x_peer, ("X", name))

            return run

        def distribute(which, held, lanes):
            def run():
                send((which, name), w.at[held, c, :, lanes], w.at[held, c, :, lanes], core_peer)

            return run

        before = ("cs", 0)
        if name != FIRST:
            before = ("cx", name)
            plan.add(before, join_here, [("cs", k) for k in parents], (), [(("g1", name), "x", load)], 0.05, rank)
        plan.add(
            ("x", name), join_x, [before], [("g1", name)] + ([("g2", name)] if name == FIRST else []),
            [(("R", 1, name), "r", load), (("L", 1, name), "l", load)], 0.05, rank,
        )
        crossing = []

        def cross(step, after):
            messages = [("X", side, step, name) for side in ("RL" if step else "R")]
            size_of = load if step < 4 else load // 2
            plan.add(("X", step, name), across(step), [after], (), [(m, "x", size_of) for m in messages], 0.05, rank + 0.05)
            crossing.extend(messages)

        if split:
            cross(0, ("x", name))
        for step in (2, 3, 4, 5):
            size_of = load if step < 4 else load // 2
            out = [((side, step, name), link, size_of) for side, link in (("R", "r"), ("L", "l"))] if step < 5 else []
            before = ("x", name) if step == 2 else (step - 1, "f", name)
            waits = [(side, step - 1, name) for side in "RL"]
            plan.add((step, "f", name), onward(step), [before], waits, out, 0.05, rank)
            if split:
                cross(step - 1, (step, "f", name))
        plan.add(("di", name), distribute("D", blocks, span), [(5, "f", name)], (), [(("D", name), "c", 8 * load)], 0.05, rank)
        plan.add(("h", name), arrive(("D", name)), [("di", name)], [("D", name)], (), 0.02, rank)
        if split:
            whole = w.at[away, c, :, away_span]
            last = [("X", step, name) for step in range(5)]
            plan.add(("xw", name), lambda: gather_up(("X", name), whole), last, crossing, (), 0.05, rank)
            plan.add(("dy", name), distribute("E", away, away_span), [("xw", name)], (), [(("E", name), "c", 8 * load)], 0.05, rank)
            plan.add(("hy", name), arrive(("E", name)), [("dy", name)], [("E", name)], (), 0.02, rank)

    def arrive(*names):
        def run():
            for name in names:
                flying[name].wait_recv()

        return run

    for k in (0, 1, 3, 4, 2, 5):
        lo, hi = spans[k]
        load = (hi - lo) * piece_bytes
        early = [((which, FIRST), "x", piece_bytes) for which in ("g1", "g2")] if k == 0 else []
        plan.add(("co", k), contribute(k), ["ms"], (), early + [(("g0", k), "c", load)], 0.04 * (hi - lo), 0.1)
        plan.add(("cs", k), join_cores(k), [("co", k)], [("g0", k)], (), 0.02 * (hi - lo), 0.1)
    for chunk in gathers:
        gather_chunk(*chunk)

    def exchange(name, buffer):
        send(name, buffer.at[0:own], buffer.at[own : 2 * own], core_peer)

    def shared(name, columns):
        return (name, "c", own * columns * 2)

    lead = 16
    tiles = range(features // TILE)

    def columns_at(tile, base=0):
        return slice(base + tile * TILE, base + (tile + 1) * TILE)

    def ends_of(micro):
        ends = []
        total = jnp.int32(0)
        for index in range(docs.shape[1] - 1):
            total = total + docs[micro, index]
            ends.append(total)
        return ends

    def kept(micro):
        ids = s * units + lax.broadcasted_iota(jnp.int32, (units, 1), 0)
        starts = (ids == 0).astype(jnp.int32)
        for end in ends_of(micro):
            starts = starts | (ids == end).astype(jnp.int32)
        return starts == 0

    def load_tokens():
        loads[1].wait()
        send("tl", tok.at[:, tokens - lead :], tail_in, (b, lax.rem(s + 1, count)))
        for micro in range(micros):
            for tile in tiles:
                wide_tok[micro, tile, lead:] = tok[micro, :, columns_at(tile)].astype(WIDE)

    def load_cotangent():
        loads[2].wait()
        for micro in range(micros):
            for tile in tiles:
                wide_cot[micro, tile] = cot[micro, :, columns_at(tile)].astype(WIDE)
                for r in range(3):
                    d_up[micro * units : (micro + 1) * units, columns_at(tile, r * features)] = wide_cot[
                        micro, tile, pl.ds(r, units, stride=3), :
                    ].astype(LOW)
        exchange("eu", d_up)

    def make_pieces():
        flying["tl"].wait_recv()
        for micro in range(micros):
            keep = kept(micro)
            for tile in tiles:
                wide_tok[micro, tile, :lead] = tail_in[micro, :, columns_at(tile)].astype(WIDE)
                for r in range(3):
                    part = wide_tok[micro, tile, pl.ds(lead - 2 + r, units, stride=3), :]
                    if r < 2:
                        part = jnp.where(keep, part, 0.0)
                    x_pool[micro * units : (micro + 1) * units, columns_at(tile, r * features)] = part.astype(LOW)
        exchange("ep", x_pool)

    plan.add("tok", load_tokens, sends=[("tl", "f", 2 * lead * features * 2)], cost=0.3, rank=1)
    plan.add(
        "pc", make_pieces, ["tok"], ["tl"], [shared("ep", 3 * features)], 0.5, rank=1
    )
    plan.add("cot", load_cotangent, (), (), [shared("eu", 3 * features)], 0.5, rank=2)

    def normal(value, which, hat, root):
        centred = value - over_last(jnp.mean, value)
        scale = lax.rsqrt(over_last(jnp.mean, centred * centred) + ln_eps)
        unit = centred * scale
        hat[...] = unit
        root[...] = scale
        return (unit * gain[which : which + 1, :] + bias[which : which + 1, :]).astype(LOW)

    def both_halves(make):
        return jnp.concatenate([make(0), make(1)], axis=1)

    def pool():
        def side(h):
            total = None
            for r in range(3):
                term = contract(x_pool[0:own, r * features : (r + 1) * features], w[r, h], 1, 0)
                total = term if total is None else total + term
            return total

        value = both_halves(side)
        pooled[...] = value
        x_norm[0:own] = normal(value, 0, hat_one, root_one)
        exchange("en", x_norm)

    lane = lambda: lax.broadcasted_iota(jnp.int32, (1, pair_width), 1)

    def swap(value):
        return pltpu.roll(value, width, axis=1)

    def to_heads(tile, target, pair, row):
        low_lanes = lane() < width
        first, second = tile[:units], tile[units:]
        target[2 * pair, row : row + units] = jnp.where(low_lanes, first, swap(second)).astype(LOW)
        target[2 * pair + 1, row : row + units] = jnp.where(low_lanes, swap(first), second).astype(LOW)

    def from_heads(source, pair, row):
        low_lanes = lane() < width
        even = source[2 * pair, row : row + units].astype(WIDE)
        odd = source[2 * pair + 1, row : row + units].astype(WIDE)
        return jnp.where(low_lanes, even, swap(odd)).astype(LOW), jnp.where(low_lanes, swap(even), odd).astype(LOW)

    def spread(name, source, target):
        for step in range(1, count):
            there = lax.rem(s + step, count)
            send((name, step), source.at[there], target.at[s], (b, there), name)
        target[s] = source[s]

    def spread_names(name):
        return [(name, step) for step in range(1, count)]

    def spread_sends(name, rows):
        return [((name, step), "f", rows * pair_width * 2) for step in range(1, count)]

    def project():
        for part in range(3):
            for h in range(2):
                value = contract(x_norm[0:own], w[3 + part, h], 1, 0)
                for tile in range(half // pair_width):
                    to_heads(
                        value[:, tile * pair_width : (tile + 1) * pair_width],
                        q_out,
                        h * (half // pair_width) + tile,
                        part * units,
                    )
        spread("q", q_out, q_in)

    lane_units = units * count

    def heads_of(source, part):
        return source[:, part * units : (part + 1) * units, :].reshape(lane_units, pair_width)

    def lanes_of(micro):
        return (lane() // width == micro).astype(WIDE).astype(LOW)

    def distances():
        row_ids = lax.broadcasted_iota(jnp.int32, (lane_units, lane_units), 0)
        col_ids = lax.broadcasted_iota(jnp.int32, (lane_units, lane_units), 1)
        return row_ids - col_ids

    def attend_now():
        gather_up("q", q_in.at[0 : count - 1])
        queries, keys, values = (heads_of(q_in, part) for part in range(3))
        slope = slopes[s]
        total = None
        for micro in range(micros):
            gap = distances()
            row_seg = jnp.zeros((lane_units, 1), jnp.int32)
            col_seg = jnp.zeros((1, lane_units), jnp.int32)
            for end in ends_of(micro):
                row_seg += (lax.broadcasted_iota(jnp.int32, (lane_units, 1), 0) >= end).astype(jnp.int32)
                col_seg += (lax.broadcasted_iota(jnp.int32, (1, lane_units), 1) >= end).astype(jnp.int32)
            allowed = (row_seg == col_seg) & (gap >= 0)
            mask = lanes_of(micro)
            raw = contract(queries * mask, keys, 1, 1) * 0.125 - slope * gap.astype(WIDE)
            scores = jnp.where(allowed, raw, masked_score)
            raised = jnp.exp(scores - over_last(jnp.max, scores))
            probability = raised / over_last(jnp.sum, raised)
            probs[micro] = probability
            term = contract(probability.astype(LOW), values * mask, 1, 0)
            total = term if total is None else total + term
        a_out[...] = total.astype(LOW).reshape(count, units, pair_width)
        spread("a", a_out, a_in)

    def merge():
        gather_up("a", a_in.at[0 : count - 1])
        for pair in range(heads // 2):
            columns = slice(pair * pair_width, (pair + 1) * pair_width)
            first, second = from_heads(a_in, pair, 0)
            x_att[0:units, columns] = first
            x_att[units:own, columns] = second
        exchange("ea", x_att)

    def project_out():
        value = pooled[...] + both_halves(lambda h: contract(x_att[0:own], w[6, h], 1, 0))
        resid[...] = value
        x_two[0:own] = normal(value, 1, hat_two, root_two)
        exchange("et", x_two)


    def widen(j):
        def run():
            for h in range(2):
                columns = slice(j * features + h * half, j * features + (h + 1) * half)
                value = contract(x_two[0:own], w[in_base + j, h], 1, 0)
                hidden[:, columns] = value
                inner, _ = gelu_parts(value)
                x_act[0:own, columns] = (0.5 * value * (1.0 + inner)).astype(LOW)
            if j == hidden_blocks - 1:
                exchange("ec", x_act)

        return run

    def narrow():
        def side(h):
            total = resid[:, h * half : (h + 1) * half]
            for j in range(hidden_blocks):
                total = total + contract(
                    x_act[0:own, j * features : (j + 1) * features], w[back_base + j, h], 1, 0
                )
            return total

        x_short[0:own] = both_halves(side).astype(LOW)
        exchange("es", x_short)

    outs = [
        pltpu.make_async_copy(mixed, mixed_hbm, local.at[3]),
        pltpu.make_async_copy(grad, grad_hbm, local.at[4]),
    ]

    def place_up(r, value, core, plane):
        for micro in range(micros):
            wide_up[micro, 2 * core + plane, pl.ds(r, units, stride=3), :] = value[micro * units : (micro + 1) * units]

    def lift_away():
        for r in range(3):
            for core in range(2):
                value = contract(t_left[QUARTERS[5], 0:own], w[up_base + r, core, :, plane_span], 1, 0)
                u_out[:, (2 * r + core) * quarter : (2 * r + core + 1) * quarter] = value.astype(LOW)
        send("ux", u_out, u_in, x_peer)

    def lift(r):
        def run():
            for core in range(2):
                place_up(r, contract(x_short[0:own], w[up_base + r, core, :, plane_span], 1, 0), core, x)

        return run

    def finish_mixed():
        arrive("ux")()
        for r in range(3):
            for core in range(2):
                begin = (2 * r + core) * quarter
                place_up(r, u_in[:, begin : begin + quarter].astype(WIDE), core, 1 - x)
        for micro in range(micros):
            for tile in tiles:
                columns = columns_at(tile)
                mixed[micro, :, columns] = tok[micro, :, columns].astype(WIDE) + wide_up[micro, tile]
        outs[0].start()

    plan.add("po", pool, ["pc", *have[0]], (), [shared("en", features)], 0.6, rank=3)
    plan.add("pr", project, ["po", *have[1]], (), spread_sends("q", 3 * units), 0.6, rank=3)
    plan.add("at", attend_now, ["pr"], spread_names("q"), spread_sends("a", units), 1.1, rank=3)
    plan.add("me", merge, ["at"], spread_names("a"), [shared("ea", features)], 0.15, rank=3)
    plan.add("ou", project_out, ["me", *have[2]], (), [shared("et", features)], 0.45, rank=3)
    for j in range(hidden_blocks):
        last = j == hidden_blocks - 1
        plan.add(
            ("wi", j), widen(j), ["ou", *have[3]] + ([("wi", i) for i in range(j)] if last else []), (),
            [shared("ec", hidden_width)] if last else (), 0.3, rank=3,
        )
    plan.add(
        "na", narrow, [("wi", j) for j in range(hidden_blocks)] + [*have[3]], (), [shared("es", features)], 0.5,
        rank=3,
    )
    for r in range(3):
        plan.add(("li", r), lift(r), ["na", *have[5]], (), (), 0.2, rank=8)
    quarter_lump = own * 3 * half * 2
    plan.add("lq", lift_away, [("tw", 5, 0), *have[5]], (), [("ux", "x", quarter_lump)], 0.6, rank=8)
    plan.add("lf", finish_mixed, ["lq", "tok"] + [("li", r) for r in range(3)], ["ux"], (), 0.4, rank=8)

    def back_short_away():
        total = None
        for r in range(3):
            for core in range(2):
                columns = slice(core * quarter, (core + 1) * quarter)
                term = contract(t_in[QUARTERS[5] + r, 0:own, columns], w[up_base + r, core, :, plane_span], 1, 1)
                total = term if total is None else total + term
        dx_out[...] = total.astype(LOW)
        send("dx", dx_out, dx_in, x_peer)

    def back_short_here():
        total = None
        for r in range(3):
            for core in range(2):
                columns = pl.ds(pl.multiple_of(r * features + core * half + x * quarter, quarter), quarter)
                term = contract(d_up[0:own, columns], w[up_base + r, core, :, plane_span], 1, 1)
                total = term if total is None else total + term
        short_grad[...] = total

    def back_short():
        arrive("dx")()
        total = short_grad[...] + dx_in[...].astype(WIDE)
        short_grad[...] = total
        d_low[0:own] = total.astype(LOW)
        exchange("el", d_low)

    def back_widen(j):
        def run():
            total = contract(d_low[0:own, 0:half], w[back_base + j, 0], 1, 1)
            total = total + contract(d_low[0:own, half:features], w[back_base + j, 1], 1, 1)
            columns = slice(j * features, (j + 1) * features)
            value = hidden[:, columns]
            inner, slope = gelu_parts(value)
            factor = 0.5 * (1.0 + inner) + 0.5 * value * (1.0 - inner * inner) * slope
            d_inner[0:own, columns] = (total * factor).astype(LOW)
            if j == hidden_blocks - 1:
                exchange("ei", d_inner)

        return run

    def back_normal(value, which, hat, root):
        unit = hat[...]
        sums[which : which + 1, :] = jnp.sum(value * unit, axis=0, keepdims=True)
        sums[2 + which : 3 + which, :] = jnp.sum(value, axis=0, keepdims=True)
        scaled = value * gain[which : which + 1, :]
        return root[...] * (
            scaled - over_last(jnp.mean, scaled) - unit * over_last(jnp.mean, scaled * unit)
        )

    def back_two():
        total = None
        for j in range(hidden_blocks):
            for h in range(2):
                begin = j * features + h * half
                term = contract(d_inner[0:own, begin : begin + half], w[in_base + j, h], 1, 1)
                total = term if total is None else total + term
        value = short_grad[...] + back_normal(total, 1, hat_two, root_two)
        res_grad[...] = value
        d_res[0:own] = value.astype(LOW)
        exchange("er", d_res)

    def back_out():
        value = contract(d_res[0:own, 0:half], w[6, 0], 1, 1)
        value = value + contract(d_res[0:own, half:features], w[6, 1], 1, 1)
        for pair in range(heads // 2):
            to_heads(value[:, pair * pair_width : (pair + 1) * pair_width], da_out, pair, 0)
        spread("da", da_out, da_in)

    def back_attend():
        gather_up("da", da_in.at[0 : count - 1])
        queries, keys, values = (heads_of(q_in, part) for part in range(3))
        grads = da_in[...].reshape(lane_units, pair_width)
        totals = [None, None, None]
        slope_total = jnp.zeros((1, 1), WIDE)
        for micro in range(micros):
            mask = lanes_of(micro)
            own_grads = grads * mask
            probability = probs[micro]
            grad_prob = contract(own_grads, values, 1, 1)
            scaled = probability * grad_prob
            score = scaled - probability * over_last(jnp.sum, scaled)
            low_score = score.astype(LOW)
            gap = distances().astype(WIDE)
            slope_total = slope_total - jnp.sum(
                jnp.sum(low_score.astype(WIDE) * gap, axis=0, keepdims=True), axis=1, keepdims=True
            )
            terms = (
                contract(low_score, keys * mask, 1, 0) * 0.125,
                contract(low_score, queries * mask, 0, 0) * 0.125,
                contract(probability.astype(LOW), own_grads, 0, 0),
            )
            totals = [term if total is None else total + term for total, term in zip(totals, terms)]
        for part in range(3):
            dq_out[:, part * units : (part + 1) * units, :] = (
                totals[part].astype(LOW).reshape(count, units, pair_width)
            )
        spread("dq", dq_out, dq_in)
        places = lax.broadcasted_iota(jnp.int32, (1, features), 1)
        sums[4:5, :] = jnp.where(places == s, slope_total, 0.0)
        sums[5:8, :] = jnp.zeros((3, features), WIDE)

    def back_project():
        gather_up("dq", dq_in.at[0 : count - 1])
        for part in range(3):
            for pair in range(heads // 2):
                begin = part * features + pair * pair_width
                first, second = from_heads(dq_in, pair, part * units)
                d_qkv[0:units, begin : begin + pair_width] = first
                d_qkv[units:own, begin : begin + pair_width] = second
        exchange("eq", d_qkv)

    def back_one():
        total = None
        for part in range(3):
            for h in range(2):
                begin = part * features + h * half
                term = contract(d_qkv[0:own, begin : begin + half], w[3 + part, h], 1, 1)
                total = term if total is None else total + term
        value = res_grad[...] + back_normal(total, 0, hat_one, root_one)
        d_pool[0:own] = value.astype(LOW)
        exchange("ed1", d_pool)

    def back_pieces():
        for r in range(3):
            value = contract(d_pool[0:own, 0:half], w[r, 0], 1, 1)
            value = value + contract(d_pool[0:own, half:features], w[r, 1], 1, 1)
            for micro in range(micros):
                part = value[micro * units : (micro + 1) * units]
                if r < 2:
                    part = jnp.where(kept(micro), part, 0.0)
                for tile in tiles:
                    wide_grad[micro, tile, pl.ds(6 + r, units, stride=3), :] = part[:, columns_at(tile)]
        send("ed", wide_grad.at[:, :, 0:8], edge_in, (b, lax.rem(s + count - 1, count)))

    def finish_grad():
        flying["ed"].wait_recv()
        inside = (s < count - 1).astype(WIDE)
        for micro in range(micros):
            for tile in tiles:
                columns = columns_at(tile)
                wide_grad[micro, tile, 6 + tokens : 8 + tokens, :] = edge_in[micro, tile, 6:8, :] * inside
                grad[micro, :, columns] = cot[micro, :, columns].astype(WIDE) + wide_grad[micro, tile, 8 : 8 + tokens]
        outs[1].start()

    plan.add(
        "bq", back_short_away, [("tz", 5, r) for r in range(3)] + have[5], (), [("dx", "x", own * features * 2)], 0.6, rank=2
    )
    plan.add("bh", back_short_here, ["cot", *have[5]], (), (), 0.6, rank=3)
    plan.add("bs", back_short, ["bq", "bh"], ["dx"], [shared("el", features)], 0.1, rank=3)
    for j in range(hidden_blocks):
        last = j == hidden_blocks - 1
        plan.add(
            ("bw", j), back_widen(j),
            ["bs", *have[3], ("wi", j)] + ([("bw", i) for i in range(j)] if last else []), (),
            [shared("ei", hidden_width)] if last else (), 0.35, rank=4,
        )
    plan.add(
        "b2", back_two, [("bw", j) for j in range(hidden_blocks)] + [*have[3]], (),
        [shared("er", features)], 0.9, rank=4,
    )
    plan.add("bo", back_out, ["b2", *have[2]], (), spread_sends("da", units), 0.45, rank=4)
    plan.add("ba", back_attend, ["bo", "at"], spread_names("da"), spread_sends("dq", 3 * units), 1.4, rank=4)
    plan.add("bp", back_project, ["ba"], spread_names("dq"), [shared("eq", 3 * features)], 0.2, rank=4)
    plan.add("b1", back_one, ["bp"], (), [shared("ed1", features)], 0.75, rank=4)
    plan.add("bx", back_pieces, ["b1"], (), [("ed", "f", 2 * 8 * features * 4)], 0.65, rank=9)
    plan.add("fg", finish_grad, ["bx", "cot"], ["ed"], (), 0.3, rank=9)

    fixes = (1.0 - beta_one**STEP, 1.0 - beta_two**STEP)

    def finish_small(total):
        for begin, values in ((0, gain), (2, bias)):
            rows = slice(begin, begin + 2)
            new = adam_update(values[...], total[rows], norm_m[rows], norm_v[rows], *fixes, rate_norm, 0.0)
            for place, value in enumerate(new):
                small[4 * place + begin : 4 * place + begin + 2] = value
        new = adam_update(slope_row[...], total[4:5, 0:heads], slope_m[...], slope_v[...], *fixes, rate_slope, 0.0)
        for place, value in enumerate(new):
            small[12 + place : 13 + place, 0:heads] = value

    def fill_slots():
        lanes = lax.broadcasted_iota(jnp.int32, (1, features), 1)
        marks = jnp.zeros((1, features), WIDE)
        for slot in range(masters.shape[0]):
            block, mark, base = jnp.int32(0), jnp.float32(0), 0
            for matrix_id, size in enumerate(sizes):
                begin = start_of(owners, matrix_id, sizes)
                inside = (owners[matrix_id] == b) & (slot >= begin) & (slot < begin + size)
                block = jnp.where(inside, base + slot - begin, block)
                mark = jnp.where(inside, 1.0, mark)
                base += size
            slot_grads[slot] = red[block]
            marks = jnp.where(lanes == slot, mark, marks)
        small[15:16, :] = marks

    def add_pair(step, device):
        def run():
            if step > 0:
                flying[("s", step - 1)].wait_recv()
                sums[8 * step : 8 * step + 8] = sums[8 * step - 8 : 8 * step] + sums_in[8 * step - 8 : 8 * step]
            if device is not None:
                send(("s", step), sums.at[8 * step : 8 * step + 8], sums_in.at[8 * step : 8 * step + 8], device)
            else:
                finish_small(sums[8 * step : 8 * step + 8])

        return run

    partners = [
        core_peer,
        x_peer,
        (b, 2 * z + 1 - y),
        (b, 2 * (z + 1 - 2 * (z % 2)) + y),
        (b, 2 * lax.rem(z + 2, 4) + y),
        None,
    ]
    for step, device in enumerate(partners):
        plan.add(
            ("sum", step), add_pair(step, device), ["b1", "ba"] if step == 0 else [("sum", step - 1)],
            [("s", step - 1)] if step else (), [(("s", step), "f", 8 * features * 4)] if device is not None else (), 0.1,
            rank=0,
        )

    for name, columns in (
        ("ep", "pc"), ("en", "po"), ("ea", "me"), ("et", "ou"), ("ec", ("wi", hidden_blocks - 1)),
        ("es", "na"), ("eu", "cot"), ("el", "bs"), ("ei", ("bw", hidden_blocks - 1)),
        ("er", "b2"), ("eq", "bp"), ("ed1", "b1"),
    ):
        plan.add(("got", name), arrive(name), [columns], [name], cost=0.02)

    def columns_of(block):
        return pl.ds(pl.multiple_of(block * features + c * half, half), half)

    def outer(block, left, left_block, right, right_block):
        def run():
            rows = left[:, left_block * features : (left_block + 1) * features]
            g[block] = contract(rows, right[:, columns_of(right_block)], 0, 0).astype(LOW)

        return run

    def send_either(name, first_source, second_source, target):
        copies = [describe(source, target, x_peer, name) for source in (first_source, second_source)]
        launch(name, copies, [lambda plane=plane: pl.when(x == plane)(copies[plane].start) for plane in range(2)], name)

    def near_away():
        send_either("sn", d_low.at[0:own], x_two.at[0:own], x_near.at[0:own])

    def near_core():
        arrive("sn")()
        exchange("cn", x_near)

    def wide_away(j):
        columns = slice(j * features, (j + 1) * features)

        def run():
            source = (x_act.at[0:own, columns], d_inner.at[0:own, columns])
            send_either(("sw", j), *source, x_wide.at[0:own, columns])

        return run

    def wide_core(j):
        columns = slice(j * features, (j + 1) * features)

        def run():
            arrive(("sw", j))()
            send(("cw", j), x_wide.at[0:own, columns], x_wide.at[own : 2 * own, columns], core_peer)

        return run

    def outer_split(j):
        columns = slice(j * features, (j + 1) * features)

        def run():
            @pl.when(x == 0)
            def _():
                total = contract(x_two[...], d_inner[:, columns_of(j)], 0, 0)
                g[in_base + j] = (total + contract(x_near[...], x_wide[:, columns_of(j)], 0, 0)).astype(LOW)

            @pl.when(x == 1)
            def _():
                total = contract(x_act[:, columns], d_low[:, my_half], 0, 0)
                g[back_base + j] = (total + contract(x_wide[:, columns], x_near[:, my_half], 0, 0)).astype(LOW)

        return run

    lump = own * features * 2
    plan.add("sn", near_away, ["bs", "ou"], (), [("sn", "x", lump)], 0.05, 2)
    plan.add("nc", near_core, ["sn"], ["sn"], [("cn", "c", lump)], 0.05, 2)
    plan.add(("got", "cn"), arrive("cn"), ["nc"], ["cn"], (), 0.02, 2)
    for j in range(hidden_blocks):
        plan.add(("sw", j), wide_away(j), [("wi", j), ("bw", j)], (), [(("sw", j), "x", lump)], 0.05, 2)
        plan.add(("wc", j), wide_core(j), [("sw", j)], [("sw", j)], [(("cw", j), "c", lump)], 0.05, 2)
        plan.add(("got", "cw", j), arrive(("cw", j)), [("wc", j)], [("cw", j)], (), 0.02, 2)
        deps = [("got", e) for e in ("et", "ec", "el", "ei", "cn")] + [("got", "cw", j)]
        plan.add(("gr", j, "s"), outer_split(j), deps, cost=0.6, rank=4.5)
    quartered = {
        0: (x_pool, 3, d_pool, 1, "pc", "b1", "ep", "ed1"),
        1: (x_norm, 1, d_qkv, 3, "po", "bp", "en", "eq"),
        2: (x_att, 1, d_res, 1, "me", "b2", "ea", "er"),
        5: (x_short, 1, d_up, 3, "na", "cot", "es", "eu"),
    }
    quartered = {k: quartered[k] for k in QUARTERS}

    def left_away(k, j):
        columns = slice(j * features, (j + 1) * features)

        def run():
            send(("tx", k, j), quartered[k][0].at[0:own, columns], t_left.at[QUARTERS[k] + j, 0:own], x_peer)

        return run

    def left_core(k, j):
        place = QUARTERS[k] + j

        def run():
            arrive(("tx", k, j))()
            send(("tc", k, j), t_left.at[place, 0:own], t_left.at[place, own : 2 * own], core_peer)

        return run

    def right_away(k, r):
        place = QUARTERS[k] + r

        def run():
            for core in range(2):
                begin = r * features + core * half + (1 - x) * quarter
                t_out[place, :, core * quarter : (core + 1) * quarter] = quartered[k][2][
                    0:own, pl.ds(pl.multiple_of(begin, quarter), quarter)
                ]
            if k == 5:
                send(("ty", k, r), t_out.at[place], t_in.at[place, 0:own], x_peer)
                return
            lanes = [pl.ds(pl.multiple_of(core * quarter, quarter), quarter) for core in (c, 1 - c)]
            send(("ty", k, r), t_out.at[place, :, lanes[0]], t_in.at[place, 0:own, 0:quarter], x_peer, ("ty", k, r))
            send(("tu", k, r), t_out.at[place, :, lanes[1]], t_in.at[place, own : 2 * own, 0:quarter], cross_peer, ("ty", k, r))

        return run

    def right_core(k, r):
        place = QUARTERS[k] + r

        def run():
            arrive(("ty", k, r))()
            send(("td", k, r), t_in.at[place, 0:own], t_in.at[place, own : 2 * own], core_peer)

        return run

    def outer_quarter(k, j, r):
        def run():
            left, _, right = quartered[k][:3]
            near = pl.ds(pl.multiple_of(r * features + c * half + x * quarter, quarter), quarter)
            away = pl.ds(pl.multiple_of(c * quarter, quarter), quarter) if k == 5 else slice(0, quarter)
            total = contract(left[:, j * features : (j + 1) * features], right[:, near], 0, 0)
            total = total + contract(t_left[QUARTERS[k] + j], t_in[QUARTERS[k] + r, :, away], 0, 0)
            g[spans[k][0] + j + r, :, plane_span] = total.astype(LOW)

        return run

    for k, (_, lefts, _, rights, left_dep, right_dep, left_got, right_got) in quartered.items():
        urgency = 3.5 if k == 0 else 2.5
        for j in range(lefts):
            plan.add(("tx", k, j), left_away(k, j), [left_dep] + list(AFTER.get(k, ())), (), [(("tx", k, j), "x", lump)], 0.05, urgency)
            plan.add(("tw", k, j), left_core(k, j), [("tx", k, j)], [("tx", k, j)], [(("tc", k, j), "c", lump)], 0.05, urgency)
            plan.add(("got", "tc", k, j), arrive(("tc", k, j)), [("tw", k, j)], [("tc", k, j)], (), 0.02, urgency)
        for r in range(rights):
            if k != 5:
                parts = [("ty", k, r), ("tu", k, r)]
                whole = t_in.at[QUARTERS[k] + r, :, 0:quarter]
                plan.add(parts[0], right_away(k, r), [right_dep], (), [(p, "x", lump // 4) for p in parts], 0.1, 2.5)
                take = lambda k=k, r=r, whole=whole: gather_up(("ty", k, r), whole)
                plan.add(("got", "td", k, r), take, parts[:1], parts, (), 0.02, 2.5)
                continue
            plan.add(("ty", k, r), right_away(k, r), [right_dep], (), [(("ty", k, r), "x", lump // 2)], 0.05, 2.5)
            plan.add(("tz", k, r), right_core(k, r), [("ty", k, r)], [("ty", k, r)], [(("td", k, r), "c", lump // 2)], 0.05, 2.5)
            plan.add(("got", "td", k, r), arrive(("td", k, r)), [("tz", k, r)], [("td", k, r)], (), 0.02, 2.5)
        for j in range(lefts if k not in WHOLE else 0):
            for r in range(rights):
                deps = [("got", left_got), ("got", right_got), ("got", "tc", k, j), ("got", "td", k, r)]
                plan.add(("gr", spans[k][0] + j + r), outer_quarter(k, j, r), deps, cost=0.4, rank=5)
    weight_grads = []
    for r in range(3):
        for k, left, left_block, right, right_block, deps in (
            (0, x_pool, r, d_pool, 0, ("ep", "ed1")), (1, x_norm, 0, d_qkv, r, ("en", "eq")),
            (2, x_att, 0, d_res, 0, ("ea", "er")), (5, x_short, 0, d_up, r, ("es", "eu")),
        ):
            if (k in WHOLE or k not in QUARTERS) and r < sizes[k]:
                deps = [("got", dep) for dep in deps]
                weight_grads.append((spans[k][0] + r, left, left_block, right, right_block, deps))
    for block, left, left_block, right, right_block, deps in weight_grads:
        plan.add(("gr", block), outer(block, left, left_block, right, right_block), deps, cost=0.3, rank=5)

    def scatter_chunk(rank, name, here, there, size, deps):
        split, quarters = there is not None, there is here
        blocks = pl.ds(here, size)
        load = size * piece_bytes // (2 if quarters else 1)
        away, span, away_span, length_out = blocks, slice(None), slice(None), half
        begin_out, away_out = c * half, c * half
        if quarters:
            span, away_span = plane_span, plane_away
            length_out, begin_out, away_out = quarter, c * half + x * quarter, c * half + (1 - x) * quarter
        elif split:
            away = pl.ds(there, size)
        out_span = pl.ds(pl.multiple_of(begin_out, length_out), length_out)
        out_away = pl.ds(pl.multiple_of(away_out, length_out), length_out)

        half_rows = rows_of // 2
        sides = (("R", 0, right_in, right_peer), ("L", half_rows, left_in, left_peer))

        def first_step():
            for side, part, inbox, peer in sides:
                source = g.at[blocks, rows_at(4, part, half_rows), span]
                target = inbox.at[0, blocks, part : part + half_rows, span]
                send((side, "s", 1, name), source, target, peer, ("s", 1, name))

        def take(step):
            gather_up(("s", step, name), g.at[blocks, 0 : rows_of * (1 if step == 1 else 2), span])

        def next_step(step):
            def run():
                take(step - 1)
                for side, half_part, inbox, peer in sides:
                    offset = (5 - step) if side == "R" else (step - 5)
                    part, length = (half_part, half_rows) if step == 2 else (0, rows_of)
                    rows = rows_at(offset, part, length)
                    g[blocks, rows, span] = g[blocks, rows, span] + inbox[step - 2, blocks, part : part + length, span]
                    source = g.at[blocks, rows_at(offset), span]
                    send((side, "s", step, name), source, inbox.at[step - 1, blocks, :, span], peer, ("s", step, name))

            return run

        def finish():
            take(4)
            total = g[blocks, rows_at(0), span].astype(WIDE)
            total = total + right_in[3, blocks, :, span].astype(WIDE) + left_in[3, blocks, :, span].astype(WIDE)
            fin_out[blocks, :, span] = total.astype(LOW)
            send(("rx", name), fin_out.at[blocks, :, span], fin_in.at[blocks, :, span], x_peer)
            if quarters:
                send(("rd", name), fin_out.at[blocks, :, span], co_in.at[blocks, :, span], cross_peer, ("rc", name))
            if split:
                send(("rc", name), fin_out.at[blocks, :, span], co_in.at[blocks, :, span], core_peer)
                red[blocks, :, out_span] = fin_out[blocks, :, span]

        def finish_x():
            arrive(("rx", name))()
            if split:
                red[away, :, out_away] = fin_in[away, :, away_span]
                if not quarters:
                    send(("rd", name), fin_in.at[away, :, away_span], co_in.at[away, :, away_span], core_peer)
            else:
                total = (fin_out[blocks].astype(WIDE) + fin_in[blocks].astype(WIDE)).astype(LOW)
                co_out[blocks] = total
                red[blocks, :, my_half] = total
                send(("rc", name), co_out.at[blocks], co_in.at[blocks], core_peer)

        def finish_core():
            if quarters:
                gather_up(("rc", name), co_in.at[blocks])
            else:
                arrive(("rc", name), *([("rd", name)] if split else []))()
            red[blocks, :, other_half] = co_in[blocks]
            if split and not quarters:
                red[away, :, other_half] = co_in[away]

        links = (("R", "r"), ("L", "l"))
        out = [((side, "s", 1, name), link, load // 2) for side, link in links]
        plan.add(("r", 1, name), first_step, deps, (), out, 0.05, rank)
        for step in (2, 3, 4):
            waits = [(side, "s", step - 1, name) for side in "RL"]
            out = [((side, "s", step, name), link, load) for side, link in links]
            plan.add(("r", step, name), next_step(step), [("r", step - 1, name)], waits, out, 0.04 * size, rank)
        own_out = [(("rc", name), "c", load)]
        plan.add(
            ("fi", name), finish, [("r", 4, name)], [("R", "s", 4, name), ("L", "s", 4, name)],
            [(("rx", name), "x", load)] + (own_out if split else []) + ([(("rd", name), "x", load)] if quarters else []),
            0.02 * size, rank,
        )
        late_out = ([] if quarters else [(("rd", name), "c", load)]) if split else own_out
        plan.add(("fx", name), finish_x, [("fi", name)], [("rx", name)], late_out, 0.02 * size, rank)
        plan.add(
            ("fc", name), finish_core, [("fx", name)], [("rc", name)] + ([("rd", name)] if split else []), (), 0.02 * size, rank
        )

    for k, offset, size, rank in SCATTERS:
        name = ("g", k, offset)
        if k == 3:
            deps = [("gr", j, "s") for j in range(offset, offset + size)]
            scatter_chunk(rank, name, ours + offset, theirs + offset, size, deps)
        else:
            begin = spans[k][0] + offset
            scatter_chunk(rank, name, begin, begin if k in QUARTERS and k not in WHOLE else None, size, [("gr", begin + j) for j in range(size)])

    plan.add("mo", lambda: [copy.start() for copy in moments], ["pc"], (), (), 0.02, rank=8)
    plan.add("sl", fill_slots, ["mo"] + [("fc", ("g", k, offset)) for k, offset, _, _ in SCATTERS], (), (), 0.2, rank=9)
    for name, _ in plan.order():
        plan.tasks[name][0]()
    assert len(boxes) <= RECEIVES
    for copy in started[-SENDS:]:
        copy.wait_send()
    for copy in outs + moments:
        copy.wait()


def adam_kernel(refs):
    grads, small, master, first, second, mixed, grad = refs[:7]
    new_w, new_m, new_v, new_low, mixed_out, grad_out = refs[7:13]
    norm_outs, slope_outs = refs[13:16], refs[16:19]
    step = pl.program_id(0)
    fixes = (1.0 - beta_one**STEP, 1.0 - beta_two**STEP)
    rows = mixed_out.shape[0]
    part = pl.ds(pl.multiple_of(step * rows, 8), rows)
    mixed_out[...] = mixed[part]
    grad_out[...] = grad[part]

    @pl.when(step == 0)
    def _():
        heads = slope_outs[0].shape[1]
        for place in range(3):
            norm_outs[place][...] = small[4 * place : 4 * place + 4]
            slope_outs[place][...] = small[12 + place : 13 + place, 0:heads]

    count = new_w.shape[0]
    lanes = lax.broadcasted_iota(jnp.int32, (1, small.shape[1]), 1)
    for place in range(count):
        slot = step * count + place
        old = (master[slot], first[slot], second[slot])
        values = adam_update(old[0], grads[slot].astype(WIDE), old[1], old[2], *fixes, rate_matrix, decay_rate)
        mark = jnp.sum(jnp.where(lanes == slot, small[15:16, :], 0.0), axis=1, keepdims=True)
        keep = jnp.broadcast_to(mark, old[0].shape) > 0.5
        weight, new_m[place], new_v[place] = (jnp.where(keep, new, was) for new, was in zip(values, old))
        new_w[place] = weight
        new_low[place] = weight.astype(LOW)


def fused_body(tokens, cotangent, doc_lengths, owners, master, first_moment, second_moment, ln_gain, ln_bias, norm_m, norm_v, slopes, slope_m, slope_v):
    micros, _, tok_rows, features = tokens.shape
    units, heads, width = tok_rows // 3, slopes.shape[0], features // slopes.shape[0]
    sizes = tuple(block_counts(features, FF))
    blocks, own, half = sum(sizes), micros * units, features // 2
    slots, rows = master.shape[1], master.shape[2]
    lane_units = units * heads
    split = features // TILE
    hbm, vmem, anywhere = (pl.BlockSpec(memory_space=m) for m in (pltpu.HBM, pltpu.VMEM, pl.ANY))
    low = lambda *shape: pltpu.VMEM(shape, LOW)
    wide = lambda *shape: pltpu.VMEM(shape, WIDE)
    pieces = lambda: low(blocks, rows, half)
    both = lambda columns: low(2 * own, columns)
    scratch = [
        pltpu.SMEM(owners.shape, jnp.int32), pltpu.SMEM((micros, doc_lengths.shape[2]), jnp.int32),
        pltpu.SMEM(slopes.shape, WIDE), wide(2, features), wide(2, features), wide(4, features), wide(4, features),
        wide(1, heads), wide(1, heads), wide(1, heads),
        low(blocks, 2, features, half), low(blocks, rows, features), low(rows, half), pieces(), pieces(), pieces(), pieces(), pieces(),
        low(micros, tok_rows, features), low(micros, tok_rows, features), low(micros, 16, features),
        wide(micros, split, 16 + tok_rows, TILE), wide(micros, split, tok_rows, TILE),
        both(3 * features), both(features), both(features), both(features), both(FF), both(features),
        both(3 * features), both(features), both(FF), both(features), both(3 * features), both(features),
        wide(own, features), wide(own, features), wide(own, features), wide(own, 1), wide(own, 1),
        wide(own, features), wide(own, FF), wide(own, features), wide(own, features),
        low(heads, 3 * units, 2 * width), low(heads, 3 * units, 2 * width), low(heads, units, 2 * width),
        low(heads, units, 2 * width), low(heads, units, 2 * width), low(heads, units, 2 * width),
        low(heads, 3 * units, 2 * width), low(heads, 3 * units, 2 * width),
        wide(micros, lane_units, lane_units), wide(micros, tok_rows, features), wide(micros, tok_rows, features),
        wide(micros, split, tok_rows, TILE), wide(micros, split, 8 + tok_rows, TILE), wide(micros, split, 8, TILE),
        low(2 * own, features), low(2 * own, FF),
        low(10, 2 * own, features), low(10, own, half), low(10, 2 * own, half),
        low(own, 3 * half), low(own, 3 * half), low(own, features), low(own, features), low(blocks, features, half), low(4, blocks, rows, half), low(4, blocks, rows, half),
        pieces(), pieces(), pieces(), pieces(), wide(48, features), wide(40, features),
        pltpu.SemaphoreType.DMA((SENDS,)), pltpu.SemaphoreType.DMA((RECEIVES,)), pltpu.SemaphoreType.DMA((17,)),
    ]
    token_shape = (micros, tok_rows, features)
    dims = (units, features, FF, heads, micros, sizes)
    moment_shape = jax.ShapeDtypeStruct((slots, rows, features), WIDE)
    mixed, grad, grads, small, weights, firsts, seconds = pl.pallas_call(
        lambda *refs: main_kernel(dims, refs),
        out_shape=(
            jax.ShapeDtypeStruct(token_shape, WIDE),
            jax.ShapeDtypeStruct(token_shape, WIDE),
            jax.ShapeDtypeStruct((slots, rows, features), LOW),
            jax.ShapeDtypeStruct((16, features), WIDE),
            moment_shape, moment_shape, moment_shape,
        ),
        in_specs=[hbm] * 15,
        out_specs=(anywhere, anywhere) + (vmem,) * 5,
        scratch_shapes=scratch,
        compiler_params=pltpu.CompilerParams(
            collective_id=0, has_side_effects=True, vmem_limit_bytes=47 * 2**20
        ),
        name="block",
    )(*[pltpu.with_memory_space_constraint(value, pltpu.HBM) for value in (
        owners, doc_lengths[:, 0], slopes, ln_gain, ln_bias, norm_m, norm_v, slopes[None], slope_m[None], slope_v[None],
        tokens[:, 0], cotangent[:, 0], master[0], first_moment[0], second_moment[0],
    )])
    steps = 2
    flat = (micros * tok_rows, features)
    slot = pl.BlockSpec((slots // steps, rows, features), lambda j: (j, 0, 0))
    some = pl.BlockSpec((flat[0] // steps, features), lambda j: (j, 0))
    norm_shape = jax.ShapeDtypeStruct((4, features), WIDE)
    slope_shape = jax.ShapeDtypeStruct((1, heads), WIDE)
    out = pl.pallas_call(
        lambda *refs: adam_kernel(refs),
        grid=(steps,),
        out_shape=(
            moment_shape, moment_shape, moment_shape, jax.ShapeDtypeStruct((slots, rows, features), LOW),
            jax.ShapeDtypeStruct(flat, WIDE), jax.ShapeDtypeStruct(flat, WIDE),
            norm_shape, norm_shape, norm_shape, slope_shape, slope_shape, slope_shape,
        ),
        in_specs=[vmem] * 7,
        out_specs=(slot, slot, slot, slot, some, some) + (vmem,) * 6,
        compiler_params=pltpu.CompilerParams(dimension_semantics=("arbitrary",), vmem_limit_bytes=12 * 2**20),
        name="adam",
    )(grads, small, weights, firsts, seconds, mixed.reshape(flat), grad.reshape(flat))
    new_w, new_m, new_v, new_low, mixed, grad, norm, norm_m, norm_v, slope, slope_m, slope_v = out
    return (
        mixed.reshape(tokens.shape), grad.reshape(tokens.shape), new_w[None], new_m[None], new_v[None], new_low[None], norm, norm_m, norm_v,
        slope[0], slope_m[0], slope_v[0],
    )


def fits(mesh, shapes):
    return mesh.shape["batch"] == 4 and mesh.shape["seq"] == 8 and shapes[0].shape[1] == 1


def solution(mesh):
    in_specs = (
        P("batch", None, "seq", None),
        P("batch", None, "seq", None),
        P("batch", None, None),
        P(),
        P("batch", None, "seq", None),
        P("batch", None, "seq", None),
        P("batch", None, "seq", None),
        P(),
        P(),
        P(),
        P(),
        P(),
        P(),
        P(),
    )
    out_specs = (
        P("batch", None, "seq", None),
        P("batch", None, "seq", None),
        P("batch", None, "seq", None),
        P("batch", None, "seq", None),
        P("batch", None, "seq", None),
        P("batch", None, "seq", None),
        P(),
        P(),
        P(),
        P(),
        P(),
        P(),
    )

    def whole(*args):
        part = fused_body if fits(mesh, args) else body
        return jax.shard_map(
            part, mesh=mesh, in_specs=in_specs, out_specs=out_specs, check_vma=False
        )(*args)

    return whole
```
